32 devices in a mesh: seq: 8 (over y, x, core), fsdp: 4 (over z).
Axes of the slice: x: 2, y: 2, z: 4, core: 2. Of those that a mesh axis runs over, the one named last changes fastest.
Arguments:
- frames: bfloat16 [4, 1024, 1024], P('fsdp', 'seq'), may hold values from -6 to 6
- lengths: int32 [4, 4], P('fsdp'), may hold values from 1 to 897, as said below
- up_first: bfloat16 [1024, 4096], P('fsdp'), may hold values from -0.1875 to 0.1875
- down_first: bfloat16 [4096, 1024], P('fsdp'), may hold values from -0.09375 to 0.09375
- joint_qkv: bfloat16 [1024, 3072], P('fsdp'), may hold values from -0.1875 to 0.1875
- attn_out: bfloat16 [1024, 1024], P('fsdp'), may hold values from -0.75 to 0.75
- conv_in: bfloat16 [1024, 2048], P('fsdp'), may hold values from -0.1875 to 0.1875
- conv_kernel: bfloat16 [5, 1024], P(None, 'fsdp'), may hold values from -2.5 to 2.5
- batch_gain: bfloat16 [1024], P('fsdp'), may hold values from 0.5 to 1.5
- conv_out: bfloat16 [1024, 1024], P('fsdp'), may hold values from -0.1875 to 0.1875
- up_second: bfloat16 [1024, 4096], P('fsdp'), may hold values from -0.1875 to 0.1875
- down_second: bfloat16 [4096, 1024], P('fsdp'), may hold values from -0.09375 to 0.09375
- norm_gains: bfloat16 [5, 1024], P(None, 'fsdp'), may hold values from 0.5 to 1.5
- slopes: float32 [8], replicated, may hold values from 0.0005 to 0.05
- out_grad: bfloat16 [4, 1024, 1024], P('fsdp', 'seq'), may hold values from -6 to 6
Outputs:
- output: bfloat16 [4, 1024, 1024], P('fsdp', 'seq')
- frames_grad: float32 [4, 1024, 1024], P('fsdp', 'seq')
- up_first_grad: float32 [1024, 4096], P(('seq', 'fsdp'))
- down_first_grad: float32 [4096, 1024], P(('seq', 'fsdp'))
- joint_qkv_grad: float32 [1024, 3072], P(('seq', 'fsdp'))
- attn_out_grad: float32 [1024, 1024], P(('seq', 'fsdp'))
- conv_in_grad: float32 [1024, 2048], P(('seq', 'fsdp'))
- conv_kernel_grad: float32 [5, 1024], P(None, ('seq', 'fsdp'))
- batch_gain_grad: float32 [1024], P(('seq', 'fsdp'))
- conv_out_grad: float32 [1024, 1024], P(('seq', 'fsdp'))
- up_second_grad: float32 [1024, 4096], P(('seq', 'fsdp'))
- down_second_grad: float32 [4096, 1024], P(('seq', 'fsdp'))
- norm_gains_grad: float32 [5, 1024], P(None, ('seq', 'fsdp'))
- slopes_grad: float32 [8], replicated
The draws below stay inside these ranges and needn't reach their ends.
Inputs may be any that keep to these rules, and one draw needn't show every extreme that they name: `lengths`: in each bucket one utterance, at a place drawn from the seed, has exactly 897 frames; each other one has at most 32 frames; the frames past the last utterance are padding.
All inputs are finite; a program needn't handle non-finite values.
Results may differ from the reference program's by a relative error of at most 0.025.
Values may be sent and summed in bfloat16 or wider, within the bound.
A program may use at most 448 MiB of HBM per device.

```python
import math
import jax
import jax.numpy as jnp
from jax import lax

D = 1024
FF = 4096
HEADS = 8
HD = 128
KW = 5
ITEMS = 4
TOK_DEV = 128
BUCKETS = 4
FRAMES = 1024


def draw_lengths(key, part):
    key = jax.random.fold_in(key, 11)
    short_key, place_key = jax.random.split(key)
    shorts = jax.random.randint(short_key, (BUCKETS, ITEMS), 1, TOK_DEV // 4 + 1)
    place = jax.random.randint(place_key, (BUCKETS, 1), 0, ITEMS)
    columns = jnp.arange(ITEMS, dtype=jnp.int32)[None, :]
    return jnp.where(columns == place, FRAMES - TOK_DEV + 1, shorts).astype(jnp.int32)


def block_scale(rng, shape, shards, least, top_value):
    level = 1.0
    for position, parts in shards:
        steps = jax.random.uniform(jax.random.fold_in(jax.random.fold_in(rng, 6), position), (parts,), jnp.float32, least / len(shards), top_value / len(shards))
        level = level * jnp.repeat(jnp.exp(steps), shape[position] // parts).reshape((-1,) + (1,) * (len(shape) - 1 - position))
    return level


def normal_values(own_key, shape, scale, limit, pieces=(), kind=jnp.bfloat16):
    values = jax.random.normal(own_key, shape, jnp.float32) * scale
    if len(pieces) > 0:
        values = block_scale(own_key, shape, pieces, -0.22, 0.18) * values
    return jnp.clip(values, min=-limit, max=limit).astype(kind)


def setup_inputs(seed: int = 0) -> dict:
    arg_keys = jax.random.split(jax.random.key(seed), 16)
    return {
        "frames": normal_values(arg_keys[0], (BUCKETS, FRAMES, D), 1.0, 6.0, ((0, 4), (1, 8))),
        "lengths": draw_lengths(jax.random.fold_in(arg_keys[15], 71), 0),
        "up_first": normal_values(arg_keys[2], (D, FF), D ** -0.5, 0.1875, ((0, 4),)),
        "down_first": normal_values(arg_keys[3], (FF, D), FF ** -0.5, 0.09375, ((0, 4),)),
        "joint_qkv": normal_values(arg_keys[4], (D, 3 * D), D ** -0.5, 0.1875, ((0, 4),)),
        "attn_out": normal_values(arg_keys[5], (D, D), (D // 16) ** -0.5, 0.75, ((0, 4),)),
        "conv_in": normal_values(arg_keys[6], (D, 2 * D), D ** -0.5, 0.1875, ((0, 4),)),
        "conv_kernel": normal_values(arg_keys[7], (KW, D), KW ** -0.5, 2.5, ((1, 4),)),
        "batch_gain": jnp.clip(1.0 + 0.1 * jax.random.normal(arg_keys[8], (D,), jnp.float32), 0.5, 1.5).astype(jnp.bfloat16),
        "conv_out": normal_values(arg_keys[9], (D, D), D ** -0.5, 0.1875, ((0, 4),)),
        "up_second": normal_values(arg_keys[10], (D, FF), D ** -0.5, 0.1875, ((0, 4),)),
        "down_second": normal_values(arg_keys[11], (FF, D), FF ** -0.5, 0.09375, ((0, 4),)),
        "norm_gains": jnp.clip(1.0 + 0.1 * jax.random.normal(arg_keys[12], (5, D), jnp.float32), 0.5, 1.5).astype(jnp.bfloat16),
        "slopes": jnp.clip(jnp.exp(jax.random.uniform(arg_keys[13], (HEADS,), jnp.float32, math.log(0.0005), math.log(0.05))), 0.0005, 0.05),
        "out_grad": normal_values(arg_keys[14], (BUCKETS, FRAMES, D), 1.0, 6.0, ((0, 4), (1, 8))),
    }


EPSILON = 1e-05
MASKED = -1e+30
HIGH = lax.Precision.HIGHEST

@jax.custom_vjp
def low(v):
    return lax.optimization_barrier(v.astype(jnp.bfloat16)).astype(jnp.float32)

@jax.custom_vjp
def low_back(v):
    return v

def low_keep(v):
    return (low(v), None)

def low_pass(kept, grad):
    return (grad,)

def back_keep(v):
    return (v, None)

def back_low(kept, grad):
    return (low(grad),)
low.defvjp(low_keep, low_pass)
low_back.defvjp(back_keep, back_low)

def normed(value, gain):
    average = lax.optimization_barrier(jnp.mean(value, axis=-1, keepdims=True))
    centred = value - average
    variance = lax.optimization_barrier(jnp.mean(centred * centred, axis=-1, keepdims=True))
    return centred * lax.rsqrt(variance + EPSILON) * gain

def matmul(left, right):
    return jnp.dot(left, right, precision=HIGH)

def feed_forward(value, gain, weight_up, weight_down):
    hidden = low(normed(value, gain))
    activation = low_back(matmul(hidden, weight_up))
    swish = low(jax.nn.silu(activation))
    return value + 0.5 * low_back(matmul(swish, weight_down))

def attention(value, gain, weight_qkv, weight_out, slopes, ids):
    hidden = low(normed(value, gain))
    joint = low(low_back(matmul(hidden, weight_qkv)))
    query = joint[:, :D].reshape(FRAMES, HEADS, HD)
    keys = joint[:, D:2 * D].reshape(FRAMES, HEADS, HD)
    values = joint[:, 2 * D:].reshape(FRAMES, HEADS, HD)
    span = min(512, FRAMES)
    positions = jnp.arange(FRAMES, dtype=jnp.int32)
    scale = 1.0 / math.sqrt(HD)

    def one_block(start):
        query_block = lax.dynamic_slice_in_dim(query, start, span, 0)
        query_pos = lax.dynamic_slice_in_dim(positions, start, span, 0)
        query_ids = lax.dynamic_slice_in_dim(ids, start, span, 0)
        raw_scores = low_back(jnp.einsum('qhd,khd->hqk', query_block, keys, precision=HIGH))
        distance = jnp.abs(query_pos[:, None] - positions[None, :]).astype(jnp.float32)
        scores = raw_scores * scale - slopes[:, None, None] * distance[None]
        shared = query_ids[:, None] == ids[None, :]
        scores = jnp.where(shared[None], scores, MASKED)
        exponent = jnp.exp(scores - lax.optimization_barrier(jnp.max(scores, axis=-1, keepdims=True)))
        probs = low(exponent / lax.optimization_barrier(jnp.sum(exponent, axis=-1, keepdims=True)))
        return jnp.einsum('hqk,khd->qhd', probs, values, precision=HIGH)
    starts = jnp.arange(FRAMES // span, dtype=jnp.int32) * span
    blocks = lax.map(jax.checkpoint(one_block), starts)
    mixed = low(low_back(blocks.reshape(FRAMES, D)))
    return value + low_back(matmul(mixed, weight_out))

def conv_front(value, gain, weight_in, kernel, ids):
    hidden = low(normed(value, gain))
    joint = low_back(matmul(hidden, weight_in))
    gated = low(joint[:, :D] * jax.nn.sigmoid(joint[:, D:]))
    rim_width = KW // 2
    padded = jnp.pad(gated, ((rim_width, rim_width), (0, 0)))
    padded_ids = jnp.pad(ids, rim_width, constant_values=-1)
    total = jnp.zeros((FRAMES, D), jnp.float32)
    for offset in range(KW):
        shared = (padded_ids[offset:offset + FRAMES] == ids).astype(jnp.float32)
        total = total + kernel[offset] * padded[offset:offset + FRAMES] * shared[:, None]
    return total

def forward(frames, up_first, down_first, joint_qkv, attn_out, conv_in, conv_kernel, batch_gain, conv_out, up_second, down_second, norm_gains, slopes, ids):

    def front(inputs):
        block, item_ids = inputs
        first = feed_forward(block, norm_gains[0], up_first, down_first)
        second = attention(first, norm_gains[1], joint_qkv, attn_out, slopes, item_ids)
        return (second, conv_front(second, norm_gains[2], conv_in, conv_kernel, item_ids))
    seconds, convs = lax.map(jax.checkpoint(front), (frames, ids))
    valid = (ids < ITEMS).astype(jnp.float32)[:, :, None]
    count = jnp.sum(valid)
    average = lax.optimization_barrier(jnp.sum(valid * convs, axis=(0, 1))) / count
    centred = convs - average
    variance = lax.optimization_barrier(jnp.sum(valid * centred * centred, axis=(0, 1))) / count
    inverse = lax.rsqrt(variance + EPSILON)

    def back_half(inputs):
        second, conv = inputs
        scaled = (conv - average) * inverse * batch_gain
        swish = low(jax.nn.silu(scaled))
        third = second + low_back(matmul(swish, conv_out))
        fourth = feed_forward(third, norm_gains[3], up_second, down_second)
        return normed(fourth, norm_gains[4])
    return lax.map(jax.checkpoint(back_half), (seconds, convs))

def reference(frames, lengths, up_first, down_first, joint_qkv, attn_out, conv_in, conv_kernel, batch_gain, conv_out, up_second, down_second, norm_gains, slopes, out_grad):
    bounds = jnp.cumsum(lengths, axis=1).astype(jnp.int32)
    positions = jnp.arange(FRAMES, dtype=jnp.int32)
    ids = lax.optimization_barrier(jnp.sum((positions[None, :, None] >= bounds[:, None, :]).astype(jnp.int32), axis=2))
    floats = [array.astype(jnp.float32) for array in (frames, up_first, down_first, joint_qkv, attn_out, conv_in, conv_kernel, batch_gain, conv_out, up_second, down_second, norm_gains)]
    floats.append(slopes.astype(jnp.float32))

    def wrapped(*arrays):
        return forward(*arrays, ids)
    result, pullback = jax.vjp(wrapped, *floats)
    grads = pullback(out_grad.astype(jnp.float32))
    return (result.astype(jnp.bfloat16), grads[0], grads[1], grads[2], grads[3], grads[4], grads[5], grads[6], grads[7], grads[8], grads[9], grads[10], grads[11], grads[12])
```

```python
import functools
import math

import jax
import jax.numpy as jnp
from jax import lax
from jax.experimental import pallas as pl
from jax.experimental.pallas import tpu as pltpu
from jax.sharding import PartitionSpec as P

EPSILON = 1e-05
MASKED = -1e30


def extended(x, sides, width):
    for axis, dim in sides:
        size, length = (lax.axis_size(axis), x.shape[dim])
        up = [(i, (i + 1) % size) for i in range(size - 1)]
        down = [(j, i) for i, j in up]
        last = lax.slice_in_dim(x, length - width, length, axis=dim)
        initial = lax.slice_in_dim(x, 0, width, axis=dim)
        before = lax.ppermute(last, axis, up)
        after = lax.ppermute(initial, axis, down)
        x = jnp.concatenate([before, x, after], axis=dim)
    return x


def normed(value, gain):
    average = jnp.mean(value, axis=-1, keepdims=True)
    centred = value - average
    variance = jnp.mean(centred * centred, axis=-1, keepdims=True)
    return centred * lax.rsqrt(variance + EPSILON) * gain


def norm_back(value, gain, gradient):
    pullback = jax.vjp(normed, value, gain)[1]
    return pullback(gradient)


def matmul(left, right):
    return jnp.dot(left, right, preferred_element_type=jnp.float32)


def transposed_left(left, right):
    return lax.dot_general(
        left, right, (((0,), (0,)), ((), ())), preferred_element_type=jnp.float32
    )


def transposed_right(left, right):
    return lax.dot_general(
        left, right, (((1,), (1,)), ((), ())), preferred_element_type=jnp.float32
    )


def item_index(positions, bounds):
    return jnp.sum((positions[:, None] >= bounds[None, :]).astype(jnp.int32), axis=1)


def unpack(weights):
    (
        first_up,
        first_down,
        qkv_full,
        out_full,
        conv_up,
        kernel_full,
        batch_full,
        conv_down,
        second_up,
        second_down,
        gains_full,
    ) = weights
    return (
        first_up,
        first_down,
        qkv_full,
        out_full,
        conv_up,
        kernel_full.astype(jnp.float32),
        batch_full.astype(jnp.float32),
        conv_down,
        second_up,
        second_down,
        gains_full.astype(jnp.float32),
    )


def feed_forward(value, gain, weight_up, weight_down):
    hidden = normed(value, gain).astype(jnp.bfloat16)
    swish = jax.nn.silu(matmul(hidden, weight_up)).astype(jnp.bfloat16)
    return value + 0.5 * matmul(swish, weight_down)


def feed_back(value, gain, weight_up, weight_down, gradient):
    hidden = normed(value, gain).astype(jnp.bfloat16)
    swish, pullback = jax.vjp(jax.nn.silu, matmul(hidden, weight_up))
    swish_low = swish.astype(jnp.bfloat16)
    branch_grad = (0.5 * gradient).astype(jnp.bfloat16)
    down_grad = transposed_left(swish_low, branch_grad)
    active_grad = pullback(transposed_right(branch_grad, weight_down))[0].astype(jnp.bfloat16)
    up_grad = transposed_left(hidden, active_grad)
    value_grad, gain_grad = norm_back(value, gain, transposed_right(active_grad, weight_up))
    return (gradient + value_grad, gain_grad, up_grad, down_grad)


def biased_scores(query_heads, key_heads, slopes, layout):
    query_pos, key_pos, query_ids, key_ids = layout
    raw_scores = jnp.einsum(
        "qhd,khd->hqk", query_heads, key_heads, preferred_element_type=jnp.float32
    )
    distance = jnp.abs(query_pos[:, None] - key_pos[None, :]).astype(jnp.float32)
    scores = (
        raw_scores * (1.0 / math.sqrt(query_heads.shape[2]))
        - slopes[:, None, None] * distance[None]
    )
    shared = query_ids[:, None] == key_ids[None, :]
    return (jnp.where(shared[None], scores, MASKED), distance)


def attention_probs(query, keys, slopes, layout):
    heads = slopes.shape[0]
    head_size = query.shape[1] // heads
    query_heads = query.reshape(query.shape[0], heads, head_size)
    key_heads = keys.reshape(keys.shape[0], heads, head_size)
    scores, distance = biased_scores(query_heads, key_heads, slopes, layout)
    top = jnp.max(scores, axis=-1, keepdims=True)
    exponent = jnp.exp(scores - top)
    total = jnp.sum(exponent, axis=-1, keepdims=True)
    probs = exponent / total
    return (probs, distance, query_heads, key_heads, top[:, :, 0], total[:, :, 0])


def attend(value, gain, weight_qkv, weight_out, slopes, layout):
    feature_width = value.shape[1]
    hidden = normed(value, gain).astype(jnp.bfloat16)
    joint = matmul(hidden, weight_qkv).astype(jnp.bfloat16)
    keys_values = lax.all_gather(joint[:, feature_width:], "seq", axis=0, tiled=True)
    probs, distance, query_heads, key_heads, top, total = attention_probs(
        joint[:, :feature_width], keys_values[:, :feature_width], slopes, layout
    )
    value_heads = keys_values[:, feature_width:].reshape(key_heads.shape)
    mixed = jnp.einsum(
        "hqk,khd->qhd", probs.astype(jnp.bfloat16), value_heads, preferred_element_type=jnp.float32
    )
    mixed = mixed.reshape(value.shape).astype(jnp.bfloat16)
    return (value + matmul(mixed, weight_out), keys_values)


def attend_back(value, gain, weight_qkv, weight_out, slopes, layout, keys_values, gradient):
    feature_width = value.shape[1]
    row_count = value.shape[0]
    hidden = normed(value, gain).astype(jnp.bfloat16)
    joint = matmul(hidden, weight_qkv).astype(jnp.bfloat16)
    probs, distance, query_heads, key_heads, top, total = attention_probs(
        joint[:, :feature_width], keys_values[:, :feature_width], slopes, layout
    )
    probs_low = probs.astype(jnp.bfloat16)
    value_heads = keys_values[:, feature_width:].reshape(key_heads.shape)
    mixed = jnp.einsum("hqk,khd->qhd", probs_low, value_heads, preferred_element_type=jnp.float32)
    mixed = mixed.reshape(value.shape).astype(jnp.bfloat16)
    branch_grad = gradient.astype(jnp.bfloat16)
    weight_out_grad = transposed_left(mixed, branch_grad)
    mixed_flat = transposed_right(branch_grad, weight_out).astype(jnp.bfloat16)
    mixed_grad = mixed_flat.reshape(query_heads.shape)
    prob_grad = jnp.einsum(
        "qhd,khd->hqk", mixed_grad, value_heads, preferred_element_type=jnp.float32
    )
    delta = jnp.sum(probs * prob_grad, axis=-1)
    score_grad = probs * (prob_grad - delta[:, :, None])
    slope_grad = -jnp.sum(score_grad * distance[None], axis=(1, 2))
    scale = 1.0 / math.sqrt(query_heads.shape[2])
    raw_grad = (score_grad * scale).astype(jnp.bfloat16)
    query_grad = jnp.einsum("hqk,khd->qhd", raw_grad, key_heads, preferred_element_type=jnp.float32)
    query_pos, key_pos, query_ids, key_ids = layout
    all_query, all_mixed = (
        lax.all_gather(joint[:, :feature_width], "seq", axis=0, tiled=True),
        lax.all_gather(mixed_flat, "seq", axis=0, tiled=True),
    )
    all_top, all_total, all_delta = (
        lax.all_gather(top, "seq", axis=1, tiled=True),
        lax.all_gather(total, "seq", axis=1, tiled=True),
        lax.all_gather(delta, "seq", axis=1, tiled=True),
    )
    heads = slopes.shape[0]
    head_size = query_heads.shape[2]
    all_query_heads = all_query.reshape(all_query.shape[0], heads, head_size)
    all_mixed_heads = all_mixed.reshape(all_query.shape[0], heads, head_size)
    own_keys = joint[:, feature_width : 2 * feature_width].reshape(row_count, heads, head_size)
    own_values = joint[:, 2 * feature_width :].reshape(row_count, heads, head_size)
    column_scores, column_distance = biased_scores(
        all_query_heads, own_keys, slopes, (key_pos, query_pos, key_ids, query_ids)
    )
    column_probs = jnp.exp(column_scores - all_top[:, :, None]) / all_total[:, :, None]
    column_prob_grad = jnp.einsum(
        "qhd,khd->hqk", all_mixed_heads, own_values, preferred_element_type=jnp.float32
    )
    column_score_grad = column_probs * (column_prob_grad - all_delta[:, :, None])
    column_raw = (column_score_grad * scale).astype(jnp.bfloat16)
    key_grad = jnp.einsum(
        "hqk,qhd->khd", column_raw, all_query_heads, preferred_element_type=jnp.float32
    )
    value_grad = jnp.einsum(
        "hqk,qhd->khd",
        column_probs.astype(jnp.bfloat16),
        all_mixed_heads,
        preferred_element_type=jnp.float32,
    )
    local_grad = jnp.concatenate(
        [key_grad.reshape(row_count, feature_width), value_grad.reshape(row_count, feature_width)],
        axis=1,
    )
    joint_grad = jnp.concatenate([query_grad.reshape(value.shape), local_grad], axis=1).astype(
        jnp.bfloat16
    )
    qkv_grad = transposed_left(hidden, joint_grad)
    input_grad, gain_grad = norm_back(value, gain, transposed_right(joint_grad, weight_qkv))
    return (gradient + input_grad, gain_grad, qkv_grad, weight_out_grad, slope_grad)


def gate_linear(joint):
    feature_width = joint.shape[1] // 2
    return joint[:, :feature_width] * jax.nn.sigmoid(joint[:, feature_width:])


def depthwise(rim, kernel, rim_ids, own_ids):
    row_count = own_ids.shape[0]
    total = jnp.zeros((row_count, rim.shape[1]), jnp.float32)
    for offset in range(kernel.shape[0]):
        shared = (rim_ids[offset : offset + row_count] == own_ids).astype(jnp.float32)
        total = (
            total
            + kernel[offset]
            * rim[offset : offset + row_count].astype(jnp.float32)
            * shared[:, None]
        )
    return total


def depthwise_back(rim, kernel, rim_ids, own_ids, conv_grad):
    row_count = own_ids.shape[0]
    reach = kernel.shape[0] - 1
    grad_rim = extended(conv_grad.astype(jnp.bfloat16), (("seq", 0),), reach // 2).astype(
        conv_grad.dtype
    )
    input_grad = jnp.zeros(conv_grad.shape, jnp.float32)
    kernel_rows = []
    for offset in range(kernel.shape[0]):
        shared = (rim_ids[offset : offset + row_count] == own_ids).astype(jnp.float32)[:, None]
        kernel_rows.append(
            jnp.sum(
                rim[offset : offset + row_count].astype(jnp.float32) * shared * conv_grad, axis=0
            )
        )
        mirror = reach - offset
        crossed = (rim_ids[mirror : mirror + row_count] == own_ids).astype(jnp.float32)[:, None]
        input_grad = input_grad + kernel[offset] * grad_rim[mirror : mirror + row_count] * crossed
    return (input_grad, jnp.stack(kernel_rows))


def body(
    frames,
    lengths,
    up_first,
    down_first,
    joint_qkv,
    attn_out,
    conv_in,
    conv_kernel,
    batch_gain,
    conv_out,
    up_second,
    down_second,
    norm_gains,
    slopes,
    out_grad,
):
    sharded = (
        up_first,
        down_first,
        joint_qkv,
        attn_out,
        conv_in,
        conv_kernel,
        batch_gain,
        conv_out,
        up_second,
        down_second,
        norm_gains,
    )
    gathered = (
        lax.all_gather(sharded[0], "fsdp", axis=0, tiled=True),
        lax.all_gather(sharded[1], "fsdp", axis=0, tiled=True),
        lax.all_gather(sharded[2], "fsdp", axis=0, tiled=True),
        lax.all_gather(sharded[3], "fsdp", axis=0, tiled=True),
        lax.all_gather(sharded[4], "fsdp", axis=0, tiled=True),
        lax.all_gather(sharded[5], "fsdp", axis=1, tiled=True),
        lax.all_gather(sharded[6], "fsdp", axis=0, tiled=True),
        lax.all_gather(sharded[7], "fsdp", axis=0, tiled=True),
        lax.all_gather(sharded[8], "fsdp", axis=0, tiled=True),
        lax.all_gather(sharded[9], "fsdp", axis=0, tiled=True),
        lax.all_gather(sharded[10], "fsdp", axis=1, tiled=True),
    )
    (
        first_up,
        first_down,
        qkv_full,
        out_full,
        conv_up,
        kernel,
        batch_scale,
        conv_down,
        second_up,
        second_down,
        gains,
    ) = unpack(gathered)
    row_count = frames.shape[1]
    feature_width = frames.shape[2]
    seq_count = lax.axis_size("seq")
    start_row = lax.axis_index("seq") * row_count
    bounds = jnp.cumsum(lengths[0])
    item_count = lengths.shape[1]
    own_pos = start_row + jnp.arange(row_count, dtype=jnp.int32)
    key_pos = jnp.arange(row_count * seq_count, dtype=jnp.int32)
    own_ids = item_index(own_pos, bounds)
    layout = (own_pos, key_pos, own_ids, item_index(key_pos, bounds))
    rim_width = conv_kernel.shape[0] // 2
    rim_ids = item_index(
        start_row - rim_width + jnp.arange(row_count + 2 * rim_width, dtype=jnp.int32), bounds
    )
    valid = (own_ids < item_count).astype(jnp.float32)[:, None]
    source = frames[0].astype(jnp.float32)
    first = feed_forward(source, gains[0], first_up, first_down)
    second, keys_values = attend(first, gains[1], qkv_full, out_full, slopes, layout)
    conv_hidden = normed(second, gains[2]).astype(jnp.bfloat16)
    conv_joint = matmul(conv_hidden, conv_up)
    rim = extended(gate_linear(conv_joint).astype(jnp.bfloat16), (("seq", 0),), rim_width)
    conv = depthwise(rim, kernel, rim_ids, own_ids)
    total, count = lax.psum((jnp.sum(valid * conv, axis=0), jnp.sum(valid)), ("seq", "fsdp"))
    average = total / count
    centred = conv - average
    spread = lax.psum(jnp.sum(valid * centred * centred, axis=0), ("seq", "fsdp"))
    variance = spread / count
    inverse = lax.rsqrt(variance + EPSILON)
    standard = (conv - average) * inverse
    pre_swish = standard * batch_scale
    swish, swish_pull = jax.vjp(jax.nn.silu, pre_swish)
    swish_low = swish.astype(jnp.bfloat16)
    third = second + matmul(swish_low, conv_down)
    fourth = feed_forward(third, gains[3], second_up, second_down)
    result = normed(fourth, gains[4])
    regathered = (
        lax.all_gather(sharded[0], "fsdp", axis=0, tiled=True),
        lax.all_gather(sharded[1], "fsdp", axis=0, tiled=True),
        lax.all_gather(sharded[2], "fsdp", axis=0, tiled=True),
        lax.all_gather(sharded[3], "fsdp", axis=0, tiled=True),
        lax.all_gather(sharded[4], "fsdp", axis=0, tiled=True),
        lax.all_gather(sharded[5], "fsdp", axis=1, tiled=True),
        lax.all_gather(sharded[6], "fsdp", axis=0, tiled=True),
        lax.all_gather(sharded[7], "fsdp", axis=0, tiled=True),
        lax.all_gather(sharded[8], "fsdp", axis=0, tiled=True),
        lax.all_gather(sharded[9], "fsdp", axis=0, tiled=True),
        lax.all_gather(sharded[10], "fsdp", axis=1, tiled=True),
    )
    (
        first_up,
        first_down,
        qkv_full,
        out_full,
        conv_up,
        kernel,
        batch_scale,
        conv_down,
        second_up,
        second_down,
        gains,
    ) = unpack(regathered)
    fourth_grad, last_gain = norm_back(fourth, gains[4], out_grad[0].astype(jnp.float32))
    third_grad, fourth_gain, second_up_grad, second_down_grad = feed_back(
        third, gains[3], second_up, second_down, fourth_grad
    )
    branch_grad = third_grad.astype(jnp.bfloat16)
    conv_down_grad = transposed_left(swish_low, branch_grad)
    scaled_grad = swish_pull(transposed_right(branch_grad, conv_down))[0]
    sum_grad, sum_cross = lax.psum(
        (jnp.sum(scaled_grad, axis=0), jnp.sum(scaled_grad * standard, axis=0)), ("seq", "fsdp")
    )
    conv_grad = inverse * (scaled_grad * batch_scale) - valid * (inverse / count) * (
        batch_scale * sum_grad + standard * (batch_scale * sum_cross)
    )
    gated_grad, kernel_grad = depthwise_back(rim, kernel, rim_ids, own_ids, conv_grad)
    joint_pull = jax.vjp(gate_linear, conv_joint)[1]
    joint_grad = joint_pull(gated_grad)[0].astype(jnp.bfloat16)
    conv_up_grad = transposed_left(conv_hidden, joint_grad)
    hidden_grad, third_gain = norm_back(second, gains[2], transposed_right(joint_grad, conv_up))
    second_grad = third_grad + hidden_grad
    late = (
        lax.psum_scatter(second_up_grad, ("seq", "fsdp"), scatter_dimension=0, tiled=True),
        lax.psum_scatter(second_down_grad, ("seq", "fsdp"), scatter_dimension=0, tiled=True),
        lax.psum_scatter(conv_down_grad, ("seq", "fsdp"), scatter_dimension=0, tiled=True),
        lax.psum_scatter(conv_up_grad, ("seq", "fsdp"), scatter_dimension=0, tiled=True),
        lax.psum_scatter(kernel_grad, ("seq", "fsdp"), scatter_dimension=1, tiled=True),
    )
    first_grad, second_gain, qkv_grad, out_weight_grad, slope_part = attend_back(
        first, gains[1], qkv_full, out_full, slopes, layout, keys_values, second_grad
    )
    source_grad, first_gain, first_up_grad, first_down_grad = feed_back(
        source, gains[0], first_up, first_down, first_grad
    )
    gain_grads = jnp.stack([first_gain, second_gain, third_gain, fourth_gain, last_gain])
    early = (
        lax.psum_scatter(first_up_grad, ("seq", "fsdp"), scatter_dimension=0, tiled=True),
        lax.psum_scatter(first_down_grad, ("seq", "fsdp"), scatter_dimension=0, tiled=True),
        lax.psum_scatter(qkv_grad, ("seq", "fsdp"), scatter_dimension=0, tiled=True),
        lax.psum_scatter(out_weight_grad, ("seq", "fsdp"), scatter_dimension=0, tiled=True),
        lax.psum_scatter(gain_grads, ("seq", "fsdp"), scatter_dimension=1, tiled=True),
    )
    slope_grad = lax.psum(slope_part, ("seq", "fsdp"))
    piece_width = feature_width // lax.axis_size(("seq", "fsdp"))
    batch_piece = lax.dynamic_slice_in_dim(
        sum_cross, lax.axis_index(("seq", "fsdp")) * piece_width, piece_width
    )
    return (
        result[None].astype(jnp.bfloat16),
        source_grad[None],
        early[0],
        early[1],
        early[2],
        early[3],
        late[3],
        late[4],
        batch_piece,
        late[2],
        late[0],
        late[1],
        early[4],
        slope_grad,
    )


BF = jnp.bfloat16
F32 = jnp.float32
MESH = pl.DeviceIdType.MESH
GRANT = 56 * 2**20
CHIPS = 4
SLOTS = 96


def mm(left, right):
    return jnp.dot(left, right, preferred_element_type=F32)


def mm_right(left, right):
    return lax.dot_general(left, right, (((1,), (1,)), ((), ())), preferred_element_type=F32)


def mm_left(left, right):
    return lax.dot_general(left, right, (((0,), (0,)), ((), ())), preferred_element_type=F32)


class Here:
    def __init__(self, planes):
        self.planes = planes
        self.seq = lax.axis_index("seq")
        self.plane = lax.axis_index("fsdp")
        self.core = lax.rem(self.seq, 2)
        self.chip = lax.div(self.seq, 2)
        column, row = lax.rem(self.chip, 2), lax.div(self.chip, 2)
        self.chips = [
            lax.rem(row + j // 2, 2) * 2 + lax.rem(column + j % 2, 2) for j in range(CHIPS)
        ]

    def peer(self, slot):
        return (self.chips[slot] * 2 + self.core, self.plane)

    def cross(self, slot):
        return (self.chips[slot] * 2 + 1 - self.core, self.plane)

    def sibling(self):
        return self.cross(0)

    def level(self, step):
        return lax.rem(self.plane + step, self.planes)

    def above(self, step):
        return (self.seq, self.level(step))

    def rows(self, slot, height):
        return pl.ds(pl.multiple_of((self.chips[slot] * 2 + self.core) * height, height), height)

    def other_rows(self, slot, height):
        return pl.ds(pl.multiple_of((self.chips[slot] * 2 + 1 - self.core) * height, height), height)


class Mail:
    def __init__(self, send, recv):
        self.send, self.recv, self.count, self.open = send, recv, 0, []

    def slot(self):
        self.count += 1
        return self.count - 1

    def post(self, src, dst, device):
        i = self.slot()
        copy = pltpu.make_async_remote_copy(
            src_ref=src,
            dst_ref=dst,
            send_sem=self.send.at[i],
            recv_sem=self.recv.at[i],
            device_id=device,
            device_id_type=MESH,
        )
        copy.start()
        self.open.append(copy)
        return copy

    def local(self, src, dst):
        copy = pltpu.make_async_copy(src, dst, self.send.at[self.slot()])
        copy.start()
        return copy

    def close(self):
        for copy in self.open:
            copy.wait_send()
        self.open = []


def greet(devices):
    barrier = pltpu.get_barrier_semaphore()
    for device in devices:
        pl.semaphore_signal(barrier, inc=1, device_id=device, device_id_type=MESH)
    pl.semaphore_wait(barrier, len(devices))


def greet_near(here):
    greet(
        [here.peer(j) for j in range(1, CHIPS)]
        + [here.sibling()]
        + [here.above(k) for k in range(1, here.planes)]
    )


def spread(mail, here, buf):
    return [None] + [mail.post(buf.at[0], buf.at[j], here.peer(j)) for j in range(1, CHIPS)]


def arrive(copies, slot):
    if copies[slot] is not None:
        copies[slot].wait_recv()


def over_planes(mail, here, src, piece):
    own = mail.local(src, piece(here.plane))
    others = [mail.post(src, piece(here.plane), here.above(k)) for k in range(1, here.planes)]

    def wait():
        own.wait()
        for copy in others:
            copy.wait_recv()

    return wait


def from_plane(mail, here, src, dst, source):
    arrived = mail.slot()
    places = [mail.slot() for _ in range(1, here.planes)]
    own = pltpu.make_async_copy(src, dst, mail.send.at[arrived])
    copies = [
        pltpu.make_async_remote_copy(
            src_ref=src,
            dst_ref=dst,
            send_sem=mail.send.at[places[k - 1]],
            recv_sem=mail.recv.at[arrived],
            device_id=here.above(k),
            device_id_type=MESH,
        )
        for k in range(1, here.planes)
    ]

    @pl.when(here.plane == source)
    def _():
        own.start()
        for copy in copies:
            copy.start()

    def wait():
        @pl.when(here.plane == source)
        def _():
            own.wait()
            for copy in copies:
                copy.wait_send()

        @pl.when(here.plane != source)
        def _():
            copies[0].wait_recv()

    return wait


def sum_over_planes(mail, here, parts, land):
    copies = [
        mail.post(parts.at[here.level(k)], land.at[k - 1], here.above(k))
        for k in range(1, here.planes)
    ]

    def total():
        for copy in copies:
            copy.wait_recv()
        value = parts[here.plane].astype(F32)
        for k in range(1, here.planes):
            value = value + land[k - 1].astype(F32)
        return value

    return total


def scale_row(small_ref, index):
    rows = [small_ref[k].astype(F32)[index : index + 1, :] for k in range(small_ref.shape[0])]
    return jnp.concatenate(rows, axis=1)


def own_channels(small_ref, here, index, width):
    block = small_ref[here.chip, :, pl.ds(pl.multiple_of(here.core * width, width), width)]
    return block.astype(F32)[index, :]


def whitened(value):
    average = jnp.mean(value, axis=-1, keepdims=True)
    centred = value - average
    inverse = lax.rsqrt(jnp.mean(centred * centred, axis=-1, keepdims=True) + EPSILON)
    return centred * inverse, inverse


def norm_grad(value, gain, gradient):
    white, inverse = whitened(value)
    inner = gradient * gain
    value_grad = inverse * (
        inner
        - jnp.mean(inner, axis=-1, keepdims=True)
        - white * jnp.mean(inner * white, axis=-1, keepdims=True)
    )
    return value_grad, jnp.sum(gradient * white, axis=0, keepdims=True)


def at_row(index, row, height=8):
    place = lax.broadcasted_iota(jnp.int32, (height, row.shape[1]), 0)
    return jnp.where(place == index, row, 0.0)


def sigmoid(value):
    return 1.0 / (1.0 + jnp.exp(-value))


def reduced(mail, here, part, stage, land, acc, between=None):
    copies = []
    for j in range(CHIPS):
        value = part(j)
        if j == 0:
            acc[...] = value
        else:
            stage[j - 1] = value.astype(BF)
            copies.append(mail.post(stage.at[j - 1], land.at[j - 1], here.peer(j)))
    if between is not None:
        between()
    for copy in copies:
        copy.wait_recv()
    total = acc[...]
    for j in range(1, CHIPS):
        total = total + land[j - 1].astype(F32)
    return total


def feed_through(mail, here, hidden, keep, up, down, stage, land, acc, down_ready=None):
    copies = spread(mail, here, hidden)
    half = up[0].shape[1]

    def part(j):
        arrive(copies, j)
        rows = hidden[j]
        total = None
        swishes = []
        for side in range(2):
            active = mm(rows, up[side][...])
            keep[j, :, side * half : (side + 1) * half] = active
            swishes.append((active * sigmoid(active)).astype(BF))
        if j == 0 and down_ready is not None:
            down_ready()
        for side in range(2):
            term = mm(swishes[side], down[side][...])
            total = term if total is None else total + term
        return total

    return reduced(mail, here, part, stage, land, acc)


def feed_return(mail, here, branch, hidden, keep, up, down, swish, active_grad, stage, land, acc, between):
    copies = spread(mail, here, branch)
    half = up[0].shape[1]

    def part(j):
        arrive(copies, j)
        rows = branch[j]
        total = None
        for side in range(2):
            span = slice(side * half, (side + 1) * half)
            active = keep[j, :, span]
            gate = sigmoid(active)
            swish[j, :, span] = (active * gate).astype(BF)
            grad = mm_right(rows, down[side][...]) * (gate * (1.0 + active * (1.0 - gate)))
            grad = grad.astype(BF)
            active_grad[j, :, span] = grad
            term = mm_right(grad, up[side][...])
            total = term if total is None else total + term
        return total

    return reduced(mail, here, part, stage, land, acc, between)


def flat(ref, span=None):
    value = ref[...] if span is None else ref[:, :, span]
    return value.reshape(value.shape[0] * value.shape[1], value.shape[2])


def feed_weight_grads(mail, here, branch, hidden, swish, active_grad, sums, up_out, down_out, pair):
    half = swish.shape[2] // 2
    up_send, up_land, down_send, down_land = pair
    own, other = slice(0, half), slice(half, 2 * half)
    branch_rows = flat(branch)
    down_send[...] = mm_left(flat(swish, other), branch_rows).astype(BF)
    down_copy = mail.post(down_send, down_land, here.sibling())
    hidden_rows = flat(hidden)
    up_send[...] = mm_left(hidden_rows, flat(active_grad, other)).astype(BF)
    up_copy = mail.post(up_send, up_land, here.sibling())
    sums[...] = mm_left(flat(swish, own), branch_rows)
    down_copy.wait_recv()
    value = (sums[...] + down_land[...].astype(F32)).astype(BF)
    down_out[...] = value.reshape(down_out.shape)
    grad = mm_left(hidden_rows, flat(active_grad, own))
    up_copy.wait_recv()
    by_owner(up_out, (grad + up_land[...].astype(F32)).astype(BF), here.planes)


def by_owner(out, value, planes):
    seqs = 2 * CHIPS
    height = value.shape[0] // (seqs * planes)
    for p in range(planes):
        for s in range(seqs):
            start = (s * planes + p) * height
            out[p, s * height : (s + 1) * height, :] = value[start : start + height, :]


def first_kernel(
    planes, frames, small, up_src, down_src, qkv_src, out_src,
    y_out, hidden, keep, up, down, small_out, qkv_out, out_out,
    up_other, down_other, stage, land, acc, send, recv,
):
    here, mail = Here(planes), Mail(send, recv)
    greet_near(here)
    rows = frames.shape[1]
    small_ready = over_planes(mail, here, small, lambda p: small_out.at[p])
    up_height, qkv_height = up_src.shape[0], qkv_src.shape[0]
    up_ready = over_planes(
        mail, here, up_src,
        lambda p: up.at[pl.ds(pl.multiple_of(p * up_height, up_height), up_height), :],
    )
    down_height = down.shape[0] // planes
    down_own = down_src.at[pl.ds(pl.multiple_of(here.seq * down_height, down_height), down_height), :]
    down_ready = over_planes(
        mail, here, down_own,
        lambda p: down.at[pl.ds(pl.multiple_of(p * down_height, down_height), down_height), :],
    )
    qkv_ready = over_planes(
        mail, here, qkv_src,
        lambda p: qkv_out.at[pl.ds(pl.multiple_of(p * qkv_height, qkv_height), qkv_height), :],
    )
    out_height = out_out.shape[0]
    out_own = out_src.at[pl.ds(pl.multiple_of(here.core * out_height, out_height), out_height), :]
    out_ready = from_plane(mail, here, out_own, out_out, here.chip)

    value = frames[0].astype(F32)
    white = whitened(value)[0]
    small_ready()
    hidden[0] = (white * scale_row(small_out, 0)).astype(BF)
    up_ready()
    up_copy = mail.post(up, up_other, here.sibling())
    up_copy.wait_recv()

    def both_down():
        down_ready()
        copy = mail.post(down, down_other, here.sibling())
        copy.wait_recv()

    total = feed_through(
        mail, here, hidden, keep, (up, up_other), (down, down_other), stage, land, acc, both_down
    )
    y_out[...] = value + 0.5 * total
    qkv_ready()
    out_ready()
    mail.close()


def attention_weights(query, keys, slope, start, marks, row_ids):
    height, width = query.shape[0], keys.shape[0]
    row = lax.broadcasted_iota(jnp.int32, (height, width), 0) + start
    column = lax.broadcasted_iota(jnp.int32, (height, width), 1)
    distance = jnp.abs(row - column).astype(F32)
    scores = mm_right(query, keys) * (1.0 / math.sqrt(query.shape[1])) - slope * distance
    scores = jnp.where(marks[:, 6:7] == row_ids, scores, MASKED)
    exponent = jnp.exp(scores - jnp.max(scores, axis=-1, keepdims=True))
    return exponent / jnp.sum(exponent, axis=-1, keepdims=True), distance


def attend_kernel(
    planes, value_ref, small, qkv, out, slope, marks, row_ids, in_src, conv_src,
    y_out, hidden, joint, mixed, in_out, conv_out,
    qkv_other, out_other, joint_stage, mixed_stage, stage, land, acc, send, recv,
):
    here, mail = Here(planes), Mail(send, recv)
    greet_near(here)
    height = value_ref.shape[0]
    size = joint.shape[1] // 3
    weight_copies = [
        mail.post(qkv, qkv_other, here.sibling()),
        mail.post(out, out_other, here.sibling()),
    ]
    value = value_ref[...]
    hidden[0] = (whitened(value)[0] * scale_row(small, 1)).astype(BF)
    copies = spread(mail, here, hidden)
    in_height = in_src.shape[0]
    in_ready = over_planes(
        mail, here, in_src,
        lambda p: in_out.at[pl.ds(pl.multiple_of(p * in_height, in_height), in_height), :],
    )
    conv_height = conv_out.shape[0]
    conv_own = conv_src.at[pl.ds(pl.multiple_of(here.core * conv_height, conv_height), conv_height), :]
    conv_ready = from_plane(mail, here, conv_own, conv_out, here.chip)
    for copy in weight_copies:
        copy.wait_recv()
    joint_copies = []
    for j in range(CHIPS):
        arrive(copies, j)
        rows = hidden[j]
        joint_stage[j] = mm(rows, qkv_other[...]).astype(BF)
        joint_copies.append(
            mail.post(joint_stage.at[j], joint.at[here.rows(j, height), :], here.sibling())
        )
        joint[here.rows(j, height), :] = mm(rows, qkv[...]).astype(BF)
    for copy in joint_copies:
        copy.wait_recv()
    mixed_copies = []
    for j in range(CHIPS):
        start = pl.multiple_of(here.chips[j] * 2 * height, 2 * height)
        block = pl.ds(start, 2 * height)
        weights = attention_weights(
            joint[block, 0:size], joint[:, size : 2 * size], slope[0], start, marks[block, :], row_ids[...]
        )[0]
        mixed_stage[j] = mm(weights.astype(BF), joint[:, 2 * size :]).astype(BF)
        own = pl.ds(pl.multiple_of(here.core * height, height), height)
        other = pl.ds(pl.multiple_of((1 - here.core) * height, height), height)
        mixed[0, j] = mixed_stage[j, own, :]
        mixed_copies.append(mail.post(mixed_stage.at[j, other, :], mixed.at[1, j], here.sibling()))

    def part(j):
        mixed_copies[j].wait_recv()
        return mm(mixed[0, j], out[...]) + mm(mixed[1, j], out_other[...])

    y_out[...] = value + reduced(mail, here, part, stage, land, acc)
    in_ready()
    conv_ready()
    mail.close()


def attend_back_kernel(
    planes, grad_ref, value_ref, small, qkv, out, slope, marks, row_ids, hidden, joint, mixed, in_parts, conv_parts,
    y_grad, small_grad, qkv_parts, out_parts, in_sum, conv_sum,
    qkv_other, out_other, branch, mixed_stage, mixed_grad, joint_grad, key_grad, value_grad, moved,
    qkv_send, qkv_land, out_send, out_land, in_land, conv_land, stage, land, acc, send, recv,
):
    here, mail = Here(planes), Mail(send, recv)
    greet_near(here)
    height = value_ref.shape[0]
    size = joint.shape[1] // 3
    weight_copies = [
        mail.post(qkv, qkv_other, here.sibling()),
        mail.post(out, out_other, here.sibling()),
    ]
    gradient = grad_ref[...]
    branch[0] = gradient.astype(BF)
    copies = spread(mail, here, branch)
    in_total = sum_over_planes(mail, here, in_parts, in_land)
    conv_total = sum_over_planes(mail, here, conv_parts, conv_land)
    for copy in weight_copies:
        copy.wait_recv()
    mixed_copies = []
    for j in range(CHIPS):
        arrive(copies, j)
        rows = branch[j]
        mixed_stage[j] = mm_right(rows, out_other[...]).astype(BF)
        mixed_copies.append(
            mail.post(mixed_stage.at[j], mixed_grad.at[here.rows(j, height), :], here.sibling())
        )
        mixed_grad[here.rows(j, height), :] = mm_right(rows, out[...]).astype(BF)
    for copy in mixed_copies:
        copy.wait_recv()
    key_grad[...] = jnp.zeros_like(key_grad)
    value_grad[...] = jnp.zeros_like(value_grad)
    scale = 1.0 / math.sqrt(size)

    def step(index, carry):
        start = pl.multiple_of(index * 2 * height, 2 * height)
        block = pl.ds(start, 2 * height)
        query, keys, values = joint[block, 0:size], joint[:, size : 2 * size], joint[:, 2 * size :]
        weights, distance = attention_weights(query, keys, slope[0], start, marks[block, :], row_ids[...])
        rows = mixed_grad[block, :]
        weight_grad = mm_right(rows, values)
        delta = jnp.sum(weights * weight_grad, axis=-1, keepdims=True)
        score_grad = weights * (weight_grad - delta)
        raw = (score_grad * scale).astype(BF)
        joint_grad[block, 0:size] = mm(raw, keys).astype(BF)
        key_grad[...] += mm_left(raw, query)
        value_grad[...] += mm_left(weights.astype(BF), rows)
        return carry - jnp.sum(score_grad * distance, axis=0, keepdims=True)

    slope_row = lax.fori_loop(0, CHIPS, step, jnp.zeros((1, joint.shape[0]), F32))
    joint_grad[:, size : 2 * size] = key_grad[...].astype(BF)
    joint_grad[:, 2 * size :] = value_grad[...].astype(BF)
    moved_copies = []
    for j in range(CHIPS):
        moved_copies.append(
            mail.post(joint_grad.at[here.other_rows(j, height), :], moved.at[1, j], here.sibling())
        )
        moved[0, j] = joint_grad[here.rows(j, height), :]

    def part(j):
        moved_copies[j].wait_recv()
        return mm_right(moved[0, j], qkv[...]) + mm_right(moved[1, j], qkv_other[...])

    def between():
        branch_rows = flat(branch)
        out_send[...] = mm_left(flat(mixed.at[1]), branch_rows).astype(BF)
        out_copy = mail.post(out_send, out_land, here.sibling())
        hidden_rows = flat(hidden)
        qkv_send[...] = mm_left(hidden_rows, flat(moved.at[1])).astype(BF)
        qkv_copy = mail.post(qkv_send, qkv_land, here.sibling())
        out_grad = mm_left(flat(mixed.at[0]), branch_rows)
        out_copy.wait_recv()
        out_parts[...] = (out_grad + out_land[...].astype(F32)).astype(BF).reshape(out_parts.shape)
        qkv_grad = mm_left(hidden_rows, flat(moved.at[0]))
        qkv_copy.wait_recv()
        by_owner(qkv_parts, (qkv_grad + qkv_land[...].astype(F32)).astype(BF), here.planes)

    total = reduced(mail, here, part, stage, land, acc, between)
    value_part, gain_part = norm_grad(value_ref[...], scale_row(small, 1), total)
    y_grad[...] = gradient + value_part
    lane = lax.broadcasted_iota(jnp.int32, gain_part.shape, 1)
    slope_total = jnp.sum(slope_row, axis=1, keepdims=True)
    small_grad[...] = at_row(1, gain_part) + at_row(5, jnp.where(lane == here.seq, slope_total, 0.0))
    in_sum[...] = in_total().astype(BF)
    conv_sum[...] = conv_total()
    mail.close()


def conv_kernel(
    planes, value_ref, small, conv_in, conv_out, marks, up_src, down_src,
    y_out, hidden, joint, gated, standard, stats, mixed, up_out, down_out,
    in_other, out_other, gate_stage, gate_rows, padded, mixed_rows, sums, sums_land, stage, land, acc, send, recv,
):
    here, mail = Here(planes), Mail(send, recv)
    greet_near(here)
    height = value_ref.shape[0]
    width = gated.shape[1]
    frames = gated.shape[0]
    weight_copies = [
        mail.post(conv_in, in_other, here.sibling()),
        mail.post(conv_out, out_other, here.sibling()),
    ]
    value = value_ref[...]
    hidden[0] = (whitened(value)[0] * scale_row(small, 2)).astype(BF)
    copies = spread(mail, here, hidden)
    up_height = up_src.shape[0]
    up_ready = over_planes(
        mail, here, up_src,
        lambda p: up_out.at[pl.ds(pl.multiple_of(p * up_height, up_height), up_height), :],
    )
    down_height = down_out.shape[0] // planes
    down_own = down_src.at[pl.ds(pl.multiple_of(here.seq * down_height, down_height), down_height), :]
    down_ready = over_planes(
        mail, here, down_own,
        lambda p: down_out.at[pl.ds(pl.multiple_of(p * down_height, down_height), down_height), :],
    )
    for copy in weight_copies:
        copy.wait_recv()
    gate_copies = []
    for j in range(CHIPS):
        arrive(copies, j)
        rows = hidden[j]
        for side, weight in ((1, in_other), (0, conv_in)):
            both = mm(rows, weight[...])
            joint[j, :, 2 * width * side : 2 * width * (side + 1)] = both
            gate = (both[:, :width] * sigmoid(both[:, width:])).astype(BF)
            if side:
                gate_stage[j] = gate
                gate_copies.append(
                    mail.post(gate_stage.at[j], gate_rows.at[here.rows(j, height), :], here.sibling())
                )
            else:
                gate_rows[here.rows(j, height), :] = gate
    for copy in gate_copies:
        copy.wait_recv()
    taps = 5
    rim = 8
    padded[0:rim, :] = jnp.zeros((rim, width), F32)
    padded[rim + frames :, :] = jnp.zeros((rim, width), F32)
    padded[rim : rim + frames, :] = gate_rows[...].astype(F32)
    gated[...] = padded[rim : rim + frames, :]
    kernel = own_channels(small, here, slice(5, 5 + taps), width)
    conv = None
    for t in range(taps):
        first = rim - taps // 2 + t
        term = kernel[t : t + 1, :] * padded[first : first + frames, :] * marks[:, t : t + 1]
        conv = term if conv is None else conv + term
    valid = marks[:, 5:6]
    count = jnp.sum(valid, axis=0, keepdims=True)
    total = jnp.sum(valid * conv, axis=0, keepdims=True)
    centred = conv - total / count
    squares = jnp.sum(valid * centred * centred, axis=0, keepdims=True)
    sums[...] = at_row(0, total) + at_row(1, squares) + at_row(2, jnp.broadcast_to(count, total.shape))
    sum_copies = [
        mail.post(sums, sums_land.at[k - 1], here.above(k)) for k in range(1, planes)
    ]
    for copy in sum_copies:
        copy.wait_recv()
    terms = [sums[...]] + [sums_land[k - 1] for k in range(1, planes)]
    whole = sum(term[2:3, :] for term in terms)
    average = sum(term[0:1, :] for term in terms) / whole
    variance = 0.0
    for term in terms:
        apart = term[0:1, :] / term[2:3, :] - average
        variance = variance + term[1:2, :] + term[2:3, :] * apart * apart
    inverse = lax.rsqrt(variance / whole + EPSILON)
    stats[...] = at_row(0, inverse) + at_row(1, whole)
    standard[...] = (conv - average) * inverse
    scaled = standard[...] * own_channels(small, here, slice(10, 11), width)
    mixed_rows[...] = (scaled * sigmoid(scaled)).astype(BF)
    mixed_copies = []
    for j in range(CHIPS):
        mixed_copies.append(
            mail.post(mixed_rows.at[here.other_rows(j, height), :], mixed.at[1, j], here.sibling())
        )
        mixed[0, j] = mixed_rows[here.rows(j, height), :]

    def part(j):
        mixed_copies[j].wait_recv()
        return mm(mixed[0, j], conv_out[...]) + mm(mixed[1, j], out_other[...])

    y_out[...] = value + reduced(mail, here, part, stage, land, acc)
    up_ready()
    down_ready()
    mail.close()


def conv_back_kernel(
    planes, grad_ref, value_ref, small, conv_in, conv_out, marks, hidden, joint, gated, standard, stats, mixed,
    up_parts, down_parts,
    y_grad, small_grad, kernel_grad, cross, in_parts, out_parts, up_sum, down_sum,
    in_other, out_other, branch, mixed_stage, mixed_grad, padded, gate_grad, moved, joint_grad, sums, sums_land,
    in_send, in_land, out_send, out_land, up_land, down_land, stage, land, acc, send, recv,
):
    here, mail = Here(planes), Mail(send, recv)
    greet_near(here)
    height = value_ref.shape[0]
    frames, width = gated.shape
    weight_copies = [
        mail.post(conv_out, out_other, here.sibling()),
        mail.post(conv_in, in_other, here.sibling()),
    ]
    gradient = grad_ref[...]
    branch[0] = gradient.astype(BF)
    copies = spread(mail, here, branch)
    up_total = sum_over_planes(mail, here, up_parts, up_land)
    down_total = sum_over_planes(mail, here, down_parts, down_land)
    for copy in weight_copies:
        copy.wait_recv()
    mixed_copies = []
    for j in range(CHIPS):
        arrive(copies, j)
        rows = branch[j]
        mixed_stage[j] = mm_right(rows, out_other[...])
        mixed_copies.append(
            mail.post(mixed_stage.at[j], mixed_grad.at[here.rows(j, height), :], here.sibling())
        )
        mixed_grad[here.rows(j, height), :] = mm_right(rows, conv_out[...])
    for copy in mixed_copies:
        copy.wait_recv()
    gain = own_channels(small, here, slice(10, 11), width)
    white = standard[...]
    scaled = white * gain
    gate = sigmoid(scaled)
    scaled_grad = mixed_grad[...] * (gate * (1.0 + scaled * (1.0 - gate)))
    sums[...] = at_row(0, jnp.sum(scaled_grad, axis=0, keepdims=True)) + at_row(
        1, jnp.sum(scaled_grad * white, axis=0, keepdims=True)
    )
    sum_copies = [
        mail.post(sums, sums_land.at[k - 1], here.above(k)) for k in range(1, planes)
    ]
    for copy in sum_copies:
        copy.wait_recv()
    both = sums[...]
    for k in range(1, planes):
        both = both + sums_land[k - 1]
    cross[...] = both
    inverse, whole = stats[0:1, :], stats[1:2, :]
    conv_grad = inverse * (scaled_grad * gain) - marks[:, 5:6] * (
        (inverse / whole) * (gain * both[0:1, :] + white * (gain * both[1:2, :]))
    )
    taps = 5
    rim = 8
    reach = taps // 2
    padded[0:rim, :] = jnp.zeros((rim, width), F32)
    padded[rim + frames :, :] = jnp.zeros((rim, width), F32)
    padded[rim : rim + frames, :] = conv_grad
    kernel = own_channels(small, here, slice(5, 5 + taps), width)
    total = None
    for t in range(taps):
        first = rim + reach - t
        mirror = taps - 1 - t
        term = kernel[t : t + 1, :] * padded[first : first + frames, :] * marks[:, mirror : mirror + 1]
        total = term if total is None else total + term
    gate_grad[...] = total
    moved_copies = []
    for j in range(CHIPS):
        moved_copies.append(
            mail.post(gate_grad.at[here.other_rows(j, height), :], moved.at[1, j], here.sibling())
        )
        moved[0, j] = gate_grad[here.rows(j, height), :]

    def part(j):
        moved_copies[j].wait_recv()
        result = None
        for side, weight in ((0, conv_in), (1, in_other)):
            left = joint[j, :, 2 * width * side : 2 * width * side + width]
            gate = sigmoid(joint[j, :, 2 * width * side + width : 2 * width * (side + 1)])
            incoming = moved[side, j]
            joint_grad[side, j, :, :width] = (incoming * gate).astype(BF)
            joint_grad[side, j, :, width:] = (incoming * left * (gate * (1.0 - gate))).astype(BF)
            term = mm_right(joint_grad[side, j], weight[...])
            result = term if result is None else result + term
        return result

    def between():
        branch_rows = flat(branch)
        out_send[...] = mm_left(flat(mixed.at[1]), branch_rows).astype(BF)
        out_copy = mail.post(out_send, out_land, here.sibling())
        hidden_rows = flat(hidden)
        in_send[...] = mm_left(hidden_rows, flat(joint_grad.at[1])).astype(BF)
        in_copy = mail.post(in_send, in_land, here.sibling())
        out_grad = mm_left(flat(mixed.at[0]), branch_rows)
        out_copy.wait_recv()
        out_parts[...] = (out_grad + out_land[...].astype(F32)).astype(BF).reshape(out_parts.shape)
        in_grad = mm_left(hidden_rows, flat(joint_grad.at[0]))
        in_copy.wait_recv()
        by_owner(in_parts, (in_grad + in_land[...].astype(F32)).astype(BF), here.planes)
        dense = padded[rim : rim + frames, :]
        padded[rim : rim + frames, :] = gated[...]
        rows = jnp.zeros((8, width), F32)
        for t in range(taps):
            first = rim - reach + t
            row = jnp.sum(padded[first : first + frames, :] * marks[:, t : t + 1] * dense, axis=0, keepdims=True)
            rows = rows + at_row(t, row)
        kernel_grad[...] = rows

    whole_grad = reduced(mail, here, part, stage, land, acc, between)
    value_part, gain_part = norm_grad(value_ref[...], scale_row(small, 2), whole_grad)
    y_grad[...] = gradient + value_part
    small_grad[...] = at_row(2, gain_part)
    up_sum[...] = up_total().astype(BF)
    down_sum[...] = down_total().astype(BF)
    mail.close()


def second_kernel(
    planes, value_ref, small, up, down, out_grad,
    result, y_grad, small_grad, up_parts, down_parts,
    up_other, down_other, hidden, keep, branch, swish, active_grad,
    stage, land, stage_back, land_back, acc, up_send, up_land, down_send, down_land, sums, send, recv,
):
    here, mail = Here(planes), Mail(send, recv)
    greet_near(here)
    weight_copies = [
        mail.post(up, up_other, here.sibling()),
        mail.post(down, down_other, here.sibling()),
    ]
    value = value_ref[...]
    gain = scale_row(small, 3)
    hidden[0] = (whitened(value)[0] * gain).astype(BF)
    for copy in weight_copies:
        copy.wait_recv()
    ups, downs = (up, up_other), (down, down_other)
    fourth = value + 0.5 * feed_through(mail, here, hidden, keep, ups, downs, stage, land, acc)
    last_gain = scale_row(small, 4)
    result[0] = (whitened(fourth)[0] * last_gain).astype(BF)
    gradient, last_part = norm_grad(fourth, last_gain, out_grad[0].astype(F32))
    branch[0] = (0.5 * gradient).astype(BF)

    def between():
        feed_weight_grads(
            mail, here, branch, hidden, swish, active_grad, sums, up_parts, down_parts,
            (up_send, up_land, down_send, down_land),
        )

    y_grad[...] = gradient
    total = feed_return(
        mail, here, branch, hidden, keep, ups, downs, swish, active_grad, stage_back, land_back, acc, between
    )
    value_part, gain_part = norm_grad(value_ref[...], gain, total)
    y_grad[...] = y_grad[...] + value_part
    small_grad[...] = at_row(3, gain_part) + at_row(4, last_part)
    mail.close()


def first_back_kernel(
    planes, grad_ref, frames, small, up, down, hidden, keep, qkv_parts, out_parts,
    x_grad, small_grad, up_parts, down_parts, qkv_sum, out_sum,
    up_other, down_other, branch, swish, active_grad, qkv_land, out_land,
    stage, land, acc, up_send, up_land, down_send, down_land, sums, send, recv,
):
    here, mail = Here(planes), Mail(send, recv)
    greet_near(here)
    weight_copies = [
        mail.post(down, down_other, here.sibling()),
        mail.post(up, up_other, here.sibling()),
    ]
    gradient = grad_ref[...]
    branch[0] = (0.5 * gradient).astype(BF)
    qkv_total = sum_over_planes(mail, here, qkv_parts, qkv_land)
    out_total = sum_over_planes(mail, here, out_parts, out_land)
    for copy in weight_copies:
        copy.wait_recv()

    def between():
        feed_weight_grads(
            mail, here, branch, hidden, swish, active_grad, sums, up_parts, down_parts,
            (up_send, up_land, down_send, down_land),
        )

    total = feed_return(
        mail, here, branch, hidden, keep, (up, up_other), (down, down_other), swish, active_grad, stage, land, acc, between
    )
    value_part, gain_part = norm_grad(frames[0].astype(F32), scale_row(small, 0), total)
    x_grad[0] = grad_ref[...] + value_part
    small_grad[...] = at_row(0, gain_part)
    qkv_sum[...] = qkv_total().astype(BF)
    out_sum[...] = out_total()
    mail.close()


def last_kernel(
    planes, up_parts, down_parts, up_second, qkv_sum, in_sum, small_a, small_b, small_c, small_d, kernel_part,
    up_first_out, up_second_out, qkv_out, in_out, down_out, small_out, kernel_out,
    up_land, down_land, up_sum, up_got, second_got, qkv_got, in_got,
    small_sum, small_land, small_near, kernel_land, send, recv,
):
    here, mail = Here(planes), Mail(send, recv)
    near = [here.peer(j) for j in range(1, CHIPS)] + [here.cross(j) for j in range(CHIPS)]
    greet(near + [here.above(k) for k in range(1, planes)])
    up_total = sum_over_planes(mail, here, up_parts, up_land)
    down_total = sum_over_planes(mail, here, down_parts, down_land)
    small_sum[...] = small_a[...] + small_b[...] + small_c[...] + small_d[...]
    small_copies = [mail.post(small_sum, small_land.at[k - 1], here.above(k)) for k in range(1, planes)]
    kernel_copies = [mail.post(kernel_part, kernel_land.at[k - 1], here.above(k)) for k in range(1, planes)]
    blocks = up_second_out.shape[0]
    lane = 128

    def swap(source, got):
        return [
            mail.post(
                source.at[pl.ds(pl.multiple_of(device[0] * blocks, blocks), blocks), :], got.at[i], device
            )
            for i, device in enumerate(near)
        ]

    def place(source, got, out, copies):
        stride = out.shape[1] // (source.shape[1] // lane)
        own = source[pl.ds(pl.multiple_of(here.seq * blocks, blocks), blocks), :]
        for i in range(len(near) + 1):
            if i:
                copies[i - 1].wait_recv()
            seq = near[i - 1][0] if i else here.seq
            value = (got[i - 1] if i else own).astype(F32)
            for g in range(source.shape[1] // lane):
                at = pl.ds(pl.multiple_of(g * stride + seq * lane, lane), lane)
                out[:, at] = value[:, g * lane : (g + 1) * lane]

    second_copies = swap(up_second, second_got)
    qkv_copies = swap(qkv_sum, qkv_got)
    in_copies = swap(in_sum, in_got)
    for copy in small_copies:
        copy.wait_recv()
    total = small_sum[...]
    for k in range(1, planes):
        total = total + small_land[k - 1]
    small_out[...] = total
    near_copies = [mail.post(small_out, small_near.at[i], device) for i, device in enumerate(near)]
    for copy in kernel_copies:
        copy.wait_recv()
    kernel_total = kernel_part[...]
    for k in range(1, planes):
        kernel_total = kernel_total + kernel_land[k - 1]
    kernel_out[...] = kernel_total
    up_sum[...] = up_total().astype(BF)
    up_copies = swap(up_sum, up_got)
    down_out[...] = down_total().astype(BF)
    place(up_second, second_got, up_second_out, second_copies)
    place(qkv_sum, qkv_got, qkv_out, qkv_copies)
    place(in_sum, in_got, in_out, in_copies)
    for copy in near_copies:
        copy.wait_recv()
    mail.close()
    total = small_out[...]
    for i in range(len(near)):
        total = total + small_near[i]
    small_out[...] = total
    place(up_sum, up_got, up_first_out, up_copies)
    mail.close()


def launch(kernel, name, index, planes, operands, results, scratch):
    spaces = {"v": pltpu.VMEM, "h": pl.ANY, "s": pltpu.SMEM}
    return pl.pallas_call(
        functools.partial(kernel, planes),
        name=name,
        out_shape=[jax.ShapeDtypeStruct(shape, kind) for shape, kind, _ in results],
        in_specs=[pl.BlockSpec(memory_space=spaces[place]) for _, place in operands],
        out_specs=[pl.BlockSpec(memory_space=spaces[place]) for _, _, place in results],
        scratch_shapes=[pltpu.VMEM(shape, kind) for shape, kind in scratch]
        + [pltpu.SemaphoreType.DMA((SLOTS,)), pltpu.SemaphoreType.DMA((SLOTS,))],
        compiler_params=pltpu.CompilerParams(
            collective_id=index, has_side_effects=True, vmem_limit_bytes=GRANT
        ),
    )(*[array for array, _ in operands])


def pieces(weight, count, seq, width):
    stride = weight.shape[1] // count
    return jnp.concatenate(
        [lax.dynamic_slice_in_dim(weight, g * stride + seq * width, width, axis=1) for g in range(count)],
        axis=1,
    )


def plane_body(
    frames, lengths, up_first, down_first, joint_qkv, attn_out, conv_in, conv_kernel_, batch_gain, conv_out,
    up_second, down_second, norm_gains, slopes, out_grad,
):
    planes = lax.axis_size("fsdp")
    seqs = lax.axis_size("seq")
    seq = lax.axis_index("seq")
    plane = lax.axis_index("fsdp")
    rows, width = frames.shape[1], frames.shape[2]
    length = rows * seqs
    heads = slopes.shape[0]
    size = width // heads
    channels = width // seqs
    hidden_units = up_first.shape[1]
    half = hidden_units // seqs
    shard = up_first.shape[0]
    taps = conv_kernel_.shape[0]
    block = width // (seqs * planes)
    down_block = hidden_units // (seqs * planes)

    bounds = jnp.cumsum(lengths[0])
    positions = jnp.arange(length, dtype=jnp.int32)
    ids = item_index(positions, bounds)
    reach = taps // 2
    rim_pos = positions[:, None] + jnp.arange(taps, dtype=jnp.int32)[None, :] - reach
    rim_ids = jnp.sum((rim_pos[:, :, None] >= bounds[None, None, :]).astype(jnp.int32), axis=2)
    shared = (rim_ids == ids[:, None]) & (rim_pos >= 0) & (rim_pos < length)
    valid = ids < lengths.shape[1]
    marks = jnp.concatenate(
        [shared.astype(F32), valid.astype(F32)[:, None], ids.astype(F32)[:, None], jnp.zeros((length, 1), F32)],
        axis=1,
    )
    row_ids = ids.astype(F32)[None, :]
    slope = lax.dynamic_slice_in_dim(slopes, seq, 1)
    small = jnp.concatenate(
        [norm_gains, conv_kernel_, batch_gain[None, :], jnp.zeros((5, batch_gain.shape[0]), BF)], axis=0
    )
    up_piece = pieces(up_first, planes, seq, half // planes)
    qkv_piece = pieces(joint_qkv, 3, seq, size)
    in_piece = pieces(conv_in, 2, seq, channels)
    second_piece = pieces(up_second, planes, seq, half // planes)

    row_f = ((rows, width), F32, "v")
    quad = (CHIPS, rows, width)
    stage = ((CHIPS - 1, rows, width), BF)
    acc = ((rows, width), F32)
    tail = [stage, stage, acc]

    first, hidden0, keep0, up1, down1, small_all, qkv, out_w = launch(
        first_kernel, "first", 0, planes,
        [(frames, "v"), (small, "v"), (up_piece, "h"), (down_first, "h"), (qkv_piece, "h"), (attn_out, "h")],
        [
            row_f, (quad, BF, "v"), ((CHIPS, rows, 2 * half), F32, "v"), ((width, half), BF, "v"),
            ((half, width), BF, "v"), ((planes,) + small.shape, BF, "v"), ((width, 3 * size), BF, "h"),
            ((size, width), BF, "h"),
        ],
        [((width, half), BF), ((half, width), BF)] + tail,
    )
    second, hidden1, joint, mixed, in_w, conv_w = launch(
        attend_kernel, "attend", 1, planes,
        [
            (first, "v"), (small_all, "v"), (qkv, "v"), (out_w, "v"), (slope, "s"), (marks, "v"), (row_ids, "v"),
            (in_piece, "h"), (conv_out, "h"),
        ],
        [
            row_f, (quad, BF, "v"), ((length, 3 * size), BF, "v"), ((2, CHIPS, rows, size), BF, "v"),
            ((width, 2 * channels), BF, "h"), ((channels, width), BF, "h"),
        ],
        [
            ((width, 3 * size), BF), ((size, width), BF), ((CHIPS, rows, 3 * size), BF),
            ((CHIPS, 2 * rows, size), BF),
        ] + tail,
    )
    third, hidden2, glu, gated, standard, stats, swish, up2, down2 = launch(
        conv_kernel, "conv", 2, planes,
        [
            (second, "v"), (small_all, "v"), (in_w, "v"), (conv_w, "v"), (marks, "v"), (second_piece, "h"),
            (down_second, "h"),
        ],
        [
            row_f, (quad, BF, "v"), ((CHIPS, rows, 4 * channels), F32, "v"), ((length, channels), F32, "v"),
            ((length, channels), F32, "v"), ((8, channels), F32, "v"), ((2, CHIPS, rows, channels), BF, "v"),
            ((width, half), BF, "h"), ((half, width), BF, "h"),
        ],
        [
            ((width, 2 * channels), BF), ((channels, width), BF), ((CHIPS, rows, channels), BF),
            ((length, channels), BF), ((length + 16, channels), F32), ((length, channels), BF),
            ((8, channels), F32), ((planes - 1, 8, channels), F32),
        ] + tail,
    )
    feed_scratch = [((width, half), BF), ((width, half), BF), ((half, width), BF), ((half, width), BF), ((half, width), F32)]
    up_blocks = ((planes, width // planes, half), BF, "v")
    down_blocks = ((planes, half // planes, width), BF, "v")
    small_row = ((8, width), F32, "v")
    result, third_grad, small_d, up2_parts, down2_parts = launch(
        second_kernel, "second", 3, planes,
        [(third, "v"), (small_all, "v"), (up2, "v"), (down2, "v"), (out_grad, "v")],
        [((1, rows, width), BF, "v"), row_f, small_row, up_blocks, down_blocks],
        [
            ((width, half), BF), ((half, width), BF), (quad, BF), ((CHIPS, rows, 2 * half), F32), (quad, BF),
            ((CHIPS, rows, 2 * half), BF), ((CHIPS, rows, 2 * half), BF), stage, stage, stage, stage, acc,
        ] + feed_scratch,
    )
    second_grad, small_c, kernel_part, cross, in_parts, conv_parts, up2_sum, down2_sum = launch(
        conv_back_kernel, "conv_back", 4, planes,
        [
            (third_grad, "v"), (second, "v"), (small_all, "v"), (in_w, "v"), (conv_w, "v"), (marks, "v"),
            (hidden2, "v"), (glu, "v"), (gated, "v"), (standard, "v"), (stats, "v"), (swish, "v"),
            (up2_parts, "v"), (down2_parts, "v"),
        ],
        [
            row_f, small_row, ((8, channels), F32, "v"), ((8, channels), F32, "v"),
            ((planes, width // planes, 2 * channels), BF, "v"), ((planes, channels // planes, width), BF, "v"),
            ((width // planes, half), BF, "v"), ((half // planes, width), BF, "v"),
        ],
        [
            ((width, 2 * channels), BF), ((channels, width), BF), (quad, BF), ((CHIPS, rows, channels), F32),
            ((length, channels), F32), ((length + 16, channels), F32), ((length, channels), F32),
            ((2, CHIPS, rows, channels), F32), ((2, CHIPS, rows, 2 * channels), BF), ((8, channels), F32),
            ((planes - 1, 8, channels), F32), ((width, 2 * channels), BF), ((width, 2 * channels), BF),
            ((channels, width), BF), ((channels, width), BF), ((planes - 1, width // planes, half), BF),
            ((planes - 1, half // planes, width), BF),
        ] + tail,
    )
    first_grad, small_b, qkv_parts, out_parts, in_sum, conv_out_grad = launch(
        attend_back_kernel, "attend_back", 5, planes,
        [
            (second_grad, "v"), (first, "v"), (small_all, "v"), (qkv, "v"), (out_w, "v"), (slope, "s"), (marks, "v"),
            (row_ids, "v"), (hidden1, "v"), (joint, "v"), (mixed, "v"), (in_parts, "v"), (conv_parts, "v"),
        ],
        [
            row_f, small_row, ((planes, width // planes, 3 * size), BF, "v"),
            ((planes, size // planes, width), BF, "v"), ((width // planes, 2 * channels), BF, "v"),
            ((channels // planes, width), F32, "v"),
        ],
        [
            ((width, 3 * size), BF), ((size, width), BF), (quad, BF), ((CHIPS, rows, size), BF),
            ((length, size), BF), ((length, 3 * size), BF), ((length, size), F32), ((length, size), F32),
            ((2, CHIPS, rows, 3 * size), BF), ((width, 3 * size), BF), ((width, 3 * size), BF),
            ((size, width), BF), ((size, width), BF), ((planes - 1, width // planes, 2 * channels), BF),
            ((planes - 1, channels // planes, width), BF),
        ] + tail,
    )
    frames_grad, small_a, up1_parts, down1_parts, qkv_sum, attn_out_grad = launch(
        first_back_kernel, "first_back", 6, planes,
        [
            (first_grad, "v"), (frames, "v"), (small_all, "v"), (up1, "v"), (down1, "v"), (hidden0, "v"),
            (keep0, "v"), (qkv_parts, "v"), (out_parts, "v"),
        ],
        [
            ((1, rows, width), F32, "v"), small_row, up_blocks, down_blocks,
            ((width // planes, 3 * size), BF, "v"), ((size // planes, width), F32, "v"),
        ],
        [
            ((width, half), BF), ((half, width), BF), (quad, BF), ((CHIPS, rows, 2 * half), BF),
            ((CHIPS, rows, 2 * half), BF), ((planes - 1, width // planes, 3 * size), BF),
            ((planes - 1, size // planes, width), BF),
        ] + tail + feed_scratch,
    )
    near = seqs - 1
    up1_grad, up2_grad, qkv_grad, in_grad, down1_sum, small_total, kernel_total = launch(
        last_kernel, "last", 7, planes,
        [
            (up1_parts, "v"), (down1_parts, "v"), (up2_sum, "v"), (qkv_sum, "v"), (in_sum, "v"), (small_a, "v"),
            (small_b, "v"), (small_c, "v"), (small_d, "v"), (kernel_part, "v"),
        ],
        [
            ((block, hidden_units), F32, "v"), ((block, hidden_units), F32, "v"), ((block, 3 * width), F32, "v"),
            ((block, 2 * width), F32, "v"), ((half // planes, width), BF, "v"), small_row,
            ((8, channels), F32, "v"),
        ],
        [
            ((planes - 1, width // planes, half), BF), ((planes - 1, half // planes, width), BF),
            ((width // planes, half), BF), ((near, block, half), BF), ((near, block, half), BF),
            ((near, block, 3 * size), BF), ((near, block, 2 * channels), BF), ((8, width), F32),
            ((planes - 1, 8, width), F32), ((near, 8, width), F32), ((planes - 1, 8, channels), F32),
        ],
    )
    total = seqs * planes
    owners = []
    for s in range(seqs):
        for p in range(planes):
            owners.append((s * planes + p, p * seqs + s))
    down1_grad = lax.ppermute(down1_sum, ("seq", "fsdp"), owners).astype(F32)
    down2_grad = lax.ppermute(down2_sum, ("seq", "fsdp"), owners).astype(F32)
    place = seq * planes + plane
    gains_grad = lax.dynamic_slice_in_dim(small_total, place * block, block, axis=1)[:5]
    kernel_grad = lax.dynamic_slice_in_dim(kernel_total, plane * block, block, axis=1)[:taps]
    batch_grad = lax.dynamic_slice_in_dim(cross[1], plane * block, block)
    slopes_grad = small_total[5, :heads]
    return (
        result, frames_grad, up1_grad, down1_grad, qkv_grad, attn_out_grad, in_grad, kernel_grad, batch_grad,
        conv_out_grad, up2_grad, down2_grad, gains_grad, slopes_grad,
    )


def solution(mesh):
    planar = mesh.shape["seq"] == 2 * CHIPS and mesh.shape["fsdp"] == CHIPS
    chosen = plane_body if planar else body
    placed = (
        P("fsdp", "seq", None),
        P("fsdp", None),
        P("fsdp", None),
        P("fsdp", None),
        P("fsdp", None),
        P("fsdp", None),
        P("fsdp", None),
        P(None, "fsdp"),
        P("fsdp"),
        P("fsdp", None),
        P("fsdp", None),
        P("fsdp", None),
        P(None, "fsdp"),
        P(),
        P("fsdp", "seq", None),
    )
    return jax.shard_map(
        chosen,
        mesh=mesh,
        in_specs=placed,
        out_specs=(
            P("fsdp", "seq", None),
            P("fsdp", "seq", None),
            P(("seq", "fsdp"), None),
            P(("seq", "fsdp"), None),
            P(("seq", "fsdp"), None),
            P(("seq", "fsdp"), None),
            P(("seq", "fsdp"), None),
            P(None, ("seq", "fsdp")),
            P(("seq", "fsdp")),
            P(("seq", "fsdp"), None),
            P(("seq", "fsdp"), None),
            P(("seq", "fsdp"), None),
            P(None, ("seq", "fsdp")),
            P(),
        ),
        check_vma=False,
    )
```

```python
import functools
import math
import types

import jax
import jax.numpy as jnp
from jax import lax
from jax.experimental import pallas as pl
from jax.experimental.pallas import tpu as pltpu
from jax.sharding import PartitionSpec as P

EPSILON = 1e-05
MASKED = -1e30


def extended(x, sides, width):
    for axis, dim in sides:
        size, length = (lax.axis_size(axis), x.shape[dim])
        up = [(i, (i + 1) % size) for i in range(size - 1)]
        down = [(j, i) for i, j in up]
        last = lax.slice_in_dim(x, length - width, length, axis=dim)
        initial = lax.slice_in_dim(x, 0, width, axis=dim)
        before = lax.ppermute(last, axis, up)
        after = lax.ppermute(initial, axis, down)
        x = jnp.concatenate([before, x, after], axis=dim)
    return x


def normed(value, gain):
    average = jnp.mean(value, axis=-1, keepdims=True)
    centred = value - average
    variance = jnp.mean(centred * centred, axis=-1, keepdims=True)
    return centred * lax.rsqrt(variance + EPSILON) * gain


def norm_back(value, gain, gradient):
    pullback = jax.vjp(normed, value, gain)[1]
    return pullback(gradient)


def matmul(left, right):
    return jnp.dot(left, right, preferred_element_type=jnp.float32)


def transposed_left(left, right):
    return lax.dot_general(
        left, right, (((0,), (0,)), ((), ())), preferred_element_type=jnp.float32
    )


def transposed_right(left, right):
    return lax.dot_general(
        left, right, (((1,), (1,)), ((), ())), preferred_element_type=jnp.float32
    )


def item_index(positions, bounds):
    return jnp.sum((positions[:, None] >= bounds[None, :]).astype(jnp.int32), axis=1)


def unpack(weights):
    (
        first_up,
        first_down,
        qkv_full,
        out_full,
        conv_up,
        kernel_full,
        batch_full,
        conv_down,
        second_up,
        second_down,
        gains_full,
    ) = weights
    return (
        first_up,
        first_down,
        qkv_full,
        out_full,
        conv_up,
        kernel_full.astype(jnp.float32),
        batch_full.astype(jnp.float32),
        conv_down,
        second_up,
        second_down,
        gains_full.astype(jnp.float32),
    )


def feed_forward(value, gain, weight_up, weight_down):
    hidden = normed(value, gain).astype(jnp.bfloat16)
    swish = jax.nn.silu(matmul(hidden, weight_up)).astype(jnp.bfloat16)
    return value + 0.5 * matmul(swish, weight_down)


def feed_back(value, gain, weight_up, weight_down, gradient):
    hidden = normed(value, gain).astype(jnp.bfloat16)
    swish, pullback = jax.vjp(jax.nn.silu, matmul(hidden, weight_up))
    swish_low = swish.astype(jnp.bfloat16)
    branch_grad = (0.5 * gradient).astype(jnp.bfloat16)
    down_grad = transposed_left(swish_low, branch_grad)
    active_grad = pullback(transposed_right(branch_grad, weight_down))[0].astype(jnp.bfloat16)
    up_grad = transposed_left(hidden, active_grad)
    value_grad, gain_grad = norm_back(value, gain, transposed_right(active_grad, weight_up))
    return (gradient + value_grad, gain_grad, up_grad, down_grad)


def biased_scores(query_heads, key_heads, slopes, layout):
    query_pos, key_pos, query_ids, key_ids = layout
    raw_scores = jnp.einsum(
        "qhd,khd->hqk", query_heads, key_heads, preferred_element_type=jnp.float32
    )
    distance = jnp.abs(query_pos[:, None] - key_pos[None, :]).astype(jnp.float32)
    scores = (
        raw_scores * (1.0 / math.sqrt(query_heads.shape[2]))
        - slopes[:, None, None] * distance[None]
    )
    shared = query_ids[:, None] == key_ids[None, :]
    return (jnp.where(shared[None], scores, MASKED), distance)


def attention_probs(query, keys, slopes, layout):
    heads = slopes.shape[0]
    head_size = query.shape[1] // heads
    query_heads = query.reshape(query.shape[0], heads, head_size)
    key_heads = keys.reshape(keys.shape[0], heads, head_size)
    scores, distance = biased_scores(query_heads, key_heads, slopes, layout)
    top = jnp.max(scores, axis=-1, keepdims=True)
    exponent = jnp.exp(scores - top)
    total = jnp.sum(exponent, axis=-1, keepdims=True)
    probs = exponent / total
    return (probs, distance, query_heads, key_heads, top[:, :, 0], total[:, :, 0])


def attend(value, gain, weight_qkv, weight_out, slopes, layout):
    feature_width = value.shape[1]
    hidden = normed(value, gain).astype(jnp.bfloat16)
    joint = matmul(hidden, weight_qkv).astype(jnp.bfloat16)
    keys_values = lax.all_gather(joint[:, feature_width:], "seq", axis=0, tiled=True)
    probs, distance, query_heads, key_heads, top, total = attention_probs(
        joint[:, :feature_width], keys_values[:, :feature_width], slopes, layout
    )
    value_heads = keys_values[:, feature_width:].reshape(key_heads.shape)
    mixed = jnp.einsum(
        "hqk,khd->qhd", probs.astype(jnp.bfloat16), value_heads, preferred_element_type=jnp.float32
    )
    mixed = mixed.reshape(value.shape).astype(jnp.bfloat16)
    return (value + matmul(mixed, weight_out), keys_values)


def attend_back(value, gain, weight_qkv, weight_out, slopes, layout, keys_values, gradient):
    feature_width = value.shape[1]
    row_count = value.shape[0]
    hidden = normed(value, gain).astype(jnp.bfloat16)
    joint = matmul(hidden, weight_qkv).astype(jnp.bfloat16)
    probs, distance, query_heads, key_heads, top, total = attention_probs(
        joint[:, :feature_width], keys_values[:, :feature_width], slopes, layout
    )
    probs_low = probs.astype(jnp.bfloat16)
    value_heads = keys_values[:, feature_width:].reshape(key_heads.shape)
    mixed = jnp.einsum("hqk,khd->qhd", probs_low, value_heads, preferred_element_type=jnp.float32)
    mixed = mixed.reshape(value.shape).astype(jnp.bfloat16)
    branch_grad = gradient.astype(jnp.bfloat16)
    weight_out_grad = transposed_left(mixed, branch_grad)
    mixed_flat = transposed_right(branch_grad, weight_out).astype(jnp.bfloat16)
    mixed_grad = mixed_flat.reshape(query_heads.shape)
    prob_grad = jnp.einsum(
        "qhd,khd->hqk", mixed_grad, value_heads, preferred_element_type=jnp.float32
    )
    delta = jnp.sum(probs * prob_grad, axis=-1)
    score_grad = probs * (prob_grad - delta[:, :, None])
    slope_grad = -jnp.sum(score_grad * distance[None], axis=(1, 2))
    scale = 1.0 / math.sqrt(query_heads.shape[2])
    raw_grad = (score_grad * scale).astype(jnp.bfloat16)
    query_grad = jnp.einsum("hqk,khd->qhd", raw_grad, key_heads, preferred_element_type=jnp.float32)
    query_pos, key_pos, query_ids, key_ids = layout
    all_query, all_mixed = (
        lax.all_gather(joint[:, :feature_width], "seq", axis=0, tiled=True),
        lax.all_gather(mixed_flat, "seq", axis=0, tiled=True),
    )
    all_top, all_total, all_delta = (
        lax.all_gather(top, "seq", axis=1, tiled=True),
        lax.all_gather(total, "seq", axis=1, tiled=True),
        lax.all_gather(delta, "seq", axis=1, tiled=True),
    )
    heads = slopes.shape[0]
    head_size = query_heads.shape[2]
    all_query_heads = all_query.reshape(all_query.shape[0], heads, head_size)
    all_mixed_heads = all_mixed.reshape(all_query.shape[0], heads, head_size)
    own_keys = joint[:, feature_width : 2 * feature_width].reshape(row_count, heads, head_size)
    own_values = joint[:, 2 * feature_width :].reshape(row_count, heads, head_size)
    column_scores, column_distance = biased_scores(
        all_query_heads, own_keys, slopes, (key_pos, query_pos, key_ids, query_ids)
    )
    column_probs = jnp.exp(column_scores - all_top[:, :, None]) / all_total[:, :, None]
    column_prob_grad = jnp.einsum(
        "qhd,khd->hqk", all_mixed_heads, own_values, preferred_element_type=jnp.float32
    )
    column_score_grad = column_probs * (column_prob_grad - all_delta[:, :, None])
    column_raw = (column_score_grad * scale).astype(jnp.bfloat16)
    key_grad = jnp.einsum(
        "hqk,qhd->khd", column_raw, all_query_heads, preferred_element_type=jnp.float32
    )
    value_grad = jnp.einsum(
        "hqk,qhd->khd",
        column_probs.astype(jnp.bfloat16),
        all_mixed_heads,
        preferred_element_type=jnp.float32,
    )
    local_grad = jnp.concatenate(
        [key_grad.reshape(row_count, feature_width), value_grad.reshape(row_count, feature_width)],
        axis=1,
    )
    joint_grad = jnp.concatenate([query_grad.reshape(value.shape), local_grad], axis=1).astype(
        jnp.bfloat16
    )
    qkv_grad = transposed_left(hidden, joint_grad)
    input_grad, gain_grad = norm_back(value, gain, transposed_right(joint_grad, weight_qkv))
    return (gradient + input_grad, gain_grad, qkv_grad, weight_out_grad, slope_grad)


def gate_linear(joint):
    feature_width = joint.shape[1] // 2
    return joint[:, :feature_width] * jax.nn.sigmoid(joint[:, feature_width:])


def depthwise(rim, kernel, rim_ids, own_ids):
    row_count = own_ids.shape[0]
    total = jnp.zeros((row_count, rim.shape[1]), jnp.float32)
    for offset in range(kernel.shape[0]):
        shared = (rim_ids[offset : offset + row_count] == own_ids).astype(jnp.float32)
        total = (
            total
            + kernel[offset]
            * rim[offset : offset + row_count].astype(jnp.float32)
            * shared[:, None]
        )
    return total


def depthwise_back(rim, kernel, rim_ids, own_ids, conv_grad):
    row_count = own_ids.shape[0]
    reach = kernel.shape[0] - 1
    grad_rim = extended(conv_grad.astype(jnp.bfloat16), (("seq", 0),), reach // 2).astype(
        conv_grad.dtype
    )
    input_grad = jnp.zeros(conv_grad.shape, jnp.float32)
    kernel_rows = []
    for offset in range(kernel.shape[0]):
        shared = (rim_ids[offset : offset + row_count] == own_ids).astype(jnp.float32)[:, None]
        kernel_rows.append(
            jnp.sum(
                rim[offset : offset + row_count].astype(jnp.float32) * shared * conv_grad, axis=0
            )
        )
        mirror = reach - offset
        crossed = (rim_ids[mirror : mirror + row_count] == own_ids).astype(jnp.float32)[:, None]
        input_grad = input_grad + kernel[offset] * grad_rim[mirror : mirror + row_count] * crossed
    return (input_grad, jnp.stack(kernel_rows))


def body(
    frames,
    lengths,
    up_first,
    down_first,
    joint_qkv,
    attn_out,
    conv_in,
    conv_kernel,
    batch_gain,
    conv_out,
    up_second,
    down_second,
    norm_gains,
    slopes,
    out_grad,
):
    sharded = (
        up_first,
        down_first,
        joint_qkv,
        attn_out,
        conv_in,
        conv_kernel,
        batch_gain,
        conv_out,
        up_second,
        down_second,
        norm_gains,
    )
    gathered = (
        lax.all_gather(sharded[0], "fsdp", axis=0, tiled=True),
        lax.all_gather(sharded[1], "fsdp", axis=0, tiled=True),
        lax.all_gather(sharded[2], "fsdp", axis=0, tiled=True),
        lax.all_gather(sharded[3], "fsdp", axis=0, tiled=True),
        lax.all_gather(sharded[4], "fsdp", axis=0, tiled=True),
        lax.all_gather(sharded[5], "fsdp", axis=1, tiled=True),
        lax.all_gather(sharded[6], "fsdp", axis=0, tiled=True),
        lax.all_gather(sharded[7], "fsdp", axis=0, tiled=True),
        lax.all_gather(sharded[8], "fsdp", axis=0, tiled=True),
        lax.all_gather(sharded[9], "fsdp", axis=0, tiled=True),
        lax.all_gather(sharded[10], "fsdp", axis=1, tiled=True),
    )
    (
        first_up,
        first_down,
        qkv_full,
        out_full,
        conv_up,
        kernel,
        batch_scale,
        conv_down,
        second_up,
        second_down,
        gains,
    ) = unpack(gathered)
    row_count = frames.shape[1]
    feature_width = frames.shape[2]
    seq_count = lax.axis_size("seq")
    start_row = lax.axis_index("seq") * row_count
    bounds = jnp.cumsum(lengths[0])
    item_count = lengths.shape[1]
    own_pos = start_row + jnp.arange(row_count, dtype=jnp.int32)
    key_pos = jnp.arange(row_count * seq_count, dtype=jnp.int32)
    own_ids = item_index(own_pos, bounds)
    layout = (own_pos, key_pos, own_ids, item_index(key_pos, bounds))
    rim_width = conv_kernel.shape[0] // 2
    rim_ids = item_index(
        start_row - rim_width + jnp.arange(row_count + 2 * rim_width, dtype=jnp.int32), bounds
    )
    valid = (own_ids < item_count).astype(jnp.float32)[:, None]
    source = frames[0].astype(jnp.float32)
    first = feed_forward(source, gains[0], first_up, first_down)
    second, keys_values = attend(first, gains[1], qkv_full, out_full, slopes, layout)
    conv_hidden = normed(second, gains[2]).astype(jnp.bfloat16)
    conv_joint = matmul(conv_hidden, conv_up)
    rim = extended(gate_linear(conv_joint).astype(jnp.bfloat16), (("seq", 0),), rim_width)
    conv = depthwise(rim, kernel, rim_ids, own_ids)
    total, count = lax.psum((jnp.sum(valid * conv, axis=0), jnp.sum(valid)), ("seq", "fsdp"))
    average = total / count
    centred = conv - average
    spread = lax.psum(jnp.sum(valid * centred * centred, axis=0), ("seq", "fsdp"))
    variance = spread / count
    inverse = lax.rsqrt(variance + EPSILON)
    standard = (conv - average) * inverse
    pre_swish = standard * batch_scale
    swish, swish_pull = jax.vjp(jax.nn.silu, pre_swish)
    swish_low = swish.astype(jnp.bfloat16)
    third = second + matmul(swish_low, conv_down)
    fourth = feed_forward(third, gains[3], second_up, second_down)
    result = normed(fourth, gains[4])
    regathered = (
        lax.all_gather(sharded[0], "fsdp", axis=0, tiled=True),
        lax.all_gather(sharded[1], "fsdp", axis=0, tiled=True),
        lax.all_gather(sharded[2], "fsdp", axis=0, tiled=True),
        lax.all_gather(sharded[3], "fsdp", axis=0, tiled=True),
        lax.all_gather(sharded[4], "fsdp", axis=0, tiled=True),
        lax.all_gather(sharded[5], "fsdp", axis=1, tiled=True),
        lax.all_gather(sharded[6], "fsdp", axis=0, tiled=True),
        lax.all_gather(sharded[7], "fsdp", axis=0, tiled=True),
        lax.all_gather(sharded[8], "fsdp", axis=0, tiled=True),
        lax.all_gather(sharded[9], "fsdp", axis=0, tiled=True),
        lax.all_gather(sharded[10], "fsdp", axis=1, tiled=True),
    )
    (
        first_up,
        first_down,
        qkv_full,
        out_full,
        conv_up,
        kernel,
        batch_scale,
        conv_down,
        second_up,
        second_down,
        gains,
    ) = unpack(regathered)
    fourth_grad, last_gain = norm_back(fourth, gains[4], out_grad[0].astype(jnp.float32))
    third_grad, fourth_gain, second_up_grad, second_down_grad = feed_back(
        third, gains[3], second_up, second_down, fourth_grad
    )
    branch_grad = third_grad.astype(jnp.bfloat16)
    conv_down_grad = transposed_left(swish_low, branch_grad)
    scaled_grad = swish_pull(transposed_right(branch_grad, conv_down))[0]
    sum_grad, sum_cross = lax.psum(
        (jnp.sum(scaled_grad, axis=0), jnp.sum(scaled_grad * standard, axis=0)), ("seq", "fsdp")
    )
    conv_grad = inverse * (scaled_grad * batch_scale) - valid * (inverse / count) * (
        batch_scale * sum_grad + standard * (batch_scale * sum_cross)
    )
    gated_grad, kernel_grad = depthwise_back(rim, kernel, rim_ids, own_ids, conv_grad)
    joint_pull = jax.vjp(gate_linear, conv_joint)[1]
    joint_grad = joint_pull(gated_grad)[0].astype(jnp.bfloat16)
    conv_up_grad = transposed_left(conv_hidden, joint_grad)
    hidden_grad, third_gain = norm_back(second, gains[2], transposed_right(joint_grad, conv_up))
    second_grad = third_grad + hidden_grad
    late = (
        lax.psum_scatter(second_up_grad, ("seq", "fsdp"), scatter_dimension=0, tiled=True),
        lax.psum_scatter(second_down_grad, ("seq", "fsdp"), scatter_dimension=0, tiled=True),
        lax.psum_scatter(conv_down_grad, ("seq", "fsdp"), scatter_dimension=0, tiled=True),
        lax.psum_scatter(conv_up_grad, ("seq", "fsdp"), scatter_dimension=0, tiled=True),
        lax.psum_scatter(kernel_grad, ("seq", "fsdp"), scatter_dimension=1, tiled=True),
    )
    first_grad, second_gain, qkv_grad, out_weight_grad, slope_part = attend_back(
        first, gains[1], qkv_full, out_full, slopes, layout, keys_values, second_grad
    )
    source_grad, first_gain, first_up_grad, first_down_grad = feed_back(
        source, gains[0], first_up, first_down, first_grad
    )
    gain_grads = jnp.stack([first_gain, second_gain, third_gain, fourth_gain, last_gain])
    early = (
        lax.psum_scatter(first_up_grad, ("seq", "fsdp"), scatter_dimension=0, tiled=True),
        lax.psum_scatter(first_down_grad, ("seq", "fsdp"), scatter_dimension=0, tiled=True),
        lax.psum_scatter(qkv_grad, ("seq", "fsdp"), scatter_dimension=0, tiled=True),
        lax.psum_scatter(out_weight_grad, ("seq", "fsdp"), scatter_dimension=0, tiled=True),
        lax.psum_scatter(gain_grads, ("seq", "fsdp"), scatter_dimension=1, tiled=True),
    )
    slope_grad = lax.psum(slope_part, ("seq", "fsdp"))
    piece_width = feature_width // lax.axis_size(("seq", "fsdp"))
    batch_piece = lax.dynamic_slice_in_dim(
        sum_cross, lax.axis_index(("seq", "fsdp")) * piece_width, piece_width
    )
    return (
        result[None].astype(jnp.bfloat16),
        source_grad[None],
        early[0],
        early[1],
        early[2],
        early[3],
        late[3],
        late[4],
        batch_piece,
        late[2],
        late[0],
        late[1],
        early[4],
        slope_grad,
    )


BF = jnp.bfloat16
F32 = jnp.float32
MESH = pl.DeviceIdType.MESH
GRANT = 63 * 2**20
CHIPS = 4
PLANES = 4
SLOTS = 320
RIM = 8
V, H, S = pltpu.VMEM, pl.ANY, pltpu.SMEM


def mm(left, right):
    return jnp.dot(left, right, preferred_element_type=F32)


def mm_right(left, right):
    return lax.dot_general(left, right, (((1,), (1,)), ((), ())), preferred_element_type=F32)


def mm_left(left, right):
    return lax.dot_general(left, right, (((0,), (0,)), ((), ())), preferred_element_type=F32)


def span(index, size):
    return pl.ds(pl.multiple_of(index * size, size), size)


class Here:
    def __init__(self):
        self.seq = lax.axis_index("seq")
        self.plane = lax.axis_index("fsdp")
        self.core = lax.rem(self.seq, 2)
        self.chip = lax.div(self.seq, 2)
        column, row = lax.rem(self.chip, 2), lax.div(self.chip, 2)
        self.chips = [
            lax.rem(row + j // 2, 2) * 2 + lax.rem(column + j % 2, 2) for j in range(CHIPS)
        ]

    def peer(self, slot):
        return (self.chips[slot] * 2 + self.core, self.plane)

    def cross(self, slot):
        return (self.chips[slot] * 2 + 1 - self.core, self.plane)

    def sibling(self):
        return self.cross(0)

    def level(self, step):
        return lax.rem(self.plane + step, PLANES)

    def above(self, step):
        return (self.seq, self.level(step))

    def rows(self, slot, half, height):
        return span((self.chips[slot] * 2 + self.core) * 2 + half, height)

    def other_rows(self, slot, half, height):
        return span((self.chips[slot] * 2 + 1 - self.core) * 2 + half, height)


class Mail:
    def __init__(self, send, recv):
        self.send, self.recv, self.count, self.open, self.kept = send, recv, 0, [], []

    def slot(self):
        self.count += 1
        return self.count - 1

    def remote(self, src, dst, device, sent, received):
        return pltpu.make_async_remote_copy(
            src_ref=src,
            dst_ref=dst,
            send_sem=self.send.at[sent],
            recv_sem=self.recv.at[received],
            device_id=device,
            device_id_type=MESH,
        )

    def post(self, src, dst, device):
        i = self.slot()
        copy = self.remote(src, dst, device, i, i)
        copy.start()
        self.open.append(copy)
        return copy

    def settle(self, copies):
        for copy in copies:
            copy.wait_send()
        self.open = [copy for copy in self.open if all(copy is not done for done in copies)]

    def local(self, src, dst):
        copy = pltpu.make_async_copy(src, dst, self.send.at[self.slot()])
        copy.start()
        return copy

    def save(self, src, dst):
        self.kept.append(self.local(src, dst))

    def close(self):
        for copy in self.open:
            copy.wait_send()
        for copy in self.kept:
            copy.wait()
        self.open, self.kept = [], []


def greet(devices, extra=None):
    barrier = pltpu.get_barrier_semaphore()
    for device in devices:
        pl.semaphore_signal(barrier, inc=1, device_id=device, device_id_type=MESH)
    count = len(devices)
    if extra is not None:
        apart, device = extra
        count = count + apart.astype(jnp.int32)

        @pl.when(apart)
        def _():
            pl.semaphore_signal(barrier, inc=1, device_id=device, device_id_type=MESH)

    pl.semaphore_wait(barrier, count)


def near(here):
    return (
        [here.peer(j) for j in range(1, CHIPS)]
        + [here.sibling()]
        + [here.above(k) for k in range(1, PLANES)]
    )


class Spread:
    def __init__(self, mail, here, buf, half):
        own = buf.at[half, 0]
        self.copies = [None] + [mail.post(own, buf.at[half, j], here.peer(j)) for j in range(1, CHIPS)]

    def near(self):
        self.copies[1].wait_recv()

    def far(self):
        self.copies[2].wait_recv()
        self.copies[3].wait_recv()


class Ring:
    def __init__(self, mail, here, dst, other, fill):
        self.mail, self.here, self.dst, self.other = mail, here, dst, other
        self.height = dst.shape[0] // PLANES
        for copy in fill(dst.at[span(here.plane, self.height)]):
            copy.wait()
        own = self.block(dst, here.plane)
        self.up = mail.post(own, own, here.above(1))
        self.down = mail.post(own, own, here.above(PLANES - 1))
        self.shared = [self.share(here.plane)]

    def block(self, ref, plane):
        return ref.at[span(plane, self.height)]

    def share(self, plane):
        return self.mail.post(self.block(self.dst, plane), self.block(self.other, plane), self.here.sibling())

    def relay(self):
        here, half = self.here, self.height // 2
        self.up.wait_recv()
        piece = self.block(self.dst, here.level(PLANES - 1)).at[pl.ds(0, half)]
        self.far_up = self.mail.post(piece, piece, here.above(1))
        self.down.wait_recv()
        piece = self.block(self.dst, here.level(1)).at[pl.ds(half, half)]
        self.far_down = self.mail.post(piece, piece, here.above(PLANES - 1))
        self.shared += [self.share(here.level(PLANES - 1)), self.share(here.level(1))]

    def finish(self):
        self.far_up.wait_recv()
        self.far_down.wait_recv()
        self.shared.append(self.share(self.here.level(2)))

    def ready(self):
        for copy in self.shared:
            copy.wait_recv()


class FromPlane:
    def __init__(self, mail, here, src, dst, other):
        self.mail, self.here, self.dst, self.other = mail, here, dst, other
        half = dst.shape[0] // 2
        top, low = pl.ds(0, half), pl.ds(half, half)
        slots = [mail.slot() for _ in range(4)]
        above, below = here.above(1), here.above(PLANES - 1)
        self.step = lax.rem(here.plane + PLANES - here.chip, PLANES)
        self.own = pltpu.make_async_copy(src, dst, mail.send.at[mail.slot()])
        self.up = mail.remote(src, dst, above, slots[0], slots[0])
        self.down = mail.remote(src, dst, below, slots[1], slots[1])
        self.far_up = mail.remote(dst.at[top], dst.at[top], above, slots[2], slots[2])
        self.far_down = mail.remote(dst.at[low], dst.at[low], below, slots[3], slots[3])

        @pl.when(self.step == 0)
        def _():
            self.own.start()
            self.up.start()
            self.down.start()

    def relay(self):
        @pl.when(self.step == 1)
        def _():
            self.up.wait_recv()
            self.far_up.start()

        @pl.when(self.step == PLANES - 1)
        def _():
            self.down.wait_recv()
            self.far_down.start()

    def finish(self):
        @pl.when(self.step == 0)
        def _():
            self.own.wait()
            self.up.wait_send()
            self.down.wait_send()

        @pl.when(self.step == 1)
        def _():
            self.far_up.wait_send()

        @pl.when(self.step == 2)
        def _():
            self.far_up.wait_recv()
            self.far_down.wait_recv()

        @pl.when(self.step == PLANES - 1)
        def _():
            self.far_down.wait_send()

        self.shared = self.mail.post(self.dst, self.other, self.here.sibling())

    def ready(self):
        self.shared.wait_recv()


class RingSum:
    def __init__(self, mail, here, parts, relays, land):
        self.mail, self.here, self.parts, self.relays, self.land = mail, here, parts, relays, land
        self.half = parts.shape[1] // 2
        self.top, self.low = pl.ds(0, self.half), pl.ds(self.half, self.half)
        far, up, down = here.level(2), here.level(1), here.level(PLANES - 1)
        above, below = here.above(1), here.above(PLANES - 1)
        self.far_up = mail.post(parts.at[far, self.top], relays.at[0], above)
        self.far_down = mail.post(parts.at[far, self.low], relays.at[1], below)
        self.up_low = mail.post(parts.at[up, self.low], land.at[0, self.low], above)
        self.down_top = mail.post(parts.at[down, self.top], land.at[1, self.top], below)

    def relay(self):
        here, relays = self.here, self.relays
        up, down = here.level(1), here.level(PLANES - 1)
        self.far_up.wait_recv()
        relays[2] = (relays[0].astype(F32) + self.parts[up, self.top].astype(F32)).astype(BF)
        self.up_top = self.mail.post(relays.at[2], self.land.at[0, self.top], here.above(1))
        self.far_down.wait_recv()
        relays[3] = (relays[1].astype(F32) + self.parts[down, self.low].astype(F32)).astype(BF)
        self.down_low = self.mail.post(relays.at[3], self.land.at[1, self.low], here.above(PLANES - 1))

    def total(self):
        for copy in (self.up_low, self.down_top, self.up_top, self.down_low):
            copy.wait_recv()
        return (
            self.parts[self.here.plane].astype(F32) + self.land[0].astype(F32) + self.land[1].astype(F32)
        )


def scale_row(small_ref, index):
    rows = [small_ref[k].astype(F32)[index : index + 1, :] for k in range(PLANES)]
    return jnp.concatenate(rows, axis=1)


def own_channels(small_ref, here, rows, width):
    return small_ref[here.chip, :, span(here.core, width)].astype(F32)[rows, :]


def whitened(value):
    average = jnp.mean(value, axis=-1, keepdims=True)
    centred = value - average
    inverse = lax.rsqrt(jnp.mean(centred * centred, axis=-1, keepdims=True) + EPSILON)
    return centred * inverse, inverse


def norm_grad(value, gain, gradient):
    white, inverse = whitened(value)
    inner = gradient * gain
    value_grad = inverse * (
        inner
        - jnp.mean(inner, axis=-1, keepdims=True)
        - white * jnp.mean(inner * white, axis=-1, keepdims=True)
    )
    return value_grad, jnp.sum(gradient * white, axis=0, keepdims=True)


def at_row(index, row, height=8):
    place = lax.broadcasted_iota(jnp.int32, (height, row.shape[1]), 0)
    return jnp.where(place == index, row, 0.0)


def sigmoid(value):
    return 1.0 / (1.0 + jnp.exp(-value))


def item_of(position, lengths):
    end, item = 0, jnp.zeros(position.shape, jnp.int32)
    for k in range(lengths.shape[1]):
        end = end + lengths[0, k]
        item = item + (position >= end).astype(jnp.int32)
    return item


def set_marks(marks, lengths):
    taps, (frames, width) = marks.shape[0] - 1, marks.shape[1:]
    position = lax.broadcasted_iota(jnp.int32, (frames, width), 0)
    item = item_of(position, lengths)
    for t in range(taps):
        other = position + (t - taps // 2)
        shared = (item_of(other, lengths) == item) & (other >= 0) & (other < frames)
        marks[t] = shared.astype(F32).astype(BF)
    marks[taps] = (item < lengths.shape[1]).astype(F32).astype(BF)


class Reduce:
    def __init__(self, mail, here, bufs, half):
        self.mail, self.here, self.half, self.copies = mail, here, half, []
        self.stage, self.land, self.acc = bufs

    def put(self, pair, value):
        rows = value.shape[0] // 2
        for k in range(2):
            slot, term = 2 * pair + k, value[k * rows : (k + 1) * rows]
            if slot == 0:
                self.acc[self.half] = term
                continue
            place = self.stage.at[self.half, slot - 1]
            place[...] = term.astype(BF)
            self.copies.append(self.mail.post(place, self.land.at[self.half, slot - 1], self.here.peer(slot)))

    def total(self):
        for copy in self.copies:
            copy.wait_recv()
        self.mail.settle(self.copies)
        value = self.acc[self.half]
        for j in range(1, CHIPS):
            value = value + self.land[self.half, j - 1].astype(F32)
        return value


def flat(ref, columns=None):
    value = ref[...] if columns is None else ref[:, :, :, columns]
    return value.reshape(-1, value.shape[-1])


def pair_of(ref, half, pair, columns=slice(None)):
    value = ref[half, 2 * pair : 2 * pair + 2, :, columns]
    return value.reshape(-1, value.shape[-1])


def set_pair(ref, half, pair, value, columns=slice(None)):
    ref[half, 2 * pair : 2 * pair + 2, :, columns] = value.reshape(2, -1, value.shape[-1])


def feed_active(hidden, keep, up, half, pair):
    width = up[0].shape[1]
    rows = pair_of(hidden, half, pair)
    for side in range(2):
        set_pair(keep, half, pair, mm(rows, up[side][...]), slice(side * width, (side + 1) * width))


def feed_out(keep, down, half, pair):
    width = down[0].shape[0]
    total = None
    for side in range(2):
        active = pair_of(keep, half, pair, slice(side * width, (side + 1) * width))
        term = mm((active * sigmoid(active)).astype(BF), down[side][...])
        total = term if total is None else total + term
    return total


def feed_slope(branch, keep, down, swish, active_grad, half, pair):
    width = down[0].shape[0]
    rows = pair_of(branch, half, pair)
    for side in range(2):
        columns = slice(side * width, (side + 1) * width)
        active = pair_of(keep, half, pair, columns)
        gate = sigmoid(active)
        set_pair(swish, half, pair, (active * gate).astype(BF), columns)
        grad = mm_right(rows, down[side][...]) * (gate * (1.0 + active * (1.0 - gate)))
        set_pair(active_grad, half, pair, grad.astype(BF), columns)


def feed_in(active_grad, up, half, pair):
    width = up[0].shape[1]
    total = None
    for side in range(2):
        term = mm_right(pair_of(active_grad, half, pair, slice(side * width, (side + 1) * width)), up[side][...])
        total = term if total is None else total + term
    return total


def pair_product(mail, here, left, right, blocks, send, land, store):
    height = send.shape[0] // blocks
    copies = []
    for i in range(blocks):
        rows = pl.ds(i * height, height)
        send[rows, :] = mm_left(left(1, i), right(1)).astype(BF)
        copies.append(mail.post(send.at[rows], land.at[rows], here.sibling()))
    for i in range(blocks):
        rows = pl.ds(i * height, height)
        grad = mm_left(left(0, i), right(0))
        copies[i].wait_recv()
        store(i, (grad + land[rows, :].astype(F32)).astype(BF))
    return copies


def by_plane(out):
    def store(i, value):
        height = out.shape[1]
        each = value.shape[0] // height
        for k in range(each):
            out[i * each + k] = value[k * height : (k + 1) * height]

    return store


def by_owner(out):
    def store(i, value):
        seqs = 2 * CHIPS
        height = out.shape[1] // seqs
        each = value.shape[0] // (height * PLANES)
        for k in range(each):
            for p in range(PLANES):
                start = (k * PLANES + p) * height
                at = (i * each + k) * height
                out[p, at : at + height, :] = value[start : start + height]

    return store


def down_grad(mail, here, branch, swish, out, send, land):
    half = swish.shape[3] // 2
    block = half // 2
    return pair_product(
        mail, here,
        lambda side, i: flat(swish, slice(side * half + i * block, side * half + (i + 1) * block)),
        lambda side: flat(branch),
        2, send, land, by_plane(out),
    )


def up_grad(mail, here, hidden, active_grad, out, send, land):
    half = active_grad.shape[3] // 2
    block = hidden.shape[3] // 4
    return pair_product(
        mail, here,
        lambda side, i: flat(hidden, slice(i * block, (i + 1) * block)),
        lambda side: flat(active_grad, slice(side * half, (side + 1) * half)),
        4, send, land, by_owner(out),
    )


def slots_grad(mail, here, rows, sides, out, send, land):
    block = rows.shape[3] // 4
    return pair_product(
        mail, here,
        lambda side, i: flat(rows, slice(i * block, (i + 1) * block)),
        lambda side: flat(sides.at[side]),
        4, send, land, by_owner(out),
    )


def sides_grad(mail, here, sides, rows, out, send, land):
    return pair_product(
        mail, here, lambda side, i: flat(sides.at[side]), lambda side: flat(rows), 1, send, land, by_plane(out)
    )


def attention_weights(query, keys, slope, row, lengths):
    column = lax.broadcasted_iota(jnp.int32, (8, keys.shape[0]), 1)[:1, :]
    distance = jnp.abs(row.astype(F32) - column.astype(F32))
    scores = mm_right(query, keys) * (1.0 / math.sqrt(query.shape[1])) - slope * distance
    scores = jnp.where(item_of(row, lengths) == item_of(column, lengths), scores, MASKED)
    exponent = jnp.exp(scores - jnp.max(scores, axis=-1, keepdims=True))
    return exponent * (1.0 / jnp.sum(exponent, axis=-1, keepdims=True)), distance


def kernel_refs(names, refs):
    return types.SimpleNamespace(**dict(zip(names, refs, strict=True)))


def forward_kernel(names, *refs):
    r = kernel_refs(names, refs)
    here, mail = Here(), Mail(r.send, r.recv)
    lengths, small, marks = r.lengths, r.small, r.marks
    rows = r.frames.shape[1] // 2
    greet(near(here))

    def columns_of(src):
        width = 128

        def fill(region):
            groups = region.shape[1] // width
            stride = src.shape[1] // groups
            return [
                mail.local(
                    src.at[:, pl.ds(pl.multiple_of(g * stride + here.seq * width, width), width)],
                    region.at[:, pl.ds(g * width, width)],
                )
                for g in range(groups)
            ]

        return fill

    def rows_of(src):
        return lambda region: [mail.local(src.at[span(here.seq, region.shape[0]), :], region)]

    def core_rows_of(src, dst, other):
        return FromPlane(mail, here, src.at[span(here.core, dst.shape[0]), :], dst, other)

    def part(half):
        return slice(half * rows, (half + 1) * rows)

    def spread(buf, half, value, gain):
        buf[half, 0] = (whitened(value)[0] * gain).astype(BF)
        return Spread(mail, here, buf, half)

    def reduce(land):
        return [Reduce(mail, here, (r.stage, land, r.acc), h) for h in range(2)]

    own_small = small.at[here.plane]
    small_copy = mail.local(r.small_src, own_small)
    small_copies = [mail.post(r.small_src, own_small, here.above(k)) for k in range(1, PLANES)]
    up1 = Ring(mail, here, r.up1, r.up1_other, columns_of(r.up1_src))
    down1 = Ring(mail, here, r.down1, r.down1_other, rows_of(r.down1_src))

    small_copy.wait()
    for copy in small_copies:
        copy.wait_recv()
    gain = scale_row(small, 0)
    sent = [spread(r.hidden0, h, r.frames[0, part(h), :].astype(F32), gain) for h in range(2)]
    set_marks(marks, lengths)
    for h in range(2):
        sent[h].near()
    up1.relay()
    for h in range(2):
        sent[h].far()
    down1.relay()
    qkv = Ring(mail, here, r.qkv, r.qkv_other, columns_of(r.qkv_src))
    out = core_rows_of(r.out_src, r.out, r.out_other)
    up1.finish()
    up1.ready()
    ups, downs = (r.up1, r.up1_other), (r.down1, r.down1_other)
    for h in range(2):
        for p in range(2):
            feed_active(r.hidden0, r.keep0, ups, h, p)
    down1.finish()
    mail.save(r.hidden0, r.hidden0_out)
    mail.save(r.keep0, r.keep0_out)
    mail.save(r.up1, r.up1_out)
    mail.save(r.down1, r.down1_out)
    down1.ready()
    sums = reduce(r.land0)
    for h in range(2):
        for p in (1, 0):
            sums[h].put(p, feed_out(r.keep0, downs, h, p))
    qkv.relay()
    conv_in = Ring(mail, here, r.conv_in, r.conv_in_other, columns_of(r.in_src))
    gain = scale_row(small, 1)
    sent = []
    for h in range(2):
        value = r.frames[0, part(h), :].astype(F32) + 0.5 * sums[h].total()
        r.first[part(h), :] = value
        sent.append(spread(r.hidden1, h, value, gain))
    out.relay()
    conv_out = core_rows_of(r.conv_src, r.conv_out, r.conv_out_other)

    joint, mixed = r.joint, r.mixed
    size = joint.shape[1] // 3
    qkv.finish()
    qkv.ready()
    mail.save(r.qkv, r.qkv_out)
    joint_copies = []
    for h in range(2):
        for p in range(2):
            if p:
                sent[h].far()
            else:
                sent[h].near()
            value = pair_of(r.hidden1, h, p)
            set_pair(r.joint_stage, h, p, mm(value, r.qkv_other[...]).astype(BF))
            for j in (2 * p, 2 * p + 1):
                joint_copies.append(
                    mail.post(r.joint_stage.at[h, j], joint.at[here.rows(j, h, rows), :], here.sibling())
                )
            value = mm(value, r.qkv[...]).astype(BF)
            for k in range(2):
                joint[here.rows(2 * p + k, h, rows), :] = value[k * rows : (k + 1) * rows]
    for copy in joint_copies:
        copy.wait_recv()
    conv_in.relay()
    up2 = Ring(mail, here, r.up2, r.up2_other, columns_of(r.up2_src))
    mail.save(r.hidden1, r.hidden1_out)
    mail.save(joint, r.joint_out)
    slope = r.slopes[here.seq]
    mixed_copies = {}
    sums = reduce(r.land1)

    def unit(h, j):
        mine, theirs = here.rows(j, h, rows), here.other_rows(j, h, rows)
        query = jnp.concatenate([joint[mine, 0:size], joint[theirs, 0:size]], axis=0)
        index = lax.broadcasted_iota(jnp.int32, (2 * rows, 128), 0)[:, :1]
        frame = jnp.where(index < rows, mine.start + index, theirs.start + index - rows)
        weights = attention_weights(query, joint[:, size : 2 * size], slope, frame, lengths)[0]
        value = mm(weights.astype(BF), joint[:, 2 * size :]).astype(BF)
        mixed[0, h, j] = value[:rows]
        r.mixed_stage[h, j] = value[rows:]
        mixed_copies[h, j] = mail.post(r.mixed_stage.at[h, j], mixed.at[1, h, j], here.sibling())

    def project(h, p):
        for j in (2 * p, 2 * p + 1):
            mixed_copies[h, j].wait_recv()
        value = mm(pair_of(mixed.at[0], h, p), r.out[...]) + mm(pair_of(mixed.at[1], h, p), r.out_other[...])
        sums[h].put(p, value)

    unit(0, 2)
    unit(0, 3)
    out.finish()
    unit(0, 0)
    out.ready()
    project(0, 1)
    unit(0, 1)
    unit(1, 2)
    project(0, 0)
    unit(1, 3)
    unit(1, 0)
    project(1, 1)
    unit(1, 1)
    project(1, 0)
    mail.save(r.out, r.out_out)
    mail.save(mixed, r.mixed_out)
    gain = scale_row(small, 2)
    sent = []
    for h in range(2):
        value = r.first[part(h), :] + sums[h].total()
        r.second[part(h), :] = value
        sent.append(spread(r.hidden2, h, value, gain))
        if h == 0:
            conv_in.finish()
            conv_out.relay()

    gated, padded, glu = r.gated, r.padded, r.glu
    frames, width = gated.shape
    conv_in.ready()
    mail.save(r.conv_in, r.in_out)
    gate_copies = []
    for h in range(2):
        for p in range(2):
            if p:
                sent[h].far()
            else:
                sent[h].near()
            value = pair_of(r.hidden2, h, p)
            for side, weight in ((1, r.conv_in_other), (0, r.conv_in)):
                both = mm(value, weight[...])
                set_pair(glu, h, p, both, slice(2 * width * side, 2 * width * (side + 1)))
                gate = (both[:, :width] * sigmoid(both[:, width:])).astype(BF)
                for k in range(2):
                    j = 2 * p + k
                    if side:
                        r.gate_stage[h, j] = gate[k * rows : (k + 1) * rows]
                        gate_copies.append(
                            mail.post(
                                r.gate_stage.at[h, j], r.gate_rows.at[here.rows(j, h, rows), :], here.sibling()
                            )
                        )
                    else:
                        r.gate_rows[here.rows(j, h, rows), :] = gate[k * rows : (k + 1) * rows]
    mail.save(r.hidden2, r.hidden2_out)
    mail.save(glu, r.glu_out)
    up2.relay()
    for copy in gate_copies:
        copy.wait_recv()
    taps = marks.shape[0] - 1
    padded[0:RIM, :] = jnp.zeros((RIM, width), F32)
    padded[RIM + frames :, :] = jnp.zeros((RIM, width), F32)
    gated[...] = r.gate_rows[...].astype(F32)
    padded[RIM : RIM + frames, :] = gated[...]
    mail.save(gated, r.gated_out)
    kernel = own_channels(small, here, slice(5, 5 + taps), width)
    conv = None
    for t in range(taps):
        first = RIM - taps // 2 + t
        term = kernel[t : t + 1, :] * padded[first : first + frames, :] * marks[t].astype(F32)
        conv = term if conv is None else conv + term
    valid = marks[taps].astype(F32)
    count = jnp.sum(valid, axis=0, keepdims=True)
    total = jnp.sum(valid * conv, axis=0, keepdims=True)
    centred = conv - total / count
    squares = jnp.sum(valid * centred * centred, axis=0, keepdims=True)
    bn, bn_land = r.bn, r.bn_land
    bn[...] = at_row(0, total) + at_row(1, squares) + at_row(2, count)
    bn_copies = [mail.post(bn, bn_land.at[k - 1], here.above(k)) for k in range(1, PLANES)]
    down2 = Ring(mail, here, r.down2, r.down2_other, rows_of(r.down2_src))
    r.standard[...] = conv
    conv_out.finish()
    for copy in bn_copies:
        copy.wait_recv()
    terms = [bn[...]] + [bn_land[k - 1] for k in range(1, PLANES)]
    whole = sum(term[2:3, :] for term in terms)
    average = sum(term[0:1, :] for term in terms) / whole
    variance = 0.0
    for term in terms:
        apart = term[0:1, :] / term[2:3, :] - average
        variance = variance + term[1:2, :] + term[2:3, :] * apart * apart
    inverse = lax.rsqrt(variance / whole + EPSILON)
    r.stats[...] = at_row(0, inverse) + at_row(1, whole)
    standard = (r.standard[...] - average) * inverse
    r.standard[...] = standard
    scaled = standard * own_channels(small, here, slice(10, 11), width)
    r.swish_rows[...] = (scaled * sigmoid(scaled)).astype(BF)
    swish = r.swish
    swish_copies = {}
    for h in range(2):
        for j in (2, 3, 0, 1):
            swish_copies[h, j] = mail.post(
                r.swish_rows.at[here.other_rows(j, h, rows), :], swish.at[1, h, j], here.sibling()
            )
            swish[0, h, j] = r.swish_rows[here.rows(j, h, rows), :]
    mail.save(r.standard, r.standard_out)
    conv_out.ready()
    mail.save(r.conv_out, r.conv_out_out)
    sums = reduce(r.land2)
    for h in range(2):
        for p in (1, 0):
            for j in (2 * p, 2 * p + 1):
                swish_copies[h, j].wait_recv()
            value = mm(pair_of(swish.at[0], h, p), r.conv_out[...])
            sums[h].put(p, value + mm(pair_of(swish.at[1], h, p), r.conv_out_other[...]))
    mail.save(swish, r.swish_out)
    up2.finish()
    gain = scale_row(small, 3)
    sent = []
    for h in range(2):
        value = r.second[part(h), :] + sums[h].total()
        r.third[part(h), :] = value
        sent.append(spread(r.hidden3, h, value, gain))
        if h == 0:
            down2.relay()

    up2.ready()
    ups, downs = (r.up2, r.up2_other), (r.down2, r.down2_other)
    sums = reduce(r.land3)
    for h in range(2):
        for p in range(2):
            if p:
                sent[h].far()
            else:
                sent[h].near()
            feed_active(r.hidden3, r.keep3, ups, h, p)
        if h == 0:
            down2.finish()
            down2.ready()
        for p in (1, 0):
            sums[h].put(p, feed_out(r.keep3, downs, h, p))

    last_gain = scale_row(small, 4)
    sent, last_parts = [], []
    for h in range(2):
        fourth = r.third[part(h), :] + 0.5 * sums[h].total()
        r.result[0, part(h), :] = (whitened(fourth)[0] * last_gain).astype(BF)
        gradient, last_part = norm_grad(fourth, last_gain, r.out_grad[0, part(h), :].astype(F32))
        last_parts.append(last_part)
        r.branch[h, 0] = (0.5 * gradient).astype(BF)
        sent.append(Spread(mail, here, r.branch, h))
        r.third_grad[part(h), :] = gradient
    sums = reduce(r.land4)
    for h in range(2):
        for p in range(2):
            if p:
                sent[h].far()
            else:
                sent[h].near()
            feed_slope(r.branch, r.keep3, downs, r.act, r.act_grad, h, p)
            sums[h].put(p, feed_in(r.act_grad, ups, h, p))
    down_grad(mail, here, r.branch, r.act, r.down2_parts, r.down_send, r.down_land)
    up_grad(mail, here, r.hidden3, r.act_grad, r.up2_parts, r.up_send, r.up_land)
    gain_parts = []
    for h in range(2):
        value_part, gain_part = norm_grad(r.third[part(h), :], gain, sums[h].total())
        r.third_grad[part(h), :] = r.third_grad[part(h), :] + value_part
        gain_parts.append(gain_part)
    r.small_d[...] = at_row(3, gain_parts[0] + gain_parts[1]) + at_row(4, last_parts[0] + last_parts[1])
    mail.close()


def backward_kernel(names, *refs):
    r = kernel_refs(names, refs)
    here, mail = Here(), Mail(r.send, r.recv)
    lengths, small, marks = r.lengths, r.small, r.marks
    rows = r.frames.shape[1] // 2
    seqs = 2 * CHIPS
    block = here.plane * seqs + here.seq
    mine = here.seq * PLANES + here.plane
    apart = block != mine
    target = (lax.div(block, PLANES), lax.rem(block, PLANES))
    source = (lax.rem(mine, seqs), lax.div(mine, seqs))
    crosses = [here.cross(j) for j in range(1, CHIPS)]
    greet(near(here) + crosses, (apart, source))

    def share(own, other):
        return mail.post(own, other, here.sibling())

    def part(half):
        return slice(half * rows, (half + 1) * rows)

    def spread(buf, half, value):
        buf[half, 0] = value.astype(BF)
        return Spread(mail, here, buf, half)

    def reduce(land):
        return [Reduce(mail, here, (r.stage, land, r.acc), h) for h in range(2)]

    conv_out_shared = share(r.conv_out_src, r.conv_out_other)
    sent = [spread(r.branch2, h, r.third_grad[part(h), :]) for h in range(2)]
    conv_out_ready = mail.local(r.conv_out_src, r.conv_out)
    standard_ready = mail.local(r.standard_src, r.standard)
    swish_ready = mail.local(r.swish_src, r.swish)
    conv_in_shared = share(r.conv_in_src, r.conv_in_other)
    conv_in_ready = mail.local(r.conv_in_src, r.conv_in)
    glu_ready = mail.local(r.glu_src, r.glu)
    hidden2_ready = mail.local(r.hidden2_src, r.hidden2)
    gated_ready = mail.local(r.gated_src, r.gated)
    down2 = RingSum(mail, here, r.down2_parts, r.down2_relay, r.down2_land)
    set_marks(marks, lengths)

    frames, width = r.gated.shape
    conv_out_shared.wait_recv()
    conv_out_ready.wait()
    copies = []
    for h in range(2):
        for p in range(2):
            if p:
                sent[h].far()
            else:
                sent[h].near()
            incoming = pair_of(r.branch2, h, p)
            set_pair(r.swish_stage, h, p, mm_right(incoming, r.conv_out_other[...]))
            for j in (2 * p, 2 * p + 1):
                copies.append(
                    mail.post(r.swish_stage.at[h, j], r.swish_grad.at[here.rows(j, h, rows), :], here.sibling())
                )
            value = mm_right(incoming, r.conv_out[...])
            for k in range(2):
                r.swish_grad[here.rows(2 * p + k, h, rows), :] = value[k * rows : (k + 1) * rows]
    standard_ready.wait()
    gain = own_channels(small, here, slice(10, 11), width)
    for copy in copies:
        copy.wait_recv()
    white = r.standard[...]
    scaled = white * gain
    gate = sigmoid(scaled)
    scaled_grad = r.swish_grad[...] * (gate * (1.0 + scaled * (1.0 - gate)))
    bn, bn_land = r.bn, r.bn_land
    bn[...] = at_row(0, jnp.sum(scaled_grad, axis=0, keepdims=True)) + at_row(
        1, jnp.sum(scaled_grad * white, axis=0, keepdims=True)
    )
    bn_copies = [mail.post(bn, bn_land.at[k - 1], here.above(k)) for k in range(1, PLANES)]
    r.swish_grad[...] = scaled_grad * gain
    swish_ready.wait()
    row_send, column_send = r.down_send, r.up_send
    row_copies = sides_grad(
        mail, here, r.swish, r.branch2, r.conv_parts, row_send.at[pl.ds(0, width), :], r.conv_land
    )
    for copy in bn_copies:
        copy.wait_recv()
    down2.relay()
    up2 = RingSum(mail, here, r.up2_parts, r.up2_relay, r.up2_land)
    both = bn[...]
    for k in range(1, PLANES):
        both = both + bn_land[k - 1]
    r.cross[...] = both
    inverse, whole = r.stats[0:1, :], r.stats[1:2, :]
    taps = marks.shape[0] - 1
    white = r.standard[...]
    conv_grad = inverse * r.swish_grad[...] - marks[taps].astype(F32) * (
        (inverse / whole) * (gain * both[0:1, :] + white * (gain * both[1:2, :]))
    )
    padded, reach = r.padded, taps // 2
    padded[0:RIM, :] = jnp.zeros((RIM, width), F32)
    padded[RIM + frames :, :] = jnp.zeros((RIM, width), F32)
    padded[RIM : RIM + frames, :] = conv_grad
    kernel = own_channels(small, here, slice(5, 5 + taps), width)
    total = None
    for t in range(taps):
        first = RIM + reach - t
        term = kernel[t : t + 1, :] * padded[first : first + frames, :] * marks[taps - 1 - t].astype(F32)
        total = term if total is None else total + term
    r.gate_grad[...] = total
    moved = r.moved2
    copies = {}
    for h in range(2):
        for j in (2, 3, 0, 1):
            copies[h, j] = mail.post(
                r.gate_grad.at[here.other_rows(j, h, rows), :], moved.at[1, h, j], here.sibling()
            )
            moved[0, h, j] = r.gate_grad[here.rows(j, h, rows), :]
    glu_ready.wait()
    conv_in_ready.wait()
    conv_in_shared.wait_recv()
    glu, glu_grad = r.glu, r.glu_grad
    sums = reduce(r.land2)
    for h in range(2):
        for p in (1, 0):
            for j in (2 * p, 2 * p + 1):
                copies[h, j].wait_recv()
            result = None
            for side, weight in ((0, r.conv_in), (1, r.conv_in_other)):
                start = 2 * width * side
                left = pair_of(glu, h, p, slice(start, start + width))
                gate = sigmoid(pair_of(glu, h, p, slice(start + width, start + 2 * width)))
                incoming = pair_of(moved.at[side], h, p)
                set_pair(glu_grad.at[side], h, p, (incoming * gate).astype(BF), slice(0, width))
                set_pair(
                    glu_grad.at[side], h, p, (incoming * left * (gate * (1.0 - gate))).astype(BF),
                    slice(width, 2 * width),
                )
                term = mm_right(pair_of(glu_grad.at[side], h, p), weight[...])
                result = term if result is None else result + term
            sums[h].put(p, result)
    out_shared, qkv_shared = share(r.out_src, r.out_other), share(r.qkv_src, r.qkv_other)
    out_ready = mail.local(r.out_src, r.out)
    joint_ready = mail.local(r.joint_src, r.joint)
    qkv_ready = mail.local(r.qkv_src, r.qkv)
    mixed_ready = mail.local(r.mixed_src, r.mixed)
    hidden1_ready = mail.local(r.hidden1_src, r.hidden1)
    first_ready = mail.local(r.first_src, r.first)
    hidden2_ready.wait()
    column_copies = slots_grad(
        mail, here, r.hidden2, glu_grad, r.in_parts, column_send.at[:, pl.ds(0, 2 * width)], r.in_land
    )
    gain = scale_row(small, 2)
    sent, gain_parts = [], []
    for h in range(2):
        value_part, gain_part = norm_grad(r.second[part(h), :], gain, sums[h].total())
        gradient = r.third_grad[part(h), :] + value_part
        r.grad[part(h), :] = gradient
        gain_parts.append(gain_part)
        sent.append(spread(r.branch1, h, gradient))
        if h == 0:
            gated_ready.wait()
            dense = padded[RIM : RIM + frames, :]
            padded[RIM : RIM + frames, :] = r.gated[...]
            kernel_rows = jnp.zeros((8, width), F32)
            for t in range(taps):
                first = RIM - reach + t
                row = jnp.sum(
                    padded[first : first + frames, :] * marks[t].astype(F32) * dense, axis=0, keepdims=True
                )
                kernel_rows = kernel_rows + at_row(t, row)
            r.kernel_part[...] = kernel_rows
    r.small_sum[...] = r.small_d[...] + at_row(2, gain_parts[0] + gain_parts[1])
    up2.relay()
    conv_sum = RingSum(mail, here, r.conv_parts, r.conv_relay, r.conv_sum_land)
    in_sum = RingSum(mail, here, r.in_parts, r.in_relay, r.in_sum_land)
    kernel_copies = [
        mail.post(r.kernel_part, r.kernel_land.at[k - 1], here.above(k)) for k in range(1, PLANES)
    ]

    out_shared.wait_recv()
    out_ready.wait()
    joint = r.joint
    size = joint.shape[1] // 3
    copies = []
    for h in range(2):
        for p in range(2):
            if p:
                sent[h].far()
            else:
                sent[h].near()
            incoming = pair_of(r.branch1, h, p)
            set_pair(r.mixed_stage, h, p, mm_right(incoming, r.out_other[...]).astype(BF))
            for j in (2 * p, 2 * p + 1):
                copies.append(
                    mail.post(r.mixed_stage.at[h, j], r.mixed_grad.at[here.rows(j, h, rows), :], here.sibling())
                )
            value = mm_right(incoming, r.out[...]).astype(BF)
            for k in range(2):
                r.mixed_grad[here.rows(2 * p + k, h, rows), :] = value[k * rows : (k + 1) * rows]
    mixed_ready.wait()
    mail.settle(row_copies)
    row_copies = sides_grad(
        mail, here, r.mixed, r.branch1, r.out_parts, row_send.at[pl.ds(0, size), :], r.out_land
    )
    joint_ready.wait()
    for copy in copies:
        copy.wait_recv()
    key_grad, value_grad, joint_grad = r.standard, r.gated, r.joint_grad
    key_grad[...] = jnp.zeros_like(key_grad)
    value_grad[...] = jnp.zeros_like(value_grad)
    scale = 1.0 / math.sqrt(size)
    slope = r.slopes[here.seq]
    height = 2 * rows

    def step(index, carry):
        start = pl.multiple_of(index * height, height)
        block_rows = pl.ds(start, height)
        query, keys, values = joint[block_rows, 0:size], joint[:, size : 2 * size], joint[:, 2 * size :]
        frame = lax.broadcasted_iota(jnp.int32, (height, 128), 0)[:, :1] + start
        weights, distance = attention_weights(query, keys, slope, frame, lengths)
        incoming = r.mixed_grad[block_rows, :]
        weight_grad = mm_right(incoming, values)
        delta = jnp.sum(weights * weight_grad, axis=-1, keepdims=True)
        score_grad = weights * (weight_grad - delta)
        raw = (score_grad * scale).astype(BF)
        joint_grad[block_rows, 0:size] = mm(raw, keys).astype(BF)
        key_grad[...] += mm_left(raw, query)
        value_grad[...] += mm_left(weights.astype(BF), incoming)
        return carry - jnp.sum(score_grad * distance, axis=0, keepdims=True)

    slope_row = lax.fori_loop(0, frames // height, step, jnp.zeros((1, frames), F32))
    joint_grad[:, size : 2 * size] = key_grad[...].astype(BF)
    joint_grad[:, 2 * size :] = value_grad[...].astype(BF)
    moved = r.moved1
    copies = {}
    for h in range(2):
        for j in (2, 3, 0, 1):
            copies[h, j] = mail.post(
                joint_grad.at[here.other_rows(j, h, rows), :], moved.at[1, h, j], here.sibling()
            )
            moved[0, h, j] = joint_grad[here.rows(j, h, rows), :]
    conv_sum.relay()
    in_sum.relay()
    out_sum = RingSum(mail, here, r.out_parts, r.out_relay, r.out_sum_land)
    qkv_shared.wait_recv()
    qkv_ready.wait()
    down_shared, up_shared = share(r.down1_src, r.down1_other), share(r.up1_src, r.up1_other)
    keep0_ready = mail.local(r.keep0_src, r.keep0)
    down1_ready = mail.local(r.down1_src, r.down1)
    up1_ready = mail.local(r.up1_src, r.up1)
    hidden0_ready = mail.local(r.hidden0_src, r.hidden0)
    sums = reduce(r.land1)
    for h in range(2):
        for p in (1, 0):
            for j in (2 * p, 2 * p + 1):
                copies[h, j].wait_recv()
            value = mm_right(pair_of(moved.at[0], h, p), r.qkv[...])
            sums[h].put(p, value + mm_right(pair_of(moved.at[1], h, p), r.qkv_other[...]))
    hidden1_ready.wait()
    mail.settle(column_copies)
    column_copies = slots_grad(
        mail, here, r.hidden1, moved, r.qkv_parts, column_send.at[:, pl.ds(0, 3 * size)], r.qkv_land
    )
    qkv_sum = RingSum(mail, here, r.qkv_parts, r.qkv_relay, r.qkv_sum_land)
    first_ready.wait()
    gain = scale_row(small, 1)
    sent, gain_parts = [], []
    for h in range(2):
        value_part, gain_part = norm_grad(r.first[part(h), :], gain, sums[h].total())
        gradient = r.grad[part(h), :] + value_part
        r.grad[part(h), :] = gradient
        gain_parts.append(gain_part)
        sent.append(spread(r.branch0, h, 0.5 * gradient))
    gain_part = gain_parts[0] + gain_parts[1]
    lane = lax.broadcasted_iota(jnp.int32, gain_part.shape, 1)
    slope_total = jnp.sum(slope_row, axis=1, keepdims=True)
    r.small_sum[...] = (
        r.small_sum[...] + at_row(1, gain_part) + at_row(5, jnp.where(lane == here.seq, slope_total, 0.0))
    )
    out_sum.relay()
    qkv_sum.relay()

    devices = [here.peer(j) for j in range(1, CHIPS)] + [here.cross(j) for j in range(CHIPS)]
    blocks = r.up2_out.shape[0]

    def swap(parts, got):
        return [mail.post(parts.at[span(device[0], blocks), :], got.at[i], device) for i, device in enumerate(devices)]

    def place(parts, got, out, copies):
        lanes = 128
        groups = parts.shape[1] // lanes
        stride = out.shape[1] // groups
        for i in range(len(devices) + 1):
            if i:
                copies[i - 1].wait_recv()
            seq = devices[i - 1][0] if i else here.seq
            value = (got[i - 1] if i else parts[span(here.seq, blocks), :]).astype(F32)
            for g in range(groups):
                at = pl.ds(pl.multiple_of(g * stride + seq * lanes, lanes), lanes)
                out[:, at] = value[:, g * lanes : (g + 1) * lanes]

    def to_owner(index):
        src, dst = r.down_moved.at[index], r.down_got.at[index]
        i = mail.slot()
        stay = pltpu.make_async_copy(src, dst, mail.send.at[mail.slot()])
        go = mail.remote(src, dst, target, i, i)

        @pl.when(apart)
        def _():
            go.start()

        @pl.when(jnp.logical_not(apart))
        def _():
            stay.start()

        def wait():
            @pl.when(apart)
            def _():
                go.wait()

            @pl.when(jnp.logical_not(apart))
            def _():
                stay.wait()

        return wait

    down_shared.wait_recv()
    down1_ready.wait()
    keep0_ready.wait()
    ups, downs = (r.up1, r.up1_other), (r.down1, r.down1_other)
    act, act_grad = r.hidden2, r.hidden1
    for h in range(2):
        for p in range(2):
            if p:
                sent[h].far()
            else:
                sent[h].near()
            feed_slope(r.branch0, r.keep0, downs, act, act_grad, h, p)
    mail.settle(row_copies + column_copies)
    down_grad(mail, here, r.branch0, act, r.down1_parts, r.down_send, r.down_land)
    down1 = RingSum(mail, here, r.down1_parts, r.down1_relay, r.down1_land)
    hidden0_ready.wait()
    up_grad(mail, here, r.hidden0, act_grad, r.up1_parts, r.up_send, r.up_land)
    up1 = RingSum(mail, here, r.up1_parts, r.up1_relay, r.up1_land)
    up_shared.wait_recv()
    up1_ready.wait()
    sums = reduce(r.land0)
    for h in range(2):
        for p in (1, 0):
            sums[h].put(p, feed_in(act_grad, ups, h, p))
    r.up2_sum[...] = up2.total().astype(BF)
    up2_copies = swap(r.up2_sum, r.up2_got)
    r.down_moved[0] = down2.total().astype(BF)
    down2_wait = to_owner(0)
    r.in_total[...] = in_sum.total().astype(BF)
    in_copies = swap(r.in_total, r.in_got)
    down1.relay()
    r.conv_out_grad[...] = conv_sum.total()
    r.out_grad[...] = out_sum.total()
    for copy in kernel_copies:
        copy.wait_recv()
    kernel_total = r.kernel_part[...]
    for k in range(1, PLANES):
        kernel_total = kernel_total + r.kernel_land[k - 1]
    r.kernel_out[...] = kernel_total
    gain = scale_row(small, 0)
    gain_parts = []
    for h in range(2):
        value_part, gain_part = norm_grad(r.frames[0, part(h), :].astype(F32), gain, sums[h].total())
        r.frames_grad[0, part(h), :] = r.grad[part(h), :] + value_part
        gain_parts.append(gain_part)
    r.small_sum[...] = r.small_sum[...] + at_row(0, gain_parts[0] + gain_parts[1])
    small_copies = [
        mail.post(r.small_sum, r.small_land.at[k - 1], here.above(k)) for k in range(1, PLANES)
    ]
    r.qkv_total[...] = qkv_sum.total().astype(BF)
    qkv_copies = swap(r.qkv_total, r.qkv_got)
    up1.relay()
    r.down_moved[1] = down1.total().astype(BF)
    down1_wait = to_owner(1)
    place(r.up2_sum, r.up2_got, r.up2_out, up2_copies)
    place(r.in_total, r.in_got, r.in_out, in_copies)
    for copy in small_copies:
        copy.wait_recv()
    total = r.small_sum[...]
    for k in range(1, PLANES):
        total = total + r.small_land[k - 1]
    r.small_mid[...] = total
    small_copies = [mail.post(r.small_mid, r.small_near.at[i], device) for i, device in enumerate(devices)]
    place(r.qkv_total, r.qkv_got, r.qkv_out, qkv_copies)
    down2_wait()
    r.down2_out[...] = r.down_got[0].astype(F32)
    r.up1_sum[...] = up1.total().astype(BF)
    up1_copies = swap(r.up1_sum, r.up1_got)
    for copy in small_copies:
        copy.wait_recv()
    total = r.small_mid[...]
    for i in range(len(devices)):
        total = total + r.small_near[i]
    r.small_out[...] = total
    down1_wait()
    r.down1_out[...] = r.down_got[1].astype(F32)
    place(r.up1_sum, r.up1_got, r.up1_out, up1_copies)
    mail.close()


def launch(kernel, name, index, operands, results, scratch):
    names = list(operands) + list(results) + list(scratch) + ["send", "recv"]
    values = pl.pallas_call(
        functools.partial(kernel, names),
        name=name,
        out_shape=[jax.ShapeDtypeStruct(shape, kind) for shape, kind, _ in results.values()],
        in_specs=[pl.BlockSpec(memory_space=place) for _, place in operands.values()],
        out_specs=[pl.BlockSpec(memory_space=place) for _, _, place in results.values()],
        scratch_shapes=[pltpu.VMEM(shape, kind) for shape, kind in scratch.values()]
        + [pltpu.SemaphoreType.DMA((SLOTS,)), pltpu.SemaphoreType.DMA((SLOTS,))],
        compiler_params=pltpu.CompilerParams(
            collective_id=index, has_side_effects=True, vmem_limit_bytes=GRANT
        ),
    )(*[array for array, _ in operands.values()])
    return types.SimpleNamespace(**dict(zip(results, values)))


def plane_body(
    frames, lengths, up_first, down_first, joint_qkv, attn_out, conv_in, conv_kernel, batch_gain, conv_out,
    up_second, down_second, norm_gains, slopes, out_grad,
):
    seqs = lax.axis_size("seq")
    seq = lax.axis_index("seq")
    plane = lax.axis_index("fsdp")
    rows, width = frames.shape[1], frames.shape[2]
    length = rows * seqs
    heads = slopes.shape[0]
    size = width // heads
    channels = width // seqs
    hidden_units = up_first.shape[1]
    half = hidden_units // seqs
    taps = conv_kernel.shape[0]
    block = width // (seqs * PLANES)
    near_count = seqs - 1
    small = jnp.concatenate(
        [norm_gains, conv_kernel, batch_gain[None, :], jnp.zeros((5, batch_gain.shape[0]), BF)], axis=0
    )
    row_f = ((rows, width), F32)
    lines = rows // 2
    quad = ((2, CHIPS, lines, width), BF)
    stage = ((2, CHIPS - 1, lines, width), BF)
    acc = ((2, lines, width), F32)
    up, down = ((width, half), BF), ((half, width), BF)
    qkv, out = ((width, 3 * size), BF), ((size, width), BF)
    conv_i, conv_o = ((width, 2 * channels), BF), ((channels, width), BF)
    keep = ((2, CHIPS, lines, 2 * half), F32)
    act = ((2, CHIPS, lines, 2 * half), BF)
    joint = ((length, 3 * size), BF)
    mixed = ((2, 2, CHIPS, lines, size), BF)
    glu = ((2, CHIPS, lines, 4 * channels), F32)
    dense = ((length, channels), F32)
    padded = ((length + 2 * RIM, channels), F32)
    marks = ((taps + 1, length, channels), BF)
    bn = ((8, channels), F32)
    bn_land = ((PLANES - 1, 8, channels), F32)
    small_row = ((8, width), F32)
    small_all = ((PLANES,) + small.shape, BF)

    def parts(shape):
        return ((PLANES, shape[0][0] // PLANES, shape[0][1]), BF)

    def land(shape):
        return ((2, shape[0][0] // PLANES, shape[0][1]), BF)

    def relay(shape):
        return ((4, shape[0][0] // (2 * PLANES), shape[0][1]), BF)

    def summed(shape):
        return ((shape[0][0] // PLANES, shape[0][1]), BF)

    a = launch(
        forward_kernel, "forward", 0,
        dict(
            frames=(frames, V), lengths=(lengths, S), small_src=(small, V), slopes=(slopes, S),
            up1_src=(up_first, H), down1_src=(down_first, H), qkv_src=(joint_qkv, H),
            out_src=(attn_out, H), in_src=(conv_in, H), conv_src=(conv_out, H),
            up2_src=(up_second, H), down2_src=(down_second, H), out_grad=(out_grad, V),
        ),
        dict(
            result=((1, rows, width), BF, V), third_grad=row_f + (V,), small_d=small_row + (V,),
            first=row_f + (V,), second=row_f + (V,), small=small_all + (V,),
            stats=bn + (V,), up2_parts=parts(up) + (V,), down2_parts=parts(down) + (V,),
            hidden0_out=quad + (H,), hidden1_out=quad + (H,), hidden2_out=quad + (H,),
            keep0_out=keep + (H,), joint_out=joint + (H,), mixed_out=mixed + (H,),
            glu_out=glu + (H,), gated_out=dense + (H,), standard_out=dense + (H,),
            swish_out=mixed + (H,), up1_out=up + (H,), down1_out=down + (H,), qkv_out=qkv + (H,),
            out_out=out + (H,), in_out=conv_i + (H,), conv_out_out=conv_o + (H,),
        ),
        dict(
            up1=up, up1_other=up, down1=down, down1_other=down, qkv=qkv, qkv_other=qkv,
            out=out, out_other=out, conv_in=conv_i, conv_in_other=conv_i, conv_out=conv_o,
            conv_out_other=conv_o, up2=up, up2_other=up, down2=down, down2_other=down,
            hidden0=quad, hidden1=quad, hidden2=quad, hidden3=quad, keep0=keep, keep3=keep,
            joint=joint, joint_stage=((2, CHIPS, lines, 3 * size), BF), mixed=mixed,
            mixed_stage=((2, CHIPS, lines, size), BF), glu=glu, gated=dense, padded=padded,
            marks=marks, gate_stage=((2, CHIPS, lines, channels), BF), gate_rows=((length, channels), BF),
            standard=dense, swish_rows=((length, channels), BF), swish=mixed, bn=bn, bn_land=bn_land,
            third=row_f, branch=quad, act=act, act_grad=act,
            stage=stage, land0=stage, land1=stage, land2=stage, land3=stage, land4=stage, acc=acc,
            down_send=down, down_land=down, up_send=up, up_land=up,
        ),
    )
    b = launch(
        backward_kernel, "backward", 1,
        dict(
            frames=(frames, V), lengths=(lengths, S), slopes=(slopes, S), small=(a.small, V),
            third_grad=(a.third_grad, V), small_d=(a.small_d, V), second=(a.second, V),
            stats=(a.stats, V), up2_parts=(a.up2_parts, V), down2_parts=(a.down2_parts, V),
            first_src=(a.first, H), hidden0_src=(a.hidden0_out, H),
            hidden1_src=(a.hidden1_out, H), hidden2_src=(a.hidden2_out, H),
            keep0_src=(a.keep0_out, H), joint_src=(a.joint_out, H), mixed_src=(a.mixed_out, H),
            glu_src=(a.glu_out, H), gated_src=(a.gated_out, H),
            standard_src=(a.standard_out, H), swish_src=(a.swish_out, H),
            up1_src=(a.up1_out, H), down1_src=(a.down1_out, H), qkv_src=(a.qkv_out, H),
            out_src=(a.out_out, H), conv_in_src=(a.in_out, H),
            conv_out_src=(a.conv_out_out, H),
        ),
        dict(
            frames_grad=((1, rows, width), F32, V), up1_out=((block, hidden_units), F32, V),
            down1_out=((half // PLANES, width), F32, V), qkv_out=((block, 3 * width), F32, V),
            out_grad=((size // PLANES, width), F32, V), in_out=((block, 2 * width), F32, V),
            kernel_out=bn + (V,), cross=bn + (V,), conv_out_grad=((channels // PLANES, width), F32, V),
            up2_out=((block, hidden_units), F32, V), down2_out=((half // PLANES, width), F32, V),
            small_out=small_row + (V,),
        ),
        dict(
            up1=up, up1_other=up, down1=down, down1_other=down, qkv=qkv, qkv_other=qkv,
            out=out, out_other=out, conv_in=conv_i, conv_in_other=conv_i, conv_out=conv_o,
            conv_out_other=conv_o, hidden0=quad, hidden1=quad, hidden2=quad, keep0=keep,
            joint=joint, mixed=mixed, glu=glu, gated=dense, standard=dense, swish=mixed,
            first=row_f, grad=row_f, acc=acc, marks=marks, padded=padded,
            branch2=quad, branch1=quad, branch0=quad, swish_stage=((2, CHIPS, lines, channels), F32),
            swish_grad=dense, gate_grad=dense, moved2=((2, 2, CHIPS, lines, channels), F32),
            glu_grad=((2, 2, CHIPS, lines, 2 * channels), BF), bn=bn, bn_land=bn_land,
            conv_land=conv_o, in_land=conv_i,
            conv_parts=parts(conv_o), in_parts=parts(conv_i), conv_relay=relay(conv_o),
            in_relay=relay(conv_i), conv_sum_land=land(conv_o), in_sum_land=land(conv_i),
            kernel_part=bn, kernel_land=bn_land, small_sum=small_row,
            up2_relay=relay(up), up2_land=land(up), down2_relay=relay(down), down2_land=land(down),
            up2_sum=summed(up), down_moved=((2,) + summed(down)[0], BF), down_got=((2,) + summed(down)[0], BF),
            mixed_stage=((2, CHIPS, lines, size), BF), mixed_grad=((length, size), BF),
            joint_grad=joint, moved1=((2, 2, CHIPS, lines, 3 * size), BF), out_land=out, qkv_land=qkv, out_parts=parts(out), qkv_parts=parts(qkv), out_relay=relay(out),
            qkv_relay=relay(qkv), out_sum_land=land(out), qkv_sum_land=land(qkv),
            down_send=down, down_land=down,
            up_send=up, up_land=up, up1_parts=parts(up), down1_parts=parts(down),
            up1_relay=relay(up), up1_land=land(up), down1_relay=relay(down), down1_land=land(down),
            up1_sum=summed(up), up1_got=((near_count, block, half), BF),
            up2_got=((near_count, block, half), BF), in_total=summed(conv_i),
            in_got=((near_count, block, 2 * channels), BF), qkv_total=summed(qkv),
            qkv_got=((near_count, block, 3 * size), BF), small_land=((PLANES - 1, 8, width), F32),
            small_mid=small_row, small_near=((near_count, 8, width), F32),
            stage=stage, land0=stage, land1=stage, land2=stage,
        ),
    )
    place = seq * PLANES + plane
    gains_grad = lax.dynamic_slice_in_dim(b.small_out, place * block, block, axis=1)[: norm_gains.shape[0]]
    kernel_grad = lax.dynamic_slice_in_dim(b.kernel_out, plane * block, block, axis=1)[:taps]
    batch_grad = lax.dynamic_slice_in_dim(b.cross[1], plane * block, block)
    slopes_grad = b.small_out[5, :heads]
    return (
        a.result, b.frames_grad, b.up1_out, b.down1_out, b.qkv_out, b.out_grad, b.in_out,
        kernel_grad, batch_grad, b.conv_out_grad, b.up2_out, b.down2_out, gains_grad, slopes_grad,
    )


def solution(mesh):
    planar = mesh.shape["seq"] == 2 * CHIPS and mesh.shape["fsdp"] == PLANES
    chosen = plane_body if planar else body
    placed = (
        P("fsdp", "seq", None),
        P("fsdp", None),
        P("fsdp", None),
        P("fsdp", None),
        P("fsdp", None),
        P("fsdp", None),
        P("fsdp", None),
        P(None, "fsdp"),
        P("fsdp"),
        P("fsdp", None),
        P("fsdp", None),
        P("fsdp", None),
        P(None, "fsdp"),
        P(),
        P("fsdp", "seq", None),
    )
    return jax.shard_map(
        chosen,
        mesh=mesh,
        in_specs=placed,
        out_specs=(
            P("fsdp", "seq", None),
            P("fsdp", "seq", None),
            P(("seq", "fsdp"), None),
            P(("seq", "fsdp"), None),
            P(("seq", "fsdp"), None),
            P(("seq", "fsdp"), None),
            P(("seq", "fsdp"), None),
            P(None, ("seq", "fsdp")),
            P(("seq", "fsdp")),
            P(("seq", "fsdp"), None),
            P(("seq", "fsdp"), None),
            P(("seq", "fsdp"), None),
            P(None, ("seq", "fsdp")),
            P(),
        ),
        check_vma=False,
    )
```

```python
import functools
import math
import types

import jax
import jax.numpy as jnp
from jax import lax
from jax.experimental import pallas as pl
from jax.experimental.pallas import tpu as pltpu
from jax.sharding import PartitionSpec as P

EPSILON = 1e-05
MASKED = -1e30


def extended(x, sides, width):
    for axis, dim in sides:
        size, length = (lax.axis_size(axis), x.shape[dim])
        up = [(i, (i + 1) % size) for i in range(size - 1)]
        down = [(j, i) for i, j in up]
        last = lax.slice_in_dim(x, length - width, length, axis=dim)
        initial = lax.slice_in_dim(x, 0, width, axis=dim)
        before = lax.ppermute(last, axis, up)
        after = lax.ppermute(initial, axis, down)
        x = jnp.concatenate([before, x, after], axis=dim)
    return x


def normed(value, gain):
    average = jnp.mean(value, axis=-1, keepdims=True)
    centred = value - average
    variance = jnp.mean(centred * centred, axis=-1, keepdims=True)
    return centred * lax.rsqrt(variance + EPSILON) * gain


def norm_back(value, gain, gradient):
    pullback = jax.vjp(normed, value, gain)[1]
    return pullback(gradient)


def matmul(left, right):
    return jnp.dot(left, right, preferred_element_type=jnp.float32)


def transposed_left(left, right):
    return lax.dot_general(
        left, right, (((0,), (0,)), ((), ())), preferred_element_type=jnp.float32
    )


def transposed_right(left, right):
    return lax.dot_general(
        left, right, (((1,), (1,)), ((), ())), preferred_element_type=jnp.float32
    )


def item_index(positions, bounds):
    return jnp.sum((positions[:, None] >= bounds[None, :]).astype(jnp.int32), axis=1)


def unpack(weights):
    (
        first_up,
        first_down,
        qkv_full,
        out_full,
        conv_up,
        kernel_full,
        batch_full,
        conv_down,
        second_up,
        second_down,
        gains_full,
    ) = weights
    return (
        first_up,
        first_down,
        qkv_full,
        out_full,
        conv_up,
        kernel_full.astype(jnp.float32),
        batch_full.astype(jnp.float32),
        conv_down,
        second_up,
        second_down,
        gains_full.astype(jnp.float32),
    )


def feed_forward(value, gain, weight_up, weight_down):
    hidden = normed(value, gain).astype(jnp.bfloat16)
    swish = jax.nn.silu(matmul(hidden, weight_up)).astype(jnp.bfloat16)
    return value + 0.5 * matmul(swish, weight_down)


def feed_back(value, gain, weight_up, weight_down, gradient):
    hidden = normed(value, gain).astype(jnp.bfloat16)
    swish, pullback = jax.vjp(jax.nn.silu, matmul(hidden, weight_up))
    swish_low = swish.astype(jnp.bfloat16)
    branch_grad = (0.5 * gradient).astype(jnp.bfloat16)
    down_grad = transposed_left(swish_low, branch_grad)
    active_grad = pullback(transposed_right(branch_grad, weight_down))[0].astype(jnp.bfloat16)
    up_grad = transposed_left(hidden, active_grad)
    value_grad, gain_grad = norm_back(value, gain, transposed_right(active_grad, weight_up))
    return (gradient + value_grad, gain_grad, up_grad, down_grad)


def biased_scores(query_heads, key_heads, slopes, layout):
    query_pos, key_pos, query_ids, key_ids = layout
    raw_scores = jnp.einsum(
        "qhd,khd->hqk", query_heads, key_heads, preferred_element_type=jnp.float32
    )
    distance = jnp.abs(query_pos[:, None] - key_pos[None, :]).astype(jnp.float32)
    scores = (
        raw_scores * (1.0 / math.sqrt(query_heads.shape[2]))
        - slopes[:, None, None] * distance[None]
    )
    shared = query_ids[:, None] == key_ids[None, :]
    return (jnp.where(shared[None], scores, MASKED), distance)


def attention_probs(query, keys, slopes, layout):
    heads = slopes.shape[0]
    head_size = query.shape[1] // heads
    query_heads = query.reshape(query.shape[0], heads, head_size)
    key_heads = keys.reshape(keys.shape[0], heads, head_size)
    scores, distance = biased_scores(query_heads, key_heads, slopes, layout)
    top = jnp.max(scores, axis=-1, keepdims=True)
    exponent = jnp.exp(scores - top)
    total = jnp.sum(exponent, axis=-1, keepdims=True)
    probs = exponent / total
    return (probs, distance, query_heads, key_heads, top[:, :, 0], total[:, :, 0])


def attend(value, gain, weight_qkv, weight_out, slopes, layout):
    feature_width = value.shape[1]
    hidden = normed(value, gain).astype(jnp.bfloat16)
    joint = matmul(hidden, weight_qkv).astype(jnp.bfloat16)
    keys_values = lax.all_gather(joint[:, feature_width:], "seq", axis=0, tiled=True)
    probs, distance, query_heads, key_heads, top, total = attention_probs(
        joint[:, :feature_width], keys_values[:, :feature_width], slopes, layout
    )
    value_heads = keys_values[:, feature_width:].reshape(key_heads.shape)
    mixed = jnp.einsum(
        "hqk,khd->qhd", probs.astype(jnp.bfloat16), value_heads, preferred_element_type=jnp.float32
    )
    mixed = mixed.reshape(value.shape).astype(jnp.bfloat16)
    return (value + matmul(mixed, weight_out), keys_values)


def attend_back(value, gain, weight_qkv, weight_out, slopes, layout, keys_values, gradient):
    feature_width = value.shape[1]
    row_count = value.shape[0]
    hidden = normed(value, gain).astype(jnp.bfloat16)
    joint = matmul(hidden, weight_qkv).astype(jnp.bfloat16)
    probs, distance, query_heads, key_heads, top, total = attention_probs(
        joint[:, :feature_width], keys_values[:, :feature_width], slopes, layout
    )
    probs_low = probs.astype(jnp.bfloat16)
    value_heads = keys_values[:, feature_width:].reshape(key_heads.shape)
    mixed = jnp.einsum("hqk,khd->qhd", probs_low, value_heads, preferred_element_type=jnp.float32)
    mixed = mixed.reshape(value.shape).astype(jnp.bfloat16)
    branch_grad = gradient.astype(jnp.bfloat16)
    weight_out_grad = transposed_left(mixed, branch_grad)
    mixed_flat = transposed_right(branch_grad, weight_out).astype(jnp.bfloat16)
    mixed_grad = mixed_flat.reshape(query_heads.shape)
    prob_grad = jnp.einsum(
        "qhd,khd->hqk", mixed_grad, value_heads, preferred_element_type=jnp.float32
    )
    delta = jnp.sum(probs * prob_grad, axis=-1)
    score_grad = probs * (prob_grad - delta[:, :, None])
    slope_grad = -jnp.sum(score_grad * distance[None], axis=(1, 2))
    scale = 1.0 / math.sqrt(query_heads.shape[2])
    raw_grad = (score_grad * scale).astype(jnp.bfloat16)
    query_grad = jnp.einsum("hqk,khd->qhd", raw_grad, key_heads, preferred_element_type=jnp.float32)
    query_pos, key_pos, query_ids, key_ids = layout
    all_query, all_mixed = (
        lax.all_gather(joint[:, :feature_width], "seq", axis=0, tiled=True),
        lax.all_gather(mixed_flat, "seq", axis=0, tiled=True),
    )
    all_top, all_total, all_delta = (
        lax.all_gather(top, "seq", axis=1, tiled=True),
        lax.all_gather(total, "seq", axis=1, tiled=True),
        lax.all_gather(delta, "seq", axis=1, tiled=True),
    )
    heads = slopes.shape[0]
    head_size = query_heads.shape[2]
    all_query_heads = all_query.reshape(all_query.shape[0], heads, head_size)
    all_mixed_heads = all_mixed.reshape(all_query.shape[0], heads, head_size)
    own_keys = joint[:, feature_width : 2 * feature_width].reshape(row_count, heads, head_size)
    own_values = joint[:, 2 * feature_width :].reshape(row_count, heads, head_size)
    column_scores, column_distance = biased_scores(
        all_query_heads, own_keys, slopes, (key_pos, query_pos, key_ids, query_ids)
    )
    column_probs = jnp.exp(column_scores - all_top[:, :, None]) / all_total[:, :, None]
    column_prob_grad = jnp.einsum(
        "qhd,khd->hqk", all_mixed_heads, own_values, preferred_element_type=jnp.float32
    )
    column_score_grad = column_probs * (column_prob_grad - all_delta[:, :, None])
    column_raw = (column_score_grad * scale).astype(jnp.bfloat16)
    key_grad = jnp.einsum(
        "hqk,qhd->khd", column_raw, all_query_heads, preferred_element_type=jnp.float32
    )
    value_grad = jnp.einsum(
        "hqk,qhd->khd",
        column_probs.astype(jnp.bfloat16),
        all_mixed_heads,
        preferred_element_type=jnp.float32,
    )
    local_grad = jnp.concatenate(
        [key_grad.reshape(row_count, feature_width), value_grad.reshape(row_count, feature_width)],
        axis=1,
    )
    joint_grad = jnp.concatenate([query_grad.reshape(value.shape), local_grad], axis=1).astype(
        jnp.bfloat16
    )
    qkv_grad = transposed_left(hidden, joint_grad)
    input_grad, gain_grad = norm_back(value, gain, transposed_right(joint_grad, weight_qkv))
    return (gradient + input_grad, gain_grad, qkv_grad, weight_out_grad, slope_grad)


def gate_linear(joint):
    feature_width = joint.shape[1] // 2
    return joint[:, :feature_width] * jax.nn.sigmoid(joint[:, feature_width:])


def depthwise(rim, kernel, rim_ids, own_ids):
    row_count = own_ids.shape[0]
    total = jnp.zeros((row_count, rim.shape[1]), jnp.float32)
    for offset in range(kernel.shape[0]):
        shared = (rim_ids[offset : offset + row_count] == own_ids).astype(jnp.float32)
        total = (
            total
            + kernel[offset]
            * rim[offset : offset + row_count].astype(jnp.float32)
            * shared[:, None]
        )
    return total


def depthwise_back(rim, kernel, rim_ids, own_ids, conv_grad):
    row_count = own_ids.shape[0]
    reach = kernel.shape[0] - 1
    grad_rim = extended(conv_grad.astype(jnp.bfloat16), (("seq", 0),), reach // 2).astype(
        conv_grad.dtype
    )
    input_grad = jnp.zeros(conv_grad.shape, jnp.float32)
    kernel_rows = []
    for offset in range(kernel.shape[0]):
        shared = (rim_ids[offset : offset + row_count] == own_ids).astype(jnp.float32)[:, None]
        kernel_rows.append(
            jnp.sum(
                rim[offset : offset + row_count].astype(jnp.float32) * shared * conv_grad, axis=0
            )
        )
        mirror = reach - offset
        crossed = (rim_ids[mirror : mirror + row_count] == own_ids).astype(jnp.float32)[:, None]
        input_grad = input_grad + kernel[offset] * grad_rim[mirror : mirror + row_count] * crossed
    return (input_grad, jnp.stack(kernel_rows))


def body(
    frames,
    lengths,
    up_first,
    down_first,
    joint_qkv,
    attn_out,
    conv_in,
    conv_kernel,
    batch_gain,
    conv_out,
    up_second,
    down_second,
    norm_gains,
    slopes,
    out_grad,
):
    sharded = (
        up_first,
        down_first,
        joint_qkv,
        attn_out,
        conv_in,
        conv_kernel,
        batch_gain,
        conv_out,
        up_second,
        down_second,
        norm_gains,
    )
    gathered = (
        lax.all_gather(sharded[0], "fsdp", axis=0, tiled=True),
        lax.all_gather(sharded[1], "fsdp", axis=0, tiled=True),
        lax.all_gather(sharded[2], "fsdp", axis=0, tiled=True),
        lax.all_gather(sharded[3], "fsdp", axis=0, tiled=True),
        lax.all_gather(sharded[4], "fsdp", axis=0, tiled=True),
        lax.all_gather(sharded[5], "fsdp", axis=1, tiled=True),
        lax.all_gather(sharded[6], "fsdp", axis=0, tiled=True),
        lax.all_gather(sharded[7], "fsdp", axis=0, tiled=True),
        lax.all_gather(sharded[8], "fsdp", axis=0, tiled=True),
        lax.all_gather(sharded[9], "fsdp", axis=0, tiled=True),
        lax.all_gather(sharded[10], "fsdp", axis=1, tiled=True),
    )
    (
        first_up,
        first_down,
        qkv_full,
        out_full,
        conv_up,
        kernel,
        batch_scale,
        conv_down,
        second_up,
        second_down,
        gains,
    ) = unpack(gathered)
    row_count = frames.shape[1]
    feature_width = frames.shape[2]
    seq_count = lax.axis_size("seq")
    start_row = lax.axis_index("seq") * row_count
    bounds = jnp.cumsum(lengths[0])
    item_count = lengths.shape[1]
    own_pos = start_row + jnp.arange(row_count, dtype=jnp.int32)
    key_pos = jnp.arange(row_count * seq_count, dtype=jnp.int32)
    own_ids = item_index(own_pos, bounds)
    layout = (own_pos, key_pos, own_ids, item_index(key_pos, bounds))
    rim_width = conv_kernel.shape[0] // 2
    rim_ids = item_index(
        start_row - rim_width + jnp.arange(row_count + 2 * rim_width, dtype=jnp.int32), bounds
    )
    valid = (own_ids < item_count).astype(jnp.float32)[:, None]
    source = frames[0].astype(jnp.float32)
    first = feed_forward(source, gains[0], first_up, first_down)
    second, keys_values = attend(first, gains[1], qkv_full, out_full, slopes, layout)
    conv_hidden = normed(second, gains[2]).astype(jnp.bfloat16)
    conv_joint = matmul(conv_hidden, conv_up)
    rim = extended(gate_linear(conv_joint).astype(jnp.bfloat16), (("seq", 0),), rim_width)
    conv = depthwise(rim, kernel, rim_ids, own_ids)
    total, count = lax.psum((jnp.sum(valid * conv, axis=0), jnp.sum(valid)), ("seq", "fsdp"))
    average = total / count
    centred = conv - average
    spread = lax.psum(jnp.sum(valid * centred * centred, axis=0), ("seq", "fsdp"))
    variance = spread / count
    inverse = lax.rsqrt(variance + EPSILON)
    standard = (conv - average) * inverse
    pre_swish = standard * batch_scale
    swish, swish_pull = jax.vjp(jax.nn.silu, pre_swish)
    swish_low = swish.astype(jnp.bfloat16)
    third = second + matmul(swish_low, conv_down)
    fourth = feed_forward(third, gains[3], second_up, second_down)
    result = normed(fourth, gains[4])
    regathered = (
        lax.all_gather(sharded[0], "fsdp", axis=0, tiled=True),
        lax.all_gather(sharded[1], "fsdp", axis=0, tiled=True),
        lax.all_gather(sharded[2], "fsdp", axis=0, tiled=True),
        lax.all_gather(sharded[3], "fsdp", axis=0, tiled=True),
        lax.all_gather(sharded[4], "fsdp", axis=0, tiled=True),
        lax.all_gather(sharded[5], "fsdp", axis=1, tiled=True),
        lax.all_gather(sharded[6], "fsdp", axis=0, tiled=True),
        lax.all_gather(sharded[7], "fsdp", axis=0, tiled=True),
        lax.all_gather(sharded[8], "fsdp", axis=0, tiled=True),
        lax.all_gather(sharded[9], "fsdp", axis=0, tiled=True),
        lax.all_gather(sharded[10], "fsdp", axis=1, tiled=True),
    )
    (
        first_up,
        first_down,
        qkv_full,
        out_full,
        conv_up,
        kernel,
        batch_scale,
        conv_down,
        second_up,
        second_down,
        gains,
    ) = unpack(regathered)
    fourth_grad, last_gain = norm_back(fourth, gains[4], out_grad[0].astype(jnp.float32))
    third_grad, fourth_gain, second_up_grad, second_down_grad = feed_back(
        third, gains[3], second_up, second_down, fourth_grad
    )
    branch_grad = third_grad.astype(jnp.bfloat16)
    conv_down_grad = transposed_left(swish_low, branch_grad)
    scaled_grad = swish_pull(transposed_right(branch_grad, conv_down))[0]
    sum_grad, sum_cross = lax.psum(
        (jnp.sum(scaled_grad, axis=0), jnp.sum(scaled_grad * standard, axis=0)), ("seq", "fsdp")
    )
    conv_grad = inverse * (scaled_grad * batch_scale) - valid * (inverse / count) * (
        batch_scale * sum_grad + standard * (batch_scale * sum_cross)
    )
    gated_grad, kernel_grad = depthwise_back(rim, kernel, rim_ids, own_ids, conv_grad)
    joint_pull = jax.vjp(gate_linear, conv_joint)[1]
    joint_grad = joint_pull(gated_grad)[0].astype(jnp.bfloat16)
    conv_up_grad = transposed_left(conv_hidden, joint_grad)
    hidden_grad, third_gain = norm_back(second, gains[2], transposed_right(joint_grad, conv_up))
    second_grad = third_grad + hidden_grad
    late = (
        lax.psum_scatter(second_up_grad, ("seq", "fsdp"), scatter_dimension=0, tiled=True),
        lax.psum_scatter(second_down_grad, ("seq", "fsdp"), scatter_dimension=0, tiled=True),
        lax.psum_scatter(conv_down_grad, ("seq", "fsdp"), scatter_dimension=0, tiled=True),
        lax.psum_scatter(conv_up_grad, ("seq", "fsdp"), scatter_dimension=0, tiled=True),
        lax.psum_scatter(kernel_grad, ("seq", "fsdp"), scatter_dimension=1, tiled=True),
    )
    first_grad, second_gain, qkv_grad, out_weight_grad, slope_part = attend_back(
        first, gains[1], qkv_full, out_full, slopes, layout, keys_values, second_grad
    )
    source_grad, first_gain, first_up_grad, first_down_grad = feed_back(
        source, gains[0], first_up, first_down, first_grad
    )
    gain_grads = jnp.stack([first_gain, second_gain, third_gain, fourth_gain, last_gain])
    early = (
        lax.psum_scatter(first_up_grad, ("seq", "fsdp"), scatter_dimension=0, tiled=True),
        lax.psum_scatter(first_down_grad, ("seq", "fsdp"), scatter_dimension=0, tiled=True),
        lax.psum_scatter(qkv_grad, ("seq", "fsdp"), scatter_dimension=0, tiled=True),
        lax.psum_scatter(out_weight_grad, ("seq", "fsdp"), scatter_dimension=0, tiled=True),
        lax.psum_scatter(gain_grads, ("seq", "fsdp"), scatter_dimension=1, tiled=True),
    )
    slope_grad = lax.psum(slope_part, ("seq", "fsdp"))
    piece_width = feature_width // lax.axis_size(("seq", "fsdp"))
    batch_piece = lax.dynamic_slice_in_dim(
        sum_cross, lax.axis_index(("seq", "fsdp")) * piece_width, piece_width
    )
    return (
        result[None].astype(jnp.bfloat16),
        source_grad[None],
        early[0],
        early[1],
        early[2],
        early[3],
        late[3],
        late[4],
        batch_piece,
        late[2],
        late[0],
        late[1],
        early[4],
        slope_grad,
    )


BF = jnp.bfloat16
F32 = jnp.float32
MESH = pl.DeviceIdType.MESH
GRANT = 63 * 2**20
CHIPS = 4
PLANES = 4
SLOTS = 320
RIM = 8
V, H, S = pltpu.VMEM, pl.ANY, pltpu.SMEM


def mm(left, right):
    return jnp.dot(left, right, preferred_element_type=F32)


def mm_right(left, right):
    return lax.dot_general(left, right, (((1,), (1,)), ((), ())), preferred_element_type=F32)


def mm_left(left, right):
    return lax.dot_general(left, right, (((0,), (0,)), ((), ())), preferred_element_type=F32)


def span(index, size):
    return pl.ds(pl.multiple_of(index * size, size), size)


class Here:
    def __init__(self):
        self.seq = lax.axis_index("seq")
        self.plane = lax.axis_index("fsdp")
        self.core = lax.rem(self.seq, 2)
        self.chip = lax.div(self.seq, 2)
        column, row = lax.rem(self.chip, 2), lax.div(self.chip, 2)
        self.chips = [
            lax.rem(row + j // 2, 2) * 2 + lax.rem(column + j % 2, 2) for j in range(CHIPS)
        ]

    def peer(self, slot):
        return (self.chips[slot] * 2 + self.core, self.plane)

    def cross(self, slot):
        return (self.chips[slot] * 2 + 1 - self.core, self.plane)

    def sibling(self):
        return self.cross(0)

    def level(self, step):
        return lax.rem(self.plane + step, PLANES)

    def turned(self, step):
        return lax.rem(self.seq + step, 2 * CHIPS)

    def above(self, step):
        return (self.seq, self.level(step))

    def rows(self, slot, half, height):
        return span((self.chips[slot] * 2 + self.core) * 2 + half, height)

    def other_rows(self, slot, half, height):
        return span((self.chips[slot] * 2 + 1 - self.core) * 2 + half, height)


class Mail:
    def __init__(self, send, recv):
        self.send, self.recv, self.count, self.open, self.kept = send, recv, 0, [], []

    def slot(self):
        self.count += 1
        return self.count - 1

    def remote(self, src, dst, device, sent, received):
        return pltpu.make_async_remote_copy(
            src_ref=src,
            dst_ref=dst,
            send_sem=self.send.at[sent],
            recv_sem=self.recv.at[received],
            device_id=device,
            device_id_type=MESH,
        )

    def post(self, src, dst, device):
        i = self.slot()
        copy = self.remote(src, dst, device, i, i)
        copy.start()
        self.open.append(copy)
        return copy

    def settle(self, copies):
        for copy in copies:
            copy.wait_send()
        self.open = [copy for copy in self.open if all(copy is not done for done in copies)]

    def local(self, src, dst):
        copy = pltpu.make_async_copy(src, dst, self.send.at[self.slot()])
        copy.start()
        return copy

    def save(self, src, dst):
        self.kept.append(self.local(src, dst))

    def close(self):
        for copy in self.open:
            copy.wait_send()
        for copy in self.kept:
            copy.wait()
        self.open, self.kept = [], []


def greet(devices, extra=None):
    barrier = pltpu.get_barrier_semaphore()
    for device in devices:
        pl.semaphore_signal(barrier, inc=1, device_id=device, device_id_type=MESH)
    count = len(devices)
    if extra is not None:
        apart, device = extra
        count = count + apart.astype(jnp.int32)

        @pl.when(apart)
        def _():
            pl.semaphore_signal(barrier, inc=1, device_id=device, device_id_type=MESH)

    pl.semaphore_wait(barrier, count)


def near(here):
    return (
        [here.peer(j) for j in range(1, CHIPS)]
        + [here.sibling()]
        + [here.above(k) for k in range(1, PLANES)]
    )


class Spread:
    def __init__(self, mail, here, buf, half):
        self.mail, self.here, self.buf = mail, here, buf.at[half]
        rows = buf.shape[2]
        self.whole, self.top, self.low = pl.ds(0, rows), pl.ds(0, rows // 2), pl.ds(rows // 2, rows // 2)
        self.x = self.send(0, 1, self.whole, 1)
        self.y = self.send(0, 2, self.whole, 2)

    def send(self, source, target, rows, slot):
        return self.mail.post(self.buf.at[source, rows], self.buf.at[target, rows], self.here.peer(slot))

    def near(self):
        self.x.wait_recv()
        self.d_top = self.send(1, 3, self.top, 2)
        self.y.wait_recv()
        self.d_low = self.send(2, 3, self.low, 1)

    def far(self):
        self.d_top.wait_recv()
        self.d_low.wait_recv()


def as_they_come(sent, work):
    sent[0].near()
    work(0, 0)
    sent[1].near()
    sent[0].far()
    work(0, 1)
    sent[1].far()
    work(1, 1)
    work(1, 0)


class Ring:
    def __init__(self, mail, here, dst, other, fill):
        self.mail, self.here, self.dst, self.other = mail, here, dst, other
        self.height = dst.shape[0] // PLANES
        for copy in fill(dst.at[span(here.plane, self.height)]):
            copy.wait()
        own = self.block(dst, here.plane)
        self.up = mail.post(own, own, here.above(1))
        self.down = mail.post(own, own, here.above(PLANES - 1))
        self.shared = [self.share(here.plane)]

    def block(self, ref, plane):
        return ref.at[span(plane, self.height)]

    def share(self, plane):
        return self.mail.post(self.block(self.dst, plane), self.block(self.other, plane), self.here.sibling())

    def relay(self):
        here, half = self.here, self.height // 2
        self.up.wait_recv()
        piece = self.block(self.dst, here.level(PLANES - 1)).at[pl.ds(0, half)]
        self.far_up = self.mail.post(piece, piece, here.above(1))
        self.down.wait_recv()
        piece = self.block(self.dst, here.level(1)).at[pl.ds(half, half)]
        self.far_down = self.mail.post(piece, piece, here.above(PLANES - 1))
        self.shared += [self.share(here.level(PLANES - 1)), self.share(here.level(1))]

    def finish(self):
        self.far_up.wait_recv()
        self.far_down.wait_recv()
        self.shared.append(self.share(self.here.level(2)))

    def ready(self):
        for copy in self.shared:
            copy.wait_recv()


class FromPlane:
    def __init__(self, mail, here, src, dst, other):
        self.mail, self.here, self.dst, self.other = mail, here, dst, other
        half = dst.shape[0] // 2
        top, low = pl.ds(0, half), pl.ds(half, half)
        slots = [mail.slot() for _ in range(4)]
        above, below = here.above(1), here.above(PLANES - 1)
        self.step = lax.rem(here.plane + PLANES - here.chip, PLANES)
        self.own = pltpu.make_async_copy(src, dst, mail.send.at[mail.slot()])
        self.up = mail.remote(src, dst, above, slots[0], slots[0])
        self.down = mail.remote(src, dst, below, slots[1], slots[1])
        self.far_up = mail.remote(dst.at[top], dst.at[top], above, slots[2], slots[2])
        self.far_down = mail.remote(dst.at[low], dst.at[low], below, slots[3], slots[3])

        @pl.when(self.step == 0)
        def _():
            self.own.start()
            self.up.start()
            self.down.start()

    def relay(self):
        @pl.when(self.step == 1)
        def _():
            self.up.wait_recv()
            self.far_up.start()

        @pl.when(self.step == PLANES - 1)
        def _():
            self.down.wait_recv()
            self.far_down.start()

    def finish(self):
        @pl.when(self.step == 0)
        def _():
            self.own.wait()
            self.up.wait_send()
            self.down.wait_send()

        @pl.when(self.step == 1)
        def _():
            self.far_up.wait_send()

        @pl.when(self.step == 2)
        def _():
            self.far_up.wait_recv()
            self.far_down.wait_recv()

        @pl.when(self.step == PLANES - 1)
        def _():
            self.far_down.wait_send()

        self.shared = self.mail.post(self.dst, self.other, self.here.sibling())

    def ready(self):
        self.shared.wait_recv()


class RingSum:
    def __init__(self, mail, here, parts, relays, land):
        self.mail, self.here, self.parts, self.relays, self.land = mail, here, parts, relays, land
        self.half = parts.shape[1] // 2
        self.top, self.low = pl.ds(0, self.half), pl.ds(self.half, self.half)
        far, up, down = here.level(2), here.level(1), here.level(PLANES - 1)
        above, below = here.above(1), here.above(PLANES - 1)
        self.far_up = mail.post(parts.at[far, self.top], relays.at[0], above)
        self.far_down = mail.post(parts.at[far, self.low], relays.at[1], below)
        self.up_low = mail.post(parts.at[up, self.low], land.at[0, self.low], above)
        self.down_top = mail.post(parts.at[down, self.top], land.at[1, self.top], below)

    def relay(self):
        here, relays = self.here, self.relays
        up, down = here.level(1), here.level(PLANES - 1)
        self.far_up.wait_recv()
        relays[2] = (relays[0].astype(F32) + self.parts[up, self.top].astype(F32)).astype(BF)
        self.up_top = self.mail.post(relays.at[2], self.land.at[0, self.top], here.above(1))
        self.far_down.wait_recv()
        relays[3] = (relays[1].astype(F32) + self.parts[down, self.low].astype(F32)).astype(BF)
        self.down_low = self.mail.post(relays.at[3], self.land.at[1, self.low], here.above(PLANES - 1))

    def total(self):
        for copy in (self.up_low, self.down_top, self.up_top, self.down_low):
            copy.wait_recv()
        return (
            self.parts[self.here.plane].astype(F32) + self.land[0].astype(F32) + self.land[1].astype(F32)
        )


def scale_row(small_ref, index):
    rows = [small_ref[k, index : index + 1, :] for k in range(PLANES)]
    return jnp.concatenate(rows, axis=1)


def own_channels(small_ref, here, rows, width):
    return small_ref[here.chip, rows, span(here.core, width)]


def whitened(value):
    average = jnp.mean(value, axis=-1, keepdims=True)
    centred = value - average
    inverse = lax.rsqrt(jnp.mean(centred * centred, axis=-1, keepdims=True) + EPSILON)
    return centred * inverse, inverse


def norm_grad(value, gain, gradient):
    white, inverse = whitened(value)
    inner = gradient * gain
    value_grad = inverse * (
        inner
        - jnp.mean(inner, axis=-1, keepdims=True)
        - white * jnp.mean(inner * white, axis=-1, keepdims=True)
    )
    return value_grad, jnp.sum(gradient * white, axis=0, keepdims=True)


def at_row(index, row, height=8):
    place = lax.broadcasted_iota(jnp.int32, (height, row.shape[1]), 0)
    return jnp.where(place == index, row, 0.0)


def sigmoid(value):
    return 1.0 / (1.0 + jnp.exp(-value))


def item_of(position, lengths):
    end, item = 0, jnp.zeros(position.shape, jnp.int32)
    for k in range(lengths.shape[1]):
        end = end + lengths[0, k]
        item = item + (position >= end).astype(jnp.int32)
    return item


def set_marks(marks, lengths):
    taps, (frames, width) = marks.shape[0] - 1, marks.shape[1:]
    position = lax.broadcasted_iota(jnp.int32, (frames, width), 0)
    item = item_of(position, lengths)
    for t in range(taps):
        other = position + (t - taps // 2)
        shared = (item_of(other, lengths) == item) & (other >= 0) & (other < frames)
        marks[t] = shared.astype(F32).astype(BF)
    marks[taps] = (item < lengths.shape[1]).astype(F32).astype(BF)


class Reduce:
    def __init__(self, mail, here, bufs, half):
        self.mail, self.here, self.half, self.copies = mail, here, half, []
        self.stage, self.land, self.acc = bufs

    def put(self, pair, value):
        rows = value.shape[0] // 2
        for k in range(2):
            slot, term = 2 * pair + k, value[k * rows : (k + 1) * rows]
            if slot == 0:
                self.acc[self.half] = term
                continue
            place = self.stage.at[self.half, slot - 1]
            place[...] = term.astype(BF)
            self.copies.append(self.mail.post(place, self.land.at[self.half, slot - 1], self.here.peer(slot)))

    def total(self):
        for copy in self.copies:
            copy.wait_recv()
        self.mail.settle(self.copies)
        value = self.acc[self.half]
        for j in range(1, CHIPS):
            value = value + self.land[self.half, j - 1].astype(F32)
        return value


def flat(ref, columns=None):
    value = ref[...] if columns is None else ref[:, :, :, columns]
    return value.reshape(-1, value.shape[-1])


def pair_of(ref, half, pair, columns=slice(None)):
    value = ref[half, 2 * pair : 2 * pair + 2, :, columns]
    return value.reshape(-1, value.shape[-1])


def set_pair(ref, half, pair, value, columns=slice(None)):
    ref[half, 2 * pair : 2 * pair + 2, :, columns] = value.reshape(2, -1, value.shape[-1])


def feed_active(hidden, keep, up, half, pair):
    width = up[0].shape[1]
    rows = pair_of(hidden, half, pair)
    for side in range(2):
        set_pair(keep, half, pair, mm(rows, up[side][...]), slice(side * width, (side + 1) * width))


def feed_out(keep, down, half, pair, swish=None):
    width = down[0].shape[0]
    total = None
    for side in range(2):
        columns = slice(side * width, (side + 1) * width)
        active = pair_of(keep, half, pair, columns)
        value = (active * sigmoid(active)).astype(BF)
        if swish is not None:
            set_pair(swish, half, pair, value, columns)
        term = mm(value, down[side][...])
        total = term if total is None else total + term
    return total


def feed_swish(keep, swish, half, pair):
    active = pair_of(keep, half, pair)
    set_pair(swish, half, pair, (active * sigmoid(active)).astype(BF))


def feed_slope(branch, keep, down, active_grad, half, pair):
    width = down[0].shape[0]
    rows = pair_of(branch, half, pair)
    for side in range(2):
        columns = slice(side * width, (side + 1) * width)
        active = pair_of(keep, half, pair, columns)
        gate = sigmoid(active)
        grad = mm_right(rows, down[side][...]) * (gate * (1.0 + active * (1.0 - gate)))
        set_pair(active_grad, half, pair, grad.astype(BF), columns)


def feed_in(active_grad, up, half, pair):
    width = up[0].shape[1]
    total = None
    for side in range(2):
        term = mm_right(pair_of(active_grad, half, pair, slice(side * width, (side + 1) * width)), up[side][...])
        total = term if total is None else total + term
    return total


def pair_product(mail, here, left, right, blocks, send, land, store):
    height = send.shape[0] // blocks
    copies = []
    for i in range(blocks):
        rows = pl.ds(i * height, height)
        send[rows, :] = mm_left(left(1, i), right(1)).astype(BF)
        copies.append(mail.post(send.at[rows], land.at[rows], here.sibling()))
    for i in range(blocks):
        rows = pl.ds(i * height, height)
        grad = mm_left(left(0, i), right(0))
        copies[i].wait_recv()
        store(i, (grad + land[rows, :].astype(F32)).astype(BF))
    return copies


def by_plane(out, first=0):
    def store(i, value):
        height = out.shape[1]
        each = value.shape[0] // height
        for k in range(each):
            out[lax.rem(first + i * each + k, PLANES)] = value[k * height : (k + 1) * height]

    return store


def by_owner(out):
    def store(i, value):
        seqs = 2 * CHIPS
        height = out.shape[1] // seqs
        each = value.shape[0] // (height * PLANES)
        for k in range(each):
            for p in range(PLANES):
                start = (k * PLANES + p) * height
                at = (i * each + k) * height
                out[p, at : at + height, :] = value[start : start + height]

    return store


def down_grad(mail, here, branch, swish, out, send, land):
    half = swish.shape[3] // 2
    block = half // 2
    return pair_product(
        mail, here,
        lambda side, i: flat(swish, slice(side * half + i * block, side * half + (i + 1) * block)),
        lambda side: flat(branch),
        2, send, land, by_plane(out, here.seq),
    )


def up_grad(mail, here, hidden, active_grad, out, send, land):
    half = active_grad.shape[3] // 2
    block = hidden.shape[3] // 4
    return pair_product(
        mail, here,
        lambda side, i: flat(hidden, slice(i * block, (i + 1) * block)),
        lambda side: flat(active_grad, slice(side * half, (side + 1) * half)),
        4, send, land, by_owner(out),
    )


def slots_grad(mail, here, rows, sides, out, send, land):
    block = rows.shape[3] // 4
    return pair_product(
        mail, here,
        lambda side, i: flat(rows, slice(i * block, (i + 1) * block)),
        lambda side: flat(sides.at[side]),
        4, send, land, by_owner(out),
    )


def sides_grad(mail, here, sides, rows, out, send, land):
    return pair_product(
        mail, here, lambda side, i: flat(sides.at[side]), lambda side: flat(rows), 1, send, land, by_plane(out)
    )


def attention_weights(query, keys, slope, row, lengths):
    column = lax.broadcasted_iota(jnp.int32, (8, keys.shape[0]), 1)[:1, :]
    distance = jnp.abs(row.astype(F32) - column.astype(F32))
    scores = mm_right(query, keys) * (1.0 / math.sqrt(query.shape[1])) - slope * distance
    scores = jnp.where(item_of(row, lengths) == item_of(column, lengths), scores, MASKED)
    exponent = jnp.exp(scores - jnp.max(scores, axis=-1, keepdims=True))
    return exponent * (1.0 / jnp.sum(exponent, axis=-1, keepdims=True)), distance


def kernel_refs(names, refs):
    return types.SimpleNamespace(**dict(zip(names, refs, strict=True)))


def forward_kernel(names, *refs):
    r = kernel_refs(names, refs)
    here, mail = Here(), Mail(r.send, r.recv)
    lengths, small, marks = r.lengths, r.small, r.marks
    rows = r.frames.shape[1] // 2
    greet(near(here))

    def columns_of(src, turn=0):
        width = 128

        def fill(region):
            groups = region.shape[1] // width
            stride = src.shape[1] // groups
            return [
                mail.local(
                    src.at[:, pl.ds(pl.multiple_of(g * stride + here.turned(turn * g) * width, width), width)],
                    region.at[:, pl.ds(g * width, width)],
                )
                for g in range(groups)
            ]

        return fill

    def rows_of(src):
        return lambda region: [mail.local(src.at[span(here.turned(here.plane), region.shape[0]), :], region)]

    def core_rows_of(src, dst, other):
        return FromPlane(mail, here, src.at[span(here.core, dst.shape[0]), :], dst, other)

    def part(half):
        return pl.ds(half * rows, rows)

    def spread(buf, half, value, gain):
        buf[half, 0] = (whitened(value)[0] * gain).astype(BF)
        return Spread(mail, here, buf, half)

    def reduce(land):
        return [Reduce(mail, here, (r.stage, land, r.acc), h) for h in range(2)]

    own_small = small.at[here.plane]
    gains, taps = r.gains.shape[0], r.taps.shape[0]
    own_small[0:gains, :] = r.gains[...].astype(F32)
    own_small[gains : gains + taps, :] = r.taps[...].astype(F32)
    own_small[gains + taps : gains + taps + 1, :] = r.batch[...].astype(F32)
    small_copies = [mail.post(own_small, own_small, here.above(k)) for k in range(1, PLANES)]
    up1 = Ring(mail, here, r.up1, r.up1_other, columns_of(r.up1_src, 1))
    down1 = Ring(mail, here, r.down1, r.down1_other, rows_of(r.down1_src))

    for copy in small_copies:
        copy.wait_recv()
    gain = scale_row(small, 0)
    sent = [spread(r.hidden0, h, r.frames[0, part(h), :].astype(F32), gain) for h in range(2)]
    set_marks(marks, lengths)
    for h in range(2):
        sent[h].near()
    up1.relay()
    for h in range(2):
        sent[h].far()
    down1.relay()
    qkv = Ring(mail, here, r.qkv, r.qkv_other, columns_of(r.qkv_src))
    out = core_rows_of(r.out_src, r.out, r.out_other)
    up1.finish()
    up1.ready()
    ups, downs = (r.up1, r.up1_other), (r.down1, r.down1_other)
    for h in range(2):
        for p in range(2):
            feed_active(r.hidden0, r.keep0, ups, h, p)
    down1.finish()
    mail.save(r.hidden0, r.hidden0_out)
    mail.save(r.keep0, r.keep0_out)
    mail.save(r.up1, r.up1_out)
    mail.save(r.down1, r.down1_out)
    down1.ready()
    sums = reduce(r.land0)
    for h in range(2):
        for p in (1, 0):
            sums[h].put(p, feed_out(r.keep0, downs, h, p))
    qkv.relay()
    conv_in = Ring(mail, here, r.conv_in, r.conv_in_other, columns_of(r.in_src))
    gain = scale_row(small, 1)
    sent = []
    for h in range(2):
        value = r.frames[0, part(h), :].astype(F32) + 0.5 * sums[h].total()
        r.first[part(h), :] = value
        mail.save(r.first.at[part(h)], r.first_out.at[part(h)])
        sent.append(spread(r.hidden1, h, value, gain))
    out.relay()
    conv_out = core_rows_of(r.conv_src, r.conv_out, r.conv_out_other)

    joint, mixed = r.joint, r.mixed
    size = joint.shape[1] // 3
    qkv.finish()
    qkv.ready()
    mail.save(r.qkv, r.qkv_out)
    joint_copies = []

    def to_heads(h, p):
        value = pair_of(r.hidden1, h, p)
        set_pair(r.joint_stage, h, p, mm(value, r.qkv_other[...]).astype(BF))
        for j in (2 * p, 2 * p + 1):
            joint_copies.append(
                mail.post(r.joint_stage.at[h, j], joint.at[here.rows(j, h, rows), :], here.sibling())
            )
        value = mm(value, r.qkv[...]).astype(BF)
        for k in range(2):
            joint[here.rows(2 * p + k, h, rows), :] = value[k * rows : (k + 1) * rows]

    as_they_come(sent, to_heads)
    for copy in joint_copies:
        copy.wait_recv()
    conv_in.relay()
    up2 = Ring(mail, here, r.up2, r.up2_other, columns_of(r.up2_src, 1))
    mail.save(r.hidden1, r.hidden1_out)
    mail.save(joint, r.joint_out)
    slope = r.slopes[here.seq]
    mixed_copies = {}
    sums = reduce(r.land1)

    def unit(h, j):
        mine, theirs = here.rows(j, h, rows), here.other_rows(j, h, rows)
        query = jnp.concatenate([joint[mine, 0:size], joint[theirs, 0:size]], axis=0)
        index = lax.broadcasted_iota(jnp.int32, (2 * rows, 128), 0)[:, :1]
        frame = jnp.where(index < rows, mine.start + index, theirs.start + index - rows)
        weights = attention_weights(query, joint[:, size : 2 * size], slope, frame, lengths)[0]
        value = mm(weights.astype(BF), joint[:, 2 * size :]).astype(BF)
        mixed[0, h, j] = value[:rows]
        r.mixed_stage[h, j] = value[rows:]
        mixed_copies[h, j] = mail.post(r.mixed_stage.at[h, j], mixed.at[1, h, j], here.sibling())

    def project(h, p):
        for j in (2 * p, 2 * p + 1):
            mixed_copies[h, j].wait_recv()
        value = mm(pair_of(mixed.at[0], h, p), r.out[...]) + mm(pair_of(mixed.at[1], h, p), r.out_other[...])
        sums[h].put(p, value)

    unit(0, 2)
    unit(0, 3)
    out.finish()
    unit(0, 0)
    out.ready()
    project(0, 1)
    unit(0, 1)
    unit(1, 2)
    project(0, 0)
    unit(1, 3)
    unit(1, 0)
    project(1, 1)
    unit(1, 1)
    project(1, 0)
    mail.save(r.out, r.out_out)
    mail.save(mixed, r.mixed_out)
    gain = scale_row(small, 2)
    sent = []
    for h in range(2):
        value = r.first[part(h), :] + sums[h].total()
        r.second[part(h), :] = value
        mail.save(r.second.at[part(h)], r.second_out.at[part(h)])
        sent.append(spread(r.hidden2, h, value, gain))
        if h == 0:
            conv_in.finish()
            conv_out.relay()

    gated, padded, glu = r.gated, r.padded, r.glu
    frames, width = gated.shape
    conv_in.ready()
    mail.save(r.conv_in, r.in_out)
    gate_copies = []

    def to_gates(h, p):
        value = pair_of(r.hidden2, h, p)
        for side, weight in ((1, r.conv_in_other), (0, r.conv_in)):
            both = mm(value, weight[...])
            set_pair(glu, h, p, both, slice(2 * width * side, 2 * width * (side + 1)))
            gate = (both[:, :width] * sigmoid(both[:, width:])).astype(BF)
            for k in range(2):
                j = 2 * p + k
                if side:
                    r.gate_stage[h, j] = gate[k * rows : (k + 1) * rows]
                    gate_copies.append(
                        mail.post(r.gate_stage.at[h, j], r.gate_rows.at[here.rows(j, h, rows), :], here.sibling())
                    )
                else:
                    r.gate_rows[here.rows(j, h, rows), :] = gate[k * rows : (k + 1) * rows]

    as_they_come(sent, to_gates)
    mail.save(r.hidden2, r.hidden2_out)
    mail.save(glu, r.glu_out)
    up2.relay()
    for copy in gate_copies:
        copy.wait_recv()
    taps = marks.shape[0] - 1
    padded[0:RIM, :] = jnp.zeros((RIM, width), F32)
    padded[RIM + frames :, :] = jnp.zeros((RIM, width), F32)
    gated[...] = r.gate_rows[...].astype(F32)
    padded[RIM : RIM + frames, :] = gated[...]
    mail.save(gated, r.gated_out)
    kernel = own_channels(small, here, slice(5, 5 + taps), width)
    conv = None
    for t in range(taps):
        first = RIM - taps // 2 + t
        term = kernel[t : t + 1, :] * padded[first : first + frames, :] * marks[t].astype(F32)
        conv = term if conv is None else conv + term
    valid = marks[taps].astype(F32)
    count = jnp.sum(valid, axis=0, keepdims=True)
    total = jnp.sum(valid * conv, axis=0, keepdims=True)
    centred = conv - total / count
    squares = jnp.sum(valid * centred * centred, axis=0, keepdims=True)
    bn, bn_land = r.bn, r.bn_land
    bn[...] = at_row(0, total) + at_row(1, squares) + at_row(2, count)
    bn_copies = [mail.post(bn, bn_land.at[k - 1], here.above(k)) for k in range(1, PLANES)]
    down2 = Ring(mail, here, r.down2, r.down2_other, rows_of(r.down2_src))
    r.standard[...] = conv
    conv_out.finish()
    for copy in bn_copies:
        copy.wait_recv()
    terms = [bn[...]] + [bn_land[k - 1] for k in range(1, PLANES)]
    whole = sum(term[2:3, :] for term in terms)
    average = sum(term[0:1, :] for term in terms) / whole
    variance = 0.0
    for term in terms:
        apart = term[0:1, :] / term[2:3, :] - average
        variance = variance + term[1:2, :] + term[2:3, :] * apart * apart
    inverse = lax.rsqrt(variance / whole + EPSILON)
    r.stats[...] = at_row(0, inverse) + at_row(1, whole)
    standard = (r.standard[...] - average) * inverse
    r.standard[...] = standard
    scaled = standard * own_channels(small, here, slice(10, 11), width)
    r.swish_rows[...] = (scaled * sigmoid(scaled)).astype(BF)
    swish = r.swish
    swish_copies = {}
    for h in range(2):
        for j in (2, 3, 0, 1):
            swish_copies[h, j] = mail.post(
                r.swish_rows.at[here.other_rows(j, h, rows), :], swish.at[1, h, j], here.sibling()
            )
            swish[0, h, j] = r.swish_rows[here.rows(j, h, rows), :]
    mail.save(r.standard, r.standard_out)
    conv_out.ready()
    mail.save(r.conv_out, r.conv_out_out)
    sums = reduce(r.land2)
    for h in range(2):
        for p in (1, 0):
            for j in (2 * p, 2 * p + 1):
                swish_copies[h, j].wait_recv()
            value = mm(pair_of(swish.at[0], h, p), r.conv_out[...])
            sums[h].put(p, value + mm(pair_of(swish.at[1], h, p), r.conv_out_other[...]))
    mail.save(swish, r.swish_out)
    up2.finish()
    gain = scale_row(small, 3)
    sent = []
    for h in range(2):
        value = r.second[part(h), :] + sums[h].total()
        r.third[part(h), :] = value
        sent.append(spread(r.hidden3, h, value, gain))
        if h == 0:
            down2.relay()

    up2.ready()
    ups, downs = (r.up2, r.up2_other), (r.down2, r.down2_other)
    sums = reduce(r.land3)
    sent[0].near()
    feed_active(r.hidden3, r.keep3, ups, 0, 0)
    sent[1].near()
    sent[0].far()
    feed_active(r.hidden3, r.keep3, ups, 0, 1)
    down2.finish()
    down2.ready()
    for p in (1, 0):
        sums[0].put(p, feed_out(r.keep3, downs, 0, p, r.act))
    sent[1].far()
    for p in (1, 0):
        feed_active(r.hidden3, r.keep3, ups, 1, p)
        sums[1].put(p, feed_out(r.keep3, downs, 1, p, r.act))

    last_gain = scale_row(small, 4)
    sent, last_parts = [], []
    for h in range(2):
        fourth = r.third[part(h), :] + 0.5 * sums[h].total()
        r.result[0, part(h), :] = (whitened(fourth)[0] * last_gain).astype(BF)
        mail.save(r.result.at[0, part(h)], r.result_out.at[0, part(h)])
        gradient, last_part = norm_grad(fourth, last_gain, r.out_grad[0, part(h), :].astype(F32))
        last_parts.append(last_part)
        r.branch[h, 0] = (0.5 * gradient).astype(BF)
        sent.append(Spread(mail, here, r.branch, h))
        r.third_grad[part(h), :] = gradient
    sums = reduce(r.land4)

    def back(h, p):
        feed_slope(r.branch, r.keep3, downs, r.act_grad, h, p)
        sums[h].put(p, feed_in(r.act_grad, ups, h, p))

    as_they_come(sent, back)
    down_grad(mail, here, r.branch, r.act, r.down2_parts, r.down_send, r.down_land)
    mail.save(r.down2_parts, r.down2_parts_out)
    up_grad(mail, here, r.hidden3, r.act_grad, r.up2_parts, r.up_send, r.up_land)
    mail.save(r.up2_parts, r.up2_parts_out)
    gain_parts = []
    for h in range(2):
        value_part, gain_part = norm_grad(r.third[part(h), :], gain, sums[h].total())
        r.third_grad[part(h), :] = r.third_grad[part(h), :] + value_part
        mail.save(r.third_grad.at[part(h)], r.third_grad_out.at[part(h)])
        gain_parts.append(gain_part)
    r.small_d[...] = at_row(3, gain_parts[0] + gain_parts[1]) + at_row(4, last_parts[0] + last_parts[1])
    mail.close()


def backward_kernel(names, *refs):
    r = kernel_refs(names, refs)
    here, mail = Here(), Mail(r.send, r.recv)
    lengths, small, marks = r.lengths, r.small, r.marks
    rows = r.frames.shape[1] // 2
    seqs = 2 * CHIPS
    group = lax.rem(here.plane + seqs - here.seq, PLANES)
    target = 2 * group + lax.div(here.turned(group), PLANES)
    apart = target != here.seq
    group = lax.div(here.seq, 2)
    source = lax.rem(here.core * PLANES + here.plane + seqs - group, seqs)
    crosses = [here.cross(j) for j in range(1, CHIPS)]
    greet(near(here) + crosses, (apart, (source, here.plane)))

    def to_owner(index):
        src, dst = r.down_moved.at[index], r.down_got.at[index]
        i = mail.slot()
        stay = pltpu.make_async_copy(src, dst, mail.send.at[mail.slot()])
        go = mail.remote(src, dst, (target, here.plane), i, i)

        @pl.when(apart)
        def _():
            go.start()

        @pl.when(jnp.logical_not(apart))
        def _():
            stay.start()

        def wait():
            @pl.when(apart)
            def _():
                go.wait()

            @pl.when(jnp.logical_not(apart))
            def _():
                stay.wait()

        return wait

    def share(own, other):
        return mail.post(own, other, here.sibling())

    def part(half):
        return pl.ds(half * rows, rows)

    def spread(buf, half, value):
        buf[half, 0] = value.astype(BF)
        return Spread(mail, here, buf, half)

    def reduce(land):
        return [Reduce(mail, here, (r.stage, land, r.acc), h) for h in range(2)]

    third_ready = mail.local(r.third_grad_src, r.third_grad)
    down2_ready = mail.local(r.down2_parts_src, r.down2_parts)
    conv_out_shared = share(r.conv_out_src, r.conv_out_other)
    third_ready.wait()
    sent = [spread(r.branch2, h, r.third_grad[part(h), :]) for h in range(2)]
    conv_out_ready = mail.local(r.conv_out_src, r.conv_out)
    standard_ready = mail.local(r.standard_src, r.standard)
    swish_ready = mail.local(r.swish_src, r.swish)
    conv_in_shared = share(r.conv_in_src, r.conv_in_other)
    conv_in_ready = mail.local(r.conv_in_src, r.conv_in)
    glu_ready = mail.local(r.glu_src, r.glu)
    hidden2_ready = mail.local(r.hidden2_src, r.hidden2)
    gated_ready = mail.local(r.gated_src, r.gated)
    up2_ready = mail.local(r.up2_parts_src, r.up2_parts)
    second_ready = mail.local(r.second_src, r.second)
    down2_ready.wait()
    down2 = RingSum(mail, here, r.down2_parts, r.down2_relay, r.down2_land)
    set_marks(marks, lengths)

    frames, width = r.gated.shape
    conv_out_shared.wait_recv()
    conv_out_ready.wait()
    copies = []

    def to_channels(h, p):
        incoming = pair_of(r.branch2, h, p)
        set_pair(r.swish_stage, h, p, mm_right(incoming, r.conv_out_other[...]))
        for j in (2 * p, 2 * p + 1):
            copies.append(
                mail.post(r.swish_stage.at[h, j], r.swish_grad.at[here.rows(j, h, rows), :], here.sibling())
            )
        value = mm_right(incoming, r.conv_out[...])
        for k in range(2):
            r.swish_grad[here.rows(2 * p + k, h, rows), :] = value[k * rows : (k + 1) * rows]

    as_they_come(sent, to_channels)
    standard_ready.wait()
    gain = own_channels(small, here, slice(10, 11), width)
    for copy in copies:
        copy.wait_recv()
    white = r.standard[...]
    scaled = white * gain
    gate = sigmoid(scaled)
    scaled_grad = r.swish_grad[...] * (gate * (1.0 + scaled * (1.0 - gate)))
    bn, bn_land = r.bn, r.bn_land
    bn[...] = at_row(0, jnp.sum(scaled_grad, axis=0, keepdims=True)) + at_row(
        1, jnp.sum(scaled_grad * white, axis=0, keepdims=True)
    )
    bn_copies = [mail.post(bn, bn_land.at[k - 1], here.above(k)) for k in range(1, PLANES)]
    r.swish_grad[...] = scaled_grad * gain
    swish_ready.wait()
    row_send, column_send = r.down_send, r.up_send
    row_copies = sides_grad(
        mail, here, r.swish, r.branch2, r.conv_parts, row_send.at[pl.ds(0, width), :], r.conv_land
    )
    for copy in bn_copies:
        copy.wait_recv()
    down2.relay()
    up2_ready.wait()
    up2 = RingSum(mail, here, r.up2_parts, r.up2_relay, r.up2_land)
    both = bn[...]
    for k in range(1, PLANES):
        both = both + bn_land[k - 1]
    r.cross[...] = both
    inverse, whole = r.stats[0:1, :], r.stats[1:2, :]
    taps = marks.shape[0] - 1
    white = r.standard[...]
    conv_grad = inverse * r.swish_grad[...] - marks[taps].astype(F32) * (
        (inverse / whole) * (gain * both[0:1, :] + white * (gain * both[1:2, :]))
    )
    padded, reach = r.padded, taps // 2
    padded[0:RIM, :] = jnp.zeros((RIM, width), F32)
    padded[RIM + frames :, :] = jnp.zeros((RIM, width), F32)
    padded[RIM : RIM + frames, :] = conv_grad
    kernel = own_channels(small, here, slice(5, 5 + taps), width)
    total = None
    for t in range(taps):
        first = RIM + reach - t
        term = kernel[t : t + 1, :] * padded[first : first + frames, :] * marks[taps - 1 - t].astype(F32)
        total = term if total is None else total + term
    r.gate_grad[...] = total
    moved = r.moved2
    copies = {}
    for h in range(2):
        for j in (2, 3, 0, 1):
            copies[h, j] = mail.post(
                r.gate_grad.at[here.other_rows(j, h, rows), :], moved.at[1, h, j], here.sibling()
            )
            moved[0, h, j] = r.gate_grad[here.rows(j, h, rows), :]
    glu_ready.wait()
    conv_in_ready.wait()
    conv_in_shared.wait_recv()
    glu, glu_grad = r.glu, r.glu_grad
    sums = reduce(r.land2)
    for h in range(2):
        for p in (1, 0):
            for j in (2 * p, 2 * p + 1):
                copies[h, j].wait_recv()
            result = None
            for side, weight in ((0, r.conv_in), (1, r.conv_in_other)):
                start = 2 * width * side
                left = pair_of(glu, h, p, slice(start, start + width))
                gate = sigmoid(pair_of(glu, h, p, slice(start + width, start + 2 * width)))
                incoming = pair_of(moved.at[side], h, p)
                set_pair(glu_grad.at[side], h, p, (incoming * gate).astype(BF), slice(0, width))
                set_pair(
                    glu_grad.at[side], h, p, (incoming * left * (gate * (1.0 - gate))).astype(BF),
                    slice(width, 2 * width),
                )
                term = mm_right(pair_of(glu_grad.at[side], h, p), weight[...])
                result = term if result is None else result + term
            sums[h].put(p, result)
    out_shared, qkv_shared = share(r.out_src, r.out_other), share(r.qkv_src, r.qkv_other)
    out_ready = mail.local(r.out_src, r.out)
    joint_ready = mail.local(r.joint_src, r.joint)
    qkv_ready = mail.local(r.qkv_src, r.qkv)
    mixed_ready = mail.local(r.mixed_src, r.mixed)
    hidden1_ready = mail.local(r.hidden1_src, r.hidden1)
    first_ready = mail.local(r.first_src, r.first)
    hidden2_ready.wait()
    column_copies = slots_grad(
        mail, here, r.hidden2, glu_grad, r.in_parts, column_send.at[:, pl.ds(0, 2 * width)], r.in_land
    )
    gain = scale_row(small, 2)
    second_ready.wait()
    sent, gain_parts = [], []
    for h in range(2):
        value_part, gain_part = norm_grad(r.second[part(h), :], gain, sums[h].total())
        gradient = r.third_grad[part(h), :] + value_part
        r.grad[part(h), :] = gradient
        gain_parts.append(gain_part)
        sent.append(spread(r.branch1, h, gradient))
        if h == 0:
            gated_ready.wait()
            dense = padded[RIM : RIM + frames, :]
            padded[RIM : RIM + frames, :] = r.gated[...]
            kernel_rows = jnp.zeros((8, width), F32)
            for t in range(taps):
                first = RIM - reach + t
                row = jnp.sum(
                    padded[first : first + frames, :] * marks[t].astype(F32) * dense, axis=0, keepdims=True
                )
                kernel_rows = kernel_rows + at_row(t, row)
            r.kernel_part[...] = kernel_rows
    r.small_sum[...] = r.small_d[...] + at_row(2, gain_parts[0] + gain_parts[1])
    up2.relay()
    r.down_moved[0] = down2.total().astype(BF)
    down2_wait = to_owner(0)
    conv_sum = RingSum(mail, here, r.conv_parts, r.conv_relay, r.conv_sum_land)
    in_sum = RingSum(mail, here, r.in_parts, r.in_relay, r.in_sum_land)
    kernel_copies = [
        mail.post(r.kernel_part, r.kernel_land.at[k - 1], here.above(k)) for k in range(1, PLANES)
    ]

    out_shared.wait_recv()
    out_ready.wait()
    joint = r.joint
    size = joint.shape[1] // 3
    mixed_copies = []

    def to_heads(h, p):
        incoming = pair_of(r.branch1, h, p)
        set_pair(r.mixed_stage, h, p, mm_right(incoming, r.out_other[...]).astype(BF))
        for j in (2 * p, 2 * p + 1):
            mixed_copies.append(
                mail.post(r.mixed_stage.at[h, j], r.mixed_grad.at[here.rows(j, h, rows), :], here.sibling())
            )
        value = mm_right(incoming, r.out[...]).astype(BF)
        for k in range(2):
            r.mixed_grad[here.rows(2 * p + k, h, rows), :] = value[k * rows : (k + 1) * rows]

    as_they_come(sent, to_heads)
    mixed_ready.wait()
    mail.settle(row_copies)
    row_copies = sides_grad(
        mail, here, r.mixed, r.branch1, r.out_parts, row_send.at[pl.ds(0, size), :], r.out_land
    )
    joint_ready.wait()
    for copy in mixed_copies:
        copy.wait_recv()
    key_grad, value_grad, joint_grad = r.standard, r.gated, r.joint_grad
    key_grad[...] = jnp.zeros_like(key_grad)
    value_grad[...] = jnp.zeros_like(value_grad)
    scale = 1.0 / math.sqrt(size)
    slope = r.slopes[here.seq]
    height = 4 * rows

    def step(index, carry):
        start = pl.multiple_of(index * height, height)
        block_rows = pl.ds(start, height)
        query, keys, values = joint[block_rows, 0:size], joint[:, size : 2 * size], joint[:, 2 * size :]
        frame = lax.broadcasted_iota(jnp.int32, (height, 128), 0)[:, :1] + start
        weights, distance = attention_weights(query, keys, slope, frame, lengths)
        incoming = r.mixed_grad[block_rows, :]
        weight_grad = mm_right(incoming, values)
        delta = jnp.sum(weights * weight_grad, axis=-1, keepdims=True)
        score_grad = weights * (weight_grad - delta)
        raw = (score_grad * scale).astype(BF)
        joint_grad[block_rows, 0:size] = mm(raw, keys).astype(BF)
        key_grad[...] += mm_left(raw, query)
        value_grad[...] += mm_left(weights.astype(BF), incoming)
        return carry - jnp.sum(score_grad * distance, axis=0, keepdims=True)

    slope_row = lax.fori_loop(0, frames // height, step, jnp.zeros((1, frames), F32))
    joint_grad[:, size : 2 * size] = key_grad[...].astype(BF)
    joint_grad[:, 2 * size :] = value_grad[...].astype(BF)
    moved = r.moved1
    copies = {}
    for h in range(2):
        for j in (2, 3, 0, 1):
            copies[h, j] = mail.post(
                joint_grad.at[here.other_rows(j, h, rows), :], moved.at[1, h, j], here.sibling()
            )
            moved[0, h, j] = joint_grad[here.rows(j, h, rows), :]
    conv_sum.relay()
    in_sum.relay()
    out_sum = RingSum(mail, here, r.out_parts, r.out_relay, r.out_sum_land)
    qkv_shared.wait_recv()
    qkv_ready.wait()
    down_shared, up_shared = share(r.down1_src, r.down1_other), share(r.up1_src, r.up1_other)
    keep0_ready = mail.local(r.keep0_src, r.keep0)
    down1_ready = mail.local(r.down1_src, r.down1)
    up1_ready = mail.local(r.up1_src, r.up1)
    hidden0_ready = mail.local(r.hidden0_src, r.hidden0)
    sums = reduce(r.land1)
    for h in range(2):
        for p in (1, 0):
            for j in (2 * p, 2 * p + 1):
                copies[h, j].wait_recv()
            value = mm_right(pair_of(moved.at[0], h, p), r.qkv[...])
            sums[h].put(p, value + mm_right(pair_of(moved.at[1], h, p), r.qkv_other[...]))
    hidden1_ready.wait()
    mail.settle(column_copies)
    column_copies = slots_grad(
        mail, here, r.hidden1, moved, r.qkv_parts, column_send.at[:, pl.ds(0, 3 * size)], r.qkv_land
    )
    qkv_sum = RingSum(mail, here, r.qkv_parts, r.qkv_relay, r.qkv_sum_land)
    first_ready.wait()
    gain = scale_row(small, 1)
    sent, gain_parts = [], []
    for h in range(2):
        value_part, gain_part = norm_grad(r.first[part(h), :], gain, sums[h].total())
        gradient = r.grad[part(h), :] + value_part
        r.grad[part(h), :] = gradient
        gain_parts.append(gain_part)
        sent.append(spread(r.branch0, h, 0.5 * gradient))
    gain_part = gain_parts[0] + gain_parts[1]
    lane = lax.broadcasted_iota(jnp.int32, gain_part.shape, 1)
    slope_total = jnp.sum(slope_row, axis=1, keepdims=True)
    r.small_sum[...] = (
        r.small_sum[...] + at_row(1, gain_part) + at_row(5, jnp.where(lane == here.seq, slope_total, 0.0))
    )
    out_sum.relay()
    qkv_sum.relay()

    devices = [here.peer(j) for j in range(1, CHIPS)] + [here.cross(j) for j in range(CHIPS)]
    blocks = r.up2_out.shape[0]

    def swap(parts, got):
        return [mail.post(parts.at[span(device[0], blocks), :], got.at[i], device) for i, device in enumerate(devices)]

    def place(parts, got, out, copies, turn=0):
        lanes = 128
        groups = parts.shape[1] // lanes
        stride = out.shape[1] // groups
        for i in range(len(devices) + 1):
            if i:
                copies[i - 1].wait_recv()
            seq = devices[i - 1][0] if i else here.seq
            value = (got[i - 1] if i else parts[span(here.seq, blocks), :]).astype(F32)
            for g in range(groups):
                at = pl.ds(pl.multiple_of(g * stride + lax.rem(seq + turn * g, seqs) * lanes, lanes), lanes)
                out[:, at] = value[:, g * lanes : (g + 1) * lanes]

    down_shared.wait_recv()
    down1_ready.wait()
    keep0_ready.wait()
    ups, downs = (r.up1, r.up1_other), (r.down1, r.down1_other)
    act, act_grad = r.hidden2, r.hidden1
    for h in range(2):
        for p in range(2):
            feed_swish(r.keep0, act, h, p)
    sent[0].near()
    feed_slope(r.branch0, r.keep0, downs, act_grad, 0, 0)
    sent[1].near()
    sent[0].far()
    feed_slope(r.branch0, r.keep0, downs, act_grad, 0, 1)
    sent[1].far()
    mail.settle(row_copies + column_copies)
    down_grad(mail, here, r.branch0, act, r.down1_parts, r.down_send, r.down_land)
    down1 = RingSum(mail, here, r.down1_parts, r.down1_relay, r.down1_land)
    for p in (1, 0):
        feed_slope(r.branch0, r.keep0, downs, act_grad, 1, p)
    hidden0_ready.wait()
    up_grad(mail, here, r.hidden0, act_grad, r.up1_parts, r.up_send, r.up_land)
    up1 = RingSum(mail, here, r.up1_parts, r.up1_relay, r.up1_land)
    up_shared.wait_recv()
    up1_ready.wait()
    sums = reduce(r.land0)
    for h in range(2):
        for p in (1, 0):
            sums[h].put(p, feed_in(act_grad, ups, h, p))
    r.up2_sum[...] = up2.total().astype(BF)
    up2_copies = swap(r.up2_sum, r.up2_got)
    r.in_total[...] = in_sum.total().astype(BF)
    in_copies = swap(r.in_total, r.in_got)
    r.qkv_total[...] = qkv_sum.total().astype(BF)
    qkv_copies = swap(r.qkv_total, r.qkv_got)
    down1.relay()
    r.conv_out_grad[...] = conv_sum.total()
    mail.save(r.conv_out_grad, r.conv_grad_out)
    r.out_grad[...] = out_sum.total()
    mail.save(r.out_grad, r.attn_grad_out)
    for copy in kernel_copies:
        copy.wait_recv()
    kernel_total = r.kernel_part[...]
    for k in range(1, PLANES):
        kernel_total = kernel_total + r.kernel_land[k - 1]
    r.kernel_out[...] = kernel_total
    place(r.up2_sum, r.up2_got, r.up2_out, up2_copies, 1)
    mail.save(r.up2_out, r.up2_grad_out)
    up1.relay()
    gain = scale_row(small, 0)
    gain_parts = []
    for h in range(2):
        value_part, gain_part = norm_grad(r.frames[0, part(h), :].astype(F32), gain, sums[h].total())
        r.frames_grad[0, part(h), :] = r.grad[part(h), :] + value_part
        mail.save(r.frames_grad.at[0, part(h)], r.frames_grad_out.at[0, part(h)])
        gain_parts.append(gain_part)
    r.small_sum[...] = r.small_sum[...] + at_row(0, gain_parts[0] + gain_parts[1])
    small_copies = [
        mail.post(r.small_sum, r.small_land.at[k - 1], here.above(k)) for k in range(1, PLANES)
    ]
    r.down_moved[1] = down1.total().astype(BF)
    down1_wait = to_owner(1)
    place(r.in_total, r.in_got, r.in_out, in_copies)
    mail.save(r.in_out, r.in_grad_out)
    place(r.qkv_total, r.qkv_got, r.qkv_out, qkv_copies)
    mail.save(r.qkv_out, r.qkv_grad_out)
    down2_wait()
    r.down2_out[...] = r.down_got[0].astype(F32)
    mail.save(r.down2_out, r.down2_grad_out)
    r.up1_sum[...] = up1.total().astype(BF)
    up1_copies = swap(r.up1_sum, r.up1_got)
    for copy in small_copies:
        copy.wait_recv()
    total = r.small_sum[...]
    for k in range(1, PLANES):
        total = total + r.small_land[k - 1]
    r.small_mid[...] = total
    small_copies = [mail.post(r.small_mid, r.small_near.at[i], device) for i, device in enumerate(devices)]
    down1_wait()
    r.down1_out[...] = r.down_got[1].astype(F32)
    mail.save(r.down1_out, r.down1_grad_out)
    place(r.up1_sum, r.up1_got, r.up1_out, up1_copies, 1)
    mail.save(r.up1_out, r.up1_grad_out)
    for copy in small_copies:
        copy.wait_recv()
    total = r.small_mid[...]
    for i in range(len(devices)):
        total = total + r.small_near[i]
    r.small_out[...] = total
    mail.close()


def finish_kernel(*refs):
    count = (len(refs) - 7) // 2
    big, (small, kernel, cross) = refs[:count], refs[count : count + 3]
    outs, (gains_out, kernel_out, batch_out, slopes_out) = refs[count + 3 : 2 * count + 3], refs[2 * count + 3 :]
    for src, dst in zip(big, outs):
        dst[...] = src[...]
    seq, plane = lax.axis_index("seq"), lax.axis_index("fsdp")

    def own(ref, first, count, width, place):
        lanes = 128
        each = lanes // width
        block = ref[first : first + count, span(lax.div(place, each), lanes)]
        value = block[:, :width]
        for k in range(1, each):
            value = jnp.where(lax.rem(place, each) == k, block[:, k * width : (k + 1) * width], value)
        return value

    width = gains_out.shape[1]
    gains = gains_out.shape[0]
    gains_out[...] = own(small, 0, gains, width, seq * PLANES + plane)
    kernel_out[...] = own(kernel, 0, kernel_out.shape[0], width, plane)
    batch_out[...] = own(cross, 1, 1, width, plane)
    slopes_out[...] = small[gains : gains + 1, : slopes_out.shape[1]]


def launch(kernel, name, index, operands, results, scratch):
    names = list(operands) + list(results) + list(scratch) + ["send", "recv"]
    values = pl.pallas_call(
        functools.partial(kernel, names),
        name=name,
        out_shape=[jax.ShapeDtypeStruct(shape, kind) for shape, kind, _ in results.values()],
        in_specs=[pl.BlockSpec(memory_space=place) for _, place in operands.values()],
        out_specs=[pl.BlockSpec(memory_space=place) for _, _, place in results.values()],
        scratch_shapes=[pltpu.VMEM(shape, kind) for shape, kind in scratch.values()]
        + [pltpu.SemaphoreType.DMA((SLOTS,)), pltpu.SemaphoreType.DMA((SLOTS,))],
        compiler_params=pltpu.CompilerParams(
            collective_id=index, has_side_effects=True, vmem_limit_bytes=GRANT
        ),
    )(*[array for array, _ in operands.values()])
    return types.SimpleNamespace(**dict(zip(results, values)))


def plane_body(
    frames, lengths, up_first, down_first, joint_qkv, attn_out, conv_in, conv_kernel, batch_gain, conv_out,
    up_second, down_second, norm_gains, slopes, out_grad,
):
    seqs = lax.axis_size("seq")
    seq = lax.axis_index("seq")
    plane = lax.axis_index("fsdp")
    rows, width = frames.shape[1], frames.shape[2]
    length = rows * seqs
    heads = slopes.shape[0]
    size = width // heads
    channels = width // seqs
    hidden_units = up_first.shape[1]
    half = hidden_units // seqs
    taps = conv_kernel.shape[0]
    block = width // (seqs * PLANES)
    near_count = seqs - 1
    row_f = ((rows, width), F32)
    lines = rows // 2
    quad = ((2, CHIPS, lines, width), BF)
    stage = ((2, CHIPS - 1, lines, width), BF)
    acc = ((2, lines, width), F32)
    up, down = ((width, half), BF), ((half, width), BF)
    qkv, out = ((width, 3 * size), BF), ((size, width), BF)
    conv_i, conv_o = ((width, 2 * channels), BF), ((channels, width), BF)
    keep = ((2, CHIPS, lines, 2 * half), F32)
    act = ((2, CHIPS, lines, 2 * half), BF)
    joint = ((length, 3 * size), BF)
    mixed = ((2, 2, CHIPS, lines, size), BF)
    glu = ((2, CHIPS, lines, 4 * channels), F32)
    dense = ((length, channels), F32)
    padded = ((length + 2 * RIM, channels), F32)
    marks = ((taps + 1, length, channels), BF)
    bn = ((8, channels), F32)
    bn_land = ((PLANES - 1, 8, channels), F32)
    small_row = ((8, width), F32)
    small_all = ((PLANES, 16, norm_gains.shape[1]), F32)

    def parts(shape):
        return ((PLANES, shape[0][0] // PLANES, shape[0][1]), BF)

    def land(shape):
        return ((2, shape[0][0] // PLANES, shape[0][1]), BF)

    def relay(shape):
        return ((4, shape[0][0] // (2 * PLANES), shape[0][1]), BF)

    def summed(shape):
        return ((shape[0][0] // PLANES, shape[0][1]), BF)

    x_grad, up_rows, down_rows = ((1, rows, width), F32), ((block, hidden_units), F32), ((half // PLANES, width), F32)
    qkv_rows, in_rows, head_rows = ((block, 3 * width), F32), ((block, 2 * width), F32), ((size // PLANES, width), F32)
    a = launch(
        forward_kernel, "forward", 0,
        dict(
            frames=(frames, V), lengths=(lengths, S), gains=(norm_gains, V), taps=(conv_kernel, V),
            batch=(batch_gain.reshape(1, -1), V), slopes=(slopes, S),
            up1_src=(up_first, H), down1_src=(down_first, H), qkv_src=(joint_qkv, H),
            out_src=(attn_out, H), in_src=(conv_in, H), conv_src=(conv_out, H),
            up2_src=(up_second, H), down2_src=(down_second, H), out_grad=(out_grad, V),
        ),
        dict(
            result_out=((1, rows, width), BF, H), third_grad_out=row_f + (H,), small_d=small_row + (V,),
            first_out=row_f + (H,), second_out=row_f + (H,), small=small_all + (V,),
            stats=bn + (V,), up2_parts_out=parts(up) + (H,), down2_parts_out=parts(down) + (H,),
            hidden0_out=quad + (H,), hidden1_out=quad + (H,), hidden2_out=quad + (H,),
            keep0_out=keep + (H,), joint_out=joint + (H,), mixed_out=mixed + (H,),
            glu_out=glu + (H,), gated_out=dense + (H,), standard_out=dense + (H,),
            swish_out=mixed + (H,), up1_out=up + (H,), down1_out=down + (H,), qkv_out=qkv + (H,),
            out_out=out + (H,), in_out=conv_i + (H,), conv_out_out=conv_o + (H,),
        ),
        dict(
            up1=up, up1_other=up, down1=down, down1_other=down, qkv=qkv, qkv_other=qkv,
            out=out, out_other=out, conv_in=conv_i, conv_in_other=conv_i, conv_out=conv_o,
            conv_out_other=conv_o, up2=up, up2_other=up, down2=down, down2_other=down,
            hidden0=quad, hidden1=quad, hidden2=quad, hidden3=quad, keep0=keep, keep3=keep,
            joint=joint, joint_stage=((2, CHIPS, lines, 3 * size), BF), mixed=mixed,
            mixed_stage=((2, CHIPS, lines, size), BF), glu=glu, gated=dense, padded=padded,
            marks=marks, gate_stage=((2, CHIPS, lines, channels), BF), gate_rows=((length, channels), BF),
            standard=dense, swish_rows=((length, channels), BF), swish=mixed, bn=bn, bn_land=bn_land,
            third=row_f, branch=quad, act=act, act_grad=act, result=((1, rows, width), BF), third_grad=row_f,
            first=row_f, second=row_f, up2_parts=parts(up), down2_parts=parts(down),
            stage=stage, land0=stage, land1=stage, land2=stage, land3=stage, land4=stage, acc=acc,
            down_send=down, down_land=down, up_send=up, up_land=up,
        ),
    )
    b = launch(
        backward_kernel, "backward", 1,
        dict(
            frames=(frames, V), lengths=(lengths, S), slopes=(slopes, S), small=(a.small, V),
            third_grad_src=(a.third_grad_out, H), small_d=(a.small_d, V), second_src=(a.second_out, H),
            stats=(a.stats, V), up2_parts_src=(a.up2_parts_out, H), down2_parts_src=(a.down2_parts_out, H),
            first_src=(a.first_out, H), hidden0_src=(a.hidden0_out, H),
            hidden1_src=(a.hidden1_out, H), hidden2_src=(a.hidden2_out, H),
            keep0_src=(a.keep0_out, H), joint_src=(a.joint_out, H), mixed_src=(a.mixed_out, H),
            glu_src=(a.glu_out, H), gated_src=(a.gated_out, H),
            standard_src=(a.standard_out, H), swish_src=(a.swish_out, H),
            up1_src=(a.up1_out, H), down1_src=(a.down1_out, H), qkv_src=(a.qkv_out, H),
            out_src=(a.out_out, H), conv_in_src=(a.in_out, H),
            conv_out_src=(a.conv_out_out, H),
        ),
        dict(
            frames_grad_out=x_grad + (H,), up1_grad_out=up_rows + (H,), up2_grad_out=up_rows + (H,),
            down1_grad_out=down_rows + (H,), down2_grad_out=down_rows + (H,), qkv_grad_out=qkv_rows + (H,),
            in_grad_out=in_rows + (H,), attn_grad_out=head_rows + (H,), conv_grad_out=head_rows + (H,),
            kernel_out=bn + (V,), cross=bn + (V,), small_out=small_row + (V,),
        ),
        dict(
            up1=up, up1_other=up, down1=down, down1_other=down, qkv=qkv, qkv_other=qkv,
            out=out, out_other=out, conv_in=conv_i, conv_in_other=conv_i, conv_out=conv_o,
            conv_out_other=conv_o, hidden0=quad, hidden1=quad, hidden2=quad, keep0=keep,
            joint=joint, mixed=mixed, glu=glu, gated=dense, standard=dense, swish=mixed,
            first=row_f, grad=row_f, acc=acc, third_grad=row_f, second=row_f, up2_parts=parts(up),
            down2_parts=parts(down), frames_grad=x_grad, up1_out=up_rows, up2_out=up_rows, down1_out=down_rows,
            down2_out=down_rows, qkv_out=qkv_rows, in_out=in_rows, out_grad=head_rows, conv_out_grad=head_rows, marks=marks, padded=padded,
            branch2=quad, branch1=quad, branch0=quad, swish_stage=((2, CHIPS, lines, channels), F32),
            swish_grad=dense, gate_grad=dense, moved2=((2, 2, CHIPS, lines, channels), F32),
            glu_grad=((2, 2, CHIPS, lines, 2 * channels), BF), bn=bn, bn_land=bn_land,
            conv_land=conv_o, in_land=conv_i,
            conv_parts=parts(conv_o), in_parts=parts(conv_i), conv_relay=relay(conv_o),
            in_relay=relay(conv_i), conv_sum_land=land(conv_o), in_sum_land=land(conv_i),
            kernel_part=bn, kernel_land=bn_land, small_sum=small_row,
            up2_relay=relay(up), up2_land=land(up), down2_relay=relay(down), down2_land=land(down),
            up2_sum=summed(up), down_moved=((2,) + summed(down)[0], BF), down_got=((2,) + summed(down)[0], BF),
            mixed_stage=((2, CHIPS, lines, size), BF), mixed_grad=((length, size), BF),
            joint_grad=joint, moved1=((2, 2, CHIPS, lines, 3 * size), BF), out_land=out, qkv_land=qkv, out_parts=parts(out), qkv_parts=parts(qkv), out_relay=relay(out),
            qkv_relay=relay(qkv), out_sum_land=land(out), qkv_sum_land=land(qkv),
            down_send=down, down_land=down,
            up_send=up, up_land=up, up1_parts=parts(up), down1_parts=parts(down),
            up1_relay=relay(up), up1_land=land(up), down1_relay=relay(down), down1_land=land(down),
            up1_sum=summed(up), up1_got=((near_count, block, half), BF),
            up2_got=((near_count, block, half), BF), in_total=summed(conv_i),
            in_got=((near_count, block, 2 * channels), BF), qkv_total=summed(qkv),
            qkv_got=((near_count, block, 3 * size), BF), small_land=((PLANES - 1, 8, width), F32),
            small_mid=small_row, small_near=((near_count, 8, width), F32),
            stage=stage, land0=stage, land1=stage, land2=stage,
        ),
    )
    big = (
        a.result_out, b.frames_grad_out, b.up1_grad_out, b.down1_grad_out, b.qkv_grad_out, b.attn_grad_out, b.in_grad_out,
        b.conv_grad_out, b.up2_grad_out, b.down2_grad_out,
    )
    shapes = [jax.ShapeDtypeStruct(array.shape, array.dtype) for array in big]
    shapes += [jax.ShapeDtypeStruct(shape, F32) for shape in ((norm_gains.shape[0], block), (taps, block), (1, block), (1, heads))]
    done = pl.pallas_call(
        finish_kernel,
        name="finish",
        out_shape=shapes,
        in_specs=[pl.BlockSpec(memory_space=V)] * (len(big) + 3),
        out_specs=[pl.BlockSpec(memory_space=V)] * len(shapes),
        compiler_params=pltpu.CompilerParams(vmem_limit_bytes=GRANT),
    )(*big, b.small_out, b.kernel_out, b.cross)
    (
        result, frames_grad, up1_grad, down1_grad, qkv_grad, attn_out_grad, in_grad, conv_out_grad, up2_grad, down2_grad,
        gains_grad, kernel_grad, batch_grad, slopes_grad,
    ) = done
    return (
        result, frames_grad, up1_grad, down1_grad, qkv_grad, attn_out_grad, in_grad, kernel_grad,
        batch_grad.reshape(-1), conv_out_grad, up2_grad, down2_grad, gains_grad, slopes_grad.reshape(-1),
    )


def solution(mesh):
    planar = mesh.shape["seq"] == 2 * CHIPS and mesh.shape["fsdp"] == PLANES
    chosen = plane_body if planar else body
    placed = (
        P("fsdp", "seq", None),
        P("fsdp", None),
        P("fsdp", None),
        P("fsdp", None),
        P("fsdp", None),
        P("fsdp", None),
        P("fsdp", None),
        P(None, "fsdp"),
        P("fsdp"),
        P("fsdp", None),
        P("fsdp", None),
        P("fsdp", None),
        P(None, "fsdp"),
        P(),
        P("fsdp", "seq", None),
    )
    return jax.shard_map(
        chosen,
        mesh=mesh,
        in_specs=placed,
        out_specs=(
            P("fsdp", "seq", None),
            P("fsdp", "seq", None),
            P(("seq", "fsdp"), None),
            P(("seq", "fsdp"), None),
            P(("seq", "fsdp"), None),
            P(("seq", "fsdp"), None),
            P(("seq", "fsdp"), None),
            P(None, ("seq", "fsdp")),
            P(("seq", "fsdp")),
            P(("seq", "fsdp"), None),
            P(("seq", "fsdp"), None),
            P(("seq", "fsdp"), None),
            P(None, ("seq", "fsdp")),
            P(),
        ),
        check_vma=False,
    )
```

```python
import functools
import math
import types

import jax
import jax.numpy as jnp
from jax import lax
from jax.experimental import pallas as pl
from jax.experimental.pallas import tpu as pltpu
from jax.sharding import PartitionSpec as P

EPSILON = 1e-05
MASKED = -1e30


def extended(x, sides, width):
    for axis, dim in sides:
        size, length = (lax.axis_size(axis), x.shape[dim])
        up = [(i, (i + 1) % size) for i in range(size - 1)]
        down = [(j, i) for i, j in up]
        last = lax.slice_in_dim(x, length - width, length, axis=dim)
        initial = lax.slice_in_dim(x, 0, width, axis=dim)
        before = lax.ppermute(last, axis, up)
        after = lax.ppermute(initial, axis, down)
        x = jnp.concatenate([before, x, after], axis=dim)
    return x


def normed(value, gain):
    average = jnp.mean(value, axis=-1, keepdims=True)
    centred = value - average
    variance = jnp.mean(centred * centred, axis=-1, keepdims=True)
    return centred * lax.rsqrt(variance + EPSILON) * gain


def norm_back(value, gain, gradient):
    pullback = jax.vjp(normed, value, gain)[1]
    return pullback(gradient)


def matmul(left, right):
    return jnp.dot(left, right, preferred_element_type=jnp.float32)


def transposed_left(left, right):
    return lax.dot_general(
        left, right, (((0,), (0,)), ((), ())), preferred_element_type=jnp.float32
    )


def transposed_right(left, right):
    return lax.dot_general(
        left, right, (((1,), (1,)), ((), ())), preferred_element_type=jnp.float32
    )


def item_index(positions, bounds):
    return jnp.sum((positions[:, None] >= bounds[None, :]).astype(jnp.int32), axis=1)


def unpack(weights):
    (
        first_up,
        first_down,
        qkv_full,
        out_full,
        conv_up,
        kernel_full,
        batch_full,
        conv_down,
        second_up,
        second_down,
        gains_full,
    ) = weights
    return (
        first_up,
        first_down,
        qkv_full,
        out_full,
        conv_up,
        kernel_full.astype(jnp.float32),
        batch_full.astype(jnp.float32),
        conv_down,
        second_up,
        second_down,
        gains_full.astype(jnp.float32),
    )


def feed_forward(value, gain, weight_up, weight_down):
    hidden = normed(value, gain).astype(jnp.bfloat16)
    swish = jax.nn.silu(matmul(hidden, weight_up)).astype(jnp.bfloat16)
    return value + 0.5 * matmul(swish, weight_down)


def feed_back(value, gain, weight_up, weight_down, gradient):
    hidden = normed(value, gain).astype(jnp.bfloat16)
    swish, pullback = jax.vjp(jax.nn.silu, matmul(hidden, weight_up))
    swish_low = swish.astype(jnp.bfloat16)
    branch_grad = (0.5 * gradient).astype(jnp.bfloat16)
    down_grad = transposed_left(swish_low, branch_grad)
    active_grad = pullback(transposed_right(branch_grad, weight_down))[0].astype(jnp.bfloat16)
    up_grad = transposed_left(hidden, active_grad)
    value_grad, gain_grad = norm_back(value, gain, transposed_right(active_grad, weight_up))
    return (gradient + value_grad, gain_grad, up_grad, down_grad)


def biased_scores(query_heads, key_heads, slopes, layout):
    query_pos, key_pos, query_ids, key_ids = layout
    raw_scores = jnp.einsum(
        "qhd,khd->hqk", query_heads, key_heads, preferred_element_type=jnp.float32
    )
    distance = jnp.abs(query_pos[:, None] - key_pos[None, :]).astype(jnp.float32)
    scores = (
        raw_scores * (1.0 / math.sqrt(query_heads.shape[2]))
        - slopes[:, None, None] * distance[None]
    )
    shared = query_ids[:, None] == key_ids[None, :]
    return (jnp.where(shared[None], scores, MASKED), distance)


def attention_probs(query, keys, slopes, layout):
    heads = slopes.shape[0]
    head_size = query.shape[1] // heads
    query_heads = query.reshape(query.shape[0], heads, head_size)
    key_heads = keys.reshape(keys.shape[0], heads, head_size)
    scores, distance = biased_scores(query_heads, key_heads, slopes, layout)
    top = jnp.max(scores, axis=-1, keepdims=True)
    exponent = jnp.exp(scores - top)
    total = jnp.sum(exponent, axis=-1, keepdims=True)
    probs = exponent / total
    return (probs, distance, query_heads, key_heads, top[:, :, 0], total[:, :, 0])


def attend(value, gain, weight_qkv, weight_out, slopes, layout):
    feature_width = value.shape[1]
    hidden = normed(value, gain).astype(jnp.bfloat16)
    joint = matmul(hidden, weight_qkv).astype(jnp.bfloat16)
    keys_values = lax.all_gather(joint[:, feature_width:], "seq", axis=0, tiled=True)
    probs, distance, query_heads, key_heads, top, total = attention_probs(
        joint[:, :feature_width], keys_values[:, :feature_width], slopes, layout
    )
    value_heads = keys_values[:, feature_width:].reshape(key_heads.shape)
    mixed = jnp.einsum(
        "hqk,khd->qhd", probs.astype(jnp.bfloat16), value_heads, preferred_element_type=jnp.float32
    )
    mixed = mixed.reshape(value.shape).astype(jnp.bfloat16)
    return (value + matmul(mixed, weight_out), keys_values)


def attend_back(value, gain, weight_qkv, weight_out, slopes, layout, keys_values, gradient):
    feature_width = value.shape[1]
    row_count = value.shape[0]
    hidden = normed(value, gain).astype(jnp.bfloat16)
    joint = matmul(hidden, weight_qkv).astype(jnp.bfloat16)
    probs, distance, query_heads, key_heads, top, total = attention_probs(
        joint[:, :feature_width], keys_values[:, :feature_width], slopes, layout
    )
    probs_low = probs.astype(jnp.bfloat16)
    value_heads = keys_values[:, feature_width:].reshape(key_heads.shape)
    mixed = jnp.einsum("hqk,khd->qhd", probs_low, value_heads, preferred_element_type=jnp.float32)
    mixed = mixed.reshape(value.shape).astype(jnp.bfloat16)
    branch_grad = gradient.astype(jnp.bfloat16)
    weight_out_grad = transposed_left(mixed, branch_grad)
    mixed_flat = transposed_right(branch_grad, weight_out).astype(jnp.bfloat16)
    mixed_grad = mixed_flat.reshape(query_heads.shape)
    prob_grad = jnp.einsum(
        "qhd,khd->hqk", mixed_grad, value_heads, preferred_element_type=jnp.float32
    )
    delta = jnp.sum(probs * prob_grad, axis=-1)
    score_grad = probs * (prob_grad - delta[:, :, None])
    slope_grad = -jnp.sum(score_grad * distance[None], axis=(1, 2))
    scale = 1.0 / math.sqrt(query_heads.shape[2])
    raw_grad = (score_grad * scale).astype(jnp.bfloat16)
    query_grad = jnp.einsum("hqk,khd->qhd", raw_grad, key_heads, preferred_element_type=jnp.float32)
    query_pos, key_pos, query_ids, key_ids = layout
    all_query, all_mixed = (
        lax.all_gather(joint[:, :feature_width], "seq", axis=0, tiled=True),
        lax.all_gather(mixed_flat, "seq", axis=0, tiled=True),
    )
    all_top, all_total, all_delta = (
        lax.all_gather(top, "seq", axis=1, tiled=True),
        lax.all_gather(total, "seq", axis=1, tiled=True),
        lax.all_gather(delta, "seq", axis=1, tiled=True),
    )
    heads = slopes.shape[0]
    head_size = query_heads.shape[2]
    all_query_heads = all_query.reshape(all_query.shape[0], heads, head_size)
    all_mixed_heads = all_mixed.reshape(all_query.shape[0], heads, head_size)
    own_keys = joint[:, feature_width : 2 * feature_width].reshape(row_count, heads, head_size)
    own_values = joint[:, 2 * feature_width :].reshape(row_count, heads, head_size)
    column_scores, column_distance = biased_scores(
        all_query_heads, own_keys, slopes, (key_pos, query_pos, key_ids, query_ids)
    )
    column_probs = jnp.exp(column_scores - all_top[:, :, None]) / all_total[:, :, None]
    column_prob_grad = jnp.einsum(
        "qhd,khd->hqk", all_mixed_heads, own_values, preferred_element_type=jnp.float32
    )
    column_score_grad = column_probs * (column_prob_grad - all_delta[:, :, None])
    column_raw = (column_score_grad * scale).astype(jnp.bfloat16)
    key_grad = jnp.einsum(
        "hqk,qhd->khd", column_raw, all_query_heads, preferred_element_type=jnp.float32
    )
    value_grad = jnp.einsum(
        "hqk,qhd->khd",
        column_probs.astype(jnp.bfloat16),
        all_mixed_heads,
        preferred_element_type=jnp.float32,
    )
    local_grad = jnp.concatenate(
        [key_grad.reshape(row_count, feature_width), value_grad.reshape(row_count, feature_width)],
        axis=1,
    )
    joint_grad = jnp.concatenate([query_grad.reshape(value.shape), local_grad], axis=1).astype(
        jnp.bfloat16
    )
    qkv_grad = transposed_left(hidden, joint_grad)
    input_grad, gain_grad = norm_back(value, gain, transposed_right(joint_grad, weight_qkv))
    return (gradient + input_grad, gain_grad, qkv_grad, weight_out_grad, slope_grad)


def gate_linear(joint):
    feature_width = joint.shape[1] // 2
    return joint[:, :feature_width] * jax.nn.sigmoid(joint[:, feature_width:])


def depthwise(rim, kernel, rim_ids, own_ids):
    row_count = own_ids.shape[0]
    total = jnp.zeros((row_count, rim.shape[1]), jnp.float32)
    for offset in range(kernel.shape[0]):
        shared = (rim_ids[offset : offset + row_count] == own_ids).astype(jnp.float32)
        total = (
            total
            + kernel[offset]
            * rim[offset : offset + row_count].astype(jnp.float32)
            * shared[:, None]
        )
    return total


def depthwise_back(rim, kernel, rim_ids, own_ids, conv_grad):
    row_count = own_ids.shape[0]
    reach = kernel.shape[0] - 1
    grad_rim = extended(conv_grad.astype(jnp.bfloat16), (("seq", 0),), reach // 2).astype(
        conv_grad.dtype
    )
    input_grad = jnp.zeros(conv_grad.shape, jnp.float32)
    kernel_rows = []
    for offset in range(kernel.shape[0]):
        shared = (rim_ids[offset : offset + row_count] == own_ids).astype(jnp.float32)[:, None]
        kernel_rows.append(
            jnp.sum(
                rim[offset : offset + row_count].astype(jnp.float32) * shared * conv_grad, axis=0
            )
        )
        mirror = reach - offset
        crossed = (rim_ids[mirror : mirror + row_count] == own_ids).astype(jnp.float32)[:, None]
        input_grad = input_grad + kernel[offset] * grad_rim[mirror : mirror + row_count] * crossed
    return (input_grad, jnp.stack(kernel_rows))


def body(
    frames,
    lengths,
    up_first,
    down_first,
    joint_qkv,
    attn_out,
    conv_in,
    conv_kernel,
    batch_gain,
    conv_out,
    up_second,
    down_second,
    norm_gains,
    slopes,
    out_grad,
):
    sharded = (
        up_first,
        down_first,
        joint_qkv,
        attn_out,
        conv_in,
        conv_kernel,
        batch_gain,
        conv_out,
        up_second,
        down_second,
        norm_gains,
    )
    gathered = (
        lax.all_gather(sharded[0], "fsdp", axis=0, tiled=True),
        lax.all_gather(sharded[1], "fsdp", axis=0, tiled=True),
        lax.all_gather(sharded[2], "fsdp", axis=0, tiled=True),
        lax.all_gather(sharded[3], "fsdp", axis=0, tiled=True),
        lax.all_gather(sharded[4], "fsdp", axis=0, tiled=True),
        lax.all_gather(sharded[5], "fsdp", axis=1, tiled=True),
        lax.all_gather(sharded[6], "fsdp", axis=0, tiled=True),
        lax.all_gather(sharded[7], "fsdp", axis=0, tiled=True),
        lax.all_gather(sharded[8], "fsdp", axis=0, tiled=True),
        lax.all_gather(sharded[9], "fsdp", axis=0, tiled=True),
        lax.all_gather(sharded[10], "fsdp", axis=1, tiled=True),
    )
    (
        first_up,
        first_down,
        qkv_full,
        out_full,
        conv_up,
        kernel,
        batch_scale,
        conv_down,
        second_up,
        second_down,
        gains,
    ) = unpack(gathered)
    row_count = frames.shape[1]
    feature_width = frames.shape[2]
    seq_count = lax.axis_size("seq")
    start_row = lax.axis_index("seq") * row_count
    bounds = jnp.cumsum(lengths[0])
    item_count = lengths.shape[1]
    own_pos = start_row + jnp.arange(row_count, dtype=jnp.int32)
    key_pos = jnp.arange(row_count * seq_count, dtype=jnp.int32)
    own_ids = item_index(own_pos, bounds)
    layout = (own_pos, key_pos, own_ids, item_index(key_pos, bounds))
    rim_width = conv_kernel.shape[0] // 2
    rim_ids = item_index(
        start_row - rim_width + jnp.arange(row_count + 2 * rim_width, dtype=jnp.int32), bounds
    )
    valid = (own_ids < item_count).astype(jnp.float32)[:, None]
    source = frames[0].astype(jnp.float32)
    first = feed_forward(source, gains[0], first_up, first_down)
    second, keys_values = attend(first, gains[1], qkv_full, out_full, slopes, layout)
    conv_hidden = normed(second, gains[2]).astype(jnp.bfloat16)
    conv_joint = matmul(conv_hidden, conv_up)
    rim = extended(gate_linear(conv_joint).astype(jnp.bfloat16), (("seq", 0),), rim_width)
    conv = depthwise(rim, kernel, rim_ids, own_ids)
    total, count = lax.psum((jnp.sum(valid * conv, axis=0), jnp.sum(valid)), ("seq", "fsdp"))
    average = total / count
    centred = conv - average
    spread = lax.psum(jnp.sum(valid * centred * centred, axis=0), ("seq", "fsdp"))
    variance = spread / count
    inverse = lax.rsqrt(variance + EPSILON)
    standard = (conv - average) * inverse
    pre_swish = standard * batch_scale
    swish, swish_pull = jax.vjp(jax.nn.silu, pre_swish)
    swish_low = swish.astype(jnp.bfloat16)
    third = second + matmul(swish_low, conv_down)
    fourth = feed_forward(third, gains[3], second_up, second_down)
    result = normed(fourth, gains[4])
    regathered = (
        lax.all_gather(sharded[0], "fsdp", axis=0, tiled=True),
        lax.all_gather(sharded[1], "fsdp", axis=0, tiled=True),
        lax.all_gather(sharded[2], "fsdp", axis=0, tiled=True),
        lax.all_gather(sharded[3], "fsdp", axis=0, tiled=True),
        lax.all_gather(sharded[4], "fsdp", axis=0, tiled=True),
        lax.all_gather(sharded[5], "fsdp", axis=1, tiled=True),
        lax.all_gather(sharded[6], "fsdp", axis=0, tiled=True),
        lax.all_gather(sharded[7], "fsdp", axis=0, tiled=True),
        lax.all_gather(sharded[8], "fsdp", axis=0, tiled=True),
        lax.all_gather(sharded[9], "fsdp", axis=0, tiled=True),
        lax.all_gather(sharded[10], "fsdp", axis=1, tiled=True),
    )
    (
        first_up,
        first_down,
        qkv_full,
        out_full,
        conv_up,
        kernel,
        batch_scale,
        conv_down,
        second_up,
        second_down,
        gains,
    ) = unpack(regathered)
    fourth_grad, last_gain = norm_back(fourth, gains[4], out_grad[0].astype(jnp.float32))
    third_grad, fourth_gain, second_up_grad, second_down_grad = feed_back(
        third, gains[3], second_up, second_down, fourth_grad
    )
    branch_grad = third_grad.astype(jnp.bfloat16)
    conv_down_grad = transposed_left(swish_low, branch_grad)
    scaled_grad = swish_pull(transposed_right(branch_grad, conv_down))[0]
    sum_grad, sum_cross = lax.psum(
        (jnp.sum(scaled_grad, axis=0), jnp.sum(scaled_grad * standard, axis=0)), ("seq", "fsdp")
    )
    conv_grad = inverse * (scaled_grad * batch_scale) - valid * (inverse / count) * (
        batch_scale * sum_grad + standard * (batch_scale * sum_cross)
    )
    gated_grad, kernel_grad = depthwise_back(rim, kernel, rim_ids, own_ids, conv_grad)
    joint_pull = jax.vjp(gate_linear, conv_joint)[1]
    joint_grad = joint_pull(gated_grad)[0].astype(jnp.bfloat16)
    conv_up_grad = transposed_left(conv_hidden, joint_grad)
    hidden_grad, third_gain = norm_back(second, gains[2], transposed_right(joint_grad, conv_up))
    second_grad = third_grad + hidden_grad
    late = (
        lax.psum_scatter(second_up_grad, ("seq", "fsdp"), scatter_dimension=0, tiled=True),
        lax.psum_scatter(second_down_grad, ("seq", "fsdp"), scatter_dimension=0, tiled=True),
        lax.psum_scatter(conv_down_grad, ("seq", "fsdp"), scatter_dimension=0, tiled=True),
        lax.psum_scatter(conv_up_grad, ("seq", "fsdp"), scatter_dimension=0, tiled=True),
        lax.psum_scatter(kernel_grad, ("seq", "fsdp"), scatter_dimension=1, tiled=True),
    )
    first_grad, second_gain, qkv_grad, out_weight_grad, slope_part = attend_back(
        first, gains[1], qkv_full, out_full, slopes, layout, keys_values, second_grad
    )
    source_grad, first_gain, first_up_grad, first_down_grad = feed_back(
        source, gains[0], first_up, first_down, first_grad
    )
    gain_grads = jnp.stack([first_gain, second_gain, third_gain, fourth_gain, last_gain])
    early = (
        lax.psum_scatter(first_up_grad, ("seq", "fsdp"), scatter_dimension=0, tiled=True),
        lax.psum_scatter(first_down_grad, ("seq", "fsdp"), scatter_dimension=0, tiled=True),
        lax.psum_scatter(qkv_grad, ("seq", "fsdp"), scatter_dimension=0, tiled=True),
        lax.psum_scatter(out_weight_grad, ("seq", "fsdp"), scatter_dimension=0, tiled=True),
        lax.psum_scatter(gain_grads, ("seq", "fsdp"), scatter_dimension=1, tiled=True),
    )
    slope_grad = lax.psum(slope_part, ("seq", "fsdp"))
    piece_width = feature_width // lax.axis_size(("seq", "fsdp"))
    batch_piece = lax.dynamic_slice_in_dim(
        sum_cross, lax.axis_index(("seq", "fsdp")) * piece_width, piece_width
    )
    return (
        result[None].astype(jnp.bfloat16),
        source_grad[None],
        early[0],
        early[1],
        early[2],
        early[3],
        late[3],
        late[4],
        batch_piece,
        late[2],
        late[0],
        late[1],
        early[4],
        slope_grad,
    )


BF = jnp.bfloat16
F32 = jnp.float32
MESH = pl.DeviceIdType.MESH
GRANT = 63 * 2**20
CHIPS = 4
PLANES = 4
SLOTS = 320
RIM = 8
V, H, S = pltpu.VMEM, pl.ANY, pltpu.SMEM


def mm(left, right):
    return jnp.dot(left, right, preferred_element_type=F32)


def mm_right(left, right):
    return lax.dot_general(left, right, (((1,), (1,)), ((), ())), preferred_element_type=F32)


def mm_left(left, right):
    return lax.dot_general(left, right, (((0,), (0,)), ((), ())), preferred_element_type=F32)


def span(index, size):
    return pl.ds(pl.multiple_of(index * size, size), size)


class Here:
    def __init__(self):
        self.seq = lax.axis_index("seq")
        self.plane = lax.axis_index("fsdp")
        self.core = lax.rem(self.seq, 2)
        self.chip = lax.div(self.seq, 2)
        column, row = lax.rem(self.chip, 2), lax.div(self.chip, 2)
        self.chips = [
            lax.rem(row + j // 2, 2) * 2 + lax.rem(column + j % 2, 2) for j in range(CHIPS)
        ]

    def peer(self, slot):
        return (self.chips[slot] * 2 + self.core, self.plane)

    def cross(self, slot):
        return (self.chips[slot] * 2 + 1 - self.core, self.plane)

    def sibling(self):
        return self.cross(0)

    def level(self, step):
        return lax.rem(self.plane + step, PLANES)

    def turned(self, step):
        return lax.rem(self.seq + step, 2 * CHIPS)

    def above(self, step):
        return (self.seq, self.level(step))

    def rows(self, slot, half, height):
        return span((self.chips[slot] * 2 + self.core) * 2 + half, height)

    def other_rows(self, slot, half, height):
        return span((self.chips[slot] * 2 + 1 - self.core) * 2 + half, height)


class Mail:
    def __init__(self, send, recv):
        self.send, self.recv, self.count, self.open, self.kept = send, recv, 0, [], []

    def slot(self):
        self.count += 1
        return self.count - 1

    def remote(self, src, dst, device, sent, received):
        return pltpu.make_async_remote_copy(
            src_ref=src,
            dst_ref=dst,
            send_sem=self.send.at[sent],
            recv_sem=self.recv.at[received],
            device_id=device,
            device_id_type=MESH,
        )

    def post(self, src, dst, device):
        i = self.slot()
        copy = self.remote(src, dst, device, i, i)
        copy.start()
        self.open.append(copy)
        return copy

    def settle(self, copies):
        for copy in copies:
            copy.wait_send()
        self.open = [copy for copy in self.open if all(copy is not done for done in copies)]

    def local(self, src, dst):
        copy = pltpu.make_async_copy(src, dst, self.send.at[self.slot()])
        copy.start()
        return copy

    def save(self, src, dst):
        self.kept.append(self.local(src, dst))

    def close(self):
        for copy in self.open:
            copy.wait_send()
        for copy in self.kept:
            copy.wait()
        self.open, self.kept = [], []


def greet(devices, extra=None):
    barrier = pltpu.get_barrier_semaphore()
    for device in devices:
        pl.semaphore_signal(barrier, inc=1, device_id=device, device_id_type=MESH)
    count = len(devices)
    if extra is not None:
        apart, device = extra
        count = count + apart.astype(jnp.int32)

        @pl.when(apart)
        def _():
            pl.semaphore_signal(barrier, inc=1, device_id=device, device_id_type=MESH)

    return lambda: pl.semaphore_wait(barrier, count)


def near(here):
    return (
        [here.peer(j) for j in range(1, CHIPS)]
        + [here.sibling()]
        + [here.above(k) for k in range(1, PLANES)]
    )


class Spread:
    def __init__(self, mail, here, buf, half):
        self.mail, self.here, self.buf = mail, here, buf.at[half]
        rows = buf.shape[2]
        self.whole, self.top, self.low = pl.ds(0, rows), pl.ds(0, rows // 2), pl.ds(rows // 2, rows // 2)
        self.x = self.send(0, 1, self.whole, 1)
        self.y = self.send(0, 2, self.whole, 2)

    def send(self, source, target, rows, slot):
        return self.mail.post(self.buf.at[source, rows], self.buf.at[target, rows], self.here.peer(slot))

    def near(self):
        self.x.wait_recv()
        self.d_top = self.send(1, 3, self.top, 2)
        self.y.wait_recv()
        self.d_low = self.send(2, 3, self.low, 1)

    def far(self):
        self.d_top.wait_recv()
        self.d_low.wait_recv()


def as_they_come(sent, work):
    sent[0].near()
    work(0, 0)
    sent[1].near()
    sent[0].far()
    work(0, 1)
    sent[1].far()
    work(1, 1)
    work(1, 0)


class Ring:
    def __init__(self, mail, here, dst, other, fill):
        self.mail, self.here, self.dst, self.other = mail, here, dst, other
        self.height = dst.shape[0] // PLANES
        self.fills = fill(self.block(dst, here.plane))

    def send(self):
        mail, here, dst = self.mail, self.here, self.dst
        for copy in self.fills:
            copy.wait()
        own = self.block(dst, here.plane)
        self.up = mail.post(own, own, here.above(1))
        self.down = mail.post(own, own, here.above(PLANES - 1))
        self.shared = [self.share(here.plane)]
        return self

    def block(self, ref, plane):
        return ref.at[span(plane, self.height)]

    def share(self, plane):
        return self.mail.post(self.block(self.dst, plane), self.block(self.other, plane), self.here.sibling())

    def relay(self):
        here, half = self.here, self.height // 2
        self.up.wait_recv()
        piece = self.block(self.dst, here.level(PLANES - 1)).at[pl.ds(0, half)]
        self.far_up = self.mail.post(piece, piece, here.above(1))
        self.down.wait_recv()
        piece = self.block(self.dst, here.level(1)).at[pl.ds(half, half)]
        self.far_down = self.mail.post(piece, piece, here.above(PLANES - 1))
        self.shared += [self.share(here.level(PLANES - 1)), self.share(here.level(1))]

    def finish(self):
        self.far_up.wait_recv()
        self.far_down.wait_recv()
        self.shared.append(self.share(self.here.level(2)))

    def ready(self):
        for copy in self.shared:
            copy.wait_recv()


class FromPlane:
    def __init__(self, mail, here, src, dst, other):
        self.mail, self.here, self.dst, self.other = mail, here, dst, other
        half = dst.shape[0] // 2
        top, low = pl.ds(0, half), pl.ds(half, half)
        slots = [mail.slot() for _ in range(4)]
        above, below = here.above(1), here.above(PLANES - 1)
        self.step = lax.rem(here.plane + PLANES - here.chip, PLANES)
        self.own = pltpu.make_async_copy(src, dst, mail.send.at[mail.slot()])
        self.up = mail.remote(src, dst, above, slots[0], slots[0])
        self.down = mail.remote(src, dst, below, slots[1], slots[1])
        self.far_up = mail.remote(dst.at[top], dst.at[top], above, slots[2], slots[2])
        self.far_down = mail.remote(dst.at[low], dst.at[low], below, slots[3], slots[3])

        @pl.when(self.step == 0)
        def _():
            self.own.start()
            self.up.start()
            self.down.start()

    def relay(self):
        @pl.when(self.step == 1)
        def _():
            self.up.wait_recv()
            self.far_up.start()

        @pl.when(self.step == PLANES - 1)
        def _():
            self.down.wait_recv()
            self.far_down.start()

    def finish(self):
        @pl.when(self.step == 0)
        def _():
            self.own.wait()
            self.up.wait_send()
            self.down.wait_send()

        @pl.when(self.step == 1)
        def _():
            self.far_up.wait_send()

        @pl.when(self.step == 2)
        def _():
            self.far_up.wait_recv()
            self.far_down.wait_recv()

        @pl.when(self.step == PLANES - 1)
        def _():
            self.far_down.wait_send()

        self.shared = self.mail.post(self.dst, self.other, self.here.sibling())

    def ready(self):
        self.shared.wait_recv()


class RingSum:
    def __init__(self, mail, here, parts, relays, land):
        self.mail, self.here, self.parts, self.relays, self.land = mail, here, parts, relays, land
        self.half = parts.shape[1] // 2
        self.top, self.low = pl.ds(0, self.half), pl.ds(self.half, self.half)
        far, up, down = here.level(2), here.level(1), here.level(PLANES - 1)
        above, below = here.above(1), here.above(PLANES - 1)
        self.far_up = mail.post(parts.at[far, self.top], relays.at[0], above)
        self.far_down = mail.post(parts.at[far, self.low], relays.at[1], below)
        self.up_low = mail.post(parts.at[up, self.low], land.at[0, self.low], above)
        self.down_top = mail.post(parts.at[down, self.top], land.at[1, self.top], below)

    def relay(self):
        here, relays = self.here, self.relays
        up, down = here.level(1), here.level(PLANES - 1)
        self.far_up.wait_recv()
        relays[2] = (relays[0].astype(F32) + self.parts[up, self.top].astype(F32)).astype(BF)
        self.up_top = self.mail.post(relays.at[2], self.land.at[0, self.top], here.above(1))
        self.far_down.wait_recv()
        relays[3] = (relays[1].astype(F32) + self.parts[down, self.low].astype(F32)).astype(BF)
        self.down_low = self.mail.post(relays.at[3], self.land.at[1, self.low], here.above(PLANES - 1))

    def total(self):
        for copy in (self.up_low, self.down_top, self.up_top, self.down_low):
            copy.wait_recv()
        return (
            self.parts[self.here.plane].astype(F32) + self.land[0].astype(F32) + self.land[1].astype(F32)
        )


def scale_row(small_ref, index):
    rows = [small_ref[k, index : index + 1, :] for k in range(PLANES)]
    return jnp.concatenate(rows, axis=1)


def own_channels(small_ref, here, rows, width):
    return small_ref[here.chip, rows, span(here.core, width)]


def whitened(value):
    average = jnp.mean(value, axis=-1, keepdims=True)
    centred = value - average
    inverse = lax.rsqrt(jnp.mean(centred * centred, axis=-1, keepdims=True) + EPSILON)
    return centred * inverse, inverse


def norm_grad(value, gain, gradient):
    white, inverse = whitened(value)
    inner = gradient * gain
    value_grad = inverse * (
        inner
        - jnp.mean(inner, axis=-1, keepdims=True)
        - white * jnp.mean(inner * white, axis=-1, keepdims=True)
    )
    return value_grad, jnp.sum(gradient * white, axis=0, keepdims=True)


def at_row(index, row, height=8):
    place = lax.broadcasted_iota(jnp.int32, (height, row.shape[1]), 0)
    return jnp.where(place == index, row, 0.0)


def sigmoid(value):
    return 1.0 / (1.0 + jnp.exp(-value))


def item_of(position, lengths):
    end, item = 0, jnp.zeros(position.shape, jnp.int32)
    for k in range(lengths.shape[1]):
        end = end + lengths[0, k]
        item = item + (position >= end).astype(jnp.int32)
    return item


def set_marks(marks, lengths):
    taps, (frames, width) = marks.shape[0] - 1, marks.shape[1:]
    position = lax.broadcasted_iota(jnp.int32, (frames, width), 0)
    item = item_of(position, lengths)
    for t in range(taps):
        other = position + (t - taps // 2)
        shared = (item_of(other, lengths) == item) & (other >= 0) & (other < frames)
        marks[t] = shared.astype(F32).astype(BF)
    marks[taps] = (item < lengths.shape[1]).astype(F32).astype(BF)


class Reduce:
    def __init__(self, mail, here, bufs, half):
        self.mail, self.here, self.half, self.copies = mail, here, half, []
        self.stage, self.land, self.acc = bufs

    def put(self, pair, value):
        rows = value.shape[0] // 2
        for k in range(2):
            slot, term = 2 * pair + k, value[k * rows : (k + 1) * rows]
            if slot == 0:
                self.acc[self.half] = term
                continue
            place = self.stage.at[self.half, slot - 1]
            place[...] = term.astype(BF)
            self.copies.append(self.mail.post(place, self.land.at[self.half, slot - 1], self.here.peer(slot)))

    def total(self):
        for copy in self.copies:
            copy.wait_recv()
        self.mail.settle(self.copies)
        value = self.acc[self.half]
        for j in range(1, CHIPS):
            value = value + self.land[self.half, j - 1].astype(F32)
        return value


class RelayReduce(Reduce):
    def __init__(self, mail, here, bufs, half):
        super().__init__(mail, here, bufs, half)
        rows = self.stage.shape[2] // 2
        self.top, self.low = pl.ds(0, rows), pl.ds(rows, rows)
        self.out, self.into, self.passed = self.stage.at[half], self.land.at[half], []

    def send(self, source, target, rows, slot):
        copy = self.mail.post(self.out.at[source, rows], self.into.at[target, rows], self.here.peer(slot))
        self.copies.append(copy)
        return copy

    def put(self, pair, value):
        rows = value.shape[0] // 2
        if pair:
            self.out[2] = value[rows:].astype(BF)
            self.far = (self.send(2, 2, self.top, 1), self.send(2, 2, self.low, 2))
            self.out[1] = value[:rows].astype(BF)
            self.send(1, 1, self.low, 2)
        else:
            self.out[0] = value[rows:].astype(BF)
            self.send(0, 0, self.top, 1)
            self.acc[self.half] = value[:rows]

    def relay(self):
        for copy, slot, rows in ((self.far[0], 1, self.top), (self.far[1], 0, self.low)):
            copy.wait_recv()
            self.copies = [other for other in self.copies if other is not copy]
            self.passed.append(copy)
            value = self.out[slot, rows].astype(F32) + self.into[2, rows].astype(F32)
            self.out[slot, rows] = value.astype(BF)
            self.send(slot, slot, rows, 2 if slot else 1)

    def total(self):
        for copy in self.copies:
            copy.wait_recv()
        self.mail.settle(self.copies + self.passed)
        return self.acc[self.half] + self.into[0].astype(F32) + self.into[1].astype(F32)


def flat(ref, columns=None):
    value = ref[...] if columns is None else ref[:, :, :, columns]
    return value.reshape(-1, value.shape[-1])


def pair_of(ref, half, pair, columns=slice(None)):
    value = ref[half, 2 * pair : 2 * pair + 2, :, columns]
    return value.reshape(-1, value.shape[-1])


def set_pair(ref, half, pair, value, columns=slice(None)):
    ref[half, 2 * pair : 2 * pair + 2, :, columns] = value.reshape(2, -1, value.shape[-1])


def feed_active(hidden, keep, up, half, pair):
    width = up[0].shape[1]
    rows = pair_of(hidden, half, pair)
    for side in range(2):
        set_pair(keep, half, pair, mm(rows, up[side][...]), slice(side * width, (side + 1) * width))


def feed_out(keep, down, half, pair, swish=None):
    width = down[0].shape[0]
    total = None
    for side in range(2):
        columns = slice(side * width, (side + 1) * width)
        active = pair_of(keep, half, pair, columns)
        value = (active * sigmoid(active)).astype(BF)
        if swish is not None:
            set_pair(swish, half, pair, value, columns)
        term = mm(value, down[side][...])
        total = term if total is None else total + term
    return total


def feed_swish(keep, swish, half, pair):
    active = pair_of(keep, half, pair)
    set_pair(swish, half, pair, (active * sigmoid(active)).astype(BF))


def feed_slope(branch, keep, down, active_grad, half, pair):
    width = down[0].shape[0]
    rows = pair_of(branch, half, pair)
    for side in range(2):
        columns = slice(side * width, (side + 1) * width)
        active = pair_of(keep, half, pair, columns)
        gate = sigmoid(active)
        grad = mm_right(rows, down[side][...]) * (gate * (1.0 + active * (1.0 - gate)))
        set_pair(active_grad, half, pair, grad.astype(BF), columns)


def feed_in(active_grad, up, half, pair):
    width = up[0].shape[1]
    total = None
    for side in range(2):
        term = mm_right(pair_of(active_grad, half, pair, slice(side * width, (side + 1) * width)), up[side][...])
        total = term if total is None else total + term
    return total


def pair_product(mail, here, left, right, blocks, send, land, store):
    height = send.shape[0] // blocks
    copies = []
    for i in range(blocks):
        rows = pl.ds(i * height, height)
        send[rows, :] = mm_left(left(1, i), right(1)).astype(BF)
        copies.append(mail.post(send.at[rows], land.at[rows], here.sibling()))
    for i in range(blocks):
        rows = pl.ds(i * height, height)
        grad = mm_left(left(0, i), right(0))
        copies[i].wait_recv()
        store(i, (grad + land[rows, :].astype(F32)).astype(BF))
    return copies


def by_plane(out, first=0):
    def store(i, value):
        height = out.shape[1]
        each = value.shape[0] // height
        for k in range(each):
            out[lax.rem(first + i * each + k, PLANES)] = value[k * height : (k + 1) * height]

    return store


def by_owner(out):
    def store(i, value):
        seqs = 2 * CHIPS
        height = out.shape[1] // seqs
        each = value.shape[0] // (height * PLANES)
        for k in range(each):
            for p in range(PLANES):
                start = (k * PLANES + p) * height
                at = (i * each + k) * height
                out[p, at : at + height, :] = value[start : start + height]

    return store


def down_grad(mail, here, branch, swish, out, send, land):
    half = swish.shape[3] // 2
    block = half // 2
    return pair_product(
        mail, here,
        lambda side, i: flat(swish, slice(side * half + i * block, side * half + (i + 1) * block)),
        lambda side: flat(branch),
        2, send, land, by_plane(out, here.seq),
    )


def up_grad(mail, here, hidden, active_grad, out, send, land):
    half = active_grad.shape[3] // 2
    block = hidden.shape[3] // 4
    return pair_product(
        mail, here,
        lambda side, i: flat(hidden, slice(i * block, (i + 1) * block)),
        lambda side: flat(active_grad, slice(side * half, (side + 1) * half)),
        4, send, land, by_owner(out),
    )


def slots_grad(mail, here, rows, sides, out, send, land):
    block = rows.shape[3] // 4
    return pair_product(
        mail, here,
        lambda side, i: flat(rows, slice(i * block, (i + 1) * block)),
        lambda side: flat(sides.at[side]),
        4, send, land, by_owner(out),
    )


def sides_grad(mail, here, sides, rows, out, send, land):
    return pair_product(
        mail, here, lambda side, i: flat(sides.at[side]), lambda side: flat(rows), 1, send, land, by_plane(out)
    )


def attention_weights(query, keys, slope, row, lengths):
    column = lax.broadcasted_iota(jnp.int32, (8, keys.shape[0]), 1)[:1, :]
    distance = jnp.abs(row.astype(F32) - column.astype(F32))
    scores = mm_right(query, keys) * (1.0 / math.sqrt(query.shape[1])) - slope * distance
    scores = jnp.where(item_of(row, lengths) == item_of(column, lengths), scores, MASKED)
    exponent = jnp.exp(scores - jnp.max(scores, axis=-1, keepdims=True))
    return exponent * (1.0 / jnp.sum(exponent, axis=-1, keepdims=True)), distance


def kernel_refs(names, refs):
    return types.SimpleNamespace(**dict(zip(names, refs, strict=True)))


def forward_kernel(names, *refs):
    r = kernel_refs(names, refs)
    here, mail = Here(), Mail(r.send, r.recv)
    lengths, small, marks = r.lengths, r.small, r.marks
    rows = r.frames.shape[1] // 2
    met = greet(near(here))

    def columns_of(src, turn=0):
        width = 128

        def fill(region):
            groups = region.shape[1] // width
            stride = src.shape[1] // groups
            return [
                mail.local(
                    src.at[:, pl.ds(pl.multiple_of(g * stride + here.turned(turn * g) * width, width), width)],
                    region.at[:, pl.ds(g * width, width)],
                )
                for g in range(groups)
            ]

        return fill

    def rows_of(src):
        return lambda region: [mail.local(src.at[span(here.turned(here.plane), region.shape[0]), :], region)]

    def core_rows_of(src, dst, other):
        return FromPlane(mail, here, src.at[span(here.core, dst.shape[0]), :], dst, other)

    def part(half):
        return pl.ds(half * rows, rows)

    def spread(buf, half, value, gain):
        buf[half, 0] = (whitened(value)[0] * gain).astype(BF)
        return Spread(mail, here, buf, half)

    def reduce(land, kind=Reduce):
        return [kind(mail, here, (r.stage, land, r.acc), h) for h in range(2)]

    own_small = small.at[here.plane]
    gains, taps = r.gains.shape[0], r.taps.shape[0]
    own_small[0:gains, :] = r.gains[...].astype(F32)
    own_small[gains : gains + taps, :] = r.taps[...].astype(F32)
    own_small[gains + taps : gains + taps + 1, :] = r.batch[...].astype(F32)
    up1 = Ring(mail, here, r.up1, r.up1_other, columns_of(r.up1_src, 1))
    down1 = Ring(mail, here, r.down1, r.down1_other, rows_of(r.down1_src))
    met()
    small_copies = [mail.post(own_small, own_small, here.above(k)) for k in range(1, PLANES)]
    up1.send()
    down1.send()

    for copy in small_copies:
        copy.wait_recv()
    gain = scale_row(small, 0)
    sent = [spread(r.hidden0, h, r.frames[0, part(h), :].astype(F32), gain) for h in range(2)]
    set_marks(marks, lengths)
    for h in range(2):
        sent[h].near()
    up1.relay()
    for h in range(2):
        sent[h].far()
    down1.relay()
    qkv = Ring(mail, here, r.qkv, r.qkv_other, columns_of(r.qkv_src)).send()
    out = core_rows_of(r.out_src, r.out, r.out_other)
    up1.finish()
    up1.ready()
    ups, downs = (r.up1, r.up1_other), (r.down1, r.down1_other)
    for h in range(2):
        for p in range(2):
            feed_active(r.hidden0, r.keep0, ups, h, p)
    down1.finish()
    mail.save(r.hidden0, r.hidden0_out)
    mail.save(r.keep0, r.keep0_out)
    mail.save(r.up1, r.up1_out)
    mail.save(r.down1, r.down1_out)
    down1.ready()
    sums = reduce(r.land0, RelayReduce)
    for p in (1, 0):
        for h in range(2):
            sums[h].put(p, feed_out(r.keep0, downs, h, p))
    for h in range(2):
        sums[h].relay()
    qkv.relay()
    conv_in = Ring(mail, here, r.conv_in, r.conv_in_other, columns_of(r.in_src)).send()
    gain = scale_row(small, 1)
    sent = []
    for h in range(2):
        value = r.frames[0, part(h), :].astype(F32) + 0.5 * sums[h].total()
        r.first[part(h), :] = value
        mail.save(r.first.at[part(h)], r.first_out.at[part(h)])
        sent.append(spread(r.hidden1, h, value, gain))
    out.relay()
    conv_out = core_rows_of(r.conv_src, r.conv_out, r.conv_out_other)

    joint, mixed = r.joint, r.mixed
    size = joint.shape[1] // 3
    qkv.finish()
    qkv.ready()
    mail.save(r.qkv, r.qkv_out)
    joint_copies = []

    def to_heads(h, p):
        value = pair_of(r.hidden1, h, p)
        set_pair(r.joint_stage, h, p, mm(value, r.qkv_other[...]).astype(BF))
        for j in (2 * p, 2 * p + 1):
            joint_copies.append(
                mail.post(r.joint_stage.at[h, j], joint.at[here.rows(j, h, rows), :], here.sibling())
            )
        value = mm(value, r.qkv[...]).astype(BF)
        for k in range(2):
            joint[here.rows(2 * p + k, h, rows), :] = value[k * rows : (k + 1) * rows]

    as_they_come(sent, to_heads)
    for copy in joint_copies:
        copy.wait_recv()
    conv_in.relay()
    up2 = Ring(mail, here, r.up2, r.up2_other, columns_of(r.up2_src, 1)).send()
    mail.save(r.hidden1, r.hidden1_out)
    mail.save(joint, r.joint_out)
    slope = r.slopes[here.seq]
    mixed_copies = {}
    sums = reduce(r.land1, RelayReduce)

    def unit(h, j):
        mine, theirs = here.rows(j, h, rows), here.other_rows(j, h, rows)
        query = jnp.concatenate([joint[mine, 0:size], joint[theirs, 0:size]], axis=0)
        index = lax.broadcasted_iota(jnp.int32, (2 * rows, 128), 0)[:, :1]
        frame = jnp.where(index < rows, mine.start + index, theirs.start + index - rows)
        weights = attention_weights(query, joint[:, size : 2 * size], slope, frame, lengths)[0]
        value = mm(weights.astype(BF), joint[:, 2 * size :]).astype(BF)
        mixed[0, h, j] = value[:rows]
        r.mixed_stage[h, j] = value[rows:]
        mixed_copies[h, j] = mail.post(r.mixed_stage.at[h, j], mixed.at[1, h, j], here.sibling())

    def project(h, p):
        for j in (2 * p, 2 * p + 1):
            mixed_copies[h, j].wait_recv()
        value = mm(pair_of(mixed.at[0], h, p), r.out[...]) + mm(pair_of(mixed.at[1], h, p), r.out_other[...])
        sums[h].put(p, value)

    unit(0, 2)
    unit(0, 3)
    out.finish()
    unit(0, 0)
    out.ready()
    project(0, 1)
    unit(0, 1)
    unit(1, 2)
    project(0, 0)
    unit(1, 3)
    unit(1, 0)
    project(1, 1)
    sums[0].relay()
    unit(1, 1)
    project(1, 0)
    sums[1].relay()
    mail.save(r.out, r.out_out)
    mail.save(mixed, r.mixed_out)
    gain = scale_row(small, 2)
    sent = []
    for h in range(2):
        value = r.first[part(h), :] + sums[h].total()
        r.second[part(h), :] = value
        mail.save(r.second.at[part(h)], r.second_out.at[part(h)])
        sent.append(spread(r.hidden2, h, value, gain))
        if h == 0:
            conv_in.finish()
            conv_out.relay()

    gated, padded, glu = r.gated, r.padded, r.glu
    frames, width = gated.shape
    conv_in.ready()
    mail.save(r.conv_in, r.in_out)
    gate_copies = []

    def to_gates(h, p):
        value = pair_of(r.hidden2, h, p)
        for side, weight in ((1, r.conv_in_other), (0, r.conv_in)):
            both = mm(value, weight[...])
            set_pair(glu, h, p, both, slice(2 * width * side, 2 * width * (side + 1)))
            gate = (both[:, :width] * sigmoid(both[:, width:])).astype(BF)
            for k in range(2):
                j = 2 * p + k
                if side:
                    r.gate_stage[h, j] = gate[k * rows : (k + 1) * rows]
                    gate_copies.append(
                        mail.post(r.gate_stage.at[h, j], r.gate_rows.at[here.rows(j, h, rows), :], here.sibling())
                    )
                else:
                    r.gate_rows[here.rows(j, h, rows), :] = gate[k * rows : (k + 1) * rows]

    as_they_come(sent, to_gates)
    mail.save(r.hidden2, r.hidden2_out)
    mail.save(glu, r.glu_out)
    up2.relay()
    for copy in gate_copies:
        copy.wait_recv()
    taps = marks.shape[0] - 1
    padded[0:RIM, :] = jnp.zeros((RIM, width), F32)
    padded[RIM + frames :, :] = jnp.zeros((RIM, width), F32)
    gated[...] = r.gate_rows[...].astype(F32)
    padded[RIM : RIM + frames, :] = gated[...]
    mail.save(gated, r.gated_out)
    kernel = own_channels(small, here, slice(5, 5 + taps), width)
    conv = None
    for t in range(taps):
        first = RIM - taps // 2 + t
        term = kernel[t : t + 1, :] * padded[first : first + frames, :] * marks[t].astype(F32)
        conv = term if conv is None else conv + term
    valid = marks[taps].astype(F32)
    count = jnp.sum(valid, axis=0, keepdims=True)
    total = jnp.sum(valid * conv, axis=0, keepdims=True)
    centred = conv - total / count
    squares = jnp.sum(valid * centred * centred, axis=0, keepdims=True)
    bn, bn_land = r.bn, r.bn_land
    bn[...] = at_row(0, total) + at_row(1, squares) + at_row(2, count)
    bn_copies = [mail.post(bn, bn_land.at[k - 1], here.above(k)) for k in range(1, PLANES)]
    down2 = Ring(mail, here, r.down2, r.down2_other, rows_of(r.down2_src)).send()
    r.standard[...] = conv
    conv_out.finish()
    for copy in bn_copies:
        copy.wait_recv()
    terms = [bn[...]] + [bn_land[k - 1] for k in range(1, PLANES)]
    whole = sum(term[2:3, :] for term in terms)
    average = sum(term[0:1, :] for term in terms) / whole
    variance = 0.0
    for term in terms:
        apart = term[0:1, :] / term[2:3, :] - average
        variance = variance + term[1:2, :] + term[2:3, :] * apart * apart
    inverse = lax.rsqrt(variance / whole + EPSILON)
    r.stats[...] = at_row(0, inverse) + at_row(1, whole)
    standard = (r.standard[...] - average) * inverse
    r.standard[...] = standard
    scaled = standard * own_channels(small, here, slice(10, 11), width)
    r.swish_rows[...] = (scaled * sigmoid(scaled)).astype(BF)
    swish = r.swish
    swish_copies = {}
    for h in range(2):
        for j in (2, 3, 0, 1):
            swish_copies[h, j] = mail.post(
                r.swish_rows.at[here.other_rows(j, h, rows), :], swish.at[1, h, j], here.sibling()
            )
            swish[0, h, j] = r.swish_rows[here.rows(j, h, rows), :]
    mail.save(r.standard, r.standard_out)
    conv_out.ready()
    mail.save(r.conv_out, r.conv_out_out)
    sums = reduce(r.land2, RelayReduce)
    for p in (1, 0):
        for h in range(2):
            for j in (2 * p, 2 * p + 1):
                swish_copies[h, j].wait_recv()
            value = mm(pair_of(swish.at[0], h, p), r.conv_out[...])
            sums[h].put(p, value + mm(pair_of(swish.at[1], h, p), r.conv_out_other[...]))
    for h in range(2):
        sums[h].relay()
    mail.save(swish, r.swish_out)
    up2.finish()
    gain = scale_row(small, 3)
    sent = []
    for h in range(2):
        value = r.second[part(h), :] + sums[h].total()
        r.third[part(h), :] = value
        sent.append(spread(r.hidden3, h, value, gain))
        if h == 0:
            down2.relay()

    up2.ready()
    ups, downs = (r.up2, r.up2_other), (r.down2, r.down2_other)
    sums = reduce(r.land3, RelayReduce)
    sent[0].near()
    feed_active(r.hidden3, r.keep3, ups, 0, 0)
    sent[1].near()
    sent[0].far()
    feed_active(r.hidden3, r.keep3, ups, 0, 1)
    down2.finish()
    down2.ready()
    for p in (1, 0):
        sums[0].put(p, feed_out(r.keep3, downs, 0, p, r.act))
    sent[1].far()
    feed_active(r.hidden3, r.keep3, ups, 1, 1)
    sums[1].put(1, feed_out(r.keep3, downs, 1, 1, r.act))
    sums[0].relay()
    feed_active(r.hidden3, r.keep3, ups, 1, 0)
    sums[1].put(0, feed_out(r.keep3, downs, 1, 0, r.act))

    last_gain = scale_row(small, 4)
    sent, last_parts = [], []
    for h in range(2):
        fourth = r.third[part(h), :] + 0.5 * sums[h].total()
        if h == 0:
            sums[1].relay()
        r.result[0, part(h), :] = (whitened(fourth)[0] * last_gain).astype(BF)
        mail.save(r.result.at[0, part(h)], r.result_out.at[0, part(h)])
        gradient, last_part = norm_grad(fourth, last_gain, r.out_grad[0, part(h), :].astype(F32))
        last_parts.append(last_part)
        r.branch[h, 0] = (0.5 * gradient).astype(BF)
        sent.append(Spread(mail, here, r.branch, h))
        r.third_grad[part(h), :] = gradient
    sums = reduce(r.land4)

    def back(h, p):
        feed_slope(r.branch, r.keep3, downs, r.act_grad, h, p)
        sums[h].put(p, feed_in(r.act_grad, ups, h, p))

    as_they_come(sent, back)
    down_grad(mail, here, r.branch, r.act, r.down2_parts, r.down_send, r.down_land)
    mail.save(r.down2_parts, r.down2_parts_out)
    up_grad(mail, here, r.hidden3, r.act_grad, r.up2_parts, r.up_send, r.up_land)
    mail.save(r.up2_parts, r.up2_parts_out)
    gain_parts = []
    for h in range(2):
        value_part, gain_part = norm_grad(r.third[part(h), :], gain, sums[h].total())
        r.third_grad[part(h), :] = r.third_grad[part(h), :] + value_part
        mail.save(r.third_grad.at[part(h)], r.third_grad_out.at[part(h)])
        gain_parts.append(gain_part)
    r.small_d[...] = at_row(3, gain_parts[0] + gain_parts[1]) + at_row(4, last_parts[0] + last_parts[1])
    mail.close()


def backward_kernel(names, *refs):
    r = kernel_refs(names, refs)
    here, mail = Here(), Mail(r.send, r.recv)
    lengths, small, marks = r.lengths, r.small, r.marks
    rows = r.frames.shape[1] // 2
    seqs = 2 * CHIPS
    group = lax.rem(here.plane + seqs - here.seq, PLANES)
    target = 2 * group + lax.div(here.turned(group), PLANES)
    apart = target != here.seq
    group = lax.div(here.seq, 2)
    source = lax.rem(here.core * PLANES + here.plane + seqs - group, seqs)
    crosses = [here.cross(j) for j in range(1, CHIPS)]
    met = greet(near(here) + crosses, (apart, (source, here.plane)))

    def to_owner(index):
        src, dst = r.down_moved.at[index], r.down_got.at[index]
        i = mail.slot()
        stay = pltpu.make_async_copy(src, dst, mail.send.at[mail.slot()])
        go = mail.remote(src, dst, (target, here.plane), i, i)

        @pl.when(apart)
        def _():
            go.start()

        @pl.when(jnp.logical_not(apart))
        def _():
            stay.start()

        def wait():
            @pl.when(apart)
            def _():
                go.wait()

            @pl.when(jnp.logical_not(apart))
            def _():
                stay.wait()

        return wait

    def share(own, other):
        return mail.post(own, other, here.sibling())

    def part(half):
        return pl.ds(half * rows, rows)

    def spread(buf, half, value):
        buf[half, 0] = value.astype(BF)
        return Spread(mail, here, buf, half)

    def reduce(land, kind=Reduce):
        return [kind(mail, here, (r.stage, land, r.acc), h) for h in range(2)]

    third_ready = mail.local(r.third_grad_src, r.third_grad)
    down2_ready = mail.local(r.down2_parts_src, r.down2_parts)
    set_marks(marks, lengths)
    third_ready.wait()
    met()
    conv_out_shared = share(r.conv_out_src, r.conv_out_other)
    sent = [spread(r.branch2, h, r.third_grad[part(h), :]) for h in range(2)]
    conv_out_ready = mail.local(r.conv_out_src, r.conv_out)
    standard_ready = mail.local(r.standard_src, r.standard)
    swish_ready = mail.local(r.swish_src, r.swish)
    conv_in_shared = share(r.conv_in_src, r.conv_in_other)
    conv_in_ready = mail.local(r.conv_in_src, r.conv_in)
    glu_ready = mail.local(r.glu_src, r.glu)
    hidden2_ready = mail.local(r.hidden2_src, r.hidden2)
    gated_ready = mail.local(r.gated_src, r.gated)
    up2_ready = mail.local(r.up2_parts_src, r.up2_parts)
    second_ready = mail.local(r.second_src, r.second)
    down2_ready.wait()
    down2 = RingSum(mail, here, r.down2_parts, r.down2_relay, r.down2_land)

    frames, width = r.gated.shape
    conv_out_shared.wait_recv()
    conv_out_ready.wait()
    copies = []

    def to_channels(h, p):
        incoming = pair_of(r.branch2, h, p)
        set_pair(r.swish_stage, h, p, mm_right(incoming, r.conv_out_other[...]))
        for j in (2 * p, 2 * p + 1):
            copies.append(
                mail.post(r.swish_stage.at[h, j], r.swish_grad.at[here.rows(j, h, rows), :], here.sibling())
            )
        value = mm_right(incoming, r.conv_out[...])
        for k in range(2):
            r.swish_grad[here.rows(2 * p + k, h, rows), :] = value[k * rows : (k + 1) * rows]

    as_they_come(sent, to_channels)
    standard_ready.wait()
    gain = own_channels(small, here, slice(10, 11), width)
    for copy in copies:
        copy.wait_recv()
    white = r.standard[...]
    scaled = white * gain
    gate = sigmoid(scaled)
    scaled_grad = r.swish_grad[...] * (gate * (1.0 + scaled * (1.0 - gate)))
    bn, bn_land = r.bn, r.bn_land
    bn[...] = at_row(0, jnp.sum(scaled_grad, axis=0, keepdims=True)) + at_row(
        1, jnp.sum(scaled_grad * white, axis=0, keepdims=True)
    )
    bn_copies = [mail.post(bn, bn_land.at[k - 1], here.above(k)) for k in range(1, PLANES)]
    r.swish_grad[...] = scaled_grad * gain
    swish_ready.wait()
    row_send, column_send = r.down_send, r.up_send
    row_copies = sides_grad(
        mail, here, r.swish, r.branch2, r.conv_parts, row_send.at[pl.ds(0, width), :], r.conv_land
    )
    for copy in bn_copies:
        copy.wait_recv()
    down2.relay()
    up2_ready.wait()
    up2 = RingSum(mail, here, r.up2_parts, r.up2_relay, r.up2_land)
    both = bn[...]
    for k in range(1, PLANES):
        both = both + bn_land[k - 1]
    r.cross[...] = both
    inverse, whole = r.stats[0:1, :], r.stats[1:2, :]
    taps = marks.shape[0] - 1
    white = r.standard[...]
    conv_grad = inverse * r.swish_grad[...] - marks[taps].astype(F32) * (
        (inverse / whole) * (gain * both[0:1, :] + white * (gain * both[1:2, :]))
    )
    padded, reach = r.padded, taps // 2
    padded[0:RIM, :] = jnp.zeros((RIM, width), F32)
    padded[RIM + frames :, :] = jnp.zeros((RIM, width), F32)
    padded[RIM : RIM + frames, :] = conv_grad
    kernel = own_channels(small, here, slice(5, 5 + taps), width)
    total = None
    for t in range(taps):
        first = RIM + reach - t
        term = kernel[t : t + 1, :] * padded[first : first + frames, :] * marks[taps - 1 - t].astype(F32)
        total = term if total is None else total + term
    r.gate_grad[...] = total
    moved = r.moved2
    copies = {}
    for h in range(2):
        for j in (2, 3, 0, 1):
            copies[h, j] = mail.post(
                r.gate_grad.at[here.other_rows(j, h, rows), :], moved.at[1, h, j], here.sibling()
            )
            moved[0, h, j] = r.gate_grad[here.rows(j, h, rows), :]
    glu_ready.wait()
    conv_in_ready.wait()
    conv_in_shared.wait_recv()
    glu, glu_grad = r.glu, r.glu_grad
    sums = reduce(r.land2, RelayReduce)
    for p in (1, 0):
        for h in range(2):
            for j in (2 * p, 2 * p + 1):
                copies[h, j].wait_recv()
            result = None
            for side, weight in ((0, r.conv_in), (1, r.conv_in_other)):
                start = 2 * width * side
                left = pair_of(glu, h, p, slice(start, start + width))
                gate = sigmoid(pair_of(glu, h, p, slice(start + width, start + 2 * width)))
                incoming = pair_of(moved.at[side], h, p)
                set_pair(glu_grad.at[side], h, p, (incoming * gate).astype(BF), slice(0, width))
                set_pair(
                    glu_grad.at[side], h, p, (incoming * left * (gate * (1.0 - gate))).astype(BF),
                    slice(width, 2 * width),
                )
                term = mm_right(pair_of(glu_grad.at[side], h, p), weight[...])
                result = term if result is None else result + term
            sums[h].put(p, result)
    for h in range(2):
        sums[h].relay()
    out_shared, qkv_shared = share(r.out_src, r.out_other), share(r.qkv_src, r.qkv_other)
    out_ready = mail.local(r.out_src, r.out)
    joint_ready = mail.local(r.joint_src, r.joint)
    qkv_ready = mail.local(r.qkv_src, r.qkv)
    mixed_ready = mail.local(r.mixed_src, r.mixed)
    hidden1_ready = mail.local(r.hidden1_src, r.hidden1)
    first_ready = mail.local(r.first_src, r.first)
    hidden2_ready.wait()
    column_copies = slots_grad(
        mail, here, r.hidden2, glu_grad, r.in_parts, column_send.at[:, pl.ds(0, 2 * width)], r.in_land
    )
    gain = scale_row(small, 2)
    second_ready.wait()
    sent, gain_parts = [], []
    for h in range(2):
        value_part, gain_part = norm_grad(r.second[part(h), :], gain, sums[h].total())
        gradient = r.third_grad[part(h), :] + value_part
        r.grad[part(h), :] = gradient
        gain_parts.append(gain_part)
        sent.append(spread(r.branch1, h, gradient))
        if h == 0:
            gated_ready.wait()
            dense = padded[RIM : RIM + frames, :]
            padded[RIM : RIM + frames, :] = r.gated[...]
            kernel_rows = jnp.zeros((8, width), F32)
            for t in range(taps):
                first = RIM - reach + t
                row = jnp.sum(
                    padded[first : first + frames, :] * marks[t].astype(F32) * dense, axis=0, keepdims=True
                )
                kernel_rows = kernel_rows + at_row(t, row)
            r.kernel_part[...] = kernel_rows
    r.small_sum[...] = r.small_d[...] + at_row(2, gain_parts[0] + gain_parts[1])
    up2.relay()
    r.down_moved[0] = down2.total().astype(BF)
    down2_wait = to_owner(0)
    conv_sum = RingSum(mail, here, r.conv_parts, r.conv_relay, r.conv_sum_land)
    in_sum = RingSum(mail, here, r.in_parts, r.in_relay, r.in_sum_land)
    kernel_copies = [
        mail.post(r.kernel_part, r.kernel_land.at[k - 1], here.above(k)) for k in range(1, PLANES)
    ]

    out_shared.wait_recv()
    out_ready.wait()
    joint = r.joint
    size = joint.shape[1] // 3
    mixed_copies = []

    def to_heads(h, p):
        incoming = pair_of(r.branch1, h, p)
        set_pair(r.mixed_stage, h, p, mm_right(incoming, r.out_other[...]).astype(BF))
        for j in (2 * p, 2 * p + 1):
            mixed_copies.append(
                mail.post(r.mixed_stage.at[h, j], r.mixed_grad.at[here.rows(j, h, rows), :], here.sibling())
            )
        value = mm_right(incoming, r.out[...]).astype(BF)
        for k in range(2):
            r.mixed_grad[here.rows(2 * p + k, h, rows), :] = value[k * rows : (k + 1) * rows]

    as_they_come(sent, to_heads)
    mixed_ready.wait()
    mail.settle(row_copies)
    row_copies = sides_grad(
        mail, here, r.mixed, r.branch1, r.out_parts, row_send.at[pl.ds(0, size), :], r.out_land
    )
    joint_ready.wait()
    for copy in mixed_copies:
        copy.wait_recv()
    key_grad, value_grad, joint_grad = r.standard, r.gated, r.joint_grad
    key_grad[...] = jnp.zeros_like(key_grad)
    value_grad[...] = jnp.zeros_like(value_grad)
    scale = 1.0 / math.sqrt(size)
    slope = r.slopes[here.seq]
    height = 4 * rows

    def step(index, carry):
        start = pl.multiple_of(index * height, height)
        block_rows = pl.ds(start, height)
        query, keys, values = joint[block_rows, 0:size], joint[:, size : 2 * size], joint[:, 2 * size :]
        frame = lax.broadcasted_iota(jnp.int32, (height, 128), 0)[:, :1] + start
        weights, distance = attention_weights(query, keys, slope, frame, lengths)
        incoming = r.mixed_grad[block_rows, :]
        weight_grad = mm_right(incoming, values)
        delta = jnp.sum(weights * weight_grad, axis=-1, keepdims=True)
        score_grad = weights * (weight_grad - delta)
        raw = (score_grad * scale).astype(BF)
        joint_grad[block_rows, 0:size] = mm(raw, keys).astype(BF)
        key_grad[...] += mm_left(raw, query)
        value_grad[...] += mm_left(weights.astype(BF), incoming)
        return carry - jnp.sum(score_grad * distance, axis=0, keepdims=True)

    slope_row = lax.fori_loop(0, frames // height, step, jnp.zeros((1, frames), F32))
    joint_grad[:, size : 2 * size] = key_grad[...].astype(BF)
    joint_grad[:, 2 * size :] = value_grad[...].astype(BF)
    moved = r.moved1
    copies = {}
    for h in range(2):
        for j in (2, 3, 0, 1):
            copies[h, j] = mail.post(
                joint_grad.at[here.other_rows(j, h, rows), :], moved.at[1, h, j], here.sibling()
            )
            moved[0, h, j] = joint_grad[here.rows(j, h, rows), :]
    conv_sum.relay()
    in_sum.relay()
    out_sum = RingSum(mail, here, r.out_parts, r.out_relay, r.out_sum_land)
    qkv_shared.wait_recv()
    qkv_ready.wait()
    down_shared, up_shared = share(r.down1_src, r.down1_other), share(r.up1_src, r.up1_other)
    keep0_ready = mail.local(r.keep0_src, r.keep0)
    down1_ready = mail.local(r.down1_src, r.down1)
    up1_ready = mail.local(r.up1_src, r.up1)
    hidden0_ready = mail.local(r.hidden0_src, r.hidden0)
    sums = reduce(r.land1, RelayReduce)
    for p in (1, 0):
        for h in range(2):
            for j in (2 * p, 2 * p + 1):
                copies[h, j].wait_recv()
            value = mm_right(pair_of(moved.at[0], h, p), r.qkv[...])
            sums[h].put(p, value + mm_right(pair_of(moved.at[1], h, p), r.qkv_other[...]))
    for h in range(2):
        sums[h].relay()
    hidden1_ready.wait()
    mail.settle(column_copies)
    column_copies = slots_grad(
        mail, here, r.hidden1, moved, r.qkv_parts, column_send.at[:, pl.ds(0, 3 * size)], r.qkv_land
    )
    qkv_sum = RingSum(mail, here, r.qkv_parts, r.qkv_relay, r.qkv_sum_land)
    first_ready.wait()
    gain = scale_row(small, 1)
    sent, gain_parts = [], []
    for h in range(2):
        value_part, gain_part = norm_grad(r.first[part(h), :], gain, sums[h].total())
        gradient = r.grad[part(h), :] + value_part
        r.grad[part(h), :] = gradient
        gain_parts.append(gain_part)
        sent.append(spread(r.branch0, h, 0.5 * gradient))
    gain_part = gain_parts[0] + gain_parts[1]
    lane = lax.broadcasted_iota(jnp.int32, gain_part.shape, 1)
    slope_total = jnp.sum(slope_row, axis=1, keepdims=True)
    r.small_sum[...] = (
        r.small_sum[...] + at_row(1, gain_part) + at_row(5, jnp.where(lane == here.seq, slope_total, 0.0))
    )
    out_sum.relay()
    qkv_sum.relay()

    devices = [here.peer(j) for j in range(1, CHIPS)] + [here.cross(j) for j in range(CHIPS)]
    blocks = r.up2_out.shape[0]

    def swap(parts, got):
        return [mail.post(parts.at[span(device[0], blocks), :], got.at[i], device) for i, device in enumerate(devices)]

    def place(parts, got, out, copies, turn=0):
        lanes = 128
        groups = parts.shape[1] // lanes
        stride = out.shape[1] // groups
        for i in range(len(devices) + 1):
            if i:
                copies[i - 1].wait_recv()
            seq = devices[i - 1][0] if i else here.seq
            value = (got[i - 1] if i else parts[span(here.seq, blocks), :]).astype(F32)
            for g in range(groups):
                at = pl.ds(pl.multiple_of(g * stride + lax.rem(seq + turn * g, seqs) * lanes, lanes), lanes)
                out[:, at] = value[:, g * lanes : (g + 1) * lanes]

    down_shared.wait_recv()
    down1_ready.wait()
    keep0_ready.wait()
    ups, downs = (r.up1, r.up1_other), (r.down1, r.down1_other)
    act, act_grad = r.hidden2, r.hidden1
    for h in range(2):
        for p in range(2):
            feed_swish(r.keep0, act, h, p)
    sent[0].near()
    feed_slope(r.branch0, r.keep0, downs, act_grad, 0, 0)
    sent[1].near()
    sent[0].far()
    feed_slope(r.branch0, r.keep0, downs, act_grad, 0, 1)
    sent[1].far()
    mail.settle(row_copies + column_copies)
    down_grad(mail, here, r.branch0, act, r.down1_parts, r.down_send, r.down_land)
    down1 = RingSum(mail, here, r.down1_parts, r.down1_relay, r.down1_land)
    for p in (1, 0):
        feed_slope(r.branch0, r.keep0, downs, act_grad, 1, p)
    hidden0_ready.wait()
    up_grad(mail, here, r.hidden0, act_grad, r.up1_parts, r.up_send, r.up_land)
    up1 = RingSum(mail, here, r.up1_parts, r.up1_relay, r.up1_land)
    up_shared.wait_recv()
    up1_ready.wait()
    sums = reduce(r.land0)
    for h in range(2):
        for p in (1, 0):
            sums[h].put(p, feed_in(act_grad, ups, h, p))
    r.up2_sum[...] = up2.total().astype(BF)
    up2_copies = swap(r.up2_sum, r.up2_got)
    r.in_total[...] = in_sum.total().astype(BF)
    in_copies = swap(r.in_total, r.in_got)
    r.qkv_total[...] = qkv_sum.total().astype(BF)
    qkv_copies = swap(r.qkv_total, r.qkv_got)
    down1.relay()
    r.conv_out_grad[...] = conv_sum.total()
    mail.save(r.conv_out_grad, r.conv_grad_out)
    r.out_grad[...] = out_sum.total()
    mail.save(r.out_grad, r.attn_grad_out)
    for copy in kernel_copies:
        copy.wait_recv()
    kernel_total = r.kernel_part[...]
    for k in range(1, PLANES):
        kernel_total = kernel_total + r.kernel_land[k - 1]
    r.kernel_out[...] = kernel_total
    place(r.up2_sum, r.up2_got, r.up2_out, up2_copies, 1)
    mail.save(r.up2_out, r.up2_grad_out)
    up1.relay()
    gain = scale_row(small, 0)
    gain_parts = []
    for h in range(2):
        value_part, gain_part = norm_grad(r.frames[0, part(h), :].astype(F32), gain, sums[h].total())
        r.frames_grad[0, part(h), :] = r.grad[part(h), :] + value_part
        mail.save(r.frames_grad.at[0, part(h)], r.frames_grad_out.at[0, part(h)])
        gain_parts.append(gain_part)
    r.small_sum[...] = r.small_sum[...] + at_row(0, gain_parts[0] + gain_parts[1])
    small_copies = [
        mail.post(r.small_sum, r.small_land.at[k - 1], here.above(k)) for k in range(1, PLANES)
    ]
    r.down_moved[1] = down1.total().astype(BF)
    down1_wait = to_owner(1)
    place(r.in_total, r.in_got, r.in_out, in_copies)
    mail.save(r.in_out, r.in_grad_out)
    place(r.qkv_total, r.qkv_got, r.qkv_out, qkv_copies)
    mail.save(r.qkv_out, r.qkv_grad_out)
    down2_wait()
    r.down2_out[...] = r.down_got[0].astype(F32)
    mail.save(r.down2_out, r.down2_grad_out)
    r.up1_sum[...] = up1.total().astype(BF)
    up1_copies = swap(r.up1_sum, r.up1_got)
    for copy in small_copies:
        copy.wait_recv()
    total = r.small_sum[...]
    for k in range(1, PLANES):
        total = total + r.small_land[k - 1]
    r.small_mid[...] = total
    small_copies = [mail.post(r.small_mid, r.small_near.at[i], device) for i, device in enumerate(devices)]
    down1_wait()
    r.down1_out[...] = r.down_got[1].astype(F32)
    mail.save(r.down1_out, r.down1_grad_out)
    place(r.up1_sum, r.up1_got, r.up1_out, up1_copies, 1)
    mail.save(r.up1_out, r.up1_grad_out)
    for copy in small_copies:
        copy.wait_recv()
    total = r.small_mid[...]
    for i in range(len(devices)):
        total = total + r.small_near[i]
    r.small_out[...] = total
    mail.close()


def finish_kernel(*refs):
    count = (len(refs) - 7) // 2
    big, (small, kernel, cross) = refs[:count], refs[count : count + 3]
    outs, (gains_out, kernel_out, batch_out, slopes_out) = refs[count + 3 : 2 * count + 3], refs[2 * count + 3 :]
    for src, dst in zip(big, outs):
        dst[...] = src[...]
    seq, plane = lax.axis_index("seq"), lax.axis_index("fsdp")

    def own(ref, first, count, width, place):
        lanes = 128
        each = lanes // width
        block = ref[first : first + count, span(lax.div(place, each), lanes)]
        value = block[:, :width]
        for k in range(1, each):
            value = jnp.where(lax.rem(place, each) == k, block[:, k * width : (k + 1) * width], value)
        return value

    width = gains_out.shape[1]
    gains = gains_out.shape[0]
    gains_out[...] = own(small, 0, gains, width, seq * PLANES + plane)
    kernel_out[...] = own(kernel, 0, kernel_out.shape[0], width, plane)
    batch_out[...] = own(cross, 1, 1, width, plane)
    slopes_out[...] = small[gains : gains + 1, : slopes_out.shape[1]]


def launch(kernel, name, index, operands, results, scratch):
    names = list(operands) + list(results) + list(scratch) + ["send", "recv"]
    values = pl.pallas_call(
        functools.partial(kernel, names),
        name=name,
        out_shape=[jax.ShapeDtypeStruct(shape, kind) for shape, kind, _ in results.values()],
        in_specs=[pl.BlockSpec(memory_space=place) for _, place in operands.values()],
        out_specs=[pl.BlockSpec(memory_space=place) for _, _, place in results.values()],
        scratch_shapes=[pltpu.VMEM(shape, kind) for shape, kind in scratch.values()]
        + [pltpu.SemaphoreType.DMA((SLOTS,)), pltpu.SemaphoreType.DMA((SLOTS,))],
        compiler_params=pltpu.CompilerParams(
            collective_id=index, has_side_effects=True, vmem_limit_bytes=GRANT
        ),
    )(*[array for array, _ in operands.values()])
    return types.SimpleNamespace(**dict(zip(results, values)))


def plane_body(
    frames, lengths, up_first, down_first, joint_qkv, attn_out, conv_in, conv_kernel, batch_gain, conv_out,
    up_second, down_second, norm_gains, slopes, out_grad,
):
    seqs = lax.axis_size("seq")
    seq = lax.axis_index("seq")
    plane = lax.axis_index("fsdp")
    rows, width = frames.shape[1], frames.shape[2]
    length = rows * seqs
    heads = slopes.shape[0]
    size = width // heads
    channels = width // seqs
    hidden_units = up_first.shape[1]
    half = hidden_units // seqs
    taps = conv_kernel.shape[0]
    block = width // (seqs * PLANES)
    near_count = seqs - 1
    row_f = ((rows, width), F32)
    lines = rows // 2
    quad = ((2, CHIPS, lines, width), BF)
    stage = ((2, CHIPS - 1, lines, width), BF)
    acc = ((2, lines, width), F32)
    up, down = ((width, half), BF), ((half, width), BF)
    qkv, out = ((width, 3 * size), BF), ((size, width), BF)
    conv_i, conv_o = ((width, 2 * channels), BF), ((channels, width), BF)
    keep = ((2, CHIPS, lines, 2 * half), F32)
    act = ((2, CHIPS, lines, 2 * half), BF)
    joint = ((length, 3 * size), BF)
    mixed = ((2, 2, CHIPS, lines, size), BF)
    glu = ((2, CHIPS, lines, 4 * channels), F32)
    dense = ((length, channels), F32)
    padded = ((length + 2 * RIM, channels), F32)
    marks = ((taps + 1, length, channels), BF)
    bn = ((8, channels), F32)
    bn_land = ((PLANES - 1, 8, channels), F32)
    small_row = ((8, width), F32)
    small_all = ((PLANES, 16, norm_gains.shape[1]), F32)

    def parts(shape):
        return ((PLANES, shape[0][0] // PLANES, shape[0][1]), BF)

    def land(shape):
        return ((2, shape[0][0] // PLANES, shape[0][1]), BF)

    def relay(shape):
        return ((4, shape[0][0] // (2 * PLANES), shape[0][1]), BF)

    def summed(shape):
        return ((shape[0][0] // PLANES, shape[0][1]), BF)

    x_grad, up_rows, down_rows = ((1, rows, width), F32), ((block, hidden_units), F32), ((half // PLANES, width), F32)
    qkv_rows, in_rows, head_rows = ((block, 3 * width), F32), ((block, 2 * width), F32), ((size // PLANES, width), F32)
    a = launch(
        forward_kernel, "forward", 0,
        dict(
            frames=(frames, V), lengths=(lengths, S), gains=(norm_gains, V), taps=(conv_kernel, V),
            batch=(batch_gain.reshape(1, -1), V), slopes=(slopes, S),
            up1_src=(up_first, H), down1_src=(down_first, H), qkv_src=(joint_qkv, H),
            out_src=(attn_out, H), in_src=(conv_in, H), conv_src=(conv_out, H),
            up2_src=(up_second, H), down2_src=(down_second, H), out_grad=(out_grad, V),
        ),
        dict(
            result_out=((1, rows, width), BF, H), third_grad_out=row_f + (H,), small_d=small_row + (V,),
            first_out=row_f + (H,), second_out=row_f + (H,), small=small_all + (V,),
            stats=bn + (V,), up2_parts_out=parts(up) + (H,), down2_parts_out=parts(down) + (H,),
            hidden0_out=quad + (H,), hidden1_out=quad + (H,), hidden2_out=quad + (H,),
            keep0_out=keep + (H,), joint_out=joint + (H,), mixed_out=mixed + (H,),
            glu_out=glu + (H,), gated_out=dense + (H,), standard_out=dense + (H,),
            swish_out=mixed + (H,), up1_out=up + (H,), down1_out=down + (H,), qkv_out=qkv + (H,),
            out_out=out + (H,), in_out=conv_i + (H,), conv_out_out=conv_o + (H,),
        ),
        dict(
            up1=up, up1_other=up, down1=down, down1_other=down, qkv=qkv, qkv_other=qkv,
            out=out, out_other=out, conv_in=conv_i, conv_in_other=conv_i, conv_out=conv_o,
            conv_out_other=conv_o, up2=up, up2_other=up, down2=down, down2_other=down,
            hidden0=quad, hidden1=quad, hidden2=quad, hidden3=quad, keep0=keep, keep3=keep,
            joint=joint, joint_stage=((2, CHIPS, lines, 3 * size), BF), mixed=mixed,
            mixed_stage=((2, CHIPS, lines, size), BF), glu=glu, gated=dense, padded=padded,
            marks=marks, gate_stage=((2, CHIPS, lines, channels), BF), gate_rows=((length, channels), BF),
            standard=dense, swish_rows=((length, channels), BF), swish=mixed, bn=bn, bn_land=bn_land,
            third=row_f, branch=quad, act=act, act_grad=act, result=((1, rows, width), BF), third_grad=row_f,
            first=row_f, second=row_f, up2_parts=parts(up), down2_parts=parts(down),
            stage=stage, land0=stage, land1=stage, land2=stage, land3=stage, land4=stage, acc=acc,
            down_send=down, down_land=down, up_send=up, up_land=up,
        ),
    )
    b = launch(
        backward_kernel, "backward", 1,
        dict(
            frames=(frames, V), lengths=(lengths, S), slopes=(slopes, S), small=(a.small, V),
            third_grad_src=(a.third_grad_out, H), small_d=(a.small_d, V), second_src=(a.second_out, H),
            stats=(a.stats, V), up2_parts_src=(a.up2_parts_out, H), down2_parts_src=(a.down2_parts_out, H),
            first_src=(a.first_out, H), hidden0_src=(a.hidden0_out, H),
            hidden1_src=(a.hidden1_out, H), hidden2_src=(a.hidden2_out, H),
            keep0_src=(a.keep0_out, H), joint_src=(a.joint_out, H), mixed_src=(a.mixed_out, H),
            glu_src=(a.glu_out, H), gated_src=(a.gated_out, H),
            standard_src=(a.standard_out, H), swish_src=(a.swish_out, H),
            up1_src=(a.up1_out, H), down1_src=(a.down1_out, H), qkv_src=(a.qkv_out, H),
            out_src=(a.out_out, H), conv_in_src=(a.in_out, H),
            conv_out_src=(a.conv_out_out, H),
        ),
        dict(
            frames_grad_out=x_grad + (H,), up1_grad_out=up_rows + (H,), up2_grad_out=up_rows + (H,),
            down1_grad_out=down_rows + (H,), down2_grad_out=down_rows + (H,), qkv_grad_out=qkv_rows + (H,),
            in_grad_out=in_rows + (H,), attn_grad_out=head_rows + (H,), conv_grad_out=head_rows + (H,),
            kernel_out=bn + (V,), cross=bn + (V,), small_out=small_row + (V,),
        ),
        dict(
            up1=up, up1_other=up, down1=down, down1_other=down, qkv=qkv, qkv_other=qkv,
            out=out, out_other=out, conv_in=conv_i, conv_in_other=conv_i, conv_out=conv_o,
            conv_out_other=conv_o, hidden0=quad, hidden1=quad, hidden2=quad, keep0=keep,
            joint=joint, mixed=mixed, glu=glu, gated=dense, standard=dense, swish=mixed,
            first=row_f, grad=row_f, acc=acc, third_grad=row_f, second=row_f, up2_parts=parts(up),
            down2_parts=parts(down), frames_grad=x_grad, up1_out=up_rows, up2_out=up_rows, down1_out=down_rows,
            down2_out=down_rows, qkv_out=qkv_rows, in_out=in_rows, out_grad=head_rows, conv_out_grad=head_rows, marks=marks, padded=padded,
            branch2=quad, branch1=quad, branch0=quad, swish_stage=((2, CHIPS, lines, channels), F32),
            swish_grad=dense, gate_grad=dense, moved2=((2, 2, CHIPS, lines, channels), F32),
            glu_grad=((2, 2, CHIPS, lines, 2 * channels), BF), bn=bn, bn_land=bn_land,
            conv_land=conv_o, in_land=conv_i,
            conv_parts=parts(conv_o), in_parts=parts(conv_i), conv_relay=relay(conv_o),
            in_relay=relay(conv_i), conv_sum_land=land(conv_o), in_sum_land=land(conv_i),
            kernel_part=bn, kernel_land=bn_land, small_sum=small_row,
            up2_relay=relay(up), up2_land=land(up), down2_relay=relay(down), down2_land=land(down),
            up2_sum=summed(up), down_moved=((2,) + summed(down)[0], BF), down_got=((2,) + summed(down)[0], BF),
            mixed_stage=((2, CHIPS, lines, size), BF), mixed_grad=((length, size), BF),
            joint_grad=joint, moved1=((2, 2, CHIPS, lines, 3 * size), BF), out_land=out, qkv_land=qkv, out_parts=parts(out), qkv_parts=parts(qkv), out_relay=relay(out),
            qkv_relay=relay(qkv), out_sum_land=land(out), qkv_sum_land=land(qkv),
            down_send=down, down_land=down,
            up_send=up, up_land=up, up1_parts=parts(up), down1_parts=parts(down),
            up1_relay=relay(up), up1_land=land(up), down1_relay=relay(down), down1_land=land(down),
            up1_sum=summed(up), up1_got=((near_count, block, half), BF),
            up2_got=((near_count, block, half), BF), in_total=summed(conv_i),
            in_got=((near_count, block, 2 * channels), BF), qkv_total=summed(qkv),
            qkv_got=((near_count, block, 3 * size), BF), small_land=((PLANES - 1, 8, width), F32),
            small_mid=small_row, small_near=((near_count, 8, width), F32),
            stage=stage, land0=stage, land1=stage, land2=stage,
        ),
    )
    big = (
        a.result_out, b.frames_grad_out, b.up1_grad_out, b.down1_grad_out, b.qkv_grad_out, b.attn_grad_out, b.in_grad_out,
        b.conv_grad_out, b.up2_grad_out, b.down2_grad_out,
    )
    shapes = [jax.ShapeDtypeStruct(array.shape, array.dtype) for array in big]
    shapes += [jax.ShapeDtypeStruct(shape, F32) for shape in ((norm_gains.shape[0], block), (taps, block), (1, block), (1, heads))]
    done = pl.pallas_call(
        finish_kernel,
        name="finish",
        out_shape=shapes,
        in_specs=[pl.BlockSpec(memory_space=V)] * (len(big) + 3),
        out_specs=[pl.BlockSpec(memory_space=V)] * len(shapes),
        compiler_params=pltpu.CompilerParams(vmem_limit_bytes=GRANT),
    )(*big, b.small_out, b.kernel_out, b.cross)
    (
        result, frames_grad, up1_grad, down1_grad, qkv_grad, attn_out_grad, in_grad, conv_out_grad, up2_grad, down2_grad,
        gains_grad, kernel_grad, batch_grad, slopes_grad,
    ) = done
    return (
        result, frames_grad, up1_grad, down1_grad, qkv_grad, attn_out_grad, in_grad, kernel_grad,
        batch_grad.reshape(-1), conv_out_grad, up2_grad, down2_grad, gains_grad, slopes_grad.reshape(-1),
    )


def solution(mesh):
    planar = mesh.shape["seq"] == 2 * CHIPS and mesh.shape["fsdp"] == PLANES
    chosen = plane_body if planar else body
    placed = (
        P("fsdp", "seq", None),
        P("fsdp", None),
        P("fsdp", None),
        P("fsdp", None),
        P("fsdp", None),
        P("fsdp", None),
        P("fsdp", None),
        P(None, "fsdp"),
        P("fsdp"),
        P("fsdp", None),
        P("fsdp", None),
        P("fsdp", None),
        P(None, "fsdp"),
        P(),
        P("fsdp", "seq", None),
    )
    return jax.shard_map(
        chosen,
        mesh=mesh,
        in_specs=placed,
        out_specs=(
            P("fsdp", "seq", None),
            P("fsdp", "seq", None),
            P(("seq", "fsdp"), None),
            P(("seq", "fsdp"), None),
            P(("seq", "fsdp"), None),
            P(("seq", "fsdp"), None),
            P(("seq", "fsdp"), None),
            P(None, ("seq", "fsdp")),
            P(("seq", "fsdp")),
            P(("seq", "fsdp"), None),
            P(("seq", "fsdp"), None),
            P(("seq", "fsdp"), None),
            P(None, ("seq", "fsdp")),
            P(),
        ),
        check_vma=False,
    )
```

```python
import functools
import math
import types

import jax
import jax.numpy as jnp
from jax import lax
from jax.experimental import pallas as pl
from jax.experimental.pallas import tpu as pltpu
from jax.sharding import PartitionSpec as P

EPSILON = 1e-05
MASKED = -1e30


def extended(x, sides, width):
    for axis, dim in sides:
        size, length = (lax.axis_size(axis), x.shape[dim])
        up = [(i, (i + 1) % size) for i in range(size - 1)]
        down = [(j, i) for i, j in up]
        last = lax.slice_in_dim(x, length - width, length, axis=dim)
        initial = lax.slice_in_dim(x, 0, width, axis=dim)
        before = lax.ppermute(last, axis, up)
        after = lax.ppermute(initial, axis, down)
        x = jnp.concatenate([before, x, after], axis=dim)
    return x


def normed(value, gain):
    average = jnp.mean(value, axis=-1, keepdims=True)
    centred = value - average
    variance = jnp.mean(centred * centred, axis=-1, keepdims=True)
    return centred * lax.rsqrt(variance + EPSILON) * gain


def norm_back(value, gain, gradient):
    pullback = jax.vjp(normed, value, gain)[1]
    return pullback(gradient)


def matmul(left, right):
    return jnp.dot(left, right, preferred_element_type=jnp.float32)


def transposed_left(left, right):
    return lax.dot_general(
        left, right, (((0,), (0,)), ((), ())), preferred_element_type=jnp.float32
    )


def transposed_right(left, right):
    return lax.dot_general(
        left, right, (((1,), (1,)), ((), ())), preferred_element_type=jnp.float32
    )


def item_index(positions, bounds):
    return jnp.sum((positions[:, None] >= bounds[None, :]).astype(jnp.int32), axis=1)


def unpack(weights):
    (
        first_up,
        first_down,
        qkv_full,
        out_full,
        conv_up,
        kernel_full,
        batch_full,
        conv_down,
        second_up,
        second_down,
        gains_full,
    ) = weights
    return (
        first_up,
        first_down,
        qkv_full,
        out_full,
        conv_up,
        kernel_full.astype(jnp.float32),
        batch_full.astype(jnp.float32),
        conv_down,
        second_up,
        second_down,
        gains_full.astype(jnp.float32),
    )


def feed_forward(value, gain, weight_up, weight_down):
    hidden = normed(value, gain).astype(jnp.bfloat16)
    swish = jax.nn.silu(matmul(hidden, weight_up)).astype(jnp.bfloat16)
    return value + 0.5 * matmul(swish, weight_down)


def feed_back(value, gain, weight_up, weight_down, gradient):
    hidden = normed(value, gain).astype(jnp.bfloat16)
    swish, pullback = jax.vjp(jax.nn.silu, matmul(hidden, weight_up))
    swish_low = swish.astype(jnp.bfloat16)
    branch_grad = (0.5 * gradient).astype(jnp.bfloat16)
    down_grad = transposed_left(swish_low, branch_grad)
    active_grad = pullback(transposed_right(branch_grad, weight_down))[0].astype(jnp.bfloat16)
    up_grad = transposed_left(hidden, active_grad)
    value_grad, gain_grad = norm_back(value, gain, transposed_right(active_grad, weight_up))
    return (gradient + value_grad, gain_grad, up_grad, down_grad)


def biased_scores(query_heads, key_heads, slopes, layout):
    query_pos, key_pos, query_ids, key_ids = layout
    raw_scores = jnp.einsum(
        "qhd,khd->hqk", query_heads, key_heads, preferred_element_type=jnp.float32
    )
    distance = jnp.abs(query_pos[:, None] - key_pos[None, :]).astype(jnp.float32)
    scores = (
        raw_scores * (1.0 / math.sqrt(query_heads.shape[2]))
        - slopes[:, None, None] * distance[None]
    )
    shared = query_ids[:, None] == key_ids[None, :]
    return (jnp.where(shared[None], scores, MASKED), distance)


def attention_probs(query, keys, slopes, layout):
    heads = slopes.shape[0]
    head_size = query.shape[1] // heads
    query_heads = query.reshape(query.shape[0], heads, head_size)
    key_heads = keys.reshape(keys.shape[0], heads, head_size)
    scores, distance = biased_scores(query_heads, key_heads, slopes, layout)
    top = jnp.max(scores, axis=-1, keepdims=True)
    exponent = jnp.exp(scores - top)
    total = jnp.sum(exponent, axis=-1, keepdims=True)
    probs = exponent / total
    return (probs, distance, query_heads, key_heads, top[:, :, 0], total[:, :, 0])


def attend(value, gain, weight_qkv, weight_out, slopes, layout):
    feature_width = value.shape[1]
    hidden = normed(value, gain).astype(jnp.bfloat16)
    joint = matmul(hidden, weight_qkv).astype(jnp.bfloat16)
    keys_values = lax.all_gather(joint[:, feature_width:], "seq", axis=0, tiled=True)
    probs, distance, query_heads, key_heads, top, total = attention_probs(
        joint[:, :feature_width], keys_values[:, :feature_width], slopes, layout
    )
    value_heads = keys_values[:, feature_width:].reshape(key_heads.shape)
    mixed = jnp.einsum(
        "hqk,khd->qhd", probs.astype(jnp.bfloat16), value_heads, preferred_element_type=jnp.float32
    )
    mixed = mixed.reshape(value.shape).astype(jnp.bfloat16)
    return (value + matmul(mixed, weight_out), keys_values)


def attend_back(value, gain, weight_qkv, weight_out, slopes, layout, keys_values, gradient):
    feature_width = value.shape[1]
    row_count = value.shape[0]
    hidden = normed(value, gain).astype(jnp.bfloat16)
    joint = matmul(hidden, weight_qkv).astype(jnp.bfloat16)
    probs, distance, query_heads, key_heads, top, total = attention_probs(
        joint[:, :feature_width], keys_values[:, :feature_width], slopes, layout
    )
    probs_low = probs.astype(jnp.bfloat16)
    value_heads = keys_values[:, feature_width:].reshape(key_heads.shape)
    mixed = jnp.einsum("hqk,khd->qhd", probs_low, value_heads, preferred_element_type=jnp.float32)
    mixed = mixed.reshape(value.shape).astype(jnp.bfloat16)
    branch_grad = gradient.astype(jnp.bfloat16)
    weight_out_grad = transposed_left(mixed, branch_grad)
    mixed_flat = transposed_right(branch_grad, weight_out).astype(jnp.bfloat16)
    mixed_grad = mixed_flat.reshape(query_heads.shape)
    prob_grad = jnp.einsum(
        "qhd,khd->hqk", mixed_grad, value_heads, preferred_element_type=jnp.float32
    )
    delta = jnp.sum(probs * prob_grad, axis=-1)
    score_grad = probs * (prob_grad - delta[:, :, None])
    slope_grad = -jnp.sum(score_grad * distance[None], axis=(1, 2))
    scale = 1.0 / math.sqrt(query_heads.shape[2])
    raw_grad = (score_grad * scale).astype(jnp.bfloat16)
    query_grad = jnp.einsum("hqk,khd->qhd", raw_grad, key_heads, preferred_element_type=jnp.float32)
    query_pos, key_pos, query_ids, key_ids = layout
    all_query, all_mixed = (
        lax.all_gather(joint[:, :feature_width], "seq", axis=0, tiled=True),
        lax.all_gather(mixed_flat, "seq", axis=0, tiled=True),
    )
    all_top, all_total, all_delta = (
        lax.all_gather(top, "seq", axis=1, tiled=True),
        lax.all_gather(total, "seq", axis=1, tiled=True),
        lax.all_gather(delta, "seq", axis=1, tiled=True),
    )
    heads = slopes.shape[0]
    head_size = query_heads.shape[2]
    all_query_heads = all_query.reshape(all_query.shape[0], heads, head_size)
    all_mixed_heads = all_mixed.reshape(all_query.shape[0], heads, head_size)
    own_keys = joint[:, feature_width : 2 * feature_width].reshape(row_count, heads, head_size)
    own_values = joint[:, 2 * feature_width :].reshape(row_count, heads, head_size)
    column_scores, column_distance = biased_scores(
        all_query_heads, own_keys, slopes, (key_pos, query_pos, key_ids, query_ids)
    )
    column_probs = jnp.exp(column_scores - all_top[:, :, None]) / all_total[:, :, None]
    column_prob_grad = jnp.einsum(
        "qhd,khd->hqk", all_mixed_heads, own_values, preferred_element_type=jnp.float32
    )
    column_score_grad = column_probs * (column_prob_grad - all_delta[:, :, None])
    column_raw = (column_score_grad * scale).astype(jnp.bfloat16)
    key_grad = jnp.einsum(
        "hqk,qhd->khd", column_raw, all_query_heads, preferred_element_type=jnp.float32
    )
    value_grad = jnp.einsum(
        "hqk,qhd->khd",
        column_probs.astype(jnp.bfloat16),
        all_mixed_heads,
        preferred_element_type=jnp.float32,
    )
    local_grad = jnp.concatenate(
        [key_grad.reshape(row_count, feature_width), value_grad.reshape(row_count, feature_width)],
        axis=1,
    )
    joint_grad = jnp.concatenate([query_grad.reshape(value.shape), local_grad], axis=1).astype(
        jnp.bfloat16
    )
    qkv_grad = transposed_left(hidden, joint_grad)
    input_grad, gain_grad = norm_back(value, gain, transposed_right(joint_grad, weight_qkv))
    return (gradient + input_grad, gain_grad, qkv_grad, weight_out_grad, slope_grad)


def gate_linear(joint):
    feature_width = joint.shape[1] // 2
    return joint[:, :feature_width] * jax.nn.sigmoid(joint[:, feature_width:])


def depthwise(rim, kernel, rim_ids, own_ids):
    row_count = own_ids.shape[0]
    total = jnp.zeros((row_count, rim.shape[1]), jnp.float32)
    for offset in range(kernel.shape[0]):
        shared = (rim_ids[offset : offset + row_count] == own_ids).astype(jnp.float32)
        total = (
            total
            + kernel[offset]
            * rim[offset : offset + row_count].astype(jnp.float32)
            * shared[:, None]
        )
    return total


def depthwise_back(rim, kernel, rim_ids, own_ids, conv_grad):
    row_count = own_ids.shape[0]
    reach = kernel.shape[0] - 1
    grad_rim = extended(conv_grad.astype(jnp.bfloat16), (("seq", 0),), reach // 2).astype(
        conv_grad.dtype
    )
    input_grad = jnp.zeros(conv_grad.shape, jnp.float32)
    kernel_rows = []
    for offset in range(kernel.shape[0]):
        shared = (rim_ids[offset : offset + row_count] == own_ids).astype(jnp.float32)[:, None]
        kernel_rows.append(
            jnp.sum(
                rim[offset : offset + row_count].astype(jnp.float32) * shared * conv_grad, axis=0
            )
        )
        mirror = reach - offset
        crossed = (rim_ids[mirror : mirror + row_count] == own_ids).astype(jnp.float32)[:, None]
        input_grad = input_grad + kernel[offset] * grad_rim[mirror : mirror + row_count] * crossed
    return (input_grad, jnp.stack(kernel_rows))


def body(
    frames,
    lengths,
    up_first,
    down_first,
    joint_qkv,
    attn_out,
    conv_in,
    conv_kernel,
    batch_gain,
    conv_out,
    up_second,
    down_second,
    norm_gains,
    slopes,
    out_grad,
):
    sharded = (
        up_first,
        down_first,
        joint_qkv,
        attn_out,
        conv_in,
        conv_kernel,
        batch_gain,
        conv_out,
        up_second,
        down_second,
        norm_gains,
    )
    gathered = (
        lax.all_gather(sharded[0], "fsdp", axis=0, tiled=True),
        lax.all_gather(sharded[1], "fsdp", axis=0, tiled=True),
        lax.all_gather(sharded[2], "fsdp", axis=0, tiled=True),
        lax.all_gather(sharded[3], "fsdp", axis=0, tiled=True),
        lax.all_gather(sharded[4], "fsdp", axis=0, tiled=True),
        lax.all_gather(sharded[5], "fsdp", axis=1, tiled=True),
        lax.all_gather(sharded[6], "fsdp", axis=0, tiled=True),
        lax.all_gather(sharded[7], "fsdp", axis=0, tiled=True),
        lax.all_gather(sharded[8], "fsdp", axis=0, tiled=True),
        lax.all_gather(sharded[9], "fsdp", axis=0, tiled=True),
        lax.all_gather(sharded[10], "fsdp", axis=1, tiled=True),
    )
    (
        first_up,
        first_down,
        qkv_full,
        out_full,
        conv_up,
        kernel,
        batch_scale,
        conv_down,
        second_up,
        second_down,
        gains,
    ) = unpack(gathered)
    row_count = frames.shape[1]
    feature_width = frames.shape[2]
    seq_count = lax.axis_size("seq")
    start_row = lax.axis_index("seq") * row_count
    bounds = jnp.cumsum(lengths[0])
    item_count = lengths.shape[1]
    own_pos = start_row + jnp.arange(row_count, dtype=jnp.int32)
    key_pos = jnp.arange(row_count * seq_count, dtype=jnp.int32)
    own_ids = item_index(own_pos, bounds)
    layout = (own_pos, key_pos, own_ids, item_index(key_pos, bounds))
    rim_width = conv_kernel.shape[0] // 2
    rim_ids = item_index(
        start_row - rim_width + jnp.arange(row_count + 2 * rim_width, dtype=jnp.int32), bounds
    )
    valid = (own_ids < item_count).astype(jnp.float32)[:, None]
    source = frames[0].astype(jnp.float32)
    first = feed_forward(source, gains[0], first_up, first_down)
    second, keys_values = attend(first, gains[1], qkv_full, out_full, slopes, layout)
    conv_hidden = normed(second, gains[2]).astype(jnp.bfloat16)
    conv_joint = matmul(conv_hidden, conv_up)
    rim = extended(gate_linear(conv_joint).astype(jnp.bfloat16), (("seq", 0),), rim_width)
    conv = depthwise(rim, kernel, rim_ids, own_ids)
    total, count = lax.psum((jnp.sum(valid * conv, axis=0), jnp.sum(valid)), ("seq", "fsdp"))
    average = total / count
    centred = conv - average
    spread = lax.psum(jnp.sum(valid * centred * centred, axis=0), ("seq", "fsdp"))
    variance = spread / count
    inverse = lax.rsqrt(variance + EPSILON)
    standard = (conv - average) * inverse
    pre_swish = standard * batch_scale
    swish, swish_pull = jax.vjp(jax.nn.silu, pre_swish)
    swish_low = swish.astype(jnp.bfloat16)
    third = second + matmul(swish_low, conv_down)
    fourth = feed_forward(third, gains[3], second_up, second_down)
    result = normed(fourth, gains[4])
    regathered = (
        lax.all_gather(sharded[0], "fsdp", axis=0, tiled=True),
        lax.all_gather(sharded[1], "fsdp", axis=0, tiled=True),
        lax.all_gather(sharded[2], "fsdp", axis=0, tiled=True),
        lax.all_gather(sharded[3], "fsdp", axis=0, tiled=True),
        lax.all_gather(sharded[4], "fsdp", axis=0, tiled=True),
        lax.all_gather(sharded[5], "fsdp", axis=1, tiled=True),
        lax.all_gather(sharded[6], "fsdp", axis=0, tiled=True),
        lax.all_gather(sharded[7], "fsdp", axis=0, tiled=True),
        lax.all_gather(sharded[8], "fsdp", axis=0, tiled=True),
        lax.all_gather(sharded[9], "fsdp", axis=0, tiled=True),
        lax.all_gather(sharded[10], "fsdp", axis=1, tiled=True),
    )
    (
        first_up,
        first_down,
        qkv_full,
        out_full,
        conv_up,
        kernel,
        batch_scale,
        conv_down,
        second_up,
        second_down,
        gains,
    ) = unpack(regathered)
    fourth_grad, last_gain = norm_back(fourth, gains[4], out_grad[0].astype(jnp.float32))
    third_grad, fourth_gain, second_up_grad, second_down_grad = feed_back(
        third, gains[3], second_up, second_down, fourth_grad
    )
    branch_grad = third_grad.astype(jnp.bfloat16)
    conv_down_grad = transposed_left(swish_low, branch_grad)
    scaled_grad = swish_pull(transposed_right(branch_grad, conv_down))[0]
    sum_grad, sum_cross = lax.psum(
        (jnp.sum(scaled_grad, axis=0), jnp.sum(scaled_grad * standard, axis=0)), ("seq", "fsdp")
    )
    conv_grad = inverse * (scaled_grad * batch_scale) - valid * (inverse / count) * (
        batch_scale * sum_grad + standard * (batch_scale * sum_cross)
    )
    gated_grad, kernel_grad = depthwise_back(rim, kernel, rim_ids, own_ids, conv_grad)
    joint_pull = jax.vjp(gate_linear, conv_joint)[1]
    joint_grad = joint_pull(gated_grad)[0].astype(jnp.bfloat16)
    conv_up_grad = transposed_left(conv_hidden, joint_grad)
    hidden_grad, third_gain = norm_back(second, gains[2], transposed_right(joint_grad, conv_up))
    second_grad = third_grad + hidden_grad
    late = (
        lax.psum_scatter(second_up_grad, ("seq", "fsdp"), scatter_dimension=0, tiled=True),
        lax.psum_scatter(second_down_grad, ("seq", "fsdp"), scatter_dimension=0, tiled=True),
        lax.psum_scatter(conv_down_grad, ("seq", "fsdp"), scatter_dimension=0, tiled=True),
        lax.psum_scatter(conv_up_grad, ("seq", "fsdp"), scatter_dimension=0, tiled=True),
        lax.psum_scatter(kernel_grad, ("seq", "fsdp"), scatter_dimension=1, tiled=True),
    )
    first_grad, second_gain, qkv_grad, out_weight_grad, slope_part = attend_back(
        first, gains[1], qkv_full, out_full, slopes, layout, keys_values, second_grad
    )
    source_grad, first_gain, first_up_grad, first_down_grad = feed_back(
        source, gains[0], first_up, first_down, first_grad
    )
    gain_grads = jnp.stack([first_gain, second_gain, third_gain, fourth_gain, last_gain])
    early = (
        lax.psum_scatter(first_up_grad, ("seq", "fsdp"), scatter_dimension=0, tiled=True),
        lax.psum_scatter(first_down_grad, ("seq", "fsdp"), scatter_dimension=0, tiled=True),
        lax.psum_scatter(qkv_grad, ("seq", "fsdp"), scatter_dimension=0, tiled=True),
        lax.psum_scatter(out_weight_grad, ("seq", "fsdp"), scatter_dimension=0, tiled=True),
        lax.psum_scatter(gain_grads, ("seq", "fsdp"), scatter_dimension=1, tiled=True),
    )
    slope_grad = lax.psum(slope_part, ("seq", "fsdp"))
    piece_width = feature_width // lax.axis_size(("seq", "fsdp"))
    batch_piece = lax.dynamic_slice_in_dim(
        sum_cross, lax.axis_index(("seq", "fsdp")) * piece_width, piece_width
    )
    return (
        result[None].astype(jnp.bfloat16),
        source_grad[None],
        early[0],
        early[1],
        early[2],
        early[3],
        late[3],
        late[4],
        batch_piece,
        late[2],
        late[0],
        late[1],
        early[4],
        slope_grad,
    )


BF = jnp.bfloat16
F32 = jnp.float32
MESH = pl.DeviceIdType.MESH
GRANT = 63 * 2**20
CHIPS = 4
PLANES = 4
SLOTS = 320
RIM = 8
V, H, S = pltpu.VMEM, pl.ANY, pltpu.SMEM


def mm(left, right):
    return jnp.dot(left, right, preferred_element_type=F32)


def mm_right(left, right):
    return lax.dot_general(left, right, (((1,), (1,)), ((), ())), preferred_element_type=F32)


def mm_left(left, right):
    return lax.dot_general(left, right, (((0,), (0,)), ((), ())), preferred_element_type=F32)


def span(index, size):
    return pl.ds(pl.multiple_of(index * size, size), size)


class Here:
    def __init__(self):
        self.seq = lax.axis_index("seq")
        self.plane = lax.axis_index("fsdp")
        self.core = lax.rem(self.seq, 2)
        self.chip = lax.div(self.seq, 2)
        column, row = lax.rem(self.chip, 2), lax.div(self.chip, 2)
        self.chips = [
            lax.rem(row + j // 2, 2) * 2 + lax.rem(column + j % 2, 2) for j in range(CHIPS)
        ]

    def peer(self, slot):
        return (self.chips[slot] * 2 + self.core, self.plane)

    def cross(self, slot):
        return (self.chips[slot] * 2 + 1 - self.core, self.plane)

    def sibling(self):
        return self.cross(0)

    def level(self, step):
        return lax.rem(self.plane + step, PLANES)

    def turned(self, step):
        return lax.rem(self.seq + step, 2 * CHIPS)

    def above(self, step):
        return (self.seq, self.level(step))

    def rows(self, slot, half, height):
        return span((self.chips[slot] * 2 + self.core) * 2 + half, height)

    def other_rows(self, slot, half, height):
        return span((self.chips[slot] * 2 + 1 - self.core) * 2 + half, height)


class Mail:
    def __init__(self, send, recv):
        self.send, self.recv, self.count, self.open, self.kept = send, recv, 0, [], []

    def slot(self):
        self.count += 1
        return self.count - 1

    def remote(self, src, dst, device, sent, received):
        return pltpu.make_async_remote_copy(
            src_ref=src,
            dst_ref=dst,
            send_sem=self.send.at[sent],
            recv_sem=self.recv.at[received],
            device_id=device,
            device_id_type=MESH,
        )

    def post(self, src, dst, device):
        i = self.slot()
        copy = self.remote(src, dst, device, i, i)
        copy.start()
        self.open.append(copy)
        return copy

    def settle(self, copies):
        for copy in copies:
            copy.wait_send()
        self.open = [copy for copy in self.open if all(copy is not done for done in copies)]

    def local(self, src, dst):
        copy = pltpu.make_async_copy(src, dst, self.send.at[self.slot()])
        copy.start()
        return copy

    def save(self, src, dst):
        self.kept.append(self.local(src, dst))

    def close(self):
        for copy in self.open:
            copy.wait_send()
        for copy in self.kept:
            copy.wait()
        self.open, self.kept = [], []


def greet(devices, extra=None):
    barrier = pltpu.get_barrier_semaphore()
    for device in devices:
        pl.semaphore_signal(barrier, inc=1, device_id=device, device_id_type=MESH)
    count = len(devices)
    if extra is not None:
        apart, device = extra
        count = count + apart.astype(jnp.int32)

        @pl.when(apart)
        def _():
            pl.semaphore_signal(barrier, inc=1, device_id=device, device_id_type=MESH)

    return lambda: pl.semaphore_wait(barrier, count)


def near(here):
    return (
        [here.peer(j) for j in range(1, CHIPS)]
        + [here.sibling()]
        + [here.above(k) for k in range(1, PLANES)]
    )


class Spread:
    def __init__(self, mail, here, buf, half):
        self.mail, self.here, self.buf = mail, here, buf.at[half]
        rows = buf.shape[2]
        self.whole, self.top, self.low = pl.ds(0, rows), pl.ds(0, rows // 2), pl.ds(rows // 2, rows // 2)
        self.x = self.send(0, 1, self.whole, 1)
        self.y = self.send(0, 2, self.whole, 2)

    def send(self, source, target, rows, slot):
        return self.mail.post(self.buf.at[source, rows], self.buf.at[target, rows], self.here.peer(slot))

    def near(self):
        self.x.wait_recv()
        self.d_top = self.send(1, 3, self.top, 2)
        self.y.wait_recv()
        self.d_low = self.send(2, 3, self.low, 1)

    def far(self):
        self.d_top.wait_recv()
        self.d_low.wait_recv()


def as_they_come(sent, work):
    sent[0].near()
    sent[1].near()
    work(0, 0)
    sent[0].far()
    work(0, 1)
    sent[1].far()
    work(1, 1)
    work(1, 0)


class Ring:
    def __init__(self, mail, here, dst, other, fill):
        self.mail, self.here, self.dst, self.other = mail, here, dst, other
        self.height = dst.shape[0] // PLANES
        self.fills = fill(self.block(dst, here.plane))

    def send(self):
        mail, here, dst = self.mail, self.here, self.dst
        for copy in self.fills:
            copy.wait()
        own = self.block(dst, here.plane)
        self.up = mail.post(own, own, here.above(1))
        self.down = mail.post(own, own, here.above(PLANES - 1))
        self.shared = [self.share(here.plane)]
        return self

    def block(self, ref, plane):
        return ref.at[span(plane, self.height)]

    def share(self, plane):
        return self.mail.post(self.block(self.dst, plane), self.block(self.other, plane), self.here.sibling())

    def relay(self):
        here, half = self.here, self.height // 2
        self.up.wait_recv()
        piece = self.block(self.dst, here.level(PLANES - 1)).at[pl.ds(0, half)]
        self.far_up = self.mail.post(piece, piece, here.above(1))
        self.down.wait_recv()
        piece = self.block(self.dst, here.level(1)).at[pl.ds(half, half)]
        self.far_down = self.mail.post(piece, piece, here.above(PLANES - 1))
        self.shared += [self.share(here.level(PLANES - 1)), self.share(here.level(1))]

    def finish(self):
        self.far_up.wait_recv()
        self.far_down.wait_recv()
        self.shared.append(self.share(self.here.level(2)))

    def ready(self):
        for copy in self.shared:
            copy.wait_recv()


class FromPlane:
    def __init__(self, mail, here, src, dst, other):
        self.mail, self.here, self.dst, self.other = mail, here, dst, other
        half = dst.shape[0] // 2
        top, low = pl.ds(0, half), pl.ds(half, half)
        slots = [mail.slot() for _ in range(4)]
        above, below = here.above(1), here.above(PLANES - 1)
        self.step = lax.rem(here.plane + PLANES - here.chip, PLANES)
        self.own = pltpu.make_async_copy(src, dst, mail.send.at[mail.slot()])
        self.up = mail.remote(src, dst, above, slots[0], slots[0])
        self.down = mail.remote(src, dst, below, slots[1], slots[1])
        self.far_up = mail.remote(dst.at[top], dst.at[top], above, slots[2], slots[2])
        self.far_down = mail.remote(dst.at[low], dst.at[low], below, slots[3], slots[3])

        @pl.when(self.step == 0)
        def _():
            self.own.start()
            self.up.start()
            self.down.start()

    def relay(self):
        @pl.when(self.step == 1)
        def _():
            self.up.wait_recv()
            self.far_up.start()

        @pl.when(self.step == PLANES - 1)
        def _():
            self.down.wait_recv()
            self.far_down.start()

    def finish(self):
        @pl.when(self.step == 0)
        def _():
            self.own.wait()
            self.up.wait_send()
            self.down.wait_send()

        @pl.when(self.step == 1)
        def _():
            self.far_up.wait_send()

        @pl.when(self.step == 2)
        def _():
            self.far_up.wait_recv()
            self.far_down.wait_recv()

        @pl.when(self.step == PLANES - 1)
        def _():
            self.far_down.wait_send()

        self.shared = self.mail.post(self.dst, self.other, self.here.sibling())

    def ready(self):
        self.shared.wait_recv()


class RingSum:
    def __init__(self, mail, here, parts, relays, land):
        self.mail, self.here, self.parts, self.relays, self.land = mail, here, parts, relays, land
        self.half = parts.shape[1] // 2
        self.top, self.low = pl.ds(0, self.half), pl.ds(self.half, self.half)
        far, up, down = here.level(2), here.level(1), here.level(PLANES - 1)
        above, below = here.above(1), here.above(PLANES - 1)
        self.far_up = mail.post(parts.at[far, self.top], relays.at[0], above)
        self.far_down = mail.post(parts.at[far, self.low], relays.at[1], below)
        self.up_low = mail.post(parts.at[up, self.low], land.at[0, self.low], above)
        self.down_top = mail.post(parts.at[down, self.top], land.at[1, self.top], below)

    def relay(self):
        here, relays = self.here, self.relays
        up, down = here.level(1), here.level(PLANES - 1)
        self.far_up.wait_recv()
        relays[2] = (relays[0].astype(F32) + self.parts[up, self.top].astype(F32)).astype(BF)
        self.up_top = self.mail.post(relays.at[2], self.land.at[0, self.top], here.above(1))
        self.far_down.wait_recv()
        relays[3] = (relays[1].astype(F32) + self.parts[down, self.low].astype(F32)).astype(BF)
        self.down_low = self.mail.post(relays.at[3], self.land.at[1, self.low], here.above(PLANES - 1))

    def total(self):
        for copy in (self.up_low, self.down_top, self.up_top, self.down_low):
            copy.wait_recv()
        return (
            self.parts[self.here.plane].astype(F32) + self.land[0].astype(F32) + self.land[1].astype(F32)
        )


def scale_row(small_ref, index):
    rows = [small_ref[k, index : index + 1, :] for k in range(PLANES)]
    return jnp.concatenate(rows, axis=1)


def own_channels(small_ref, here, rows, width):
    return small_ref[here.chip, rows, span(here.core, width)]


def whitened(value):
    average = jnp.mean(value, axis=-1, keepdims=True)
    centred = value - average
    inverse = lax.rsqrt(jnp.mean(centred * centred, axis=-1, keepdims=True) + EPSILON)
    return centred * inverse, inverse


def norm_grad(value, gain, gradient):
    white, inverse = whitened(value)
    inner = gradient * gain
    value_grad = inverse * (
        inner
        - jnp.mean(inner, axis=-1, keepdims=True)
        - white * jnp.mean(inner * white, axis=-1, keepdims=True)
    )
    return value_grad, jnp.sum(gradient * white, axis=0, keepdims=True)


def at_row(index, row, height=8):
    place = lax.broadcasted_iota(jnp.int32, (height, row.shape[1]), 0)
    return jnp.where(place == index, row, 0.0)


def sigmoid(value):
    return 1.0 / (1.0 + jnp.exp(-value))


def item_of(position, lengths):
    end, item = 0, jnp.zeros(position.shape, jnp.int32)
    for k in range(lengths.shape[1]):
        end = end + lengths[0, k]
        item = item + (position >= end).astype(jnp.int32)
    return item


def set_marks(marks, lengths):
    taps, (frames, width) = marks.shape[0] - 1, marks.shape[1:]
    position = lax.broadcasted_iota(jnp.int32, (frames, width), 0)
    item = item_of(position, lengths)
    for t in range(taps):
        other = position + (t - taps // 2)
        shared = (item_of(other, lengths) == item) & (other >= 0) & (other < frames)
        marks[t] = shared.astype(F32).astype(BF)
    marks[taps] = (item < lengths.shape[1]).astype(F32).astype(BF)


class Reduce:
    def __init__(self, mail, here, bufs, half):
        self.mail, self.here, self.half, self.copies = mail, here, half, []
        self.stage, self.land, self.acc = bufs

    def put(self, pair, value):
        rows = value.shape[0] // 2
        for k in range(2):
            slot, term = 2 * pair + k, value[k * rows : (k + 1) * rows]
            if slot == 0:
                self.acc[self.half] = term
                continue
            place = self.stage.at[self.half, slot - 1]
            place[...] = term.astype(BF)
            self.copies.append(self.mail.post(place, self.land.at[self.half, slot - 1], self.here.peer(slot)))

    def total(self):
        for copy in self.copies:
            copy.wait_recv()
        self.mail.settle(self.copies)
        value = self.acc[self.half]
        for j in range(1, CHIPS):
            value = value + self.land[self.half, j - 1].astype(F32)
        return value


class RelayReduce(Reduce):
    def __init__(self, mail, here, bufs, half):
        super().__init__(mail, here, bufs, half)
        rows = self.stage.shape[2] // 2
        self.top, self.low = pl.ds(0, rows), pl.ds(rows, rows)
        self.out, self.into, self.passed = self.stage.at[half], self.land.at[half], []

    def send(self, source, target, rows, slot):
        copy = self.mail.post(self.out.at[source, rows], self.into.at[target, rows], self.here.peer(slot))
        self.copies.append(copy)
        return copy

    def put(self, pair, value):
        rows = value.shape[0] // 2
        if pair:
            self.out[2] = value[rows:].astype(BF)
            self.far = (self.send(2, 2, self.top, 1), self.send(2, 2, self.low, 2))
            self.out[1] = value[:rows].astype(BF)
            self.send(1, 1, self.low, 2)
        else:
            self.out[0] = value[rows:].astype(BF)
            self.send(0, 0, self.top, 1)
            self.acc[self.half] = value[:rows]

    def relay(self):
        for copy, slot, rows in ((self.far[0], 1, self.top), (self.far[1], 0, self.low)):
            copy.wait_recv()
            self.copies = [other for other in self.copies if other is not copy]
            self.passed.append(copy)
            value = self.out[slot, rows].astype(F32) + self.into[2, rows].astype(F32)
            self.out[slot, rows] = value.astype(BF)
            self.send(slot, slot, rows, 2 if slot else 1)

    def total(self):
        for copy in self.copies:
            copy.wait_recv()
        self.mail.settle(self.copies + self.passed)
        return self.acc[self.half] + self.into[0].astype(F32) + self.into[1].astype(F32)


def flat(ref, columns=None):
    value = ref[...] if columns is None else ref[:, :, :, columns]
    return value.reshape(-1, value.shape[-1])


def pair_of(ref, half, pair, columns=slice(None)):
    value = ref[half, 2 * pair : 2 * pair + 2, :, columns]
    return value.reshape(-1, value.shape[-1])


def set_pair(ref, half, pair, value, columns=slice(None)):
    ref[half, 2 * pair : 2 * pair + 2, :, columns] = value.reshape(2, -1, value.shape[-1])


def feed_active(hidden, keep, up, half, pair):
    width = up[0].shape[1]
    rows = pair_of(hidden, half, pair)
    for side in range(2):
        set_pair(keep, half, pair, mm(rows, up[side][...]), slice(side * width, (side + 1) * width))


def feed_out(keep, down, half, pair, swish=None):
    width = down[0].shape[0]
    total = None
    for side in range(2):
        columns = slice(side * width, (side + 1) * width)
        active = pair_of(keep, half, pair, columns)
        value = (active * sigmoid(active)).astype(BF)
        if swish is not None:
            set_pair(swish, half, pair, value, columns)
        term = mm(value, down[side][...])
        total = term if total is None else total + term
    return total


def feed_swish(keep, swish, half, pair):
    active = pair_of(keep, half, pair)
    set_pair(swish, half, pair, (active * sigmoid(active)).astype(BF))


def feed_slope(branch, keep, down, active_grad, half, pair):
    width = down[0].shape[0]
    rows = pair_of(branch, half, pair)
    for side in range(2):
        columns = slice(side * width, (side + 1) * width)
        active = pair_of(keep, half, pair, columns)
        gate = sigmoid(active)
        grad = mm_right(rows, down[side][...]) * (gate * (1.0 + active * (1.0 - gate)))
        set_pair(active_grad, half, pair, grad.astype(BF), columns)


def feed_in(active_grad, up, half, pair):
    width = up[0].shape[1]
    total = None
    for side in range(2):
        term = mm_right(pair_of(active_grad, half, pair, slice(side * width, (side + 1) * width)), up[side][...])
        total = term if total is None else total + term
    return total


def pair_product(mail, here, left, right, blocks, send, land, store):
    height = send.shape[0] // blocks
    copies = []
    for i in range(blocks):
        rows = pl.ds(i * height, height)
        send[rows, :] = mm_left(left(1, i), right(1)).astype(BF)
        copies.append(mail.post(send.at[rows], land.at[rows], here.sibling()))
    for i in range(blocks):
        rows = pl.ds(i * height, height)
        grad = mm_left(left(0, i), right(0))
        copies[i].wait_recv()
        store(i, (grad + land[rows, :].astype(F32)).astype(BF))
    return copies


def by_plane(out, first=0):
    def store(i, value):
        height = out.shape[1]
        each = value.shape[0] // height
        for k in range(each):
            out[lax.rem(first + i * each + k, PLANES)] = value[k * height : (k + 1) * height]

    return store


def by_owner(out):
    def store(i, value):
        seqs = 2 * CHIPS
        height = out.shape[1] // seqs
        each = value.shape[0] // (height * PLANES)
        for k in range(each):
            for p in range(PLANES):
                start = (k * PLANES + p) * height
                at = (i * each + k) * height
                out[p, at : at + height, :] = value[start : start + height]

    return store


def down_grad(mail, here, branch, swish, out, send, land):
    half = swish.shape[3] // 2
    block = half // 2
    return pair_product(
        mail, here,
        lambda side, i: flat(swish, slice(side * half + i * block, side * half + (i + 1) * block)),
        lambda side: flat(branch),
        2, send, land, by_plane(out, here.seq),
    )


def up_grad(mail, here, hidden, active_grad, out, send, land):
    half = active_grad.shape[3] // 2
    block = hidden.shape[3] // 4
    return pair_product(
        mail, here,
        lambda side, i: flat(hidden, slice(i * block, (i + 1) * block)),
        lambda side: flat(active_grad, slice(side * half, (side + 1) * half)),
        4, send, land, by_owner(out),
    )


def slots_grad(mail, here, rows, sides, out, send, land):
    block = rows.shape[3] // 4
    return pair_product(
        mail, here,
        lambda side, i: flat(rows, slice(i * block, (i + 1) * block)),
        lambda side: flat(sides.at[side]),
        4, send, land, by_owner(out),
    )


def sides_grad(mail, here, sides, rows, out, send, land):
    return pair_product(
        mail, here, lambda side, i: flat(sides.at[side]), lambda side: flat(rows), 1, send, land, by_plane(out)
    )


def attention_weights(query, keys, slope, row, lengths):
    column = lax.broadcasted_iota(jnp.int32, (8, keys.shape[0]), 1)[:1, :]
    distance = jnp.abs(row.astype(F32) - column.astype(F32))
    scores = mm_right(query, keys) * (1.0 / math.sqrt(query.shape[1])) - slope * distance
    scores = jnp.where(item_of(row, lengths) == item_of(column, lengths), scores, MASKED)
    exponent = jnp.exp(scores - jnp.max(scores, axis=-1, keepdims=True))
    return exponent * (1.0 / jnp.sum(exponent, axis=-1, keepdims=True)), distance


def kernel_refs(names, refs):
    return types.SimpleNamespace(**dict(zip(names, refs, strict=True)))


def forward_kernel(names, *refs):
    r = kernel_refs(names, refs)
    here, mail = Here(), Mail(r.send, r.recv)
    lengths, small, marks = r.lengths, r.small, r.marks
    rows = r.frames.shape[1] // 2
    met = greet(near(here))

    def columns_of(src, turn=0):
        width = 128

        def fill(region):
            groups = region.shape[1] // width
            stride = src.shape[1] // groups
            return [
                mail.local(
                    src.at[:, pl.ds(pl.multiple_of(g * stride + here.turned(turn * g) * width, width), width)],
                    region.at[:, pl.ds(g * width, width)],
                )
                for g in range(groups)
            ]

        return fill

    def rows_of(src):
        return lambda region: [mail.local(src.at[span(here.turned(here.plane), region.shape[0]), :], region)]

    def core_rows_of(src, dst, other):
        return FromPlane(mail, here, src.at[span(here.core, dst.shape[0]), :], dst, other)

    def part(half):
        return pl.ds(half * rows, rows)

    def spread(buf, half, value, gain):
        buf[half, 0] = (whitened(value)[0] * gain).astype(BF)
        return Spread(mail, here, buf, half)

    def reduce(land, kind=Reduce):
        return [kind(mail, here, (r.stage, land, r.acc), h) for h in range(2)]

    own_small = small.at[here.plane]
    gains, taps = r.gains.shape[0], r.taps.shape[0]
    own_small[0:gains, :] = r.gains[...].astype(F32)
    own_small[gains : gains + taps, :] = r.taps[...].astype(F32)
    own_small[gains + taps : gains + taps + 1, :] = r.batch[...].astype(F32).reshape(1, -1)
    up1 = Ring(mail, here, r.up1, r.up1_other, columns_of(r.up1_src, 1))
    down1 = Ring(mail, here, r.down1, r.down1_other, rows_of(r.down1_src))
    met()
    small_copies = [mail.post(own_small, own_small, here.above(k)) for k in range(1, PLANES)]
    up1.send()
    down1.send()

    for copy in small_copies:
        copy.wait_recv()
    gain = scale_row(small, 0)
    sent = [spread(r.hidden0, h, r.frames[0, part(h), :].astype(F32), gain) for h in range(2)]
    set_marks(marks, lengths)
    for h in range(2):
        sent[h].near()
    up1.relay()
    for h in range(2):
        sent[h].far()
    down1.relay()
    qkv = Ring(mail, here, r.qkv, r.qkv_other, columns_of(r.qkv_src)).send()
    out = core_rows_of(r.out_src, r.out, r.out_other)
    up1.finish()
    up1.ready()
    ups, downs = (r.up1, r.up1_other), (r.down1, r.down1_other)
    for h in range(2):
        for p in range(2):
            feed_active(r.hidden0, r.keep0, ups, h, p)
    down1.finish()
    mail.save(r.hidden0, r.hidden0_out)
    mail.save(r.keep0, r.keep0_out)
    mail.save(r.up1, r.up1_out)
    mail.save(r.down1, r.down1_out)
    down1.ready()
    sums = reduce(r.land0, RelayReduce)
    for p in (1, 0):
        for h in range(2):
            sums[h].put(p, feed_out(r.keep0, downs, h, p))
    for h in range(2):
        sums[h].relay()
    qkv.relay()
    conv_in = Ring(mail, here, r.conv_in, r.conv_in_other, columns_of(r.in_src)).send()
    gain = scale_row(small, 1)
    sent = []
    for h in range(2):
        value = r.frames[0, part(h), :].astype(F32) + 0.5 * sums[h].total()
        r.first[part(h), :] = value
        mail.save(r.first.at[part(h)], r.first_out.at[part(h)])
        sent.append(spread(r.hidden1, h, value, gain))
    out.relay()
    conv_out = core_rows_of(r.conv_src, r.conv_out, r.conv_out_other)

    joint, mixed = r.joint, r.mixed
    size = joint.shape[1] // 3
    qkv.finish()
    qkv.ready()
    mail.save(r.qkv, r.qkv_out)
    joint_copies = []

    def to_heads(h, p):
        value = pair_of(r.hidden1, h, p)
        set_pair(r.joint_stage, h, p, mm(value, r.qkv_other[...]).astype(BF))
        for j in (2 * p, 2 * p + 1):
            joint_copies.append(
                mail.post(r.joint_stage.at[h, j], joint.at[here.rows(j, h, rows), :], here.sibling())
            )
        value = mm(value, r.qkv[...]).astype(BF)
        for k in range(2):
            joint[here.rows(2 * p + k, h, rows), :] = value[k * rows : (k + 1) * rows]

    as_they_come(sent, to_heads)
    for copy in joint_copies:
        copy.wait_recv()
    conv_in.relay()
    up2 = Ring(mail, here, r.up2, r.up2_other, columns_of(r.up2_src, 1)).send()
    mail.save(r.hidden1, r.hidden1_out)
    mail.save(joint, r.joint_out)
    slope = r.slopes[here.seq]
    mixed_copies = {}
    sums = reduce(r.land1, RelayReduce)

    def unit(h, j):
        mine, theirs = here.rows(j, h, rows), here.other_rows(j, h, rows)
        query = jnp.concatenate([joint[mine, 0:size], joint[theirs, 0:size]], axis=0)
        index = lax.broadcasted_iota(jnp.int32, (2 * rows, 128), 0)[:, :1]
        frame = jnp.where(index < rows, mine.start + index, theirs.start + index - rows)
        weights = attention_weights(query, joint[:, size : 2 * size], slope, frame, lengths)[0]
        value = mm(weights.astype(BF), joint[:, 2 * size :]).astype(BF)
        mixed[0, h, j] = value[:rows]
        r.mixed_stage[h, j] = value[rows:]
        mixed_copies[h, j] = mail.post(r.mixed_stage.at[h, j], mixed.at[1, h, j], here.sibling())

    def project(h, p):
        for j in (2 * p, 2 * p + 1):
            mixed_copies[h, j].wait_recv()
        value = mm(pair_of(mixed.at[0], h, p), r.out[...]) + mm(pair_of(mixed.at[1], h, p), r.out_other[...])
        sums[h].put(p, value)

    unit(0, 2)
    unit(0, 3)
    out.finish()
    unit(0, 0)
    out.ready()
    project(0, 1)
    unit(0, 1)
    unit(1, 2)
    project(0, 0)
    unit(1, 3)
    unit(1, 0)
    project(1, 1)
    sums[0].relay()
    unit(1, 1)
    project(1, 0)
    sums[1].relay()
    mail.save(r.out, r.out_out)
    mail.save(mixed, r.mixed_out)
    gain = scale_row(small, 2)
    sent = []
    for h in range(2):
        value = r.first[part(h), :] + sums[h].total()
        r.second[part(h), :] = value
        mail.save(r.second.at[part(h)], r.second_out.at[part(h)])
        sent.append(spread(r.hidden2, h, value, gain))
        if h == 0:
            conv_in.finish()
            conv_out.relay()

    gated, padded, glu = r.gated, r.padded, r.glu
    frames, width = gated.shape
    conv_in.ready()
    mail.save(r.conv_in, r.in_out)
    gate_copies = []

    def to_gates(h, p):
        value = pair_of(r.hidden2, h, p)
        for side, weight in ((1, r.conv_in_other), (0, r.conv_in)):
            both = mm(value, weight[...])
            set_pair(glu, h, p, both, slice(2 * width * side, 2 * width * (side + 1)))
            gate = (both[:, :width] * sigmoid(both[:, width:])).astype(BF)
            for k in range(2):
                j = 2 * p + k
                if side:
                    r.gate_stage[h, j] = gate[k * rows : (k + 1) * rows]
                    gate_copies.append(
                        mail.post(r.gate_stage.at[h, j], r.gate_rows.at[here.rows(j, h, rows), :], here.sibling())
                    )
                else:
                    r.gate_rows[here.rows(j, h, rows), :] = gate[k * rows : (k + 1) * rows]

    as_they_come(sent, to_gates)
    mail.save(r.hidden2, r.hidden2_out)
    mail.save(glu, r.glu_out)
    up2.relay()
    for copy in gate_copies:
        copy.wait_recv()
    taps = marks.shape[0] - 1
    padded[0:RIM, :] = jnp.zeros((RIM, width), F32)
    padded[RIM + frames :, :] = jnp.zeros((RIM, width), F32)
    gated[...] = r.gate_rows[...].astype(F32)
    padded[RIM : RIM + frames, :] = gated[...]
    mail.save(gated, r.gated_out)
    kernel = own_channels(small, here, slice(5, 5 + taps), width)
    conv = None
    for t in range(taps):
        first = RIM - taps // 2 + t
        term = kernel[t : t + 1, :] * padded[first : first + frames, :] * marks[t].astype(F32)
        conv = term if conv is None else conv + term
    valid = marks[taps].astype(F32)
    count = jnp.sum(valid, axis=0, keepdims=True)
    total = jnp.sum(valid * conv, axis=0, keepdims=True)
    centred = conv - total / count
    squares = jnp.sum(valid * centred * centred, axis=0, keepdims=True)
    bn, bn_land = r.bn, r.bn_land
    bn[...] = at_row(0, total) + at_row(1, squares) + at_row(2, count)
    bn_copies = [mail.post(bn, bn_land.at[k - 1], here.above(k)) for k in range(1, PLANES)]
    down2 = Ring(mail, here, r.down2, r.down2_other, rows_of(r.down2_src)).send()
    r.standard[...] = conv
    conv_out.finish()
    for copy in bn_copies:
        copy.wait_recv()
    terms = [bn[...]] + [bn_land[k - 1] for k in range(1, PLANES)]
    whole = sum(term[2:3, :] for term in terms)
    average = sum(term[0:1, :] for term in terms) / whole
    variance = 0.0
    for term in terms:
        apart = term[0:1, :] / term[2:3, :] - average
        variance = variance + term[1:2, :] + term[2:3, :] * apart * apart
    inverse = lax.rsqrt(variance / whole + EPSILON)
    r.stats[...] = at_row(0, inverse) + at_row(1, whole)
    standard = (r.standard[...] - average) * inverse
    r.standard[...] = standard
    scaled = standard * own_channels(small, here, slice(10, 11), width)
    r.swish_rows[...] = (scaled * sigmoid(scaled)).astype(BF)
    swish = r.swish
    swish_copies = {}
    for h in range(2):
        for j in (2, 3, 0, 1):
            swish_copies[h, j] = mail.post(
                r.swish_rows.at[here.other_rows(j, h, rows), :], swish.at[1, h, j], here.sibling()
            )
            swish[0, h, j] = r.swish_rows[here.rows(j, h, rows), :]
    mail.save(r.standard, r.standard_out)
    conv_out.ready()
    mail.save(r.conv_out, r.conv_out_out)
    sums = reduce(r.land2, RelayReduce)
    for p in (1, 0):
        for h in range(2):
            for j in (2 * p, 2 * p + 1):
                swish_copies[h, j].wait_recv()
            value = mm(pair_of(swish.at[0], h, p), r.conv_out[...])
            sums[h].put(p, value + mm(pair_of(swish.at[1], h, p), r.conv_out_other[...]))
    for h in range(2):
        sums[h].relay()
    mail.save(swish, r.swish_out)
    up2.finish()
    gain = scale_row(small, 3)
    sent = []
    for h in range(2):
        value = r.second[part(h), :] + sums[h].total()
        r.third[part(h), :] = value
        sent.append(spread(r.hidden3, h, value, gain))
        if h == 0:
            down2.relay()

    up2.ready()
    ups, downs = (r.up2, r.up2_other), (r.down2, r.down2_other)
    sums = reduce(r.land3, RelayReduce)
    sent[0].near()
    feed_active(r.hidden3, r.keep3, ups, 0, 0)
    sent[1].near()
    sent[0].far()
    feed_active(r.hidden3, r.keep3, ups, 0, 1)
    down2.finish()
    down2.ready()
    for p in (1, 0):
        sums[0].put(p, feed_out(r.keep3, downs, 0, p, r.act))
    sent[1].far()
    feed_active(r.hidden3, r.keep3, ups, 1, 1)
    sums[1].put(1, feed_out(r.keep3, downs, 1, 1, r.act))
    sums[0].relay()
    feed_active(r.hidden3, r.keep3, ups, 1, 0)
    sums[1].put(0, feed_out(r.keep3, downs, 1, 0, r.act))

    last_gain = scale_row(small, 4)
    sent, last_parts = [], []
    for h in range(2):
        fourth = r.third[part(h), :] + 0.5 * sums[h].total()
        if h == 0:
            sums[1].relay()
        r.result[0, part(h), :] = (whitened(fourth)[0] * last_gain).astype(BF)
        mail.save(r.result.at[0, part(h)], r.result_out.at[0, part(h)])
        gradient, last_part = norm_grad(fourth, last_gain, r.out_grad[0, part(h), :].astype(F32))
        last_parts.append(last_part)
        r.branch[h, 0] = (0.5 * gradient).astype(BF)
        sent.append(Spread(mail, here, r.branch, h))
        r.third_grad[part(h), :] = gradient
    sums = reduce(r.land4)

    def back(h, p):
        feed_slope(r.branch, r.keep3, downs, r.act_grad, h, p)
        sums[h].put(p, feed_in(r.act_grad, ups, h, p))

    as_they_come(sent, back)
    down_grad(mail, here, r.branch, r.act, r.down2_parts, r.down_send, r.down_land)
    mail.save(r.down2_parts, r.down2_parts_out)
    up_grad(mail, here, r.hidden3, r.act_grad, r.up2_parts, r.up_send, r.up_land)
    mail.save(r.up2_parts, r.up2_parts_out)
    gain_parts = []
    for h in range(2):
        value_part, gain_part = norm_grad(r.third[part(h), :], gain, sums[h].total())
        r.third_grad[part(h), :] = r.third_grad[part(h), :] + value_part
        mail.save(r.third_grad.at[part(h)], r.third_grad_out.at[part(h)])
        gain_parts.append(gain_part)
    r.small_d[...] = at_row(3, gain_parts[0] + gain_parts[1]) + at_row(4, last_parts[0] + last_parts[1])
    mail.close()


def backward_kernel(names, *refs):
    r = kernel_refs(names, refs)
    here, mail = Here(), Mail(r.send, r.recv)
    lengths, small, marks = r.lengths, r.small, r.marks
    rows = r.frames.shape[1] // 2
    seqs = 2 * CHIPS
    group = lax.rem(here.plane + seqs - here.seq, PLANES)
    target = 2 * group + lax.div(here.turned(group), PLANES)
    apart = target != here.seq
    group = lax.div(here.seq, 2)
    source = lax.rem(here.core * PLANES + here.plane + seqs - group, seqs)
    crosses = [here.cross(j) for j in range(1, CHIPS)]
    met = greet(near(here) + crosses, (apart, (source, here.plane)))

    def to_owner(index):
        src, dst = r.down_moved.at[index], r.down_got.at[index]
        i = mail.slot()
        stay = pltpu.make_async_copy(src, dst, mail.send.at[mail.slot()])
        go = mail.remote(src, dst, (target, here.plane), i, i)

        @pl.when(apart)
        def _():
            go.start()

        @pl.when(jnp.logical_not(apart))
        def _():
            stay.start()

        def wait():
            @pl.when(apart)
            def _():
                go.wait()

            @pl.when(jnp.logical_not(apart))
            def _():
                stay.wait()

        return wait

    def share(own, other):
        return mail.post(own, other, here.sibling())

    def part(half):
        return pl.ds(half * rows, rows)

    def spread(buf, half, value):
        buf[half, 0] = value.astype(BF)
        return Spread(mail, here, buf, half)

    def reduce(land, kind=Reduce):
        return [kind(mail, here, (r.stage, land, r.acc), h) for h in range(2)]

    third_ready = mail.local(r.third_grad_src, r.third_grad)
    down2_ready = mail.local(r.down2_parts_src, r.down2_parts)
    set_marks(marks, lengths)
    third_ready.wait()
    met()
    conv_out_shared = share(r.conv_out_src, r.conv_out_other)
    sent = [spread(r.branch2, h, r.third_grad[part(h), :]) for h in range(2)]
    conv_out_ready = mail.local(r.conv_out_src, r.conv_out)
    standard_ready = mail.local(r.standard_src, r.standard)
    swish_ready = mail.local(r.swish_src, r.swish)
    conv_in_shared = share(r.conv_in_src, r.conv_in_other)
    conv_in_ready = mail.local(r.conv_in_src, r.conv_in)
    glu_ready = mail.local(r.glu_src, r.glu)
    hidden2_ready = mail.local(r.hidden2_src, r.hidden2)
    gated_ready = mail.local(r.gated_src, r.gated)
    up2_ready = mail.local(r.up2_parts_src, r.up2_parts)
    second_ready = mail.local(r.second_src, r.second)
    down2_ready.wait()
    down2 = RingSum(mail, here, r.down2_parts, r.down2_relay, r.down2_land)

    frames, width = r.gated.shape
    conv_out_shared.wait_recv()
    conv_out_ready.wait()
    copies = []

    def to_channels(h, p):
        incoming = pair_of(r.branch2, h, p)
        set_pair(r.swish_stage, h, p, mm_right(incoming, r.conv_out_other[...]))
        for j in (2 * p, 2 * p + 1):
            copies.append(
                mail.post(r.swish_stage.at[h, j], r.swish_grad.at[here.rows(j, h, rows), :], here.sibling())
            )
        value = mm_right(incoming, r.conv_out[...])
        for k in range(2):
            r.swish_grad[here.rows(2 * p + k, h, rows), :] = value[k * rows : (k + 1) * rows]

    as_they_come(sent, to_channels)
    standard_ready.wait()
    gain = own_channels(small, here, slice(10, 11), width)
    for copy in copies:
        copy.wait_recv()
    white = r.standard[...]
    scaled = white * gain
    gate = sigmoid(scaled)
    scaled_grad = r.swish_grad[...] * (gate * (1.0 + scaled * (1.0 - gate)))
    bn, bn_land = r.bn, r.bn_land
    bn[...] = at_row(0, jnp.sum(scaled_grad, axis=0, keepdims=True)) + at_row(
        1, jnp.sum(scaled_grad * white, axis=0, keepdims=True)
    )
    bn_copies = [mail.post(bn, bn_land.at[k - 1], here.above(k)) for k in range(1, PLANES)]
    r.swish_grad[...] = scaled_grad * gain
    swish_ready.wait()
    row_send, column_send = r.down_send, r.up_send
    row_copies = sides_grad(
        mail, here, r.swish, r.branch2, r.conv_parts, row_send.at[pl.ds(0, width), :], r.conv_land
    )
    for copy in bn_copies:
        copy.wait_recv()
    down2.relay()
    up2_ready.wait()
    up2 = RingSum(mail, here, r.up2_parts, r.up2_relay, r.up2_land)
    both = bn[...]
    for k in range(1, PLANES):
        both = both + bn_land[k - 1]
    r.cross[...] = both
    inverse, whole = r.stats[0:1, :], r.stats[1:2, :]
    taps = marks.shape[0] - 1
    white = r.standard[...]
    conv_grad = inverse * r.swish_grad[...] - marks[taps].astype(F32) * (
        (inverse / whole) * (gain * both[0:1, :] + white * (gain * both[1:2, :]))
    )
    padded, reach = r.padded, taps // 2
    padded[0:RIM, :] = jnp.zeros((RIM, width), F32)
    padded[RIM + frames :, :] = jnp.zeros((RIM, width), F32)
    padded[RIM : RIM + frames, :] = conv_grad
    kernel = own_channels(small, here, slice(5, 5 + taps), width)
    total = None
    for t in range(taps):
        first = RIM + reach - t
        term = kernel[t : t + 1, :] * padded[first : first + frames, :] * marks[taps - 1 - t].astype(F32)
        total = term if total is None else total + term
    r.gate_grad[...] = total
    moved = r.moved2
    copies = {}
    for h in range(2):
        for j in (2, 3, 0, 1):
            copies[h, j] = mail.post(
                r.gate_grad.at[here.other_rows(j, h, rows), :], moved.at[1, h, j], here.sibling()
            )
            moved[0, h, j] = r.gate_grad[here.rows(j, h, rows), :]
    glu_ready.wait()
    conv_in_ready.wait()
    conv_in_shared.wait_recv()
    glu, glu_grad = r.glu, r.glu_grad
    sums = reduce(r.land2, RelayReduce)
    for p in (1, 0):
        for h in range(2):
            for j in (2 * p, 2 * p + 1):
                copies[h, j].wait_recv()
            result = None
            for side, weight in ((0, r.conv_in), (1, r.conv_in_other)):
                start = 2 * width * side
                left = pair_of(glu, h, p, slice(start, start + width))
                gate = sigmoid(pair_of(glu, h, p, slice(start + width, start + 2 * width)))
                incoming = pair_of(moved.at[side], h, p)
                set_pair(glu_grad.at[side], h, p, (incoming * gate).astype(BF), slice(0, width))
                set_pair(
                    glu_grad.at[side], h, p, (incoming * left * (gate * (1.0 - gate))).astype(BF),
                    slice(width, 2 * width),
                )
                term = mm_right(pair_of(glu_grad.at[side], h, p), weight[...])
                result = term if result is None else result + term
            sums[h].put(p, result)
    for h in range(2):
        sums[h].relay()
    out_shared, qkv_shared = share(r.out_src, r.out_other), share(r.qkv_src, r.qkv_other)
    out_ready = mail.local(r.out_src, r.out)
    joint_ready = mail.local(r.joint_src, r.joint)
    qkv_ready = mail.local(r.qkv_src, r.qkv)
    mixed_ready = mail.local(r.mixed_src, r.mixed)
    hidden1_ready = mail.local(r.hidden1_src, r.hidden1)
    first_ready = mail.local(r.first_src, r.first)
    hidden2_ready.wait()
    column_copies = slots_grad(
        mail, here, r.hidden2, glu_grad, r.in_parts, column_send.at[:, pl.ds(0, 2 * width)], r.in_land
    )
    gain = scale_row(small, 2)
    second_ready.wait()
    sent, gain_parts = [], []
    for h in range(2):
        value_part, gain_part = norm_grad(r.second[part(h), :], gain, sums[h].total())
        gradient = r.third_grad[part(h), :] + value_part
        r.grad[part(h), :] = gradient
        gain_parts.append(gain_part)
        sent.append(spread(r.branch1, h, gradient))
        if h == 0:
            gated_ready.wait()
            dense = padded[RIM : RIM + frames, :]
            padded[RIM : RIM + frames, :] = r.gated[...]
            kernel_rows = jnp.zeros((8, width), F32)
            for t in range(taps):
                first = RIM - reach + t
                row = jnp.sum(
                    padded[first : first + frames, :] * marks[t].astype(F32) * dense, axis=0, keepdims=True
                )
                kernel_rows = kernel_rows + at_row(t, row)
            r.kernel_part[...] = kernel_rows
    r.small_sum[...] = r.small_d[...] + at_row(2, gain_parts[0] + gain_parts[1])
    up2.relay()
    r.down_moved[0] = down2.total().astype(BF)
    down2_wait = to_owner(0)
    conv_sum = RingSum(mail, here, r.conv_parts, r.conv_relay, r.conv_sum_land)
    in_sum = RingSum(mail, here, r.in_parts, r.in_relay, r.in_sum_land)
    kernel_copies = [
        mail.post(r.kernel_part, r.kernel_land.at[k - 1], here.above(k)) for k in range(1, PLANES)
    ]

    out_shared.wait_recv()
    out_ready.wait()
    joint = r.joint
    size = joint.shape[1] // 3
    mixed_copies = []

    def to_heads(h, p):
        incoming = pair_of(r.branch1, h, p)
        set_pair(r.mixed_stage, h, p, mm_right(incoming, r.out_other[...]).astype(BF))
        for j in (2 * p, 2 * p + 1):
            mixed_copies.append(
                mail.post(r.mixed_stage.at[h, j], r.mixed_grad.at[here.rows(j, h, rows), :], here.sibling())
            )
        value = mm_right(incoming, r.out[...]).astype(BF)
        for k in range(2):
            r.mixed_grad[here.rows(2 * p + k, h, rows), :] = value[k * rows : (k + 1) * rows]

    as_they_come(sent, to_heads)
    joint_ready.wait()
    for copy in mixed_copies:
        copy.wait_recv()
    key_grad, value_grad, joint_grad = r.standard, r.gated, r.joint_grad
    key_grad[...] = jnp.zeros_like(key_grad)
    value_grad[...] = jnp.zeros_like(value_grad)
    scale = 1.0 / math.sqrt(size)
    slope = r.slopes[here.seq]
    height = 4 * rows

    def step(index, carry):
        start = pl.multiple_of(index * height, height)
        block_rows = pl.ds(start, height)
        query, keys, values = joint[block_rows, 0:size], joint[:, size : 2 * size], joint[:, 2 * size :]
        frame = lax.broadcasted_iota(jnp.int32, (height, 128), 0)[:, :1] + start
        weights, distance = attention_weights(query, keys, slope, frame, lengths)
        incoming = r.mixed_grad[block_rows, :]
        weight_grad = mm_right(incoming, values)
        delta = jnp.sum(weights * weight_grad, axis=-1, keepdims=True)
        score_grad = weights * (weight_grad - delta)
        raw = (score_grad * scale).astype(BF)
        joint_grad[block_rows, 0:size] = mm(raw, keys).astype(BF)
        key_grad[...] += mm_left(raw, query)
        value_grad[...] += mm_left(weights.astype(BF), incoming)
        return carry - jnp.sum(score_grad * distance, axis=0, keepdims=True)

    slope_row = lax.fori_loop(0, frames // height, step, jnp.zeros((1, frames), F32))
    joint_grad[:, size : 2 * size] = key_grad[...].astype(BF)
    joint_grad[:, 2 * size :] = value_grad[...].astype(BF)
    moved = r.moved1
    copies = {}
    for h in range(2):
        for j in (2, 3, 0, 1):
            copies[h, j] = mail.post(
                joint_grad.at[here.other_rows(j, h, rows), :], moved.at[1, h, j], here.sibling()
            )
            moved[0, h, j] = joint_grad[here.rows(j, h, rows), :]
    conv_sum.relay()
    in_sum.relay()
    qkv_shared.wait_recv()
    qkv_ready.wait()
    down_shared, up_shared = share(r.down1_src, r.down1_other), share(r.up1_src, r.up1_other)
    keep0_ready = mail.local(r.keep0_src, r.keep0)
    down1_ready = mail.local(r.down1_src, r.down1)
    up1_ready = mail.local(r.up1_src, r.up1)
    hidden0_ready = mail.local(r.hidden0_src, r.hidden0)
    sums = reduce(r.land1, RelayReduce)
    for p in (1, 0):
        for h in range(2):
            for j in (2 * p, 2 * p + 1):
                copies[h, j].wait_recv()
            value = mm_right(pair_of(moved.at[0], h, p), r.qkv[...])
            sums[h].put(p, value + mm_right(pair_of(moved.at[1], h, p), r.qkv_other[...]))
    for h in range(2):
        sums[h].relay()
    mixed_ready.wait()
    mail.settle(row_copies)
    row_copies = sides_grad(
        mail, here, r.mixed, r.branch1, r.out_parts, row_send.at[pl.ds(0, size), :], r.out_land
    )
    out_sum = RingSum(mail, here, r.out_parts, r.out_relay, r.out_sum_land)
    hidden1_ready.wait()
    mail.settle(column_copies)
    column_copies = slots_grad(
        mail, here, r.hidden1, moved, r.qkv_parts, column_send.at[:, pl.ds(0, 3 * size)], r.qkv_land
    )
    qkv_sum = RingSum(mail, here, r.qkv_parts, r.qkv_relay, r.qkv_sum_land)
    first_ready.wait()
    gain = scale_row(small, 1)
    sent, gain_parts = [], []
    for h in range(2):
        value_part, gain_part = norm_grad(r.first[part(h), :], gain, sums[h].total())
        gradient = r.grad[part(h), :] + value_part
        r.grad[part(h), :] = gradient
        gain_parts.append(gain_part)
        sent.append(spread(r.branch0, h, 0.5 * gradient))
    gain_part = gain_parts[0] + gain_parts[1]
    lane = lax.broadcasted_iota(jnp.int32, gain_part.shape, 1)
    slope_total = jnp.sum(slope_row, axis=1, keepdims=True)
    r.small_sum[...] = (
        r.small_sum[...] + at_row(1, gain_part) + at_row(5, jnp.where(lane == here.seq, slope_total, 0.0))
    )
    out_sum.relay()
    qkv_sum.relay()

    devices = [here.peer(j) for j in range(1, CHIPS)] + [here.cross(j) for j in range(CHIPS)]
    blocks = r.up2_out.shape[0]

    def swap(parts, got):
        return [mail.post(parts.at[span(device[0], blocks), :], got.at[i], device) for i, device in enumerate(devices)]

    def place(parts, got, out, copies, turn=0):
        lanes = 128
        groups = parts.shape[1] // lanes
        stride = out.shape[1] // groups
        for i in range(len(devices) + 1):
            if i:
                copies[i - 1].wait_recv()
            seq = devices[i - 1][0] if i else here.seq
            value = (got[i - 1] if i else parts[span(here.seq, blocks), :]).astype(F32)
            for g in range(groups):
                at = pl.ds(pl.multiple_of(g * stride + lax.rem(seq + turn * g, seqs) * lanes, lanes), lanes)
                out[:, at] = value[:, g * lanes : (g + 1) * lanes]

    down_shared.wait_recv()
    down1_ready.wait()
    keep0_ready.wait()
    ups, downs = (r.up1, r.up1_other), (r.down1, r.down1_other)
    act, act_grad = r.hidden2, r.hidden1
    for h in range(2):
        for p in range(2):
            feed_swish(r.keep0, act, h, p)
    sent[0].near()
    feed_slope(r.branch0, r.keep0, downs, act_grad, 0, 0)
    sent[1].near()
    sent[0].far()
    feed_slope(r.branch0, r.keep0, downs, act_grad, 0, 1)
    sent[1].far()
    mail.settle(row_copies + column_copies)
    down_grad(mail, here, r.branch0, act, r.down1_parts, r.down_send, r.down_land)
    down1 = RingSum(mail, here, r.down1_parts, r.down1_relay, r.down1_land)
    for p in (1, 0):
        feed_slope(r.branch0, r.keep0, downs, act_grad, 1, p)
    hidden0_ready.wait()
    up_grad(mail, here, r.hidden0, act_grad, r.up1_parts, r.up_send, r.up_land)
    up1 = RingSum(mail, here, r.up1_parts, r.up1_relay, r.up1_land)
    up_shared.wait_recv()
    up1_ready.wait()
    sums = reduce(r.land0)
    for h in range(2):
        for p in (1, 0):
            sums[h].put(p, feed_in(act_grad, ups, h, p))
    r.up2_sum[...] = up2.total().astype(BF)
    up2_copies = swap(r.up2_sum, r.up2_got)
    r.in_total[...] = in_sum.total().astype(BF)
    in_copies = swap(r.in_total, r.in_got)
    r.qkv_total[...] = qkv_sum.total().astype(BF)
    qkv_copies = swap(r.qkv_total, r.qkv_got)
    down1.relay()
    r.conv_out_grad[...] = conv_sum.total()
    mail.save(r.conv_out_grad, r.conv_grad_out)
    r.out_grad[...] = out_sum.total()
    mail.save(r.out_grad, r.attn_grad_out)
    for copy in kernel_copies:
        copy.wait_recv()
    kernel_total = r.kernel_part[...]
    for k in range(1, PLANES):
        kernel_total = kernel_total + r.kernel_land[k - 1]
    r.kernel_out[...] = kernel_total
    place(r.up2_sum, r.up2_got, r.up2_out, up2_copies, 1)
    mail.save(r.up2_out, r.up2_grad_out)
    up1.relay()
    gain = scale_row(small, 0)
    gain_parts = []
    for h in range(2):
        value_part, gain_part = norm_grad(r.frames[0, part(h), :].astype(F32), gain, sums[h].total())
        r.frames_grad[0, part(h), :] = r.grad[part(h), :] + value_part
        mail.save(r.frames_grad.at[0, part(h)], r.frames_grad_out.at[0, part(h)])
        gain_parts.append(gain_part)
    r.small_sum[...] = r.small_sum[...] + at_row(0, gain_parts[0] + gain_parts[1])
    small_copies = [
        mail.post(r.small_sum, r.small_land.at[k - 1], here.above(k)) for k in range(1, PLANES)
    ]
    r.down_moved[1] = down1.total().astype(BF)
    down1_wait = to_owner(1)
    place(r.in_total, r.in_got, r.in_out, in_copies)
    mail.save(r.in_out, r.in_grad_out)
    place(r.qkv_total, r.qkv_got, r.qkv_out, qkv_copies)
    mail.save(r.qkv_out, r.qkv_grad_out)
    down2_wait()
    r.down2_out[...] = r.down_got[0].astype(F32)
    mail.save(r.down2_out, r.down2_grad_out)
    r.up1_sum[...] = up1.total().astype(BF)
    up1_copies = swap(r.up1_sum, r.up1_got)
    for copy in small_copies:
        copy.wait_recv()
    total = r.small_sum[...]
    for k in range(1, PLANES):
        total = total + r.small_land[k - 1]
    r.small_mid[...] = total
    small_copies = [mail.post(r.small_mid, r.small_near.at[i], device) for i, device in enumerate(devices)]
    down1_wait()
    r.down1_out[...] = r.down_got[1].astype(F32)
    mail.save(r.down1_out, r.down1_grad_out)
    place(r.up1_sum, r.up1_got, r.up1_out, up1_copies, 1)
    mail.save(r.up1_out, r.up1_grad_out)
    for copy in small_copies:
        copy.wait_recv()
    total = r.small_mid[...]
    for i in range(len(devices)):
        total = total + r.small_near[i]
    r.small_out[...] = total
    mail.close()


def finish_kernel(*refs):
    count = (len(refs) - 7) // 2
    big, (small, kernel, cross) = refs[:count], refs[count : count + 3]
    outs, (gains_out, kernel_out, batch_out, slopes_out) = refs[count + 3 : 2 * count + 3], refs[2 * count + 3 :]
    for src, dst in zip(big, outs):
        dst[...] = src[...]
    seq, plane = lax.axis_index("seq"), lax.axis_index("fsdp")

    def own(ref, first, count, width, place):
        lanes = 128
        each = lanes // width
        block = ref[first : first + count, span(lax.div(place, each), lanes)]
        value = block[:, :width]
        for k in range(1, each):
            value = jnp.where(lax.rem(place, each) == k, block[:, k * width : (k + 1) * width], value)
        return value

    width = gains_out.shape[1]
    gains = gains_out.shape[0]
    gains_out[...] = own(small, 0, gains, width, seq * PLANES + plane)
    kernel_out[...] = own(kernel, 0, kernel_out.shape[0], width, plane)
    batch_out[...] = own(cross, 1, 1, width, plane)
    slopes_out[...] = small[gains : gains + 1, : slopes_out.shape[1]]


def launch(kernel, name, index, operands, results, scratch):
    names = list(operands) + list(results) + list(scratch) + ["send", "recv"]
    values = pl.pallas_call(
        functools.partial(kernel, names),
        name=name,
        out_shape=[jax.ShapeDtypeStruct(shape, kind) for shape, kind, _ in results.values()],
        in_specs=[pl.BlockSpec(memory_space=place) for _, place in operands.values()],
        out_specs=[pl.BlockSpec(memory_space=place) for _, _, place in results.values()],
        scratch_shapes=[pltpu.VMEM(shape, kind) for shape, kind in scratch.values()]
        + [pltpu.SemaphoreType.DMA((SLOTS,)), pltpu.SemaphoreType.DMA((SLOTS,))],
        compiler_params=pltpu.CompilerParams(
            collective_id=index, has_side_effects=True, vmem_limit_bytes=GRANT
        ),
    )(*[array for array, _ in operands.values()])
    return types.SimpleNamespace(**dict(zip(results, values)))


def plane_body(
    frames, lengths, up_first, down_first, joint_qkv, attn_out, conv_in, conv_kernel, batch_gain, conv_out,
    up_second, down_second, norm_gains, slopes, out_grad,
):
    seqs = lax.axis_size("seq")
    seq = lax.axis_index("seq")
    plane = lax.axis_index("fsdp")
    rows, width = frames.shape[1], frames.shape[2]
    length = rows * seqs
    heads = slopes.shape[0]
    size = width // heads
    channels = width // seqs
    hidden_units = up_first.shape[1]
    half = hidden_units // seqs
    taps = conv_kernel.shape[0]
    block = width // (seqs * PLANES)
    near_count = seqs - 1
    row_f = ((rows, width), F32)
    lines = rows // 2
    quad = ((2, CHIPS, lines, width), BF)
    stage = ((2, CHIPS - 1, lines, width), BF)
    acc = ((2, lines, width), F32)
    up, down = ((width, half), BF), ((half, width), BF)
    qkv, out = ((width, 3 * size), BF), ((size, width), BF)
    conv_i, conv_o = ((width, 2 * channels), BF), ((channels, width), BF)
    keep = ((2, CHIPS, lines, 2 * half), F32)
    act = ((2, CHIPS, lines, 2 * half), BF)
    joint = ((length, 3 * size), BF)
    mixed = ((2, 2, CHIPS, lines, size), BF)
    glu = ((2, CHIPS, lines, 4 * channels), F32)
    dense = ((length, channels), F32)
    padded = ((length + 2 * RIM, channels), F32)
    marks = ((taps + 1, length, channels), BF)
    bn = ((8, channels), F32)
    bn_land = ((PLANES - 1, 8, channels), F32)
    small_row = ((8, width), F32)
    small_all = ((PLANES, 16, norm_gains.shape[1]), F32)

    def parts(shape):
        return ((PLANES, shape[0][0] // PLANES, shape[0][1]), BF)

    def land(shape):
        return ((2, shape[0][0] // PLANES, shape[0][1]), BF)

    def relay(shape):
        return ((4, shape[0][0] // (2 * PLANES), shape[0][1]), BF)

    def summed(shape):
        return ((shape[0][0] // PLANES, shape[0][1]), BF)

    x_grad, up_rows, down_rows = ((1, rows, width), F32), ((block, hidden_units), F32), ((half // PLANES, width), F32)
    qkv_rows, in_rows, head_rows = ((block, 3 * width), F32), ((block, 2 * width), F32), ((size // PLANES, width), F32)
    a = launch(
        forward_kernel, "forward", 0,
        dict(
            frames=(frames, V), lengths=(lengths, S), gains=(norm_gains, V), taps=(conv_kernel, V),
            batch=(batch_gain, V), slopes=(slopes, S),
            up1_src=(up_first, H), down1_src=(down_first, H), qkv_src=(joint_qkv, H),
            out_src=(attn_out, H), in_src=(conv_in, H), conv_src=(conv_out, H),
            up2_src=(up_second, H), down2_src=(down_second, H), out_grad=(out_grad, V),
        ),
        dict(
            result_out=((1, rows, width), BF, H), third_grad_out=row_f + (H,), small_d=small_row + (V,),
            first_out=row_f + (H,), second_out=row_f + (H,), small=small_all + (V,),
            stats=bn + (V,), up2_parts_out=parts(up) + (H,), down2_parts_out=parts(down) + (H,),
            hidden0_out=quad + (H,), hidden1_out=quad + (H,), hidden2_out=quad + (H,),
            keep0_out=keep + (H,), joint_out=joint + (H,), mixed_out=mixed + (H,),
            glu_out=glu + (H,), gated_out=dense + (H,), standard_out=dense + (H,),
            swish_out=mixed + (H,), up1_out=up + (H,), down1_out=down + (H,), qkv_out=qkv + (H,),
            out_out=out + (H,), in_out=conv_i + (H,), conv_out_out=conv_o + (H,),
        ),
        dict(
            up1=up, up1_other=up, down1=down, down1_other=down, qkv=qkv, qkv_other=qkv,
            out=out, out_other=out, conv_in=conv_i, conv_in_other=conv_i, conv_out=conv_o,
            conv_out_other=conv_o, up2=up, up2_other=up, down2=down, down2_other=down,
            hidden0=quad, hidden1=quad, hidden2=quad, hidden3=quad, keep0=keep, keep3=keep,
            joint=joint, joint_stage=((2, CHIPS, lines, 3 * size), BF), mixed=mixed,
            mixed_stage=((2, CHIPS, lines, size), BF), glu=glu, gated=dense, padded=padded,
            marks=marks, gate_stage=((2, CHIPS, lines, channels), BF), gate_rows=((length, channels), BF),
            standard=dense, swish_rows=((length, channels), BF), swish=mixed, bn=bn, bn_land=bn_land,
            third=row_f, branch=quad, act=act, act_grad=act, result=((1, rows, width), BF), third_grad=row_f,
            first=row_f, second=row_f, up2_parts=parts(up), down2_parts=parts(down),
            stage=stage, land0=stage, land1=stage, land2=stage, land3=stage, land4=stage, acc=acc,
            down_send=down, down_land=down, up_send=up, up_land=up,
        ),
    )
    b = launch(
        backward_kernel, "backward", 1,
        dict(
            frames=(frames, V), lengths=(lengths, S), slopes=(slopes, S), small=(a.small, V),
            third_grad_src=(a.third_grad_out, H), small_d=(a.small_d, V), second_src=(a.second_out, H),
            stats=(a.stats, V), up2_parts_src=(a.up2_parts_out, H), down2_parts_src=(a.down2_parts_out, H),
            first_src=(a.first_out, H), hidden0_src=(a.hidden0_out, H),
            hidden1_src=(a.hidden1_out, H), hidden2_src=(a.hidden2_out, H),
            keep0_src=(a.keep0_out, H), joint_src=(a.joint_out, H), mixed_src=(a.mixed_out, H),
            glu_src=(a.glu_out, H), gated_src=(a.gated_out, H),
            standard_src=(a.standard_out, H), swish_src=(a.swish_out, H),
            up1_src=(a.up1_out, H), down1_src=(a.down1_out, H), qkv_src=(a.qkv_out, H),
            out_src=(a.out_out, H), conv_in_src=(a.in_out, H),
            conv_out_src=(a.conv_out_out, H),
        ),
        dict(
            frames_grad_out=x_grad + (H,), up1_grad_out=up_rows + (H,), up2_grad_out=up_rows + (H,),
            down1_grad_out=down_rows + (H,), down2_grad_out=down_rows + (H,), qkv_grad_out=qkv_rows + (H,),
            in_grad_out=in_rows + (H,), attn_grad_out=head_rows + (H,), conv_grad_out=head_rows + (H,),
            kernel_out=bn + (V,), cross=bn + (V,), small_out=small_row + (V,),
        ),
        dict(
            up1=up, up1_other=up, down1=down, down1_other=down, qkv=qkv, qkv_other=qkv,
            out=out, out_other=out, conv_in=conv_i, conv_in_other=conv_i, conv_out=conv_o,
            conv_out_other=conv_o, hidden0=quad, hidden1=quad, hidden2=quad, keep0=keep,
            joint=joint, mixed=mixed, glu=glu, gated=dense, standard=dense, swish=mixed,
            first=row_f, grad=row_f, acc=acc, third_grad=row_f, second=row_f, up2_parts=parts(up),
            down2_parts=parts(down), frames_grad=x_grad, up1_out=up_rows, up2_out=up_rows, down1_out=down_rows,
            down2_out=down_rows, qkv_out=qkv_rows, in_out=in_rows, out_grad=head_rows, conv_out_grad=head_rows, marks=marks, padded=padded,
            branch2=quad, branch1=quad, branch0=quad, swish_stage=((2, CHIPS, lines, channels), F32),
            swish_grad=dense, gate_grad=dense, moved2=((2, 2, CHIPS, lines, channels), F32),
            glu_grad=((2, 2, CHIPS, lines, 2 * channels), BF), bn=bn, bn_land=bn_land,
            conv_land=conv_o, in_land=conv_i,
            conv_parts=parts(conv_o), in_parts=parts(conv_i), conv_relay=relay(conv_o),
            in_relay=relay(conv_i), conv_sum_land=land(conv_o), in_sum_land=land(conv_i),
            kernel_part=bn, kernel_land=bn_land, small_sum=small_row,
            up2_relay=relay(up), up2_land=land(up), down2_relay=relay(down), down2_land=land(down),
            up2_sum=summed(up), down_moved=((2,) + summed(down)[0], BF), down_got=((2,) + summed(down)[0], BF),
            mixed_stage=((2, CHIPS, lines, size), BF), mixed_grad=((length, size), BF),
            joint_grad=joint, moved1=((2, 2, CHIPS, lines, 3 * size), BF), out_land=out, qkv_land=qkv, out_parts=parts(out), qkv_parts=parts(qkv), out_relay=relay(out),
            qkv_relay=relay(qkv), out_sum_land=land(out), qkv_sum_land=land(qkv),
            down_send=down, down_land=down,
            up_send=up, up_land=up, up1_parts=parts(up), down1_parts=parts(down),
            up1_relay=relay(up), up1_land=land(up), down1_relay=relay(down), down1_land=land(down),
            up1_sum=summed(up), up1_got=((near_count, block, half), BF),
            up2_got=((near_count, block, half), BF), in_total=summed(conv_i),
            in_got=((near_count, block, 2 * channels), BF), qkv_total=summed(qkv),
            qkv_got=((near_count, block, 3 * size), BF), small_land=((PLANES - 1, 8, width), F32),
            small_mid=small_row, small_near=((near_count, 8, width), F32),
            stage=stage, land0=stage, land1=stage, land2=stage,
        ),
    )
    big = (
        a.result_out, b.frames_grad_out, b.up1_grad_out, b.down1_grad_out, b.qkv_grad_out, b.attn_grad_out, b.in_grad_out,
        b.conv_grad_out, b.up2_grad_out, b.down2_grad_out,
    )
    shapes = [jax.ShapeDtypeStruct(array.shape, array.dtype) for array in big]
    shapes += [jax.ShapeDtypeStruct(shape, F32) for shape in ((norm_gains.shape[0], block), (taps, block), (1, block), (1, heads))]
    done = pl.pallas_call(
        finish_kernel,
        name="finish",
        out_shape=shapes,
        in_specs=[pl.BlockSpec(memory_space=V)] * (len(big) + 3),
        out_specs=[pl.BlockSpec(memory_space=V)] * len(shapes),
        compiler_params=pltpu.CompilerParams(vmem_limit_bytes=GRANT),
    )(*big, b.small_out, b.kernel_out, b.cross)
    (
        result, frames_grad, up1_grad, down1_grad, qkv_grad, attn_out_grad, in_grad, conv_out_grad, up2_grad, down2_grad,
        gains_grad, kernel_grad, batch_grad, slopes_grad,
    ) = done
    return (
        result, frames_grad, up1_grad, down1_grad, qkv_grad, attn_out_grad, in_grad, kernel_grad,
        batch_grad.reshape(-1), conv_out_grad, up2_grad, down2_grad, gains_grad, slopes_grad.reshape(-1),
    )


def solution(mesh):
    planar = mesh.shape["seq"] == 2 * CHIPS and mesh.shape["fsdp"] == PLANES
    chosen = plane_body if planar else body
    placed = (
        P("fsdp", "seq", None),
        P("fsdp", None),
        P("fsdp", None),
        P("fsdp", None),
        P("fsdp", None),
        P("fsdp", None),
        P("fsdp", None),
        P(None, "fsdp"),
        P("fsdp"),
        P("fsdp", None),
        P("fsdp", None),
        P("fsdp", None),
        P(None, "fsdp"),
        P(),
        P("fsdp", "seq", None),
    )
    return jax.shard_map(
        chosen,
        mesh=mesh,
        in_specs=placed,
        out_specs=(
            P("fsdp", "seq", None),
            P("fsdp", "seq", None),
            P(("seq", "fsdp"), None),
            P(("seq", "fsdp"), None),
            P(("seq", "fsdp"), None),
            P(("seq", "fsdp"), None),
            P(("seq", "fsdp"), None),
            P(None, ("seq", "fsdp")),
            P(("seq", "fsdp")),
            P(("seq", "fsdp"), None),
            P(("seq", "fsdp"), None),
            P(("seq", "fsdp"), None),
            P(None, ("seq", "fsdp")),
            P(),
        ),
        check_vma=False,
    )
```
